32 devices in a mesh: dp: 8 (over z, y), tensor: 4 (over x, core).
Axes of the slice: x: 2, y: 2, z: 4, core: 2. Of those that a mesh axis runs over, the one named last changes fastest.
Arguments:
- queries: bfloat16 [4096, 3072], P('dp', 'tensor'), may hold values from -6 to 6
- keys: bfloat16 [4096, 3072], P('dp', 'tensor'), may hold values from -6 to 6
- values: bfloat16 [4096, 3072], P('dp', 'tensor'), may hold values from -6 to 6
- out_grad: bfloat16 [4096, 3072], P('dp', 'tensor'), may hold values from -6 to 6
- lengths: int32 [32], replicated, may hold values from 1 to 512, 4096 in all
Outputs:
- attn_out: bfloat16 [4096, 3072], P('dp', 'tensor')
- query_grad: bfloat16 [4096, 3072], P('dp', 'tensor')
- key_grad: bfloat16 [4096, 3072], P('dp', 'tensor')
- value_grad: bfloat16 [4096, 3072], P('dp', 'tensor')
The draws below stay inside these ranges and needn't reach their ends.
Inputs may be any that keep to these rules, and one draw needn't show every extreme that they name: `lengths`: 32 token counts that sum to 4096, at least one image 512 long.
All inputs are finite; a program needn't handle non-finite values.
Results may differ from the reference program's by a relative error of at most 0.012.
Values may be sent and summed in bfloat16 or wider, within the bound.
No kernel may reach another device: no remote copies, remote signals or barrier semaphores. Data moves between devices by JAX's collectives and lax.ppermute only.
A program may use at most 64 MiB of HBM per device.

```python
import math
import jax
import jax.numpy as jnp
import numpy as np
from jax import lax

HEADS = 24
HEAD_DIM = 128
TOK_DEV = 512
MOST = 512
IMAGES = 32
TOKENS = 4096
N_DP = 8


def draw_queries(key, part):
    shape = (TOKENS, HEADS * HEAD_DIM)
    return jnp.clip(jax.random.normal(jax.random.fold_in(key, 21), shape, jnp.float32), -6.0, 6.0).astype(jnp.bfloat16)


def draw_keys(key, part):
    shape = (TOKENS, HEADS * HEAD_DIM)
    return jnp.clip(jax.random.normal(jax.random.fold_in(key, 31), shape, jnp.float32), -6.0, 6.0).astype(jnp.bfloat16)


def levels(key, extent, split, smallest, top_value):
    factor_of = 1.0
    for dim, blocks in split:
        steps = jax.random.uniform(jax.random.fold_in(jax.random.fold_in(key, 6), dim), (blocks,), jnp.float32, smallest / len(split), top_value / len(split))
        factor_of = factor_of * jnp.repeat(jnp.exp(steps), extent[dim] // blocks).reshape((-1,) + (1,) * (len(extent) - 1 - dim))
    return factor_of


def length_profile(amount, total, limit, skew):
    weights = [(1 << 20) // math.isqrt(rank ** skew) + 1 for rank in range(2, amount + 1)]
    rest, counts = total - limit - (amount - 1), [1] * (amount - 1)
    while rest > 0:
        free = [i for i in range(amount - 1) if counts[i] < limit]
        pool, left = sum([weights[i] for i in free]), rest
        for i in free:
            extra = min(limit - counts[i], max(1, left * weights[i] // pool), rest)
            counts[i] = counts[i] + extra
            rest = rest - extra
    return np.array([limit] + counts)


def ragged(rng, number_of, total, most, slope):
    if number_of == 2:
        one = jax.random.randint(rng, (), max(1, total - most), min(most, total - 1) + 1)
        return jnp.stack([one, total - one])
    sizes = jnp.asarray(length_profile(number_of, total, most, slope), jnp.int32)
    couples = (number_of - 1) // 2
    donor, taker = sizes[1:1 + 2 * couples:2], sizes[2:2 + 2 * couples:2]
    room = jnp.minimum(donor - 1, most - taker)
    shifted = jax.random.randint(jax.random.fold_in(rng, 1), (couples,), 0, 1 << 20) % (room + 1)
    sizes = sizes.at[1:1 + 2 * couples:2].set(donor - shifted).at[2:2 + 2 * couples:2].set(taker + shifted)
    return sizes[jax.random.permutation(jax.random.fold_in(rng, 2), number_of)]


def centred(stream_key, extent, scale, bound, shards=(), kind=jnp.bfloat16):
    factor_of = levels(stream_key, extent, shards, -0.22, 0.18) if shards else 1.0
    values = jax.random.normal(stream_key, extent, jnp.float32) * scale * factor_of
    return jnp.minimum(jnp.maximum(values, -bound), bound).astype(kind)


def setup_inputs(seed: int = 0) -> dict:
    arg_keys = jax.random.split(jax.random.key(seed), 6)
    queries = draw_queries(jax.random.fold_in(arg_keys[5], 71), 0)
    keys = draw_keys(jax.random.fold_in(arg_keys[5], 71), 0)
    values = centred(arg_keys[2], (TOKENS, HEADS * HEAD_DIM), 1.0, 6.0, ((0, 8), (1, 4)))
    out_grad = centred(arg_keys[3], (TOKENS, HEADS * HEAD_DIM), 1.0, 6.0, ((0, 8), (1, 4)))
    lengths = ragged(arg_keys[4], IMAGES, TOKENS, MOST, 2).astype(jnp.int32)
    return {"queries": queries, "keys": keys, "values": values, "out_grad": out_grad, "lengths": lengths}


def image_masks(lengths, first_row, count, total_rows, span):
    ends = jnp.cumsum(lengths).astype(jnp.int32)
    starts = ends - lengths.astype(jnp.int32)
    positions = first_row + jnp.arange(count, dtype=jnp.int32)
    begin = lax.optimization_barrier(jnp.max(jnp.where(starts[None, :] <= positions[:, None], starts[None, :], -1), axis=1))
    valid = positions < total_rows
    owned_rows = valid & (begin >= first_row) & (begin < first_row + span)
    window_mask = owned_rows[:, None] & valid[None, :] & (begin[:, None] == begin[None, :])
    return (window_mask, owned_rows)

def head_attention(operands, window_mask, owned_rows, factor):
    query_head, key_head, value_head, grad_head = operands
    scores = jnp.dot(query_head, key_head.T, preferred_element_type=jnp.float32) * factor
    scores = jnp.where(window_mask, scores, -1e+30)
    top_score = lax.optimization_barrier(jnp.max(scores, axis=1, keepdims=True))
    weights = jnp.where(window_mask, jnp.exp(scores - top_score), 0.0)
    totals = lax.optimization_barrier(jnp.sum(weights, axis=1, keepdims=True))
    totals = jnp.where(owned_rows[:, None], totals, 1.0)
    probs = weights / totals
    probs_low = probs.astype(jnp.bfloat16)
    result = jnp.dot(probs_low, value_head, preferred_element_type=jnp.float32).astype(jnp.bfloat16)
    grad_probs = jnp.dot(grad_head, value_head.T, preferred_element_type=jnp.float32)
    centre = lax.optimization_barrier(jnp.sum(grad_head.astype(jnp.float32) * result.astype(jnp.float32), axis=1, keepdims=True))
    grad_scores = (probs * (grad_probs - centre)).astype(jnp.bfloat16)
    grad_query = (jnp.dot(grad_scores, key_head, preferred_element_type=jnp.float32) * factor).astype(jnp.bfloat16)
    grad_key = (jnp.dot(grad_scores.T, query_head, preferred_element_type=jnp.float32) * factor).astype(jnp.bfloat16)
    grad_value = jnp.dot(probs_low.T, grad_head, preferred_element_type=jnp.float32).astype(jnp.bfloat16)
    return (result, grad_query, grad_key, grad_value)

def all_heads(window, window_mask, owned_rows):
    count = window[0].shape[0]
    factor = 1.0 / math.sqrt(HEAD_DIM)

    def split_heads(block):
        return block.reshape(count, -1, HEAD_DIM).transpose(1, 0, 2)
    stacked = (split_heads(window[0]), split_heads(window[1]), split_heads(window[2]), split_heads(window[3]))

    def one_head(operands):
        return head_attention(operands, window_mask, owned_rows, factor)
    outputs = lax.map(one_head, stacked)
    return tuple((output.transpose(1, 0, 2).reshape(count, -1) for output in outputs))

def reference(queries, keys, values, out_grad, lengths):
    rows = TOK_DEV
    padded = tuple((jnp.concatenate([array, jnp.zeros((rows, array.shape[1]), array.dtype)], axis=0) for array in (queries, keys, values, out_grad)))

    def window_results(index):
        first_row = (index * rows).astype(jnp.int32)
        window = tuple((lax.dynamic_slice_in_dim(array, first_row, 2 * rows, 0) for array in padded))
        window_mask, owned_rows = image_masks(lengths, first_row, 2 * rows, TOKENS, rows)
        return all_heads(window, window_mask, owned_rows)
    results = lax.map(window_results, jnp.arange(N_DP, dtype=jnp.int32))
    combined = []
    for stacked in results:
        own_part = stacked[:, :rows]
        spill = stacked[:, rows:]
        moved = jnp.concatenate([jnp.zeros_like(spill[:1]), spill[:-1]], axis=0)
        combined.append((own_part + moved).reshape(TOKENS, -1))
    return (combined[0], combined[1], combined[2], combined[3])
```

```python
import functools
import math

import jax
import jax.numpy as jnp
from jax import lax
from jax.experimental import pallas as pl
from jax.experimental.pallas import tpu as pltpu
from jax.sharding import PartitionSpec as P

HEAD_DIM = 128
TILE = 16
CHUNK = 256
FACTOR = 1.0 / math.sqrt(HEAD_DIM)
LOG2E = 1.4426950408889634
VMEM_LIMIT = 48 * 1024 * 1024

A_BELOW, C_BELOW, HERE_BELOW, THERE_BELOW, A_ABOVE, C_ABOVE, HERE_ABOVE, THERE_ABOVE = range(8)


def round_up(value):
    return (value + (TILE - 1)) // TILE * TILE


def worst_case_rows(rows, heads):
    worst = 0
    for before in range(TILE, rows + 1, TILE):
        for after in range(TILE, rows + TILE - before + 1, TILE):
            needed = min(max(after * low, before * (heads - low)) for low in range(heads + 1))
            worst = max(worst, needed)
    return worst


def image_edges(lengths):
    ends = jnp.cumsum(lengths)
    return ends - lengths, ends


def crossings(lengths, rows, blocks):
    starts, ends = image_edges(lengths)
    edges = rows * jnp.arange(1, blocks, dtype=jnp.int32)
    across = (starts[None, :] < edges[:, None]) & (ends[None, :] > edges[:, None])
    before = jnp.max(jnp.where(across, edges[:, None] - starts[None, :], 0), axis=1)
    after = jnp.max(jnp.where(across, ends[None, :] - edges[:, None], 0), axis=1)
    return before, after


def device_plan(lengths, rows, blocks, heads, down_rows, up_rows):
    before, after = crossings(lengths, rows, blocks)
    low = jnp.arange(heads + 1, dtype=jnp.int32)[None, :]
    fits = (round_up(after)[:, None] * low <= down_rows) & (
        round_up(before)[:, None] * (heads - low) <= up_rows
    )
    cost = jnp.abs(2 * low - heads) * 2 + (2 * low > heads) + jnp.where(fits, 0, 1000)
    chosen = jnp.argmin(cost, axis=1).astype(jnp.int32)
    crossed = before > 0
    at_lower = jnp.where(crossed, chosen, 0)
    at_upper = jnp.where(crossed, heads - chosen, 0)
    table = jnp.pad(jnp.stack([before, after, at_lower, at_upper], axis=1), ((1, 1), (0, 0)))
    return lax.dynamic_slice(table, (lax.axis_index("dp"), 0), (2, 4)).reshape(8)


def tiles(start, size):
    return pl.ds(pl.multiple_of(start, TILE), pl.multiple_of(size, TILE))


def lanes(head):
    return pl.ds(pl.multiple_of(head * HEAD_DIM, HEAD_DIM), HEAD_DIM)


def attention(query, key, value, grad, mask_columns, store):
    count = query.shape[0]
    value_t = value.T
    key_t = key.T
    grad_t = grad.T
    grad_key = jnp.zeros((count, HEAD_DIM), jnp.float32)
    grad_value = jnp.zeros((count, HEAD_DIM), jnp.float32)
    across = (((1,), (1,)), ((), ()))
    for first in range(0, count, CHUNK):
        cols = slice(first, first + CHUNK)
        scores = lax.dot_general(key, query[cols], across, preferred_element_type=jnp.float32)
        scores = jnp.where(mask_columns(cols), scores, -1e30)
        top = jnp.max(scores, axis=0, keepdims=True)
        weights = jnp.exp2((scores - top) * (FACTOR * LOG2E))
        total = jnp.sum(weights, axis=0, keepdims=True)
        probs = weights * (1.0 / total)
        probs_low = probs.astype(jnp.bfloat16)
        result_t = jnp.dot(value_t, probs_low, preferred_element_type=jnp.float32).astype(
            jnp.bfloat16
        )
        grad_probs = lax.dot_general(
            value, grad[cols], across, preferred_element_type=jnp.float32
        )
        centre = jnp.sum(
            grad_t[:, cols].astype(jnp.float32) * result_t.astype(jnp.float32),
            axis=0,
            keepdims=True,
        )
        grad_scores = (probs * (grad_probs - centre)).astype(jnp.bfloat16)
        grad_query_t = jnp.dot(key_t, grad_scores, preferred_element_type=jnp.float32) * FACTOR
        grad_key += jnp.dot(grad_scores, query[cols], preferred_element_type=jnp.float32)
        grad_value += jnp.dot(probs_low, grad[cols], preferred_element_type=jnp.float32)
        store(0, cols, result_t.T)
        store(1, cols, grad_query_t.astype(jnp.bfloat16).T)
    store(2, slice(None), (grad_key * FACTOR).astype(jnp.bfloat16))
    store(3, slice(None), grad_value.astype(jnp.bfloat16))


def local_kernel(image_ref, query_ref, key_ref, value_ref, grad_ref, *outs):
    count = query_ref.shape[0]
    image_row = image_ref[...]
    image_col = jnp.broadcast_to(image_row, (8, count)).T[:, :1]

    def store(which, rows, part):
        outs[which][rows, :] = part

    attention(
        query_ref[...],
        key_ref[...],
        value_ref[...],
        grad_ref[...],
        lambda cols: image_col == image_row[:, cols],
        store,
    )


def local_attention(image, arrays):
    rows, width = arrays[0].shape
    heads = width // HEAD_DIM
    block = pl.BlockSpec((rows, HEAD_DIM), lambda head: (0, head))
    return pl.pallas_call(
        local_kernel,
        grid=(heads,),
        in_specs=[pl.BlockSpec((1, rows), lambda head: (0, 0))] + [block] * 4,
        out_specs=[block] * 4,
        out_shape=[jax.ShapeDtypeStruct((rows, width), jnp.bfloat16)] * 4,
        compiler_params=pltpu.CompilerParams(vmem_limit_bytes=VMEM_LIMIT),
        cost_estimate=pl.CostEstimate(
            flops=12 * rows * rows * width, bytes_accessed=16 * rows * width, transcendentals=0
        ),
        name="local_images",
    )(image, *arrays)


def pack_kernel(plan, query, key, value, grad, down, up, down_sem, up_sem):
    rows, width = query.shape
    heads = width // HEAD_DIM
    arrays = (query, key, value, grad)
    after = round_up(plan[C_BELOW])
    before = round_up(plan[A_ABOVE])
    to_lower = plan[HERE_BELOW]
    to_upper = plan[THERE_ABOVE]

    def down_copy(head, which):
        return pltpu.make_async_copy(
            arrays[which].at[tiles(0, after), lanes(head)],
            down.at[tiles(head * after, after), lanes(which)],
            down_sem.at[head, which],
        )

    def up_copy(slot, which):
        return pltpu.make_async_copy(
            arrays[which].at[tiles(rows - before, before), lanes(heads - to_upper + slot)],
            up.at[tiles(slot * before, before), lanes(which)],
            up_sem.at[slot, which],
        )

    def each(action):
        for head in range(heads):
            @pl.when(head < to_lower)
            def _():
                for which in range(4):
                    action(down_copy(head, which))

            @pl.when(head < to_upper)
            def _():
                for which in range(4):
                    action(up_copy(head, which))

    each(lambda copy: copy.start())
    each(lambda copy: copy.wait())


def pack(plan, arrays, down_rows, up_rows):
    heads = arrays[0].shape[1] // HEAD_DIM
    anywhere = pl.BlockSpec(memory_space=pl.ANY)
    return pl.pallas_call(
        pack_kernel,
        in_specs=[pl.BlockSpec(memory_space=pltpu.SMEM)] + [anywhere] * 4,
        out_specs=[anywhere] * 2,
        out_shape=[
            jax.ShapeDtypeStruct((down_rows, 4 * HEAD_DIM), jnp.bfloat16),
            jax.ShapeDtypeStruct((up_rows, 4 * HEAD_DIM), jnp.bfloat16),
        ],
        scratch_shapes=[pltpu.SemaphoreType.DMA((heads, 4)), pltpu.SemaphoreType.DMA((heads, 4))],
        name="pack",
    )(plan, *arrays)


def crossing_kernel(
    plan, query, key, value, grad, from_above, from_below, back_up, back_down, done,
    first_part, last_part, window, result, in_sem, out_sem,
):
    rows, width = query.shape
    heads = width // HEAD_DIM
    arrays = (query, key, value, grad)
    jobs_above = plan[HERE_ABOVE]
    jobs_below = plan[THERE_BELOW]
    jobs = jobs_above + jobs_below

    def describe(job):
        above = job < jobs_above
        slot = jnp.where(above, job, job - jobs_above)
        head = jnp.where(above, job, heads - jobs_below + slot)
        before = jnp.where(above, plan[A_ABOVE], plan[A_BELOW])
        after = jnp.where(above, plan[C_ABOVE], plan[C_BELOW])
        return above, slot, head, before, after

    def fetch(job, action):
        above, slot, head, before, after = describe(job)
        before = round_up(before)
        after = round_up(after)
        buffer = lax.rem(job, 2)
        first = first_part.at[buffer]
        last = last_part.at[buffer]

        @pl.when(above)
        def _():
            for which in range(4):
                action(pltpu.make_async_copy(
                    arrays[which].at[tiles(rows - before, before), lanes(head)],
                    last.at[tiles(rows - before, before), lanes(which)],
                    in_sem.at[buffer, which],
                ))
            action(pltpu.make_async_copy(
                from_above.at[tiles(slot * after, after)],
                first.at[tiles(0, after)],
                in_sem.at[buffer, 4],
            ))

        @pl.when(jnp.logical_not(above))
        def _():
            for which in range(4):
                action(pltpu.make_async_copy(
                    arrays[which].at[tiles(0, after), lanes(head)],
                    first.at[tiles(0, after), lanes(which)],
                    in_sem.at[buffer, which],
                ))
            action(pltpu.make_async_copy(
                from_below.at[tiles(slot * before, before)],
                last.at[tiles(rows - before, before)],
                in_sem.at[buffer, 4],
            ))

    def deliver(job, action):
        above, slot, _, before, after = describe(job)
        before = round_up(before)
        after = round_up(after)
        buffer = lax.rem(job, 2)
        action(pltpu.make_async_copy(result.at[buffer], done.at[job], out_sem.at[buffer, 0]))

        @pl.when(above)
        def _():
            action(pltpu.make_async_copy(
                result.at[buffer, tiles(0, after)],
                back_up.at[tiles(slot * after, after)],
                out_sem.at[buffer, 1],
            ))

        @pl.when(jnp.logical_not(above))
        def _():
            action(pltpu.make_async_copy(
                result.at[buffer, tiles(rows - before, before)],
                back_down.at[tiles(slot * before, before)],
                out_sem.at[buffer, 1],
            ))

    start = lambda copy: copy.start()
    wait = lambda copy: copy.wait()

    @pl.when(jobs > 0)
    def _():
        fetch(0, start)

    def one_job(job, carry):
        buffer = lax.rem(job, 2)
        _, _, _, before, after = describe(job)

        @pl.when(job + 1 < jobs)
        def _():
            fetch(job + 1, start)

        fetch(job, wait)

        @pl.when(job >= 2)
        def _():
            deliver(job - 2, wait)

        position = lax.broadcasted_iota(jnp.int32, (rows, HEAD_DIM), 0)
        in_first = position < after
        in_last = position >= rows - before
        zero = jnp.zeros((rows, HEAD_DIM), jnp.bfloat16)
        operands = []
        for which in range(4):
            columns = slice(which * HEAD_DIM, (which + 1) * HEAD_DIM)
            operands.append(jnp.where(
                in_first,
                first_part[buffer, :, columns],
                jnp.where(in_last, last_part[buffer, :, columns], zero),
            ))
        key_position = lax.broadcasted_iota(jnp.int32, (rows, 1), 0)
        in_image = (key_position < after) | (key_position >= rows - before)

        def store(which, part_rows, part):
            result[buffer, part_rows, which * HEAD_DIM:(which + 1) * HEAD_DIM] = part

        attention(*operands, lambda cols: in_image, store)
        deliver(job, start)
        return carry

    lax.fori_loop(0, jobs, one_job, 0)

    @pl.when(jobs >= 2)
    def _():
        deliver(jobs - 2, wait)

    @pl.when(jobs >= 1)
    def _():
        deliver(jobs - 1, wait)


def crossing_images(plan, arrays, from_above, from_below):
    rows, width = arrays[0].shape
    heads = width // HEAD_DIM
    four = 4 * HEAD_DIM
    anywhere = pl.BlockSpec(memory_space=pl.ANY)
    return pl.pallas_call(
        crossing_kernel,
        in_specs=[pl.BlockSpec(memory_space=pltpu.SMEM)] + [anywhere] * 6,
        out_specs=[anywhere] * 3,
        out_shape=[
            jax.ShapeDtypeStruct(from_above.shape, jnp.bfloat16),
            jax.ShapeDtypeStruct(from_below.shape, jnp.bfloat16),
            jax.ShapeDtypeStruct((2 * heads, rows, four), jnp.bfloat16),
        ],
        scratch_shapes=[
            pltpu.VMEM((2, rows, four), jnp.bfloat16),
            pltpu.VMEM((2, rows, four), jnp.bfloat16),
            pltpu.VMEM((rows, four), jnp.bfloat16),
            pltpu.VMEM((2, rows, four), jnp.bfloat16),
            pltpu.SemaphoreType.DMA((2, 5)),
            pltpu.SemaphoreType.DMA((2, 2)),
        ],
        compiler_params=pltpu.CompilerParams(vmem_limit_bytes=VMEM_LIMIT),
        name="crossing_images",
    )(plan, *arrays, from_above, from_below)


def merge_kernel(
    plan, done, from_above, from_below, local0, local1, local2, local3, *rest
):
    outs = rest[:4]
    first_part, last_part, sems = rest[4:]
    head = pl.program_id(0)
    heads = pl.num_programs(0)
    rows = local0.shape[0]
    after = plan[C_BELOW]
    before = plan[A_ABOVE]
    after_tiles = round_up(after)
    before_tiles = round_up(before)
    low_here = plan[HERE_BELOW]
    here_above = plan[HERE_ABOVE]
    there_above = plan[THERE_ABOVE]

    def each(which_head, action):
        buffer = lax.rem(which_head, 2)
        first = first_part.at[buffer, tiles(0, after_tiles)]
        last = last_part.at[buffer, tiles(rows - before_tiles, before_tiles)]

        @pl.when((after > 0) & (which_head < low_here))
        def _():
            action(pltpu.make_async_copy(
                from_below.at[tiles(which_head * after_tiles, after_tiles)],
                first, sems.at[buffer, 0]))

        @pl.when((after > 0) & (which_head >= low_here))
        def _():
            action(pltpu.make_async_copy(
                done.at[here_above + which_head - low_here, tiles(0, after_tiles)],
                first, sems.at[buffer, 0]))

        @pl.when((before > 0) & (which_head < here_above))
        def _():
            action(pltpu.make_async_copy(
                done.at[which_head, tiles(rows - before_tiles, before_tiles)],
                last, sems.at[buffer, 1]))

        @pl.when((before > 0) & (which_head >= here_above))
        def _():
            action(pltpu.make_async_copy(
                from_above.at[tiles((which_head - here_above) * before_tiles, before_tiles)],
                last, sems.at[buffer, 1]))

    @pl.when(head == 0)
    def _():
        each(head, lambda copy: copy.start())

    @pl.when(head + 1 < heads)
    def _():
        each(head + 1, lambda copy: copy.start())

    each(head, lambda copy: copy.wait())
    buffer = lax.rem(head, 2)
    position = lax.broadcasted_iota(jnp.int32, (rows, HEAD_DIM), 0)
    for which, (local, out) in enumerate(zip((local0, local1, local2, local3), outs)):
        columns = slice(which * HEAD_DIM, (which + 1) * HEAD_DIM)
        out[...] = jnp.where(
            position < after,
            first_part[buffer, :, columns],
            jnp.where(position >= rows - before, last_part[buffer, :, columns], local[...]),
        )


def merge(plan, done, from_above, from_below, local):
    rows, width = local[0].shape
    heads = width // HEAD_DIM
    anywhere = pl.BlockSpec(memory_space=pl.ANY)
    block = pl.BlockSpec((rows, HEAD_DIM), lambda head: (0, head))
    four = 4 * HEAD_DIM
    return pl.pallas_call(
        merge_kernel,
        grid=(heads,),
        in_specs=[pl.BlockSpec(memory_space=pltpu.SMEM)] + [anywhere] * 3 + [block] * 4,
        out_specs=[block] * 4,
        out_shape=[jax.ShapeDtypeStruct((rows, width), jnp.bfloat16)] * 4,
        scratch_shapes=[
            pltpu.VMEM((2, rows, four), jnp.bfloat16),
            pltpu.VMEM((2, rows, four), jnp.bfloat16),
            pltpu.SemaphoreType.DMA((2, 2)),
        ],
        compiler_params=pltpu.CompilerParams(vmem_limit_bytes=VMEM_LIMIT),
        name="merge",
    )(plan, done, from_above, from_below, *local)


def passed_along(value, steps):
    count = lax.axis_size("dp")
    leading, last = max(0, -steps), min(count, count - steps)
    return lax.ppermute(value, "dp", [(source, source + steps) for source in range(leading, last)])


def body(queries, keys, values, out_grad, lengths):
    rows, width = queries.shape
    heads = width // HEAD_DIM
    blocks = lax.axis_size("dp")
    arrays = (queries, keys, values, out_grad)
    packed_rows = worst_case_rows(rows, heads)
    plan = device_plan(lengths, rows, blocks, heads, packed_rows, packed_rows)
    starts, _ = image_edges(lengths)
    position = lax.axis_index("dp") * rows + jnp.arange(rows, dtype=jnp.int32)
    image = jnp.max(jnp.where(starts[:, None] <= position[None, :], starts[:, None], -1), axis=0)
    image = image.astype(jnp.float32)[None, :]

    down, up = pack(plan, arrays, packed_rows, packed_rows)
    from_above = passed_along(down, -1)
    from_below = passed_along(up, 1)
    local = local_attention(image, arrays)
    back_up, back_down, done = crossing_images(plan, arrays, from_above, from_below)
    returned_below = passed_along(back_up, 1)
    returned_above = passed_along(back_down, -1)
    return tuple(merge(plan, done, returned_above, returned_below, local))


def solution(mesh):
    in_specs = (P("dp", "tensor"), P("dp", "tensor"), P("dp", "tensor"), P("dp", "tensor"), P())
    out_specs = (P("dp", "tensor"), P("dp", "tensor"), P("dp", "tensor"), P("dp", "tensor"))
    return jax.shard_map(body, mesh=mesh, in_specs=in_specs, out_specs=out_specs, check_vma=False)
```

```python
import functools
import math

import jax
import jax.numpy as jnp
from jax import lax
from jax.experimental import pallas as pl
from jax.experimental.pallas import tpu as pltpu
from jax.sharding import PartitionSpec as P

HEAD_DIM = 128
TILE = 16
CHUNK = 256
FACTOR = 1.0 / math.sqrt(HEAD_DIM)
LOG2E = 1.4426950408889634
VMEM_LIMIT = 56 * 1024 * 1024

A_BELOW, C_BELOW, HERE_BELOW, THERE_BELOW, A_ABOVE, C_ABOVE, HERE_ABOVE, THERE_ABOVE, MENU = range(9)

MENU_UNITS = (
    (6, 9), (9, 10), (15, 2), (15, 6), (6, 15), (0, 18), (12, 11), (15, 10), (5, 20),
)


def round_up(value):
    return (value + (TILE - 1)) // TILE * TILE


def worst_case_rows(rows, heads):
    worst = 0
    for before in range(TILE, rows + 1, TILE):
        for after in range(TILE, rows + TILE - before + 1, TILE):
            needed = min(max(after * low, before * (heads - low)) for low in range(heads + 1))
            worst = max(worst, needed)
    return worst


def size_menu(rows, heads):
    unit = rows * heads // 48
    most = worst_case_rows(rows, heads)
    pairs = {(down * unit, up * unit) for down, up in MENU_UNITS}
    pairs = sorted((pair for pair in pairs if sum(pair) < 2 * most), key=lambda pair: (sum(pair), pair))
    return pairs + [(most, most)]


def plan_kernel(rows, heads, blocks, menu, lengths, plan, before_edge, after_edge):
    def clear(edge, carry):
        before_edge[edge] = 0
        after_edge[edge] = 0
        return carry

    lax.fori_loop(0, blocks + 1, clear, 0)

    def place(image, start):
        end = start + lengths[image]
        edge = (end - 1) // rows

        @pl.when(edge > start // rows)
        def _():
            before_edge[edge] = edge * rows - start
            after_edge[edge] = end - edge * rows

        return end

    lax.fori_loop(0, lengths.shape[0], place, 0)

    entry = lax.broadcasted_iota(jnp.int32, (8, 128), 1)
    down_limit = jnp.full((8, 128), -1, jnp.int32)
    up_limit = jnp.full((8, 128), -1, jnp.int32)
    for number, (down, up) in enumerate(menu):
        down_limit = jnp.where(entry == number, down, down_limit)
        up_limit = jnp.where(entry == number, up, up_limit)

    def check(edge, fits):
        after = round_up(after_edge[edge])
        before = round_up(before_edge[edge])
        taken = jnp.zeros((8, 128), jnp.int32)
        for count in range(1, heads + 1):
            taken += jnp.where(after * count <= down_limit, 1, 0)
            taken += jnp.where(before * count <= up_limit, 1, 0)
        return jnp.minimum(fits, jnp.where(taken >= heads, 1, 0))

    fits = lax.fori_loop(1, blocks, check, jnp.ones((8, 128), jnp.int32))
    chosen = jnp.min(jnp.where(fits == 1, entry, len(menu) - 1))
    down_rows = jnp.int32(menu[-1][0])
    up_rows = jnp.int32(menu[-1][1])
    for number, (down, up) in enumerate(menu[:-1]):
        down_rows = jnp.where(chosen == number, down, down_rows)
        up_rows = jnp.where(chosen == number, up, up_rows)
    plan[MENU] = chosen

    block = lax.axis_index("dp")
    for field, edge in ((A_BELOW, block), (A_ABOVE, block + 1)):
        before = before_edge[edge]
        after = after_edge[edge]
        most = jnp.int32(0)
        least = jnp.int32(heads)
        for count in range(1, heads + 1):
            most += jnp.where(round_up(after) * count <= down_rows, 1, 0)
            least -= jnp.where(round_up(before) * count <= up_rows, 1, 0)
        low = jnp.clip(jnp.int32(heads // 2), least, most)
        plan[field] = before
        plan[field + 1] = after
        plan[field + 2] = jnp.where(before > 0, low, 0)
        plan[field + 3] = jnp.where(before > 0, heads - low, 0)


def make_plan(lengths, rows, heads, blocks, menu):
    scalars = pl.BlockSpec(memory_space=pltpu.SMEM)
    return pl.pallas_call(
        functools.partial(plan_kernel, rows, heads, blocks, menu),
        in_specs=[scalars],
        out_specs=scalars,
        out_shape=jax.ShapeDtypeStruct((MENU + 1,), jnp.int32),
        scratch_shapes=[pltpu.SMEM((blocks + 1,), jnp.int32), pltpu.SMEM((blocks + 1,), jnp.int32)],
        name="plan",
    )(lengths)


def tiles(start, size):
    return pl.ds(pl.multiple_of(start, TILE), pl.multiple_of(size, TILE))


def lanes(head):
    return pl.ds(pl.multiple_of(head * HEAD_DIM, HEAD_DIM), HEAD_DIM)


def attention(query, key, value, grad, mask_columns, store):
    count = query.shape[0]
    value_t = value.T
    key_t = key.T
    grad_t = grad.T
    grad_key = jnp.zeros((count, HEAD_DIM), jnp.float32)
    grad_value = jnp.zeros((count, HEAD_DIM), jnp.float32)
    across = (((1,), (1,)), ((), ()))
    for first in range(0, count, CHUNK):
        cols = slice(first, first + CHUNK)
        scores = lax.dot_general(key, query[cols], across, preferred_element_type=jnp.float32)
        scores = jnp.where(mask_columns(cols), scores, -1e30)
        top = jnp.max(scores, axis=0, keepdims=True)
        weights = jnp.exp2((scores - top) * (FACTOR * LOG2E))
        total = jnp.sum(weights, axis=0, keepdims=True)
        probs = weights * (1.0 / total)
        probs_low = probs.astype(jnp.bfloat16)
        result_t = jnp.dot(value_t, probs_low, preferred_element_type=jnp.float32).astype(
            jnp.bfloat16
        )
        grad_probs = lax.dot_general(
            value, grad[cols], across, preferred_element_type=jnp.float32
        )
        centre = jnp.sum(
            grad_t[:, cols].astype(jnp.float32) * result_t.astype(jnp.float32),
            axis=0,
            keepdims=True,
        )
        grad_scores = (probs * (grad_probs - centre)).astype(jnp.bfloat16)
        grad_query_t = jnp.dot(key_t, grad_scores, preferred_element_type=jnp.float32) * FACTOR
        grad_key += jnp.dot(grad_scores, query[cols], preferred_element_type=jnp.float32)
        grad_value += jnp.dot(probs_low, grad[cols], preferred_element_type=jnp.float32)
        store(0, cols, result_t.T)
        store(1, cols, grad_query_t.astype(jnp.bfloat16).T)
    store(2, slice(None), (grad_key * FACTOR).astype(jnp.bfloat16))
    store(3, slice(None), grad_value.astype(jnp.bfloat16))


def local_kernel(lengths, query_ref, key_ref, value_ref, grad_ref, *rest):
    outs = rest[:4]
    image_rows, = rest[4:]
    count = query_ref.shape[0]

    @pl.when(pl.program_id(0) == 0)
    def _():
        position = lax.axis_index("dp") * count + lax.broadcasted_iota(jnp.int32, (8, count), 1)

        def place(image, carry):
            start, begin = carry
            return start + lengths[image], jnp.where(position >= start, start, begin)

        first = (jnp.int32(0), jnp.zeros((8, count), jnp.int32))
        _, begin = lax.fori_loop(0, lengths.shape[0], place, first)
        image_rows[...] = begin.astype(jnp.float32)

    image_row = image_rows[:1]
    image_col = image_rows[...].T[:, :1]

    def store(which, rows, part):
        outs[which][rows, :] = part

    attention(
        query_ref[...],
        key_ref[...],
        value_ref[...],
        grad_ref[...],
        lambda cols: image_col == image_row[:, cols],
        store,
    )


def local_attention(lengths, arrays):
    rows, width = arrays[0].shape
    heads = width // HEAD_DIM
    block = pl.BlockSpec((rows, HEAD_DIM), lambda head: (0, head))
    return pl.pallas_call(
        local_kernel,
        grid=(heads,),
        in_specs=[pl.BlockSpec(memory_space=pltpu.SMEM)] + [block] * 4,
        out_specs=[block] * 4,
        out_shape=[jax.ShapeDtypeStruct((rows, width), jnp.bfloat16)] * 4,
        scratch_shapes=[pltpu.VMEM((8, rows), jnp.float32)],
        compiler_params=pltpu.CompilerParams(vmem_limit_bytes=VMEM_LIMIT),
        cost_estimate=pl.CostEstimate(
            flops=12 * rows * rows * width, bytes_accessed=16 * rows * width, transcendentals=0
        ),
        name="local_images",
    )(lengths, *arrays)


START = lambda copy: copy.start()
WAIT = lambda copy: copy.wait()


def pack_kernel(down_rows, up_rows, plan, query, key, value, grad, *rest):
    rest = list(rest)
    down = rest.pop(0) if down_rows else None
    up = rest.pop(0) if up_rows else None
    held, sems = rest
    rows, width = query.shape
    heads = width // HEAD_DIM
    after = round_up(plan[C_BELOW])
    before = round_up(plan[A_ABOVE])
    to_lower = plan[HERE_BELOW]
    to_upper = plan[THERE_ABOVE]

    def load(action):
        for which, array in enumerate((query, key, value, grad)):
            if down_rows:
                @pl.when(to_lower > 0)
                def _():
                    part = tiles(0, after)
                    action(pltpu.make_async_copy(
                        array.at[part], held.at[2 * which, part], sems.at[2 * which]))
            if up_rows:
                @pl.when(to_upper > 0)
                def _():
                    part = tiles(rows - before, before)
                    action(pltpu.make_async_copy(
                        array.at[part], held.at[2 * which + 1, part], sems.at[2 * which + 1]))

    def gather(out, count, first_head, taken, first_row, which_part):
        steps = taken // TILE

        def one_head(slot, carry):
            def one_tile(step, carry):
                source = pl.ds(pl.multiple_of(first_row + step * TILE, TILE), TILE)
                target = pl.ds(pl.multiple_of(slot * taken + step * TILE, TILE), TILE)
                for which in range(4):
                    out[target, which * HEAD_DIM:(which + 1) * HEAD_DIM] = held[
                        2 * which + which_part, source, lanes(first_head + slot)]
                return carry

            return lax.fori_loop(0, steps, one_tile, carry)

        lax.fori_loop(0, count, one_head, 0)

    load(START)
    load(WAIT)
    if down_rows:
        gather(down, to_lower, 0, after, 0, 0)
    if up_rows:
        gather(up, to_upper, heads - to_upper, before, rows - before, 1)


def pack(plan, arrays, down_rows, up_rows):
    rows, width = arrays[0].shape
    sizes = [size for size in (down_rows, up_rows) if size]
    outs = pl.pallas_call(
        functools.partial(pack_kernel, down_rows, up_rows),
        in_specs=[pl.BlockSpec(memory_space=pltpu.SMEM)] + [pl.BlockSpec(memory_space=pl.ANY)] * 4,
        out_specs=[pl.BlockSpec(memory_space=pltpu.VMEM)] * len(sizes),
        out_shape=[jax.ShapeDtypeStruct((size, 4 * HEAD_DIM), jnp.bfloat16) for size in sizes],
        scratch_shapes=[pltpu.VMEM((8, rows, width), jnp.bfloat16), pltpu.SemaphoreType.DMA((8,))],
        compiler_params=pltpu.CompilerParams(vmem_limit_bytes=VMEM_LIMIT),
        name="pack",
    )(plan, *arrays)
    outs = list(outs)
    down = outs.pop(0) if down_rows else None
    up = outs.pop(0) if up_rows else None
    return down, up


def crossing_kernel(
    above, plan, query, key, value, grad, received, back, kept,
    own, moved, result, own_sem, in_sem, out_sem,
):
    rows, width = query.shape
    heads = width // HEAD_DIM
    jobs = plan[HERE_ABOVE] if above else plan[THERE_BELOW]
    before = plan[A_ABOVE] if above else plan[A_BELOW]
    after = plan[C_ABOVE] if above else plan[C_BELOW]
    first_head = 0 if above else heads - jobs
    first_part = tiles(0, round_up(after))
    last_part = tiles(rows - round_up(before), round_up(before))
    own_part, moved_part = (last_part, first_part) if above else (first_part, last_part)
    moved_rows = round_up(after if above else before)

    def load_own(action):
        for which, array in enumerate((query, key, value, grad)):
            action(pltpu.make_async_copy(
                array.at[own_part], own.at[which, own_part], own_sem.at[which]))

    def fetch(job, action):
        buffer = lax.rem(job, 2)
        action(pltpu.make_async_copy(
            received.at[tiles(job * moved_rows, moved_rows)],
            moved.at[buffer, moved_part],
            in_sem.at[buffer],
        ))

    def deliver(job, action):
        buffer = lax.rem(job, 2)
        action(pltpu.make_async_copy(
            result.at[buffer, own_part], kept.at[job, own_part], out_sem.at[buffer, 0]))
        action(pltpu.make_async_copy(
            result.at[buffer, moved_part],
            back.at[tiles(job * moved_rows, moved_rows)],
            out_sem.at[buffer, 1],
        ))

    @pl.when(jobs > 0)
    def _():
        fetch(0, START)
        load_own(START)
        load_own(WAIT)

    def one_job(job, carry):
        buffer = lax.rem(job, 2)

        @pl.when(job + 1 < jobs)
        def _():
            fetch(job + 1, START)

        fetch(job, WAIT)

        @pl.when(job >= 2)
        def _():
            deliver(job - 2, WAIT)

        position = lax.broadcasted_iota(jnp.int32, (rows, HEAD_DIM), 0)
        in_first = position < after
        in_last = position >= rows - before
        in_moved, in_own = (in_first, in_last) if above else (in_last, in_first)
        zero = jnp.zeros((rows, HEAD_DIM), jnp.bfloat16)
        operands = []
        for which in range(4):
            columns = slice(which * HEAD_DIM, (which + 1) * HEAD_DIM)
            operands.append(jnp.where(
                in_moved,
                moved[buffer, :, columns],
                jnp.where(in_own, own[which, :, lanes(first_head + job)], zero),
            ))
        key_position = lax.broadcasted_iota(jnp.int32, (rows, 1), 0)
        in_image = (key_position < after) | (key_position >= rows - before)

        def store(which, part_rows, part):
            result[buffer, part_rows, which * HEAD_DIM:(which + 1) * HEAD_DIM] = part

        attention(*operands, lambda cols: in_image, store)
        deliver(job, START)
        return carry

    lax.fori_loop(0, jobs, one_job, 0)

    @pl.when(jobs >= 2)
    def _():
        deliver(jobs - 2, WAIT)

    @pl.when(jobs >= 1)
    def _():
        deliver(jobs - 1, WAIT)


def crossing_images(above, plan, arrays, received):
    rows, width = arrays[0].shape
    heads = width // HEAD_DIM
    four = 4 * HEAD_DIM
    anywhere = pl.BlockSpec(memory_space=pl.ANY)
    return pl.pallas_call(
        functools.partial(crossing_kernel, above),
        in_specs=[pl.BlockSpec(memory_space=pltpu.SMEM)] + [anywhere] * 5,
        out_specs=[anywhere] * 2,
        out_shape=[
            jax.ShapeDtypeStruct(received.shape, jnp.bfloat16),
            jax.ShapeDtypeStruct((heads, rows, four), jnp.bfloat16),
        ],
        scratch_shapes=[
            pltpu.VMEM((4, rows, width), jnp.bfloat16),
            pltpu.VMEM((2, rows, four), jnp.bfloat16),
            pltpu.VMEM((2, rows, four), jnp.bfloat16),
            pltpu.SemaphoreType.DMA((4,)),
            pltpu.SemaphoreType.DMA((2,)),
            pltpu.SemaphoreType.DMA((2, 2)),
        ],
        compiler_params=pltpu.CompilerParams(vmem_limit_bytes=VMEM_LIMIT),
        name="above_images" if above else "below_images",
    )(plan, *arrays, received)


def merge_kernel(down_rows, up_rows, plan, *rest):
    rest = list(rest)
    kept_above, from_below = (rest.pop(0), rest.pop(0)) if down_rows else (None, None)
    kept_below, from_above = (rest.pop(0), rest.pop(0)) if up_rows else (None, None)
    local = rest[:4]
    outs = rest[4:8]
    whole, first_part, last_part, whole_sem, part_sem, out_sem = rest[8:]
    rows, width = local[0].shape
    heads = width // HEAD_DIM
    after = plan[C_BELOW]
    before = plan[A_ABOVE]
    after_rows = round_up(after)
    before_rows = round_up(before)
    low_below = plan[HERE_BELOW]
    low_above = plan[HERE_ABOVE]
    first_tiles = tiles(0, after_rows)
    last_tiles = tiles(rows - before_rows, before_rows)

    def parts(action):
        for head in range(heads):
            first = first_part.at[head, first_tiles]
            last = last_part.at[head, last_tiles]
            if down_rows:
                @pl.when((after > 0) & (head < low_below))
                def _():
                    action(pltpu.make_async_copy(
                        from_below.at[tiles(head * after_rows, after_rows)],
                        first, part_sem.at[head, 0]))

                @pl.when((before > 0) & (head < low_above))
                def _():
                    action(pltpu.make_async_copy(
                        kept_above.at[head, last_tiles], last, part_sem.at[head, 1]))

            if up_rows:
                @pl.when((after > 0) & (head >= low_below))
                def _():
                    action(pltpu.make_async_copy(
                        kept_below.at[head - low_below, first_tiles],
                        first, part_sem.at[head, 0]))

                @pl.when((before > 0) & (head >= low_above))
                def _():
                    action(pltpu.make_async_copy(
                        from_above.at[tiles((head - low_above) * before_rows, before_rows)],
                        last, part_sem.at[head, 1]))

    def load(which):
        return pltpu.make_async_copy(local[which], whole.at[which], whole_sem.at[which])

    def save(which):
        return pltpu.make_async_copy(whole.at[which], outs[which], out_sem.at[which])

    parts(START)
    for which in range(4):
        load(which).start()
    parts(WAIT)
    position = lax.broadcasted_iota(jnp.int32, (rows, HEAD_DIM), 0)
    in_first = position < after
    in_last = position >= rows - before
    for which in range(4):
        load(which).wait()
        columns = slice(which * HEAD_DIM, (which + 1) * HEAD_DIM)
        for head in range(heads):
            place = slice(head * HEAD_DIM, (head + 1) * HEAD_DIM)
            whole[which, :, place] = jnp.where(
                in_first,
                first_part[head, :, columns],
                jnp.where(in_last, last_part[head, :, columns], whole[which, :, place]),
            )
        save(which).start()
    for which in range(4):
        save(which).wait()


def merge(plan, kept_above, from_below, kept_below, from_above, local):
    rows, width = local[0].shape
    heads = width // HEAD_DIM
    four = 4 * HEAD_DIM
    anywhere = pl.BlockSpec(memory_space=pl.ANY)
    down_rows = 0 if from_below is None else from_below.shape[0]
    up_rows = 0 if from_above is None else from_above.shape[0]
    crossing = [
        array for array in (kept_above, from_below, kept_below, from_above) if array is not None
    ]
    return pl.pallas_call(
        functools.partial(merge_kernel, down_rows, up_rows),
        in_specs=[pl.BlockSpec(memory_space=pltpu.SMEM)] + [anywhere] * (len(crossing) + 4),
        out_specs=[anywhere] * 4,
        out_shape=[jax.ShapeDtypeStruct((rows, width), jnp.bfloat16)] * 4,
        scratch_shapes=[
            pltpu.VMEM((4, rows, width), jnp.bfloat16),
            pltpu.VMEM((heads, rows, four), jnp.bfloat16),
            pltpu.VMEM((heads, rows, four), jnp.bfloat16),
            pltpu.SemaphoreType.DMA((4,)),
            pltpu.SemaphoreType.DMA((heads, 2)),
            pltpu.SemaphoreType.DMA((4,)),
        ],
        compiler_params=pltpu.CompilerParams(vmem_limit_bytes=VMEM_LIMIT),
        name="merge",
    )(plan, *crossing, *local)


def passed_along(value, steps):
    count = lax.axis_size("dp")
    leading, last = max(0, -steps), min(count, count - steps)
    return lax.ppermute(value, "dp", [(source, source + steps) for source in range(leading, last)])


def with_sizes(down_rows, up_rows, plan, lengths, arrays):
    down, up = pack(plan, arrays, down_rows, up_rows)
    kept_above = from_below = kept_below = from_above = None
    received_above = passed_along(down, -1) if down_rows else None
    received_below = passed_along(up, 1) if up_rows else None
    local = local_attention(lengths, arrays)
    if down_rows:
        back_up, kept_above = crossing_images(True, plan, arrays, received_above)
        from_below = passed_along(back_up, 1)
    if up_rows:
        back_down, kept_below = crossing_images(False, plan, arrays, received_below)
        from_above = passed_along(back_down, -1)
    return tuple(merge(plan, kept_above, from_below, kept_below, from_above, local))


def body(queries, keys, values, out_grad, lengths):
    rows, width = queries.shape
    heads = width // HEAD_DIM
    menu = size_menu(rows, heads)
    plan = make_plan(lengths, rows, heads, lax.axis_size("dp"), menu)
    branches = [functools.partial(with_sizes, down, up) for down, up in menu]
    return lax.switch(plan[MENU], branches, plan, lengths, (queries, keys, values, out_grad))


def solution(mesh):
    in_specs = (P("dp", "tensor"), P("dp", "tensor"), P("dp", "tensor"), P("dp", "tensor"), P())
    out_specs = (P("dp", "tensor"), P("dp", "tensor"), P("dp", "tensor"), P("dp", "tensor"))
    return jax.shard_map(body, mesh=mesh, in_specs=in_specs, out_specs=out_specs, check_vma=False)
```

```python
import functools
import math

import jax
import jax.numpy as jnp
from jax import lax
from jax.experimental import pallas as pl
from jax.experimental.pallas import tpu as pltpu
from jax.sharding import PartitionSpec as P

HEAD_DIM = 128
TILE = 16
LOCAL_CHUNK = 256
CROSSING_CHUNK = 128
FACTOR = 1.0 / math.sqrt(HEAD_DIM)
LOG2E = 1.4426950408889634
VMEM_LIMIT = 28 * 1024 * 1024

A_BELOW, C_BELOW, HERE_BELOW, THERE_BELOW, A_ABOVE, C_ABOVE, HERE_ABOVE, THERE_ABOVE, MENU = range(9)

MENU_UNITS = (
    (6, 9), (9, 10), (15, 2), (15, 6), (6, 15), (0, 18), (12, 11), (15, 10), (5, 20),
)


def round_up(value):
    return (value + (TILE - 1)) // TILE * TILE


def worst_case_rows(rows, heads):
    worst = 0
    for before in range(TILE, rows + 1, TILE):
        for after in range(TILE, rows + TILE - before + 1, TILE):
            needed = min(max(after * low, before * (heads - low)) for low in range(heads + 1))
            worst = max(worst, needed)
    return worst


def size_menu(rows, heads):
    unit = rows * heads // 48
    most = worst_case_rows(rows, heads)
    pairs = {(down * unit, up * unit) for down, up in MENU_UNITS}
    pairs = sorted((pair for pair in pairs if sum(pair) < 2 * most), key=lambda pair: (sum(pair), pair))
    return pairs + [(most, most)]


def plan_kernel(rows, heads, blocks, menu, lengths, plan, before_edge, after_edge):
    def clear(edge, carry):
        before_edge[edge] = 0
        after_edge[edge] = 0
        return carry

    lax.fori_loop(0, blocks + 1, clear, 0)

    def place(image, start):
        end = start + lengths[image]
        edge = (end - 1) // rows

        @pl.when(edge > start // rows)
        def _():
            before_edge[edge] = edge * rows - start
            after_edge[edge] = end - edge * rows

        return end

    lax.fori_loop(0, lengths.shape[0], place, 0)

    entry = lax.broadcasted_iota(jnp.int32, (8, 128), 1)
    down_limit = jnp.full((8, 128), -1, jnp.int32)
    up_limit = jnp.full((8, 128), -1, jnp.int32)
    for number, (down, up) in enumerate(menu):
        down_limit = jnp.where(entry == number, down, down_limit)
        up_limit = jnp.where(entry == number, up, up_limit)

    def check(edge, fits):
        after = round_up(after_edge[edge])
        before = round_up(before_edge[edge])
        taken = jnp.zeros((8, 128), jnp.int32)
        for count in range(1, heads + 1):
            taken += jnp.where(after * count <= down_limit, 1, 0)
            taken += jnp.where(before * count <= up_limit, 1, 0)
        return jnp.minimum(fits, jnp.where(taken >= heads, 1, 0))

    fits = lax.fori_loop(1, blocks, check, jnp.ones((8, 128), jnp.int32))
    chosen = jnp.min(jnp.where(fits == 1, entry, len(menu) - 1))
    down_rows = jnp.int32(menu[-1][0])
    up_rows = jnp.int32(menu[-1][1])
    for number, (down, up) in enumerate(menu[:-1]):
        down_rows = jnp.where(chosen == number, down, down_rows)
        up_rows = jnp.where(chosen == number, up, up_rows)
    plan[MENU] = chosen

    block = lax.axis_index("dp")
    for field, edge in ((A_BELOW, block), (A_ABOVE, block + 1)):
        before = before_edge[edge]
        after = after_edge[edge]
        most = jnp.int32(0)
        least = jnp.int32(heads)
        for count in range(1, heads + 1):
            most += jnp.where(round_up(after) * count <= down_rows, 1, 0)
            least -= jnp.where(round_up(before) * count <= up_rows, 1, 0)
        low = jnp.clip(jnp.int32(heads // 2), least, most)
        plan[field] = before
        plan[field + 1] = after
        plan[field + 2] = jnp.where(before > 0, low, 0)
        plan[field + 3] = jnp.where(before > 0, heads - low, 0)


def make_plan(lengths, rows, heads, blocks, menu):
    scalars = pl.BlockSpec(memory_space=pltpu.SMEM)
    return pl.pallas_call(
        functools.partial(plan_kernel, rows, heads, blocks, menu),
        in_specs=[scalars],
        out_specs=scalars,
        out_shape=jax.ShapeDtypeStruct((MENU + 1,), jnp.int32),
        scratch_shapes=[pltpu.SMEM((blocks + 1,), jnp.int32), pltpu.SMEM((blocks + 1,), jnp.int32)],
        name="plan",
    )(lengths)


def tiles(start, size):
    return pl.ds(pl.multiple_of(start, TILE), pl.multiple_of(size, TILE))


def lanes(head):
    return pl.ds(pl.multiple_of(head * HEAD_DIM, HEAD_DIM), HEAD_DIM)


def attention(query, key, value, grad, mask_columns, store, chunk, scratch):
    key_t, value_t, probs_all, grad_scores_all = scratch
    count = query.shape[0]
    key_t[...] = key[...].T
    value_t[...] = value[...].T
    across = (((1,), (1,)), ((), ()))

    def one_chunk(number, carry):
        cols = pl.ds(pl.multiple_of(number * chunk, chunk), chunk)
        scores = lax.dot_general(
            key[...], query[cols, :], across, preferred_element_type=jnp.float32)
        grad_probs = lax.dot_general(
            value[...], grad[cols, :], across, preferred_element_type=jnp.float32)
        scores = jnp.where(mask_columns(cols), scores, -1e30)
        top = jnp.max(scores, axis=0, keepdims=True)
        weights = jnp.exp2((scores - top) * (FACTOR * LOG2E))
        total = jnp.sum(weights, axis=0, keepdims=True)
        probs = weights * (1.0 / total)
        probs_low = probs.astype(jnp.bfloat16)
        probs_all[:, cols] = probs_low
        result_t = jnp.dot(value_t[...], probs_low, preferred_element_type=jnp.float32)
        weighted = probs * grad_probs
        centre = jnp.sum(weighted, axis=0, keepdims=True)
        grad_scores = (weighted - probs * centre).astype(jnp.bfloat16)
        grad_scores_all[:, cols] = grad_scores
        grad_query_t = jnp.dot(key_t[...], grad_scores, preferred_element_type=jnp.float32) * FACTOR
        store(0, cols, result_t.astype(jnp.bfloat16).T)
        store(1, cols, grad_query_t.astype(jnp.bfloat16).T)
        return carry

    lax.fori_loop(0, count // chunk, one_chunk, 0)
    grad_key = jnp.dot(grad_scores_all[...], query[...], preferred_element_type=jnp.float32)
    store(2, slice(None), (grad_key * FACTOR).astype(jnp.bfloat16))
    grad_value = jnp.dot(probs_all[...], grad[...], preferred_element_type=jnp.float32)
    store(3, slice(None), grad_value.astype(jnp.bfloat16))


def attention_scratch(rows):
    return [
        pltpu.VMEM((HEAD_DIM, rows), jnp.bfloat16),
        pltpu.VMEM((HEAD_DIM, rows), jnp.bfloat16),
        pltpu.VMEM((rows, rows), jnp.bfloat16),
        pltpu.VMEM((rows, rows), jnp.bfloat16),
    ]


def local_kernel(lengths, query_ref, key_ref, value_ref, grad_ref, *rest):
    outs = rest[:4]
    image_rows = rest[4]
    count = query_ref.shape[0]

    @pl.when(pl.program_id(0) == 0)
    def _():
        position = lax.axis_index("dp") * count + lax.broadcasted_iota(jnp.int32, (8, count), 1)

        def place(image, carry):
            start, begin = carry
            return start + lengths[image], jnp.where(position >= start, start, begin)

        first = (jnp.int32(0), jnp.zeros((8, count), jnp.int32))
        _, begin = lax.fori_loop(0, lengths.shape[0], place, first)
        image_rows[...] = begin.astype(jnp.float32)

    image_col = image_rows[...].T[:, :1]

    def store(which, rows, part):
        outs[which][rows, :] = part

    attention(
        query_ref,
        key_ref,
        value_ref,
        grad_ref,
        lambda cols: image_col == image_rows[:1, cols],
        store,
        LOCAL_CHUNK,
        rest[5:],
    )


def local_attention(lengths, arrays):
    rows, width = arrays[0].shape
    heads = width // HEAD_DIM
    block = pl.BlockSpec((rows, HEAD_DIM), lambda head: (0, head))
    return pl.pallas_call(
        local_kernel,
        grid=(heads,),
        in_specs=[pl.BlockSpec(memory_space=pltpu.SMEM)] + [block] * 4,
        out_specs=[block] * 4,
        out_shape=[jax.ShapeDtypeStruct((rows, width), jnp.bfloat16)] * 4,
        scratch_shapes=[pltpu.VMEM((8, rows), jnp.float32)] + attention_scratch(rows),
        compiler_params=pltpu.CompilerParams(vmem_limit_bytes=VMEM_LIMIT),
        cost_estimate=pl.CostEstimate(
            flops=12 * rows * rows * width, bytes_accessed=16 * rows * width, transcendentals=0
        ),
        name="local_images",
    )(lengths, *arrays)


START = lambda copy: copy.start()
WAIT = lambda copy: copy.wait()


def pack_kernel(down_rows, up_rows, plan, query, key, value, grad, *rest):
    rest = list(rest)
    down = rest.pop(0) if down_rows else None
    up = rest.pop(0) if up_rows else None
    held, sems = rest
    rows, width = query.shape
    heads = width // HEAD_DIM
    after = round_up(plan[C_BELOW])
    before = round_up(plan[A_ABOVE])
    to_lower = plan[HERE_BELOW]
    to_upper = plan[THERE_ABOVE]

    def load(action):
        for which, array in enumerate((query, key, value, grad)):
            if down_rows:
                @pl.when(to_lower > 0)
                def _():
                    part = tiles(0, after)
                    action(pltpu.make_async_copy(
                        array.at[part], held.at[2 * which, part], sems.at[2 * which]))
            if up_rows:
                @pl.when(to_upper > 0)
                def _():
                    part = tiles(rows - before, before)
                    action(pltpu.make_async_copy(
                        array.at[part], held.at[2 * which + 1, part], sems.at[2 * which + 1]))

    def gather(out, count, first_head, taken, first_row, which_part):
        steps = taken // TILE

        def one_head(slot, carry):
            def one_tile(step, carry):
                source = pl.ds(pl.multiple_of(first_row + step * TILE, TILE), TILE)
                target = pl.ds(pl.multiple_of(slot * taken + step * TILE, TILE), TILE)
                for which in range(4):
                    out[target, which * HEAD_DIM:(which + 1) * HEAD_DIM] = held[
                        2 * which + which_part, source, lanes(first_head + slot)]
                return carry

            return lax.fori_loop(0, steps, one_tile, carry)

        lax.fori_loop(0, count, one_head, 0)

    load(START)
    load(WAIT)
    if down_rows:
        gather(down, to_lower, 0, after, 0, 0)
    if up_rows:
        gather(up, to_upper, heads - to_upper, before, rows - before, 1)


def pack(plan, arrays, down_rows, up_rows):
    rows, width = arrays[0].shape
    sizes = [size for size in (down_rows, up_rows) if size]
    outs = pl.pallas_call(
        functools.partial(pack_kernel, down_rows, up_rows),
        in_specs=[pl.BlockSpec(memory_space=pltpu.SMEM)] + [pl.BlockSpec(memory_space=pl.ANY)] * 4,
        out_specs=[pl.BlockSpec(memory_space=pltpu.VMEM)] * len(sizes),
        out_shape=[jax.ShapeDtypeStruct((size, 4 * HEAD_DIM), jnp.bfloat16) for size in sizes],
        scratch_shapes=[pltpu.VMEM((8, rows, width), jnp.bfloat16), pltpu.SemaphoreType.DMA((8,))],
        compiler_params=pltpu.CompilerParams(vmem_limit_bytes=VMEM_LIMIT),
        name="pack",
    )(plan, *arrays)
    outs = list(outs)
    down = outs.pop(0) if down_rows else None
    up = outs.pop(0) if up_rows else None
    return down, up


def crossing_kernel(
    above, plan, query, key, value, grad, received, back, kept,
    own, moved, result, window, own_sem, in_sem, out_sem, *scratch,
):
    rows, width = query.shape
    heads = width // HEAD_DIM
    jobs = plan[HERE_ABOVE] if above else plan[THERE_BELOW]
    before = plan[A_ABOVE] if above else plan[A_BELOW]
    after = plan[C_ABOVE] if above else plan[C_BELOW]
    first_head = 0 if above else heads - jobs
    first_part = tiles(0, round_up(after))
    last_part = tiles(rows - round_up(before), round_up(before))
    own_part, moved_part = (last_part, first_part) if above else (first_part, last_part)
    moved_rows = round_up(after if above else before)

    def load_own(action):
        for which, array in enumerate((query, key, value, grad)):
            action(pltpu.make_async_copy(
                array.at[own_part], own.at[which, own_part], own_sem.at[which]))

    def fetch(job, action):
        buffer = lax.rem(job, 2)
        action(pltpu.make_async_copy(
            received.at[tiles(job * moved_rows, moved_rows)],
            moved.at[buffer, moved_part],
            in_sem.at[buffer],
        ))

    def deliver(job, action):
        buffer = lax.rem(job, 2)
        action(pltpu.make_async_copy(
            result.at[buffer, own_part], kept.at[job, own_part], out_sem.at[buffer, 0]))
        action(pltpu.make_async_copy(
            result.at[buffer, moved_part],
            back.at[tiles(job * moved_rows, moved_rows)],
            out_sem.at[buffer, 1],
        ))

    @pl.when(jobs > 0)
    def _():
        fetch(0, START)
        load_own(START)
        load_own(WAIT)

    def one_job(job, carry):
        buffer = lax.rem(job, 2)

        @pl.when(job + 1 < jobs)
        def _():
            fetch(job + 1, START)

        fetch(job, WAIT)

        @pl.when(job >= 2)
        def _():
            deliver(job - 2, WAIT)

        fill = 128

        def fill_rows(step, carry):
            part = pl.ds(pl.multiple_of(step * fill, fill), fill)
            position = step * fill + lax.broadcasted_iota(jnp.int32, (fill, HEAD_DIM), 0)
            in_first = position < after
            in_last = position >= rows - before
            in_moved, in_own = (in_first, in_last) if above else (in_last, in_first)
            zero = jnp.zeros((fill, HEAD_DIM), jnp.bfloat16)
            for which in range(4):
                columns = slice(which * HEAD_DIM, (which + 1) * HEAD_DIM)
                window[part, columns] = jnp.where(
                    in_moved,
                    moved[buffer, part, columns],
                    jnp.where(in_own, own[which, part, lanes(first_head + job)], zero),
                )
            return carry

        lax.fori_loop(0, rows // fill, fill_rows, 0)
        key_position = lax.broadcasted_iota(jnp.int32, (rows, 1), 0)
        in_image = (key_position < after) | (key_position >= rows - before)

        def store(which, part_rows, part):
            result[buffer, part_rows, which * HEAD_DIM:(which + 1) * HEAD_DIM] = part

        operands = [window.at[:, pl.ds(which * HEAD_DIM, HEAD_DIM)] for which in range(4)]
        attention(*operands, lambda cols: in_image, store, CROSSING_CHUNK, scratch)
        deliver(job, START)
        return carry

    lax.fori_loop(0, jobs, one_job, 0)

    @pl.when(jobs >= 2)
    def _():
        deliver(jobs - 2, WAIT)

    @pl.when(jobs >= 1)
    def _():
        deliver(jobs - 1, WAIT)


def crossing_images(above, plan, arrays, received):
    rows, width = arrays[0].shape
    heads = width // HEAD_DIM
    four = 4 * HEAD_DIM
    anywhere = pl.BlockSpec(memory_space=pl.ANY)
    return pl.pallas_call(
        functools.partial(crossing_kernel, above),
        in_specs=[pl.BlockSpec(memory_space=pltpu.SMEM)] + [anywhere] * 5,
        out_specs=[anywhere] * 2,
        out_shape=[
            jax.ShapeDtypeStruct(received.shape, jnp.bfloat16),
            jax.ShapeDtypeStruct((heads, rows, four), jnp.bfloat16),
        ],
        scratch_shapes=[
            pltpu.VMEM((4, rows, width), jnp.bfloat16),
            pltpu.VMEM((2, rows, four), jnp.bfloat16),
            pltpu.VMEM((2, rows, four), jnp.bfloat16),
            pltpu.VMEM((rows, four), jnp.bfloat16),
            pltpu.SemaphoreType.DMA((4,)),
            pltpu.SemaphoreType.DMA((2,)),
            pltpu.SemaphoreType.DMA((2, 2)),
        ] + attention_scratch(rows),
        compiler_params=pltpu.CompilerParams(vmem_limit_bytes=VMEM_LIMIT),
        name="above_images" if above else "below_images",
    )(plan, *arrays, received)


def merge_kernel(down_rows, up_rows, plan, *rest):
    rest = list(rest)
    kept_above, from_below = (rest.pop(0), rest.pop(0)) if down_rows else (None, None)
    kept_below, from_above = (rest.pop(0), rest.pop(0)) if up_rows else (None, None)
    local = rest[:4]
    outs = rest[4:8]
    whole, first_part, last_part, whole_sem, part_sem, out_sem = rest[8:]
    rows, width = local[0].shape
    heads = width // HEAD_DIM
    after = plan[C_BELOW]
    before = plan[A_ABOVE]
    after_rows = round_up(after)
    before_rows = round_up(before)
    low_below = plan[HERE_BELOW]
    low_above = plan[HERE_ABOVE]
    first_tiles = tiles(0, after_rows)
    last_tiles = tiles(rows - before_rows, before_rows)

    def parts(action):
        for head in range(heads):
            first = first_part.at[head, first_tiles]
            last = last_part.at[head, last_tiles]
            if down_rows:
                @pl.when((after > 0) & (head < low_below))
                def _():
                    action(pltpu.make_async_copy(
                        from_below.at[tiles(head * after_rows, after_rows)],
                        first, part_sem.at[head, 0]))

                @pl.when((before > 0) & (head < low_above))
                def _():
                    action(pltpu.make_async_copy(
                        kept_above.at[head, last_tiles], last, part_sem.at[head, 1]))

            if up_rows:
                @pl.when((after > 0) & (head >= low_below))
                def _():
                    action(pltpu.make_async_copy(
                        kept_below.at[head - low_below, first_tiles],
                        first, part_sem.at[head, 0]))

                @pl.when((before > 0) & (head >= low_above))
                def _():
                    action(pltpu.make_async_copy(
                        from_above.at[tiles((head - low_above) * before_rows, before_rows)],
                        last, part_sem.at[head, 1]))

    def load(which):
        return pltpu.make_async_copy(local[which], whole.at[which], whole_sem.at[which])

    def save(which):
        return pltpu.make_async_copy(whole.at[which], outs[which], out_sem.at[which])

    parts(START)
    for which in range(4):
        load(which).start()
    parts(WAIT)
    fill = 128
    steps = rows // fill
    for which in range(4):
        load(which).wait()
        columns = slice(which * HEAD_DIM, (which + 1) * HEAD_DIM)

        def fill_rows(number, carry):
            head = number // steps
            first_row = lax.rem(number, steps) * fill
            part = pl.ds(pl.multiple_of(first_row, fill), fill)
            position = first_row + lax.broadcasted_iota(jnp.int32, (fill, HEAD_DIM), 0)
            whole[which, part, lanes(head)] = jnp.where(
                position < after,
                first_part[head, part, columns],
                jnp.where(
                    position >= rows - before,
                    last_part[head, part, columns],
                    whole[which, part, lanes(head)],
                ),
            )
            return carry

        lax.fori_loop(0, heads * steps, fill_rows, 0)
        save(which).start()
    for which in range(4):
        save(which).wait()


def merge(plan, kept_above, from_below, kept_below, from_above, local):
    rows, width = local[0].shape
    heads = width // HEAD_DIM
    four = 4 * HEAD_DIM
    anywhere = pl.BlockSpec(memory_space=pl.ANY)
    down_rows = 0 if from_below is None else from_below.shape[0]
    up_rows = 0 if from_above is None else from_above.shape[0]
    crossing = [
        array for array in (kept_above, from_below, kept_below, from_above) if array is not None
    ]
    return pl.pallas_call(
        functools.partial(merge_kernel, down_rows, up_rows),
        in_specs=[pl.BlockSpec(memory_space=pltpu.SMEM)] + [anywhere] * (len(crossing) + 4),
        out_specs=[anywhere] * 4,
        out_shape=[jax.ShapeDtypeStruct((rows, width), jnp.bfloat16)] * 4,
        scratch_shapes=[
            pltpu.VMEM((4, rows, width), jnp.bfloat16),
            pltpu.VMEM((heads, rows, four), jnp.bfloat16),
            pltpu.VMEM((heads, rows, four), jnp.bfloat16),
            pltpu.SemaphoreType.DMA((4,)),
            pltpu.SemaphoreType.DMA((heads, 2)),
            pltpu.SemaphoreType.DMA((4,)),
        ],
        compiler_params=pltpu.CompilerParams(vmem_limit_bytes=VMEM_LIMIT),
        name="merge",
    )(plan, *crossing, *local)


def passed_along(value, steps):
    count = lax.axis_size("dp")
    leading, last = max(0, -steps), min(count, count - steps)
    return lax.ppermute(value, "dp", [(source, source + steps) for source in range(leading, last)])


def with_sizes(down_rows, up_rows, plan, lengths, arrays):
    down, up = pack(plan, arrays, down_rows, up_rows)
    kept_above = from_below = kept_below = from_above = None
    received_above = passed_along(down, -1) if down_rows else None
    received_below = passed_along(up, 1) if up_rows else None
    local = local_attention(lengths, arrays)
    if down_rows:
        back_up, kept_above = crossing_images(True, plan, arrays, received_above)
        from_below = passed_along(back_up, 1)
    if up_rows:
        back_down, kept_below = crossing_images(False, plan, arrays, received_below)
        from_above = passed_along(back_down, -1)
    return tuple(merge(plan, kept_above, from_below, kept_below, from_above, local))


def body(queries, keys, values, out_grad, lengths):
    rows, width = queries.shape
    heads = width // HEAD_DIM
    menu = size_menu(rows, heads)
    plan = make_plan(lengths, rows, heads, lax.axis_size("dp"), menu)
    branches = [functools.partial(with_sizes, down, up) for down, up in menu]
    return lax.switch(plan[MENU], branches, plan, lengths, (queries, keys, values, out_grad))


def solution(mesh):
    in_specs = (P("dp", "tensor"), P("dp", "tensor"), P("dp", "tensor"), P("dp", "tensor"), P())
    out_specs = (P("dp", "tensor"), P("dp", "tensor"), P("dp", "tensor"), P("dp", "tensor"))
    return jax.shard_map(body, mesh=mesh, in_specs=in_specs, out_specs=out_specs, check_vma=False)
```

```python
import functools
import math

import jax
import jax.numpy as jnp
from jax import lax
from jax.experimental import pallas as pl
from jax.experimental.pallas import tpu as pltpu
from jax.sharding import PartitionSpec as P

HEAD_DIM = 128
TILE = 16
BLOCK = 64
LOCAL_CHUNK = 256
CROSSING_CHUNK = 512
FACTOR = 1.0 / math.sqrt(HEAD_DIM)
LOG2E = 1.4426950408889634
VMEM_LIMIT = 32 * 1024 * 1024

A_BELOW, C_BELOW, HERE_BELOW, THERE_BELOW, A_ABOVE, C_ABOVE, HERE_ABOVE, THERE_ABOVE = range(8)

LEVEL_UNITS = ()


def round_up(value):
    return (value + (TILE - 1)) // TILE * TILE


def worst_case_rows(rows, heads):
    worst = 0
    for before in range(TILE, rows + 1, TILE):
        for after in range(TILE, rows + TILE - before + 1, TILE):
            needed = min(max(after * low, before * (heads - low)) for low in range(heads + 1))
            worst = max(worst, needed)
    return worst


def size_levels(rows, heads):
    unit = rows * heads // 48
    most = worst_case_rows(rows, heads)
    return tuple(sorted(level * unit for level in LEVEL_UNITS if level * unit < most)) + (most,)


def size_menu(levels):
    count = len(levels)
    pairs = [(down, up) for down in range(count) for up in range(count)]
    return sorted(pairs, key=lambda pair: (levels[pair[0]] + levels[pair[1]], pair))


def plan_kernel(rows, heads, blocks, menu, lengths, plan, choice, before_edge, after_edge):
    def clear(edge, carry):
        before_edge[edge] = 0
        after_edge[edge] = 0
        return carry

    lax.fori_loop(0, blocks + 1, clear, 0)

    def place(image, start):
        end = start + lengths[image]
        edge = (end - 1) // rows

        @pl.when(edge > start // rows)
        def _():
            before_edge[edge] = edge * rows - start
            after_edge[edge] = end - edge * rows

        return end

    lax.fori_loop(0, lengths.shape[0], place, 0)

    entry = lax.broadcasted_iota(jnp.int32, (8, 128), 1)
    down_limit = jnp.full((8, 128), -1, jnp.int32)
    up_limit = jnp.full((8, 128), -1, jnp.int32)
    for number, (down, up) in enumerate(menu):
        down_limit = jnp.where(entry == number, down, down_limit)
        up_limit = jnp.where(entry == number, up, up_limit)

    def check(edge, fits):
        after = round_up(after_edge[edge])
        before = round_up(before_edge[edge])
        taken = jnp.zeros((8, 128), jnp.int32)
        for count in range(1, heads + 1):
            taken += jnp.where(after * count <= down_limit, 1, 0)
            taken += jnp.where(before * count <= up_limit, 1, 0)
        return jnp.minimum(fits, jnp.where(taken >= heads, 1, 0))

    fits = lax.fori_loop(1, blocks, check, jnp.ones((8, 128), jnp.int32))
    chosen = jnp.min(jnp.where(fits == 1, entry, len(menu) - 1))
    down_rows = jnp.int32(menu[-1][0])
    up_rows = jnp.int32(menu[-1][1])
    for number, (down, up) in enumerate(menu[:-1]):
        down_rows = jnp.where(chosen == number, down, down_rows)
        up_rows = jnp.where(chosen == number, up, up_rows)
    choice[0] = chosen

    block = lax.axis_index("dp")
    for field, edge in ((A_BELOW, block), (A_ABOVE, block + 1)):
        before = before_edge[edge]
        after = after_edge[edge]
        most = jnp.int32(0)
        least = jnp.int32(heads)
        for count in range(1, heads + 1):
            most += jnp.where(round_up(after) * count <= down_rows, 1, 0)
            least -= jnp.where(round_up(before) * count <= up_rows, 1, 0)
        low = jnp.clip(jnp.int32(heads // 2), least, most)
        plan[field] = before
        plan[field + 1] = after
        plan[field + 2] = jnp.where(before > 0, low, 0)
        plan[field + 3] = jnp.where(before > 0, heads - low, 0)


def make_plan(lengths, rows, heads, blocks, menu):
    scalars = pl.BlockSpec(memory_space=pltpu.SMEM)
    return pl.pallas_call(
        functools.partial(plan_kernel, rows, heads, blocks, menu),
        in_specs=[scalars],
        out_specs=[scalars] * 2,
        out_shape=[
            jax.ShapeDtypeStruct((THERE_ABOVE + 1,), jnp.int32),
            jax.ShapeDtypeStruct((1,), jnp.int32),
        ],
        scratch_shapes=[pltpu.SMEM((blocks + 1,), jnp.int32), pltpu.SMEM((blocks + 1,), jnp.int32)],
        name="plan",
    )(lengths)


def tiles(start, size):
    return pl.ds(pl.multiple_of(start, TILE), pl.multiple_of(size, TILE))


def lanes(head):
    return pl.ds(pl.multiple_of(head * HEAD_DIM, HEAD_DIM), HEAD_DIM)


def attention(query, key, value, grad, mask_columns, store, chunk):
    count = query.shape[0]
    key_t = key.T
    value_t = value.T
    across = (((1,), (1,)), ((), ()))
    chunks = [slice(first, first + chunk) for first in range(0, count, chunk)]
    scores = [
        lax.dot_general(key, query[cols], across, preferred_element_type=jnp.float32)
        for cols in chunks
    ]
    grad_probs = [
        lax.dot_general(value, grad[cols], across, preferred_element_type=jnp.float32)
        for cols in chunks
    ]
    probs_low = []
    grad_scores = []
    for number, cols in enumerate(chunks):
        masked = jnp.where(mask_columns(cols), scores[number], -1e30)
        top = jnp.max(masked, axis=0, keepdims=True)
        weights = jnp.exp2((masked - top) * (FACTOR * LOG2E))
        total = jnp.sum(weights, axis=0, keepdims=True)
        probs = weights * (1.0 / total)
        probs_low.append(probs.astype(jnp.bfloat16))
        result_t = jnp.dot(value_t, probs_low[-1], preferred_element_type=jnp.float32)
        weighted = probs * grad_probs[number]
        centre = jnp.sum(weighted, axis=0, keepdims=True)
        grad_scores.append((weighted - probs * centre).astype(jnp.bfloat16))
        grad_query_t = jnp.dot(key_t, grad_scores[-1], preferred_element_type=jnp.float32) * FACTOR
        store(0, cols, result_t.astype(jnp.bfloat16).T)
        store(1, cols, grad_query_t.astype(jnp.bfloat16).T)
    probs_low = jnp.concatenate(probs_low, axis=1)
    grad_scores = jnp.concatenate(grad_scores, axis=1)
    grad_value = jnp.dot(probs_low, grad, preferred_element_type=jnp.float32)
    store(3, slice(None), grad_value.astype(jnp.bfloat16))
    grad_key = jnp.dot(grad_scores, query, preferred_element_type=jnp.float32)
    store(2, slice(None), (grad_key * FACTOR).astype(jnp.bfloat16))


def local_kernel(lengths, query_ref, key_ref, value_ref, grad_ref, *rest):
    outs = rest[:4]
    image_rows = rest[4]
    count = query_ref.shape[0]

    @pl.when(pl.program_id(0) == 0)
    def _():
        position = lax.axis_index("dp") * count + lax.broadcasted_iota(jnp.int32, (8, count), 1)

        def place(image, carry):
            start, begin = carry
            return start + lengths[image], jnp.where(position >= start, start, begin)

        first = (jnp.int32(0), jnp.zeros((8, count), jnp.int32))
        _, begin = lax.fori_loop(0, lengths.shape[0], place, first)
        image_rows[...] = begin.astype(jnp.float32)

    image_col = image_rows[...].T[:, :1]

    def store(which, rows, part):
        outs[which][rows, :] = part

    attention(
        query_ref[...],
        key_ref[...],
        value_ref[...],
        grad_ref[...],
        lambda cols: image_col == image_rows[:1, cols],
        store,
        LOCAL_CHUNK,
    )


def local_attention(lengths, arrays):
    rows, width = arrays[0].shape
    heads = width // HEAD_DIM
    block = pl.BlockSpec((rows, HEAD_DIM), lambda head: (0, head))
    return pl.pallas_call(
        local_kernel,
        grid=(heads,),
        in_specs=[pl.BlockSpec(memory_space=pltpu.SMEM)] + [block] * 4,
        out_specs=[block] * 4,
        out_shape=[jax.ShapeDtypeStruct((rows, width), jnp.bfloat16)] * 4,
        scratch_shapes=[pltpu.VMEM((8, rows), jnp.float32)],
        compiler_params=pltpu.CompilerParams(vmem_limit_bytes=VMEM_LIMIT),
        cost_estimate=pl.CostEstimate(
            flops=12 * rows * rows * width, bytes_accessed=16 * rows * width, transcendentals=0
        ),
        name="local_images",
    )(lengths, *arrays)


START = lambda copy: copy.start()
WAIT = lambda copy: copy.wait()


def pieces(levels):
    starts = (0,) + levels[:-1]
    return [(start, end - start) for start, end in zip(starts, levels)]


def copy_pieces(levels, staged, offset, arrays, sems, out):
    copies = []
    for number, (start, size) in enumerate(pieces(levels)):
        inside = staged.at[pl.ds(offset + start, size)]
        outside = arrays[number]
        source, target = (inside, outside) if out else (outside, inside)
        copies.append(pltpu.make_async_copy(source, target, sems.at[number]))
    return copies


def pack_kernel(levels, plan, query, key, value, grad, *rest):
    count = len(levels)
    down, up = rest[:count], rest[count:2 * count]
    held, down_staged, up_staged, sems, down_sem, up_sem = rest[2 * count:]
    rows, width = query.shape
    heads = width // HEAD_DIM
    after = round_up(plan[C_BELOW])
    before = round_up(plan[A_ABOVE])
    to_lower = plan[HERE_BELOW]
    to_upper = plan[THERE_ABOVE]

    def load(action):
        for which, array in enumerate((query, key, value, grad)):
            @pl.when(to_lower > 0)
            def _():
                part = tiles(0, after)
                action(pltpu.make_async_copy(
                    array.at[part], held.at[2 * which, part], sems.at[2 * which]))

            @pl.when(to_upper > 0)
            def _():
                part = tiles(rows - before, before)
                action(pltpu.make_async_copy(
                    array.at[part], held.at[2 * which + 1, part], sems.at[2 * which + 1]))

    def gather(staged, count, first_head, taken, first_row, which_part):
        steps = taken // TILE

        def one_head(slot, carry):
            def one_tile(step, carry):
                source = pl.ds(pl.multiple_of(first_row + step * TILE, TILE), TILE)
                target = pl.ds(pl.multiple_of(slot * taken + step * TILE, TILE), TILE)
                for which in range(4):
                    staged[target, which * HEAD_DIM:(which + 1) * HEAD_DIM] = held[
                        2 * which + which_part, source, lanes(first_head + slot)]
                return carry

            return lax.fori_loop(0, steps, one_tile, carry)

        lax.fori_loop(0, count, one_head, 0)

    load(START)
    load(WAIT)
    gather(down_staged, to_lower, 0, after, 0, 0)
    down_copies = copy_pieces(levels, down_staged, 0, down, down_sem, True)
    for copy in down_copies:
        copy.start()
    gather(up_staged, to_upper, heads - to_upper, before, rows - before, 1)
    up_copies = copy_pieces(levels, up_staged, 0, up, up_sem, True)
    for copy in up_copies:
        copy.start()
    for copy in down_copies + up_copies:
        copy.wait()


def piece_shapes(levels):
    return [jax.ShapeDtypeStruct((size, 4 * HEAD_DIM), jnp.bfloat16) for _, size in pieces(levels)]


def pack(plan, arrays, levels):
    rows, width = arrays[0].shape
    count = len(levels)
    anywhere = pl.BlockSpec(memory_space=pl.ANY)
    staged = pltpu.VMEM((levels[-1], 4 * HEAD_DIM), jnp.bfloat16)
    outs = pl.pallas_call(
        functools.partial(pack_kernel, levels),
        in_specs=[pl.BlockSpec(memory_space=pltpu.SMEM)] + [anywhere] * 4,
        out_specs=[anywhere] * (2 * count),
        out_shape=piece_shapes(levels) * 2,
        scratch_shapes=[
            pltpu.VMEM((8, rows, width), jnp.bfloat16),
            staged,
            staged,
            pltpu.SemaphoreType.DMA((8,)),
            pltpu.SemaphoreType.DMA((count,)),
            pltpu.SemaphoreType.DMA((count,)),
        ],
        compiler_params=pltpu.CompilerParams(vmem_limit_bytes=VMEM_LIMIT),
        name="pack",
    )(plan, *arrays)
    return outs[:count], outs[count:]


def crossing_kernel(levels, above, plan, query, key, value, grad, *rest):
    count = len(levels)
    received, back, kept = rest[:count], rest[count:2 * count], rest[2 * count]
    own, staged_in, staged_out, result, own_sem, in_sem, out_sem, kept_sem = rest[2 * count + 1:]
    rows, width = query.shape
    heads = width // HEAD_DIM
    jobs = plan[HERE_ABOVE] if above else plan[THERE_BELOW]
    before = plan[A_ABOVE] if above else plan[A_BELOW]
    after = plan[C_ABOVE] if above else plan[C_BELOW]
    first_head = 0 if above else heads - jobs
    if above:
        own_part = tiles(rows - round_up(before), round_up(before))
        moved_rows = round_up(after)
        margin = 0
        shift = 0
    else:
        own_part = tiles(0, round_up(after))
        moved_rows = round_up(before)
        margin = rows
        shift = moved_rows

    def load_own(action):
        for which, array in enumerate((query, key, value, grad)):
            action(pltpu.make_async_copy(
                array.at[own_part], own.at[which, own_part], own_sem.at[which]))

    def keep(job):
        buffer = lax.rem(job, 2)
        return pltpu.make_async_copy(
            result.at[buffer, own_part], kept.at[job, own_part], kept_sem.at[buffer])

    position = lax.broadcasted_iota(jnp.int32, (rows, HEAD_DIM), 0)
    in_first = position < after
    in_last = position >= rows - before
    in_moved, in_own = (in_first, in_last) if above else (in_last, in_first)
    key_position = lax.broadcasted_iota(jnp.int32, (rows, 1), 0)
    in_image = (key_position < after) | (key_position >= rows - before)

    def one_job(step, carry):
        job = step if above else jobs - 1 - step
        buffer = lax.rem(job, 2)
        window = pl.ds(pl.multiple_of(job * moved_rows + shift, TILE), rows)

        @pl.when(step >= 2)
        def _():
            keep(job).wait()

        zero = jnp.zeros((rows, HEAD_DIM), jnp.bfloat16)
        operands = []
        for which in range(4):
            columns = slice(which * HEAD_DIM, (which + 1) * HEAD_DIM)
            operands.append(jnp.where(
                in_moved,
                staged_in[window, columns],
                jnp.where(in_own, own[which, :, lanes(first_head + job)], zero),
            ))

        def store(which, part_rows, part):
            result[buffer, part_rows, which * HEAD_DIM:(which + 1) * HEAD_DIM] = part

        attention(*operands, lambda cols: in_image, store, CROSSING_CHUNK)
        staged_out[window, :] = result[buffer]
        keep(job).start()
        return carry

    @pl.when(jobs > 0)
    def _():
        copies = copy_pieces(levels, staged_in, margin, received, in_sem, False)
        for copy in copies:
            copy.start()
        load_own(START)
        load_own(WAIT)
        for copy in copies:
            copy.wait()
        lax.fori_loop(0, jobs, one_job, 0)
        copies = copy_pieces(levels, staged_out, margin, back, out_sem, True)
        for copy in copies:
            copy.start()

        @pl.when(jobs >= 2)
        def _():
            keep(jobs - 2 if above else 1).wait()

        keep(jobs - 1 if above else 0).wait()
        for copy in copies:
            copy.wait()


def crossing_images(above, plan, arrays, received, levels):
    rows, width = arrays[0].shape
    heads = width // HEAD_DIM
    four = 4 * HEAD_DIM
    count = len(levels)
    anywhere = pl.BlockSpec(memory_space=pl.ANY)
    staged = pltpu.VMEM((levels[-1] + rows, four), jnp.bfloat16)
    outs = pl.pallas_call(
        functools.partial(crossing_kernel, levels, above),
        in_specs=[pl.BlockSpec(memory_space=pltpu.SMEM)] + [anywhere] * (4 + count),
        out_specs=[anywhere] * (count + 1),
        out_shape=piece_shapes(levels)
        + [jax.ShapeDtypeStruct((heads, rows, four), jnp.bfloat16)],
        scratch_shapes=[
            pltpu.VMEM((4, rows, width), jnp.bfloat16),
            staged,
            staged,
            pltpu.VMEM((2, rows, four), jnp.bfloat16),
            pltpu.SemaphoreType.DMA((4,)),
            pltpu.SemaphoreType.DMA((count,)),
            pltpu.SemaphoreType.DMA((count,)),
            pltpu.SemaphoreType.DMA((2,)),
        ],
        compiler_params=pltpu.CompilerParams(vmem_limit_bytes=VMEM_LIMIT),
        name="above_images" if above else "below_images",
    )(plan, *arrays, *received)
    return outs[:count], outs[count]


def overlay(whole, which, first_head, last_head, first_block, last_block, wanted, source):
    def one_head(head, carry):
        def one_block(block, carry):
            part = pl.ds(pl.multiple_of(block * BLOCK, BLOCK), BLOCK)
            position = block * BLOCK + lax.broadcasted_iota(jnp.int32, (BLOCK, HEAD_DIM), 0)
            whole[which, part, lanes(head)] = jnp.where(
                wanted(position), source(head, block), whole[which, part, lanes(head)])
            return carry

        return lax.fori_loop(first_block, last_block, one_block, carry)

    lax.fori_loop(first_head, last_head, one_head, 0)


def overlay_both(plan, whole, which, first_heads, last_heads, first_source, last_source):
    rows = whole.shape[1]
    after = plan[C_BELOW]
    begin = rows - plan[A_ABOVE]
    overlay(whole, which, *first_heads, 0, (after + BLOCK - 1) // BLOCK,
            lambda position: position < after, first_source)
    overlay(whole, which, *last_heads, begin // BLOCK, rows // BLOCK,
            lambda position: position >= begin, last_source)


def keep_kernel(plan, kept_above, kept_below, *rest):
    local, outs = rest[:4], rest[4:8]
    whole, first_part, last_part, whole_sem, first_sem, last_sem, out_sem = rest[8:]
    rows, width = local[0].shape
    heads = width // HEAD_DIM
    low_below = plan[HERE_BELOW]
    low_above = plan[HERE_ABOVE]
    below_jobs = plan[THERE_BELOW]
    first_tiles = tiles(0, round_up(plan[C_BELOW]))
    last_tiles = tiles(rows - round_up(plan[A_ABOVE]), round_up(plan[A_ABOVE]))

    def parts(action):
        for slot in range(heads):
            @pl.when(slot < below_jobs)
            def _():
                action(pltpu.make_async_copy(
                    kept_below.at[slot, first_tiles], first_part.at[slot, first_tiles],
                    first_sem.at[slot]))

            @pl.when(slot < low_above)
            def _():
                action(pltpu.make_async_copy(
                    kept_above.at[slot, last_tiles], last_part.at[slot, last_tiles],
                    last_sem.at[slot]))

    loads = [
        pltpu.make_async_copy(local[which], whole.at[which], whole_sem.at[which])
        for which in range(4)
    ]
    saves = [
        pltpu.make_async_copy(whole.at[which], outs[which], out_sem.at[which])
        for which in range(4)
    ]
    parts(START)
    for copy in loads:
        copy.start()
    parts(WAIT)
    for which in range(4):
        columns = slice(which * HEAD_DIM, (which + 1) * HEAD_DIM)

        def first_source(head, block):
            part = pl.ds(pl.multiple_of(block * BLOCK, BLOCK), BLOCK)
            return first_part[head - low_below, part, columns]

        def last_source(head, block):
            part = pl.ds(pl.multiple_of(block * BLOCK, BLOCK), BLOCK)
            return last_part[head, part, columns]

        loads[which].wait()
        overlay_both(
            plan, whole, which, (low_below, low_below + below_jobs), (0, low_above),
            first_source, last_source)
        saves[which].start()
    for copy in saves:
        copy.wait()


def merge_kept(plan, kept_above, kept_below, local):
    rows, width = local[0].shape
    heads = width // HEAD_DIM
    anywhere = pl.BlockSpec(memory_space=pl.ANY)
    windows = pltpu.VMEM((heads, rows, 4 * HEAD_DIM), jnp.bfloat16)
    return pl.pallas_call(
        keep_kernel,
        in_specs=[pl.BlockSpec(memory_space=pltpu.SMEM)] + [anywhere] * 6,
        out_specs=[anywhere] * 4,
        out_shape=[jax.ShapeDtypeStruct((rows, width), jnp.bfloat16)] * 4,
        scratch_shapes=[
            pltpu.VMEM((4, rows, width), jnp.bfloat16),
            windows,
            windows,
            pltpu.SemaphoreType.DMA((4,)),
            pltpu.SemaphoreType.DMA((heads,)),
            pltpu.SemaphoreType.DMA((heads,)),
            pltpu.SemaphoreType.DMA((4,)),
        ],
        compiler_params=pltpu.CompilerParams(vmem_limit_bytes=VMEM_LIMIT),
        cost_estimate=pl.CostEstimate(
            flops=0, bytes_accessed=32 * rows * width, transcendentals=0
        ),
        name="merge_kept",
    )(plan, kept_above, kept_below, *local)


def return_kernel(levels, plan, *rest):
    count = len(levels)
    from_below, from_above = rest[:count], rest[count:2 * count]
    outs = rest[2 * count + 4:2 * count + 8]
    whole, below_staged, above_staged, first_sem, last_sem, below_sem, above_sem = rest[2 * count + 8:]
    rows = whole.shape[1]
    heads = whole.shape[2] // HEAD_DIM
    after_rows = round_up(plan[C_BELOW])
    before_rows = round_up(plan[A_ABOVE])
    first_heads = plan[HERE_BELOW]
    last_heads = plan[THERE_ABOVE]
    begin = (rows - plan[A_ABOVE]) // BLOCK * BLOCK
    end = (plan[C_BELOW] + BLOCK - 1) // BLOCK * BLOCK
    both = (first_heads > 0) & (last_heads > 0)
    first_end = jnp.where(both, jnp.minimum(end, begin), end)

    def block_rows(start, size):
        return pl.ds(pl.multiple_of(start, BLOCK), pl.multiple_of(size, BLOCK))

    first_copied = (first_heads > 0) & (first_end > 0)

    def move(which, out, action):
        @pl.when(first_copied)
        def _():
            part = block_rows(0, first_end)
            inside, outside = whole.at[which, part], outs[which].at[part]
            source, target = (inside, outside) if out else (outside, inside)
            action(pltpu.make_async_copy(source, target, first_sem.at[which]))

        @pl.when(last_heads > 0)
        def _():
            part = block_rows(begin, rows - begin)
            inside, outside = whole.at[which, part], outs[which].at[part]
            source, target = (inside, outside) if out else (outside, inside)
            action(pltpu.make_async_copy(source, target, last_sem.at[which]))

    staged = copy_pieces(levels, below_staged, BLOCK, from_below, below_sem, False)
    staged += copy_pieces(levels, above_staged, BLOCK, from_above, above_sem, False)
    for copy in staged:
        copy.start()
    for which in range(4):
        move(which, False, START)
    for copy in staged:
        copy.wait()
    for which in range(4):
        columns = slice(which * HEAD_DIM, (which + 1) * HEAD_DIM)

        def first_source(head, block):
            start = pl.multiple_of(BLOCK + head * after_rows + block * BLOCK, TILE)
            return below_staged[pl.ds(start, BLOCK), columns]

        def last_source(head, block):
            slot = head - (heads - last_heads)
            start = BLOCK + slot * before_rows + block * BLOCK - (rows - before_rows)
            return above_staged[pl.ds(pl.multiple_of(start, TILE), BLOCK), columns]

        move(which, False, WAIT)
        overlay_both(
            plan, whole, which, (0, first_heads), (heads - last_heads, heads),
            first_source, last_source)
        move(which, True, START)
    for which in range(4):
        move(which, True, WAIT)


def merge_returned(plan, from_below, from_above, outs, levels):
    rows, width = outs[0].shape
    count = len(levels)
    anywhere = pl.BlockSpec(memory_space=pl.ANY)
    staged = pltpu.VMEM((levels[-1] + 2 * BLOCK, 4 * HEAD_DIM), jnp.bfloat16)
    return pl.pallas_call(
        functools.partial(return_kernel, levels),
        in_specs=[pl.BlockSpec(memory_space=pltpu.SMEM)] + [anywhere] * (2 * count + 4),
        out_specs=[anywhere] * 4,
        out_shape=[jax.ShapeDtypeStruct((rows, width), jnp.bfloat16)] * 4,
        input_output_aliases={1 + 2 * count + which: which for which in range(4)},
        scratch_shapes=[
            pltpu.VMEM((4, rows, width), jnp.bfloat16),
            staged,
            staged,
            pltpu.SemaphoreType.DMA((4,)),
            pltpu.SemaphoreType.DMA((4,)),
            pltpu.SemaphoreType.DMA((count,)),
            pltpu.SemaphoreType.DMA((count,)),
        ],
        compiler_params=pltpu.CompilerParams(vmem_limit_bytes=VMEM_LIMIT),
        name="merge_returned",
    )(plan, *from_below, *from_above, *outs)


def passed_along(value, steps):
    count = lax.axis_size("dp")
    leading, last = max(0, -steps), min(count, count - steps)
    return lax.ppermute(value, "dp", [(source, source + steps) for source in range(leading, last)])


def body(queries, keys, values, out_grad, lengths):
    rows, width = queries.shape
    heads = width // HEAD_DIM
    arrays = (queries, keys, values, out_grad)
    levels = size_levels(rows, heads)
    menu = [(levels[down], levels[up]) for down, up in size_menu(levels)]
    plan, choice = make_plan(lengths, rows, heads, lax.axis_size("dp"), menu)
    down, up = pack(plan, arrays, levels)
    from_above = [passed_along(down[0], -1)]
    from_below = [passed_along(up[0], 1)]
    local = local_attention(lengths, arrays)
    back_up, kept_above = crossing_images(True, plan, arrays, from_above, levels)
    back_down, kept_below = crossing_images(False, plan, arrays, from_below, levels)
    returned_below = [passed_along(back_up[0], 1)]
    returned_above = [passed_along(back_down[0], -1)]
    outs = merge_kept(plan, kept_above, kept_below, local)
    return tuple(merge_returned(plan, returned_below, returned_above, outs, levels))


def solution(mesh):
    in_specs = (P("dp", "tensor"), P("dp", "tensor"), P("dp", "tensor"), P("dp", "tensor"), P())
    out_specs = (P("dp", "tensor"), P("dp", "tensor"), P("dp", "tensor"), P("dp", "tensor"))
    return jax.shard_map(body, mesh=mesh, in_specs=in_specs, out_specs=out_specs, check_vma=False)
```

```python
import functools
import math

import jax
import jax.numpy as jnp
from jax import lax
from jax.experimental import pallas as pl
from jax.experimental.pallas import tpu as pltpu
from jax.sharding import PartitionSpec as P

HEAD_DIM = 128
TILE = 16
BLOCK = 64
LOCAL_CHUNK = 256
CROSSING_CHUNK = 512
FACTOR = 1.0 / math.sqrt(HEAD_DIM)
LOG2E = 1.4426950408889634
VMEM_LIMIT = 32 * 1024 * 1024
PACK_VMEM_LIMIT = 60 * 1024 * 1024

(A_BELOW, C_BELOW, HERE_BELOW, THERE_BELOW, A_ABOVE, C_ABOVE, HERE_ABOVE, THERE_ABOVE,
 DOWN_LEVEL, UP_LEVEL) = range(10)

LEVEL_UNITS = (6, 12)


def round_up(value):
    return (value + (TILE - 1)) // TILE * TILE


def worst_case_rows(rows, heads):
    worst = 0
    for before in range(TILE, rows + 1, TILE):
        for after in range(TILE, rows + TILE - before + 1, TILE):
            needed = min(max(after * low, before * (heads - low)) for low in range(heads + 1))
            worst = max(worst, needed)
    return worst


def size_levels(rows, heads):
    unit = rows * heads // 48
    most = worst_case_rows(rows, heads)
    return tuple(sorted(level * unit for level in LEVEL_UNITS if level * unit < most)) + (most,)


def size_menu(levels):
    count = len(levels)
    pairs = [(down, up) for down in range(count) for up in range(count)]
    return sorted(pairs, key=lambda pair: (levels[pair[0]] + levels[pair[1]], pair))


def make_plan(heads, rows, blocks, levels, lengths, plan, choice, before_edge, after_edge):
    menu = size_menu(levels)

    def clear(edge, carry):
        before_edge[edge] = 0
        after_edge[edge] = 0
        return carry

    lax.fori_loop(0, blocks + 1, clear, 0)

    def place(image, start):
        end = start + lengths[image]
        edge = (end - 1) // rows

        @pl.when(edge > start // rows)
        def _():
            before_edge[edge] = edge * rows - start
            after_edge[edge] = end - edge * rows

        return end

    lax.fori_loop(0, lengths.shape[0], place, 0)

    entry = lax.broadcasted_iota(jnp.int32, (8, 128), 1)
    down_limit = jnp.full((8, 128), -1, jnp.int32)
    up_limit = jnp.full((8, 128), -1, jnp.int32)
    for number, (down, up) in enumerate(menu):
        down_limit = jnp.where(entry == number, levels[down], down_limit)
        up_limit = jnp.where(entry == number, levels[up], up_limit)

    def check(edge, fits):
        after = round_up(after_edge[edge])
        before = round_up(before_edge[edge])
        taken = jnp.zeros((8, 128), jnp.int32)
        for count in range(1, heads + 1):
            taken += jnp.where(after * count <= down_limit, 1, 0)
            taken += jnp.where(before * count <= up_limit, 1, 0)
        return jnp.minimum(fits, jnp.where(taken >= heads, 1, 0))

    fits = lax.fori_loop(1, blocks, check, jnp.ones((8, 128), jnp.int32))
    chosen = jnp.min(jnp.where(fits == 1, entry, len(menu) - 1))
    down_level = jnp.int32(len(levels) - 1)
    up_level = jnp.int32(len(levels) - 1)
    down_rows = jnp.int32(levels[-1])
    up_rows = jnp.int32(levels[-1])
    for number, (down, up) in enumerate(menu[:-1]):
        down_level = jnp.where(chosen == number, down, down_level)
        up_level = jnp.where(chosen == number, up, up_level)
        down_rows = jnp.where(chosen == number, levels[down], down_rows)
        up_rows = jnp.where(chosen == number, levels[up], up_rows)
    choice[0] = chosen
    plan[DOWN_LEVEL] = down_level
    plan[UP_LEVEL] = up_level

    block = lax.axis_index("dp")
    for field, edge in ((A_BELOW, block), (A_ABOVE, block + 1)):
        before = before_edge[edge]
        after = after_edge[edge]
        most = jnp.int32(0)
        least = jnp.int32(heads)
        for count in range(1, heads + 1):
            most += jnp.where(round_up(after) * count <= down_rows, 1, 0)
            least -= jnp.where(round_up(before) * count <= up_rows, 1, 0)
        low = jnp.clip(jnp.int32(heads // 2), least, most)
        plan[field] = before
        plan[field + 1] = after
        plan[field + 2] = jnp.where(before > 0, low, 0)
        plan[field + 3] = jnp.where(before > 0, heads - low, 0)


def tiles(start, size):
    return pl.ds(pl.multiple_of(start, TILE), pl.multiple_of(size, TILE))


def lanes(head):
    return pl.ds(pl.multiple_of(head * HEAD_DIM, HEAD_DIM), HEAD_DIM)


def attention(query, key, value, grad, mask_columns, store, chunk):
    count = query.shape[0]
    key_t = key.T
    value_t = value.T
    across = (((1,), (1,)), ((), ()))
    chunks = [slice(first, first + chunk) for first in range(0, count, chunk)]
    scores = [
        lax.dot_general(key, query[cols], across, preferred_element_type=jnp.float32)
        for cols in chunks
    ]
    grad_probs = [
        lax.dot_general(value, grad[cols], across, preferred_element_type=jnp.float32)
        for cols in chunks
    ]
    probs_low = []
    grad_scores = []
    for number, cols in enumerate(chunks):
        masked = jnp.where(mask_columns(cols), scores[number], -1e30)
        top = jnp.max(masked, axis=0, keepdims=True)
        weights = jnp.exp2((masked - top) * (FACTOR * LOG2E))
        total = jnp.sum(weights, axis=0, keepdims=True)
        probs = weights * (1.0 / total)
        probs_low.append(probs.astype(jnp.bfloat16))
        result_t = jnp.dot(value_t, probs_low[-1], preferred_element_type=jnp.float32)
        weighted = probs * grad_probs[number]
        centre = jnp.sum(weighted, axis=0, keepdims=True)
        grad_scores.append((weighted - probs * centre).astype(jnp.bfloat16))
        grad_query_t = jnp.dot(key_t, grad_scores[-1], preferred_element_type=jnp.float32) * FACTOR
        store(0, cols, result_t.astype(jnp.bfloat16).T)
        store(1, cols, grad_query_t.astype(jnp.bfloat16).T)
    probs_low = jnp.concatenate(probs_low, axis=1)
    grad_scores = jnp.concatenate(grad_scores, axis=1)
    grad_value = jnp.dot(probs_low, grad, preferred_element_type=jnp.float32)
    store(3, slice(None), grad_value.astype(jnp.bfloat16))
    grad_key = jnp.dot(grad_scores, query, preferred_element_type=jnp.float32)
    store(2, slice(None), (grad_key * FACTOR).astype(jnp.bfloat16))


def local_kernel(lengths, query_ref, key_ref, value_ref, grad_ref, *rest):
    outs = rest[:4]
    image_rows = rest[4]
    count = query_ref.shape[0]

    @pl.when(pl.program_id(0) == 0)
    def _():
        position = lax.axis_index("dp") * count + lax.broadcasted_iota(jnp.int32, (8, count), 1)

        def place(image, carry):
            start, begin = carry
            return start + lengths[image], jnp.where(position >= start, start, begin)

        first = (jnp.int32(0), jnp.zeros((8, count), jnp.int32))
        _, begin = lax.fori_loop(0, lengths.shape[0], place, first)
        image_rows[...] = begin.astype(jnp.float32)

    image_col = image_rows[...].T[:, :1]

    def store(which, rows, part):
        outs[which][rows, :] = part

    attention(
        query_ref[...],
        key_ref[...],
        value_ref[...],
        grad_ref[...],
        lambda cols: image_col == image_rows[:1, cols],
        store,
        LOCAL_CHUNK,
    )


def local_attention(lengths, arrays):
    rows, width = arrays[0].shape
    heads = width // HEAD_DIM
    block = pl.BlockSpec((rows, HEAD_DIM), lambda head: (0, head))
    return pl.pallas_call(
        local_kernel,
        grid=(heads,),
        in_specs=[pl.BlockSpec(memory_space=pltpu.SMEM)] + [block] * 4,
        out_specs=[block] * 4,
        out_shape=[jax.ShapeDtypeStruct((rows, width), jnp.bfloat16)] * 4,
        scratch_shapes=[pltpu.VMEM((8, rows), jnp.float32)],
        compiler_params=pltpu.CompilerParams(vmem_limit_bytes=VMEM_LIMIT),
        cost_estimate=pl.CostEstimate(
            flops=12 * rows * rows * width, bytes_accessed=16 * rows * width, transcendentals=0
        ),
        name="local_images",
    )(lengths, *arrays)


START = lambda copy: copy.start()
WAIT = lambda copy: copy.wait()


def pieces(levels):
    return [(0, levels[0])] + [(levels[0], level - levels[0]) for level in levels[1:]]


def copy_pieces(levels, level, staged, offset, arrays, sems, out, action):
    for number, (start, size) in enumerate(pieces(levels)):
        inside = staged.at[pl.ds(offset + start, size)]
        outside = arrays[number]
        source, target = (inside, outside) if out else (outside, inside)

        @pl.when(True if number == 0 else level == number)
        def _():
            action(pltpu.make_async_copy(source, target, sems.at[number]))


def pack_kernel(levels, blocks, lengths, query, key, value, grad, *rest):
    count = len(levels)
    plan, choice = rest[:2]
    down, up = rest[2:2 + count], rest[2 + count:2 + 2 * count]
    before_edge, after_edge, held, down_staged, up_staged, sems, down_sem, up_sem = rest[
        2 + 2 * count:]
    rows, width = query.shape
    heads = width // HEAD_DIM
    loads = [
        pltpu.make_async_copy(array, held.at[which, pl.ds(0, rows)], sems.at[which])
        for which, array in enumerate((query, key, value, grad))
    ]
    for copy in loads:
        copy.start()
    make_plan(heads, rows, blocks, levels, lengths, plan, choice, before_edge, after_edge)
    after = round_up(plan[C_BELOW])
    before = round_up(plan[A_ABOVE])
    to_lower = plan[HERE_BELOW]
    to_upper = plan[THERE_ABOVE]

    def gather(staged, count, first_head, taken, first_row):
        steps = (taken + BLOCK - 1) // BLOCK

        def one_head(slot, carry):
            def one_block(step, carry):
                source = pl.ds(pl.multiple_of(first_row + step * BLOCK, TILE), BLOCK)
                target = pl.ds(pl.multiple_of(slot * taken + step * BLOCK, TILE), BLOCK)
                for which in range(4):
                    staged[target, which * HEAD_DIM:(which + 1) * HEAD_DIM] = held[
                        which, source, lanes(first_head + slot)]
                return carry

            return lax.fori_loop(0, steps, one_block, carry)

        lax.fori_loop(0, count, one_head, 0)

    for copy in loads:
        copy.wait()
    gather(down_staged, to_lower, 0, after, 0)
    move_down = functools.partial(
        copy_pieces, levels, plan[DOWN_LEVEL], down_staged, 0, down, down_sem, True)
    move_down(START)
    gather(up_staged, to_upper, heads - to_upper, before, rows - before)
    move_up = functools.partial(
        copy_pieces, levels, plan[UP_LEVEL], up_staged, 0, up, up_sem, True)
    move_up(START)
    move_down(WAIT)
    move_up(WAIT)


def piece_shapes(levels):
    return [jax.ShapeDtypeStruct((size, 4 * HEAD_DIM), jnp.bfloat16) for _, size in pieces(levels)]


def pack(lengths, arrays, levels, blocks):
    rows, width = arrays[0].shape
    count = len(levels)
    anywhere = pl.BlockSpec(memory_space=pl.ANY)
    scalars = pl.BlockSpec(memory_space=pltpu.SMEM)
    staged = pltpu.VMEM((levels[-1] + BLOCK, 4 * HEAD_DIM), jnp.bfloat16)
    plan, choice, *outs = pl.pallas_call(
        functools.partial(pack_kernel, levels, blocks),
        in_specs=[scalars] + [anywhere] * 4,
        out_specs=[scalars] * 2 + [anywhere] * (2 * count),
        out_shape=[
            jax.ShapeDtypeStruct((UP_LEVEL + 1,), jnp.int32),
            jax.ShapeDtypeStruct((1,), jnp.int32),
        ] + piece_shapes(levels) * 2,
        scratch_shapes=[
            pltpu.SMEM((blocks + 1,), jnp.int32),
            pltpu.SMEM((blocks + 1,), jnp.int32),
            pltpu.VMEM((4, rows + BLOCK, width), jnp.bfloat16),
            staged,
            staged,
            pltpu.SemaphoreType.DMA((4,)),
            pltpu.SemaphoreType.DMA((count,)),
            pltpu.SemaphoreType.DMA((count,)),
        ],
        compiler_params=pltpu.CompilerParams(vmem_limit_bytes=PACK_VMEM_LIMIT),
        name="pack",
    )(lengths, *arrays)
    return plan, choice, outs[:count], outs[count:]


def crossing_kernel(levels, above, plan, query, key, value, grad, *rest):
    count = len(levels)
    received, back, kept = rest[:count], rest[count:2 * count], rest[2 * count]
    own, staged_in, staged_out, result, own_sem, in_sem, out_sem, kept_sem = rest[2 * count + 1:]
    rows, width = query.shape
    heads = width // HEAD_DIM
    jobs = plan[HERE_ABOVE] if above else plan[THERE_BELOW]
    before = plan[A_ABOVE] if above else plan[A_BELOW]
    after = plan[C_ABOVE] if above else plan[C_BELOW]
    first_head = 0 if above else heads - jobs
    if above:
        own_part = tiles(rows - round_up(before), round_up(before))
        moved_rows = round_up(after)
        margin = 0
        shift = 0
    else:
        own_part = tiles(0, round_up(after))
        moved_rows = round_up(before)
        margin = rows
        shift = moved_rows

    def load_own(action):
        for which, array in enumerate((query, key, value, grad)):
            action(pltpu.make_async_copy(
                array.at[own_part], own.at[which, own_part], own_sem.at[which]))

    def keep(job):
        buffer = lax.rem(job, 2)
        return pltpu.make_async_copy(
            result.at[buffer, own_part], kept.at[job, own_part], kept_sem.at[buffer])

    position = lax.broadcasted_iota(jnp.int32, (rows, HEAD_DIM), 0)
    in_first = position < after
    in_last = position >= rows - before
    in_moved, in_own = (in_first, in_last) if above else (in_last, in_first)
    key_position = lax.broadcasted_iota(jnp.int32, (rows, 1), 0)
    in_image = (key_position < after) | (key_position >= rows - before)

    def one_job(step, carry):
        job = step if above else jobs - 1 - step
        buffer = lax.rem(job, 2)
        window = pl.ds(pl.multiple_of(job * moved_rows + shift, TILE), rows)

        @pl.when(step >= 2)
        def _():
            keep(job).wait()

        zero = jnp.zeros((rows, HEAD_DIM), jnp.bfloat16)
        operands = []
        for which in range(4):
            columns = slice(which * HEAD_DIM, (which + 1) * HEAD_DIM)
            operands.append(jnp.where(
                in_moved,
                staged_in[window, columns],
                jnp.where(in_own, own[which, :, lanes(first_head + job)], zero),
            ))

        def store(which, part_rows, part):
            result[buffer, part_rows, which * HEAD_DIM:(which + 1) * HEAD_DIM] = part

        attention(*operands, lambda cols: in_image, store, CROSSING_CHUNK)
        staged_out[window, :] = result[buffer]
        keep(job).start()
        return carry

    @pl.when(jobs > 0)
    def _():
        level = plan[DOWN_LEVEL] if above else plan[UP_LEVEL]
        stage = functools.partial(
            copy_pieces, levels, level, staged_in, margin, received, in_sem, False)
        send = functools.partial(
            copy_pieces, levels, level, staged_out, margin, back, out_sem, True)
        stage(START)
        load_own(START)
        load_own(WAIT)
        stage(WAIT)
        lax.fori_loop(0, jobs, one_job, 0)
        send(START)

        @pl.when(jobs >= 2)
        def _():
            keep(jobs - 2 if above else 1).wait()

        keep(jobs - 1 if above else 0).wait()
        send(WAIT)


def crossing_images(above, plan, arrays, received, levels):
    rows, width = arrays[0].shape
    heads = width // HEAD_DIM
    four = 4 * HEAD_DIM
    count = len(levels)
    anywhere = pl.BlockSpec(memory_space=pl.ANY)
    staged = pltpu.VMEM((levels[-1] + rows, four), jnp.bfloat16)
    outs = pl.pallas_call(
        functools.partial(crossing_kernel, levels, above),
        in_specs=[pl.BlockSpec(memory_space=pltpu.SMEM)] + [anywhere] * (4 + count),
        out_specs=[anywhere] * (count + 1),
        out_shape=piece_shapes(levels)
        + [jax.ShapeDtypeStruct((heads, rows, four), jnp.bfloat16)],
        scratch_shapes=[
            pltpu.VMEM((4, rows, width), jnp.bfloat16),
            staged,
            staged,
            pltpu.VMEM((2, rows, four), jnp.bfloat16),
            pltpu.SemaphoreType.DMA((4,)),
            pltpu.SemaphoreType.DMA((count,)),
            pltpu.SemaphoreType.DMA((count,)),
            pltpu.SemaphoreType.DMA((2,)),
        ],
        compiler_params=pltpu.CompilerParams(vmem_limit_bytes=VMEM_LIMIT),
        name="above_images" if above else "below_images",
    )(plan, *arrays, *received)
    return outs[:count], outs[count]


def overlay(whole, which, first_head, last_head, first_block, last_block, wanted, source):
    def one_head(head, carry):
        def one_block(block, carry):
            part = pl.ds(pl.multiple_of(block * BLOCK, BLOCK), BLOCK)
            position = block * BLOCK + lax.broadcasted_iota(jnp.int32, (BLOCK, HEAD_DIM), 0)
            whole[which, part, lanes(head)] = jnp.where(
                wanted(position), source(head, block), whole[which, part, lanes(head)])
            return carry

        return lax.fori_loop(first_block, last_block, one_block, carry)

    lax.fori_loop(first_head, last_head, one_head, 0)


def overlay_both(plan, whole, which, first_heads, last_heads, first_source, last_source):
    rows = whole.shape[1]
    after = plan[C_BELOW]
    begin = rows - plan[A_ABOVE]
    overlay(whole, which, *first_heads, 0, (after + BLOCK - 1) // BLOCK,
            lambda position: position < after, first_source)
    overlay(whole, which, *last_heads, begin // BLOCK, rows // BLOCK,
            lambda position: position >= begin, last_source)


def keep_kernel(plan, kept_above, kept_below, *rest):
    local, outs = rest[:4], rest[4:8]
    whole, first_part, last_part, whole_sem, first_sem, last_sem, out_sem = rest[8:]
    rows, width = local[0].shape
    heads = width // HEAD_DIM
    low_below = plan[HERE_BELOW]
    low_above = plan[HERE_ABOVE]
    below_jobs = plan[THERE_BELOW]
    first_tiles = tiles(0, round_up(plan[C_BELOW]))
    last_tiles = tiles(rows - round_up(plan[A_ABOVE]), round_up(plan[A_ABOVE]))

    def parts(action):
        for slot in range(heads):
            @pl.when(slot < below_jobs)
            def _():
                action(pltpu.make_async_copy(
                    kept_below.at[slot, first_tiles], first_part.at[slot, first_tiles],
                    first_sem.at[slot]))

            @pl.when(slot < low_above)
            def _():
                action(pltpu.make_async_copy(
                    kept_above.at[slot, last_tiles], last_part.at[slot, last_tiles],
                    last_sem.at[slot]))

    loads = [
        pltpu.make_async_copy(local[which], whole.at[which], whole_sem.at[which])
        for which in range(4)
    ]
    saves = [
        pltpu.make_async_copy(whole.at[which], outs[which], out_sem.at[which])
        for which in range(4)
    ]
    parts(START)
    for copy in loads:
        copy.start()
    parts(WAIT)
    for which in range(4):
        columns = slice(which * HEAD_DIM, (which + 1) * HEAD_DIM)

        def first_source(head, block):
            part = pl.ds(pl.multiple_of(block * BLOCK, BLOCK), BLOCK)
            return first_part[head - low_below, part, columns]

        def last_source(head, block):
            part = pl.ds(pl.multiple_of(block * BLOCK, BLOCK), BLOCK)
            return last_part[head, part, columns]

        loads[which].wait()
        overlay_both(
            plan, whole, which, (low_below, low_below + below_jobs), (0, low_above),
            first_source, last_source)
        saves[which].start()
    for copy in saves:
        copy.wait()


def merge_kept(plan, kept_above, kept_below, local):
    rows, width = local[0].shape
    heads = width // HEAD_DIM
    anywhere = pl.BlockSpec(memory_space=pl.ANY)
    windows = pltpu.VMEM((heads, rows, 4 * HEAD_DIM), jnp.bfloat16)
    return pl.pallas_call(
        keep_kernel,
        in_specs=[pl.BlockSpec(memory_space=pltpu.SMEM)] + [anywhere] * 6,
        out_specs=[anywhere] * 4,
        out_shape=[jax.ShapeDtypeStruct((rows, width), jnp.bfloat16)] * 4,
        scratch_shapes=[
            pltpu.VMEM((4, rows, width), jnp.bfloat16),
            windows,
            windows,
            pltpu.SemaphoreType.DMA((4,)),
            pltpu.SemaphoreType.DMA((heads,)),
            pltpu.SemaphoreType.DMA((heads,)),
            pltpu.SemaphoreType.DMA((4,)),
        ],
        compiler_params=pltpu.CompilerParams(vmem_limit_bytes=VMEM_LIMIT),
        cost_estimate=pl.CostEstimate(
            flops=0, bytes_accessed=32 * rows * width, transcendentals=0
        ),
        name="merge_kept",
    )(plan, kept_above, kept_below, *local)


def return_kernel(levels, plan, *rest):
    count = len(levels)
    from_below, from_above = rest[:count], rest[count:2 * count]
    outs = rest[2 * count + 4:2 * count + 8]
    whole, below_staged, above_staged, first_sem, last_sem, below_sem, above_sem = rest[2 * count + 8:]
    rows = whole.shape[1]
    heads = whole.shape[2] // HEAD_DIM
    after_rows = round_up(plan[C_BELOW])
    before_rows = round_up(plan[A_ABOVE])
    first_heads = plan[HERE_BELOW]
    last_heads = plan[THERE_ABOVE]
    begin = (rows - plan[A_ABOVE]) // BLOCK * BLOCK
    end = (plan[C_BELOW] + BLOCK - 1) // BLOCK * BLOCK
    both = (first_heads > 0) & (last_heads > 0)
    first_end = jnp.where(both, jnp.minimum(end, begin), end)

    def block_rows(start, size):
        return pl.ds(pl.multiple_of(start, BLOCK), pl.multiple_of(size, BLOCK))

    first_copied = (first_heads > 0) & (first_end > 0)

    def move(which, out, action):
        @pl.when(first_copied)
        def _():
            part = block_rows(0, first_end)
            inside, outside = whole.at[which, part], outs[which].at[part]
            source, target = (inside, outside) if out else (outside, inside)
            action(pltpu.make_async_copy(source, target, first_sem.at[which]))

        @pl.when(last_heads > 0)
        def _():
            part = block_rows(begin, rows - begin)
            inside, outside = whole.at[which, part], outs[which].at[part]
            source, target = (inside, outside) if out else (outside, inside)
            action(pltpu.make_async_copy(source, target, last_sem.at[which]))

    stage_below = functools.partial(
        copy_pieces, levels, plan[DOWN_LEVEL], below_staged, BLOCK, from_below, below_sem, False)
    stage_above = functools.partial(
        copy_pieces, levels, plan[UP_LEVEL], above_staged, BLOCK, from_above, above_sem, False)
    stage_below(START)
    stage_above(START)
    for which in range(4):
        move(which, False, START)
    stage_below(WAIT)
    stage_above(WAIT)
    for which in range(4):
        columns = slice(which * HEAD_DIM, (which + 1) * HEAD_DIM)

        def first_source(head, block):
            start = pl.multiple_of(BLOCK + head * after_rows + block * BLOCK, TILE)
            return below_staged[pl.ds(start, BLOCK), columns]

        def last_source(head, block):
            slot = head - (heads - last_heads)
            start = BLOCK + slot * before_rows + block * BLOCK - (rows - before_rows)
            return above_staged[pl.ds(pl.multiple_of(start, TILE), BLOCK), columns]

        move(which, False, WAIT)
        overlay_both(
            plan, whole, which, (0, first_heads), (heads - last_heads, heads),
            first_source, last_source)
        move(which, True, START)
    for which in range(4):
        move(which, True, WAIT)


def merge_returned(plan, from_below, from_above, outs, levels):
    rows, width = outs[0].shape
    count = len(levels)
    anywhere = pl.BlockSpec(memory_space=pl.ANY)
    staged = pltpu.VMEM((levels[-1] + 2 * BLOCK, 4 * HEAD_DIM), jnp.bfloat16)
    return pl.pallas_call(
        functools.partial(return_kernel, levels),
        in_specs=[pl.BlockSpec(memory_space=pltpu.SMEM)] + [anywhere] * (2 * count + 4),
        out_specs=[anywhere] * 4,
        out_shape=[jax.ShapeDtypeStruct((rows, width), jnp.bfloat16)] * 4,
        input_output_aliases={1 + 2 * count + which: which for which in range(4)},
        scratch_shapes=[
            pltpu.VMEM((4, rows, width), jnp.bfloat16),
            staged,
            staged,
            pltpu.SemaphoreType.DMA((4,)),
            pltpu.SemaphoreType.DMA((4,)),
            pltpu.SemaphoreType.DMA((count,)),
            pltpu.SemaphoreType.DMA((count,)),
        ],
        compiler_params=pltpu.CompilerParams(vmem_limit_bytes=VMEM_LIMIT),
        name="merge_returned",
    )(plan, *from_below, *from_above, *outs)


def passed_along(value, steps):
    count = lax.axis_size("dp")
    leading, last = max(0, -steps), min(count, count - steps)
    return lax.ppermute(value, "dp", [(source, source + steps) for source in range(leading, last)])


def pass_further(choice, levels, down, down_steps, up, up_steps):
    if len(levels) == 1:
        return [], []

    def send(pair, down, up):
        sent = []
        for level, arrays, steps in ((pair[0], down, down_steps), (pair[1], up, up_steps)):
            for number, array in enumerate(arrays, start=1):
                chosen = number == level
                sent.append(passed_along(array, steps) if chosen else jnp.zeros_like(array))
        return sent

    branches = [functools.partial(send, pair) for pair in size_menu(levels)]
    sent = lax.switch(choice[0], branches, list(down), list(up))
    return sent[:len(down)], sent[len(down):]


def body(queries, keys, values, out_grad, lengths):
    rows, width = queries.shape
    arrays = (queries, keys, values, out_grad)
    levels = size_levels(rows, width // HEAD_DIM)
    plan, choice, down, up = pack(lengths, arrays, levels, lax.axis_size("dp"))
    from_above = passed_along(down[0], -1)
    from_below = passed_along(up[0], 1)
    local = local_attention(lengths, arrays)
    choice, local = lax.optimization_barrier((choice, local))
    more_above, more_below = pass_further(choice, levels, down[1:], -1, up[1:], 1)
    from_above, from_below = [from_above, *more_above], [from_below, *more_below]
    back_up, kept_above = crossing_images(True, plan, arrays, from_above, levels)
    returned_below = passed_along(back_up[0], 1)
    back_down, kept_below = crossing_images(False, plan, arrays, from_below, levels)
    returned_above = passed_along(back_down[0], -1)
    outs = merge_kept(plan, kept_above, kept_below, local)
    choice, outs = lax.optimization_barrier((choice, outs))
    more_below, more_above = pass_further(choice, levels, back_up[1:], 1, back_down[1:], -1)
    returned_below, returned_above = [returned_below, *more_below], [returned_above, *more_above]
    return tuple(merge_returned(plan, returned_below, returned_above, outs, levels))


def solution(mesh):
    in_specs = (P("dp", "tensor"), P("dp", "tensor"), P("dp", "tensor"), P("dp", "tensor"), P())
    out_specs = (P("dp", "tensor"), P("dp", "tensor"), P("dp", "tensor"), P("dp", "tensor"))
    return jax.shard_map(body, mesh=mesh, in_specs=in_specs, out_specs=out_specs, check_vma=False)
```

```python
import functools
import math

import jax
import jax.numpy as jnp
from jax import lax
from jax.experimental import pallas as pl
from jax.experimental.pallas import tpu as pltpu
from jax.sharding import PartitionSpec as P

HEAD_DIM = 128
TILE = 16
BLOCK = 64
LOCAL_CHUNK = 256
CROSSING_CHUNK = 512
FACTOR = 1.0 / math.sqrt(HEAD_DIM)
LOG2E = 1.4426950408889634
VMEM_LIMIT = 32 * 1024 * 1024
PACK_VMEM_LIMIT = 60 * 1024 * 1024

(A_BELOW, C_BELOW, HERE_BELOW, THERE_BELOW, A_ABOVE, C_ABOVE, HERE_ABOVE, THERE_ABOVE,
 DOWN_LEVEL, UP_LEVEL) = range(10)

LEVEL_UNITS = ()


def round_up(value):
    return (value + (TILE - 1)) // TILE * TILE


def worst_case_rows(rows, heads):
    worst = 0
    for before in range(TILE, rows + 1, TILE):
        for after in range(TILE, rows + TILE - before + 1, TILE):
            needed = min(max(after * low, before * (heads - low)) for low in range(heads + 1))
            worst = max(worst, needed)
    return worst


def size_levels(rows, heads):
    unit = rows * heads // 48
    most = worst_case_rows(rows, heads)
    return tuple(sorted(level * unit for level in LEVEL_UNITS if level * unit < most)) + (most,)


def size_menu(levels):
    count = len(levels)
    pairs = [(down, up) for down in range(count) for up in range(count)]
    return sorted(pairs, key=lambda pair: (levels[pair[0]] + levels[pair[1]], pair))


def make_plan(heads, rows, blocks, levels, lengths, plan, down_choice, up_choice, before_edge, after_edge):
    menu = size_menu(levels)

    def clear(edge, carry):
        before_edge[edge] = 0
        after_edge[edge] = 0
        return carry

    lax.fori_loop(0, blocks + 1, clear, 0)

    def place(image, start):
        end = start + lengths[image]
        edge = (end - 1) // rows

        @pl.when(edge > start // rows)
        def _():
            before_edge[edge] = edge * rows - start
            after_edge[edge] = end - edge * rows

        return end

    lax.fori_loop(0, lengths.shape[0], place, 0)

    entry = lax.broadcasted_iota(jnp.int32, (8, 128), 1)
    down_limit = jnp.full((8, 128), -1, jnp.int32)
    up_limit = jnp.full((8, 128), -1, jnp.int32)
    for number, (down, up) in enumerate(menu):
        down_limit = jnp.where(entry == number, levels[down], down_limit)
        up_limit = jnp.where(entry == number, levels[up], up_limit)

    def check(edge, fits):
        after = round_up(after_edge[edge])
        before = round_up(before_edge[edge])
        taken = jnp.zeros((8, 128), jnp.int32)
        for count in range(1, heads + 1):
            taken += jnp.where(after * count <= down_limit, 1, 0)
            taken += jnp.where(before * count <= up_limit, 1, 0)
        return jnp.minimum(fits, jnp.where(taken >= heads, 1, 0))

    fits = lax.fori_loop(1, blocks, check, jnp.ones((8, 128), jnp.int32))
    chosen = jnp.min(jnp.where(fits == 1, entry, len(menu) - 1))
    down_level = jnp.int32(len(levels) - 1)
    up_level = jnp.int32(len(levels) - 1)
    down_rows = jnp.int32(levels[-1])
    up_rows = jnp.int32(levels[-1])
    for number, (down, up) in enumerate(menu[:-1]):
        down_level = jnp.where(chosen == number, down, down_level)
        up_level = jnp.where(chosen == number, up, up_level)
        down_rows = jnp.where(chosen == number, levels[down], down_rows)
        up_rows = jnp.where(chosen == number, levels[up], up_rows)
    down_choice[0] = down_level
    up_choice[0] = up_level
    plan[DOWN_LEVEL] = down_level
    plan[UP_LEVEL] = up_level

    block = lax.axis_index("dp")
    for field, edge in ((A_BELOW, block), (A_ABOVE, block + 1)):
        before = before_edge[edge]
        after = after_edge[edge]
        most = jnp.int32(0)
        least = jnp.int32(heads)
        for count in range(1, heads + 1):
            most += jnp.where(round_up(after) * count <= down_rows, 1, 0)
            least -= jnp.where(round_up(before) * count <= up_rows, 1, 0)
        low = jnp.clip(jnp.int32(heads // 2), least, most)
        plan[field] = before
        plan[field + 1] = after
        plan[field + 2] = jnp.where(before > 0, low, 0)
        plan[field + 3] = jnp.where(before > 0, heads - low, 0)


def tiles(start, size):
    return pl.ds(pl.multiple_of(start, TILE), pl.multiple_of(size, TILE))


def lanes(head):
    return pl.ds(pl.multiple_of(head * HEAD_DIM, HEAD_DIM), HEAD_DIM)


def attention(query, key, value, grad, mask_columns, store, chunk):
    count = query.shape[0]
    key_t = key.T
    value_t = value.T
    across = (((1,), (1,)), ((), ()))
    chunks = [slice(first, first + chunk) for first in range(0, count, chunk)]
    scores = [
        lax.dot_general(key, query[cols], across, preferred_element_type=jnp.float32)
        for cols in chunks
    ]
    grad_probs = [
        lax.dot_general(value, grad[cols], across, preferred_element_type=jnp.float32)
        for cols in chunks
    ]
    probs_low = []
    grad_scores = []
    for number, cols in enumerate(chunks):
        masked = jnp.where(mask_columns(cols), scores[number], -1e30)
        top = jnp.max(masked, axis=0, keepdims=True)
        weights = jnp.exp2((masked - top) * (FACTOR * LOG2E))
        total = jnp.sum(weights, axis=0, keepdims=True)
        probs = weights * (1.0 / total)
        probs_low.append(probs.astype(jnp.bfloat16))
        result_t = jnp.dot(value_t, probs_low[-1], preferred_element_type=jnp.float32)
        weighted = probs * grad_probs[number]
        centre = jnp.sum(weighted, axis=0, keepdims=True)
        grad_scores.append((weighted - probs * centre).astype(jnp.bfloat16))
        grad_query_t = jnp.dot(key_t, grad_scores[-1], preferred_element_type=jnp.float32) * FACTOR
        store(0, cols, result_t.astype(jnp.bfloat16).T)
        store(1, cols, grad_query_t.astype(jnp.bfloat16).T)
    probs_low = jnp.concatenate(probs_low, axis=1)
    grad_scores = jnp.concatenate(grad_scores, axis=1)
    grad_value = jnp.dot(probs_low, grad, preferred_element_type=jnp.float32)
    store(3, slice(None), grad_value.astype(jnp.bfloat16))
    grad_key = jnp.dot(grad_scores, query, preferred_element_type=jnp.float32)
    store(2, slice(None), (grad_key * FACTOR).astype(jnp.bfloat16))


def local_kernel(lengths, query_ref, key_ref, value_ref, grad_ref, *rest):
    outs = rest[:4]
    image_rows = rest[4]
    count = query_ref.shape[0]

    @pl.when(pl.program_id(0) == 0)
    def _():
        position = lax.axis_index("dp") * count + lax.broadcasted_iota(jnp.int32, (8, count), 1)

        def place(image, carry):
            start, begin = carry
            return start + lengths[image], jnp.where(position >= start, start, begin)

        first = (jnp.int32(0), jnp.zeros((8, count), jnp.int32))
        _, begin = lax.fori_loop(0, lengths.shape[0], place, first)
        image_rows[...] = begin.astype(jnp.float32)

    image_col = image_rows[...].T[:, :1]

    def store(which, rows, part):
        outs[which][rows, :] = part

    attention(
        query_ref[...],
        key_ref[...],
        value_ref[...],
        grad_ref[...],
        lambda cols: image_col == image_rows[:1, cols],
        store,
        LOCAL_CHUNK,
    )


def local_attention(lengths, arrays):
    rows, width = arrays[0].shape
    heads = width // HEAD_DIM
    block = pl.BlockSpec((rows, HEAD_DIM), lambda head: (0, head))
    return pl.pallas_call(
        local_kernel,
        grid=(heads,),
        in_specs=[pl.BlockSpec(memory_space=pltpu.SMEM)] + [block] * 4,
        out_specs=[block] * 4,
        out_shape=[jax.ShapeDtypeStruct((rows, width), jnp.bfloat16)] * 4,
        scratch_shapes=[pltpu.VMEM((8, rows), jnp.float32)],
        compiler_params=pltpu.CompilerParams(vmem_limit_bytes=VMEM_LIMIT),
        cost_estimate=pl.CostEstimate(
            flops=12 * rows * rows * width, bytes_accessed=16 * rows * width, transcendentals=0
        ),
        name="local_images",
    )(lengths, *arrays)


START = lambda copy: copy.start()
WAIT = lambda copy: copy.wait()


def pieces(levels):
    starts = (0,) + levels[:-1]
    return [(start, end - start) for start, end in zip(starts, levels)]


def copy_pieces(levels, level, staged, offset, arrays, sems, out, action):
    for number, (start, size) in enumerate(pieces(levels)):
        inside = staged.at[pl.ds(offset + start, size)]
        outside = arrays[number]
        source, target = (inside, outside) if out else (outside, inside)

        @pl.when(True if number == 0 else level >= number)
        def _():
            action(pltpu.make_async_copy(source, target, sems.at[number]))


def pack_kernel(levels, blocks, lengths, query, key, value, grad, *rest):
    count = len(levels)
    plan, down_choice, up_choice = rest[:3]
    down, up = rest[3:3 + count], rest[3 + count:3 + 2 * count]
    before_edge, after_edge, held, down_staged, up_staged, sems, down_sem, up_sem = rest[
        3 + 2 * count:]
    rows, width = query.shape
    heads = width // HEAD_DIM
    loads = [
        pltpu.make_async_copy(array, held.at[which, pl.ds(0, rows)], sems.at[which])
        for which, array in enumerate((query, key, value, grad))
    ]
    for copy in loads:
        copy.start()
    make_plan(
        heads, rows, blocks, levels, lengths, plan, down_choice, up_choice,
        before_edge, after_edge)
    after = round_up(plan[C_BELOW])
    before = round_up(plan[A_ABOVE])
    to_lower = plan[HERE_BELOW]
    to_upper = plan[THERE_ABOVE]

    def gather(staged, count, first_head, taken, first_row):
        steps = (taken + BLOCK - 1) // BLOCK

        def one_head(slot, carry):
            def one_block(step, carry):
                source = pl.ds(pl.multiple_of(first_row + step * BLOCK, TILE), BLOCK)
                target = pl.ds(pl.multiple_of(slot * taken + step * BLOCK, TILE), BLOCK)
                for which in range(4):
                    staged[target, which * HEAD_DIM:(which + 1) * HEAD_DIM] = held[
                        which, source, lanes(first_head + slot)]
                return carry

            return lax.fori_loop(0, steps, one_block, carry)

        lax.fori_loop(0, count, one_head, 0)

    for copy in loads:
        copy.wait()
    gather(down_staged, to_lower, 0, after, 0)
    move_down = functools.partial(
        copy_pieces, levels, plan[DOWN_LEVEL], down_staged, 0, down, down_sem, True)
    move_down(START)
    gather(up_staged, to_upper, heads - to_upper, before, rows - before)
    move_up = functools.partial(
        copy_pieces, levels, plan[UP_LEVEL], up_staged, 0, up, up_sem, True)
    move_up(START)
    move_down(WAIT)
    move_up(WAIT)


def piece_shapes(levels):
    return [jax.ShapeDtypeStruct((size, 4 * HEAD_DIM), jnp.bfloat16) for _, size in pieces(levels)]


def pack(lengths, arrays, levels, blocks):
    rows, width = arrays[0].shape
    count = len(levels)
    anywhere = pl.BlockSpec(memory_space=pl.ANY)
    scalars = pl.BlockSpec(memory_space=pltpu.SMEM)
    staged = pltpu.VMEM((levels[-1] + BLOCK, 4 * HEAD_DIM), jnp.bfloat16)
    plan, down_choice, up_choice, *outs = pl.pallas_call(
        functools.partial(pack_kernel, levels, blocks),
        in_specs=[scalars] + [anywhere] * 4,
        out_specs=[scalars] * 3 + [anywhere] * (2 * count),
        out_shape=[
            jax.ShapeDtypeStruct((UP_LEVEL + 1,), jnp.int32),
            jax.ShapeDtypeStruct((1,), jnp.int32),
            jax.ShapeDtypeStruct((1,), jnp.int32),
        ] + piece_shapes(levels) * 2,
        scratch_shapes=[
            pltpu.SMEM((blocks + 1,), jnp.int32),
            pltpu.SMEM((blocks + 1,), jnp.int32),
            pltpu.VMEM((4, rows + BLOCK, width), jnp.bfloat16),
            staged,
            staged,
            pltpu.SemaphoreType.DMA((4,)),
            pltpu.SemaphoreType.DMA((count,)),
            pltpu.SemaphoreType.DMA((count,)),
        ],
        compiler_params=pltpu.CompilerParams(vmem_limit_bytes=PACK_VMEM_LIMIT),
        name="pack",
    )(lengths, *arrays)
    return plan, down_choice, up_choice, outs[:count], outs[count:]


def crossing_kernel(levels, above, plan, query, key, value, grad, *rest):
    count = len(levels)
    received, back, kept = rest[:count], rest[count:2 * count], rest[2 * count]
    own, staged_in, staged_out, result, own_sem, in_sem, out_sem, kept_sem = rest[2 * count + 1:]
    rows, width = query.shape
    heads = width // HEAD_DIM
    jobs = plan[HERE_ABOVE] if above else plan[THERE_BELOW]
    before = plan[A_ABOVE] if above else plan[A_BELOW]
    after = plan[C_ABOVE] if above else plan[C_BELOW]
    first_head = 0 if above else heads - jobs
    if above:
        own_part = tiles(rows - round_up(before), round_up(before))
        moved_rows = round_up(after)
        margin = 0
        shift = 0
    else:
        own_part = tiles(0, round_up(after))
        moved_rows = round_up(before)
        margin = rows
        shift = moved_rows

    def load_own(action):
        for which, array in enumerate((query, key, value, grad)):
            action(pltpu.make_async_copy(
                array.at[own_part], own.at[which, own_part], own_sem.at[which]))

    def keep(job):
        buffer = lax.rem(job, 2)
        return pltpu.make_async_copy(
            result.at[buffer, own_part], kept.at[job, own_part], kept_sem.at[buffer])

    position = lax.broadcasted_iota(jnp.int32, (rows, HEAD_DIM), 0)
    in_first = position < after
    in_last = position >= rows - before
    in_moved, in_own = (in_first, in_last) if above else (in_last, in_first)
    key_position = lax.broadcasted_iota(jnp.int32, (rows, 1), 0)
    in_image = (key_position < after) | (key_position >= rows - before)

    def one_job(step, carry):
        job = step if above else jobs - 1 - step
        buffer = lax.rem(job, 2)
        window = pl.ds(pl.multiple_of(job * moved_rows + shift, TILE), rows)

        @pl.when(step >= 2)
        def _():
            keep(job).wait()

        zero = jnp.zeros((rows, HEAD_DIM), jnp.bfloat16)
        operands = []
        for which in range(4):
            columns = slice(which * HEAD_DIM, (which + 1) * HEAD_DIM)
            operands.append(jnp.where(
                in_moved,
                staged_in[window, columns],
                jnp.where(in_own, own[which, :, lanes(first_head + job)], zero),
            ))

        def store(which, part_rows, part):
            result[buffer, part_rows, which * HEAD_DIM:(which + 1) * HEAD_DIM] = part

        attention(*operands, lambda cols: in_image, store, CROSSING_CHUNK)
        staged_out[window, :] = result[buffer]
        keep(job).start()
        return carry

    @pl.when(jobs > 0)
    def _():
        level = plan[DOWN_LEVEL] if above else plan[UP_LEVEL]
        stage = functools.partial(
            copy_pieces, levels, level, staged_in, margin, received, in_sem, False)
        send = functools.partial(
            copy_pieces, levels, level, staged_out, margin, back, out_sem, True)
        stage(START)
        load_own(START)
        load_own(WAIT)
        stage(WAIT)
        lax.fori_loop(0, jobs, one_job, 0)
        send(START)

        @pl.when(jobs >= 2)
        def _():
            keep(jobs - 2 if above else 1).wait()

        keep(jobs - 1 if above else 0).wait()
        send(WAIT)


def crossing_images(above, plan, arrays, received, levels):
    rows, width = arrays[0].shape
    heads = width // HEAD_DIM
    four = 4 * HEAD_DIM
    count = len(levels)
    anywhere = pl.BlockSpec(memory_space=pl.ANY)
    staged = pltpu.VMEM((levels[-1] + rows, four), jnp.bfloat16)
    outs = pl.pallas_call(
        functools.partial(crossing_kernel, levels, above),
        in_specs=[pl.BlockSpec(memory_space=pltpu.SMEM)] + [anywhere] * (4 + count),
        out_specs=[anywhere] * (count + 1),
        out_shape=piece_shapes(levels)
        + [jax.ShapeDtypeStruct((heads, rows, four), jnp.bfloat16)],
        scratch_shapes=[
            pltpu.VMEM((4, rows, width), jnp.bfloat16),
            staged,
            staged,
            pltpu.VMEM((2, rows, four), jnp.bfloat16),
            pltpu.SemaphoreType.DMA((4,)),
            pltpu.SemaphoreType.DMA((count,)),
            pltpu.SemaphoreType.DMA((count,)),
            pltpu.SemaphoreType.DMA((2,)),
        ],
        compiler_params=pltpu.CompilerParams(vmem_limit_bytes=VMEM_LIMIT),
        name="above_images" if above else "below_images",
    )(plan, *arrays, *received)
    return outs[:count], outs[count]


def overlay(whole, which, first_head, last_head, first_block, last_block, wanted, source):
    def one_head(head, carry):
        def one_block(block, carry):
            part = pl.ds(pl.multiple_of(block * BLOCK, BLOCK), BLOCK)
            position = block * BLOCK + lax.broadcasted_iota(jnp.int32, (BLOCK, HEAD_DIM), 0)
            whole[which, part, lanes(head)] = jnp.where(
                wanted(position), source(head, block), whole[which, part, lanes(head)])
            return carry

        return lax.fori_loop(first_block, last_block, one_block, carry)

    lax.fori_loop(first_head, last_head, one_head, 0)


def block_part(block):
    return pl.ds(pl.multiple_of(block * BLOCK, BLOCK), BLOCK)


def most_kernel(levels, plan, kept_above, kept_below, *rest):
    count = len(levels)
    from_below, local, outs = rest[:count], rest[count:count + 4], rest[count + 4:count + 8]
    (whole, first_part, last_part, below_staged, whole_sem, first_sem, last_sem, below_sem,
     out_sem) = rest[count + 8:]
    rows, width = local[0].shape
    heads = width // HEAD_DIM
    low_below = plan[HERE_BELOW]
    low_above = plan[HERE_ABOVE]
    below_jobs = plan[THERE_BELOW]
    after = plan[C_BELOW]
    begin = rows - plan[A_ABOVE]
    after_rows = round_up(after)
    first_tiles = tiles(0, after_rows)
    last_tiles = tiles(rows - round_up(plan[A_ABOVE]), round_up(plan[A_ABOVE]))

    def parts(action):
        for slot in range(heads):
            @pl.when(slot < below_jobs)
            def _():
                action(pltpu.make_async_copy(
                    kept_below.at[slot, first_tiles], first_part.at[slot, first_tiles],
                    first_sem.at[slot]))

            @pl.when(slot < low_above)
            def _():
                action(pltpu.make_async_copy(
                    kept_above.at[slot, last_tiles], last_part.at[slot, last_tiles],
                    last_sem.at[slot]))

    loads = [
        pltpu.make_async_copy(local[which], whole.at[which], whole_sem.at[which])
        for which in range(4)
    ]
    saves = [
        pltpu.make_async_copy(whole.at[which], outs[which], out_sem.at[which])
        for which in range(4)
    ]
    stage = functools.partial(
        copy_pieces, levels, plan[DOWN_LEVEL], below_staged, 0, from_below, below_sem, False)
    parts(START)
    stage(START)
    for copy in loads:
        copy.start()
    parts(WAIT)
    stage(WAIT)
    for which in range(4):
        columns = slice(which * HEAD_DIM, (which + 1) * HEAD_DIM)

        def moved_source(head, block):
            start = pl.multiple_of(head * after_rows + block * BLOCK, TILE)
            return below_staged[pl.ds(start, BLOCK), columns]

        def kept_source(head, block):
            return first_part[head - low_below, block_part(block), columns]

        def last_source(head, block):
            return last_part[head, block_part(block), columns]

        in_first = lambda position: position < after
        first_blocks = (0, (after + BLOCK - 1) // BLOCK)
        loads[which].wait()
        overlay(whole, which, 0, low_below, *first_blocks, in_first, moved_source)
        overlay(whole, which, low_below, low_below + below_jobs, *first_blocks, in_first,
                kept_source)
        overlay(whole, which, 0, low_above, begin // BLOCK, rows // BLOCK,
                lambda position: position >= begin, last_source)
        saves[which].start()
    for copy in saves:
        copy.wait()


def merge_most(plan, kept_above, kept_below, from_below, local, levels):
    rows, width = local[0].shape
    heads = width // HEAD_DIM
    four = 4 * HEAD_DIM
    count = len(levels)
    anywhere = pl.BlockSpec(memory_space=pl.ANY)
    windows = pltpu.VMEM((heads, rows, four), jnp.bfloat16)
    return pl.pallas_call(
        functools.partial(most_kernel, levels),
        in_specs=[pl.BlockSpec(memory_space=pltpu.SMEM)] + [anywhere] * (6 + count),
        out_specs=[anywhere] * 4,
        out_shape=[jax.ShapeDtypeStruct((rows, width), jnp.bfloat16)] * 4,
        scratch_shapes=[
            pltpu.VMEM((4, rows, width), jnp.bfloat16),
            windows,
            windows,
            pltpu.VMEM((levels[-1] + BLOCK, four), jnp.bfloat16),
            pltpu.SemaphoreType.DMA((4,)),
            pltpu.SemaphoreType.DMA((heads,)),
            pltpu.SemaphoreType.DMA((heads,)),
            pltpu.SemaphoreType.DMA((count,)),
            pltpu.SemaphoreType.DMA((4,)),
        ],
        compiler_params=pltpu.CompilerParams(vmem_limit_bytes=VMEM_LIMIT),
        cost_estimate=pl.CostEstimate(
            flops=0, bytes_accessed=32 * rows * width, transcendentals=0
        ),
        name="merge_most",
    )(plan, kept_above, kept_below, *from_below, *local)


def last_kernel(levels, plan, *rest):
    count = len(levels)
    from_above = rest[:count]
    outs = rest[count + 4:count + 8]
    whole, staged, whole_sem, staged_sem = rest[count + 8:]
    rows = whole.shape[1]
    heads = whole.shape[2] // HEAD_DIM
    before = plan[A_ABOVE]
    before_rows = round_up(before)
    moved = plan[THERE_ABOVE]
    begin = rows - before
    first_block = begin // BLOCK
    part = pl.ds(
        pl.multiple_of(first_block * BLOCK, BLOCK),
        pl.multiple_of(rows - first_block * BLOCK, BLOCK))

    def move(which, out):
        inside, outside = whole.at[which, part], outs[which].at[part]
        source, target = (inside, outside) if out else (outside, inside)
        return pltpu.make_async_copy(source, target, whole_sem.at[which])

    stage = functools.partial(
        copy_pieces, levels, plan[UP_LEVEL], staged, BLOCK, from_above, staged_sem, False)

    @pl.when(moved > 0)
    def _():
        stage(START)
        for which in range(4):
            move(which, False).start()
        stage(WAIT)
        for which in range(4):
            columns = slice(which * HEAD_DIM, (which + 1) * HEAD_DIM)

            def source(head, block):
                slot = head - (heads - moved)
                start = BLOCK + slot * before_rows + block * BLOCK - (rows - before_rows)
                return staged[pl.ds(pl.multiple_of(start, TILE), BLOCK), columns]

            move(which, False).wait()
            overlay(whole, which, heads - moved, heads, first_block, rows // BLOCK,
                    lambda position: position >= begin, source)
            move(which, True).start()
        for which in range(4):
            move(which, True).wait()


def merge_last(plan, from_above, outs, levels):
    rows, width = outs[0].shape
    count = len(levels)
    anywhere = pl.BlockSpec(memory_space=pl.ANY)
    return pl.pallas_call(
        functools.partial(last_kernel, levels),
        in_specs=[pl.BlockSpec(memory_space=pltpu.SMEM)] + [anywhere] * (count + 4),
        out_specs=[anywhere] * 4,
        out_shape=[jax.ShapeDtypeStruct((rows, width), jnp.bfloat16)] * 4,
        input_output_aliases={1 + count + which: which for which in range(4)},
        scratch_shapes=[
            pltpu.VMEM((4, rows, width), jnp.bfloat16),
            pltpu.VMEM((levels[-1] + 2 * BLOCK, 4 * HEAD_DIM), jnp.bfloat16),
            pltpu.SemaphoreType.DMA((4,)),
            pltpu.SemaphoreType.DMA((count,)),
        ],
        compiler_params=pltpu.CompilerParams(vmem_limit_bytes=VMEM_LIMIT),
        name="merge_last",
    )(plan, *from_above, *outs)


def passed_along(value, steps):
    count = lax.axis_size("dp")
    leading, last = max(0, -steps), min(count, count - steps)
    return lax.ppermute(value, "dp", [(source, source + steps) for source in range(leading, last)])


def pass_further(level, arrays, steps):
    if not arrays:
        return []

    def send(used, arrays):
        return [
            passed_along(array, steps) if number < used else jnp.zeros_like(array)
            for number, array in enumerate(arrays)
        ]

    branches = [functools.partial(send, used) for used in range(len(arrays) + 1)]
    return lax.switch(level[0], branches, list(arrays))


def body(queries, keys, values, out_grad, lengths):
    rows, width = queries.shape
    arrays = (queries, keys, values, out_grad)
    levels = size_levels(rows, width // HEAD_DIM)
    plan, down_level, up_level, down, up = pack(lengths, arrays, levels, lax.axis_size("dp"))
    from_above = passed_along(down[0], -1)
    local = local_attention(lengths, arrays)
    up_first, down_level, local = lax.optimization_barrier((up[0], down_level, local))
    from_below = passed_along(up_first, 1)
    from_above = [from_above, *pass_further(down_level, down[1:], -1)]
    back_up, kept_above = crossing_images(True, plan, arrays, from_above, levels)
    back_below = passed_along(back_up[0], 1)
    up_level, kept_above = lax.optimization_barrier((up_level, kept_above))
    from_below = [from_below, *pass_further(up_level, up[1:], 1)]
    back_down, kept_below = crossing_images(False, plan, arrays, from_below, levels)
    back_above = passed_along(back_down[0], -1)
    down_level, kept_below = lax.optimization_barrier((down_level, kept_below))
    back_below = [back_below, *pass_further(down_level, back_up[1:], 1)]
    outs = merge_most(plan, kept_above, kept_below, back_below, local, levels)
    up_level, outs = lax.optimization_barrier((up_level, outs))
    back_above = [back_above, *pass_further(up_level, back_down[1:], -1)]
    return tuple(merge_last(plan, back_above, outs, levels))


def solution(mesh):
    in_specs = (P("dp", "tensor"), P("dp", "tensor"), P("dp", "tensor"), P("dp", "tensor"), P())
    out_specs = (P("dp", "tensor"), P("dp", "tensor"), P("dp", "tensor"), P("dp", "tensor"))
    return jax.shard_map(body, mesh=mesh, in_specs=in_specs, out_specs=out_specs, check_vma=False)
```

```python
import functools
import math

import jax
import jax.numpy as jnp
from jax import lax
from jax.experimental import pallas as pl
from jax.experimental.pallas import tpu as pltpu
from jax.sharding import PartitionSpec as P

HEAD_DIM = 128
TILE = 16
BLOCK = 64
LOCAL_CHUNK = 256
CROSSING_CHUNK = 512
FACTOR = 1.0 / math.sqrt(HEAD_DIM)
LOG2E = 1.4426950408889634
VMEM_LIMIT = 32 * 1024 * 1024
PACK_VMEM_LIMIT = 60 * 1024 * 1024

FIELDS = 8
BEFORE, AFTER, LOWER, JOBS, JOB_HEAD, SENT, SENT_HEAD, LEVEL = range(FIELDS)
ODD, EVEN = 0, 1

LEVEL_UNITS = ((), ())


def round_up(value):
    return (value + (TILE - 1)) // TILE * TILE


def worst_case_rows(rows, heads):
    worst = 0
    for before in range(TILE, rows + 1, TILE):
        for after in range(TILE, rows + TILE - before + 1, TILE):
            needed = min(max(after * low, before * (heads - low)) for low in range(heads + 1))
            worst = max(worst, needed)
    return worst


def size_levels(kind, rows, heads):
    unit = rows * heads // 48
    most = worst_case_rows(rows, heads)
    below = sorted(level * unit for level in LEVEL_UNITS[kind] if level * unit < most)
    return tuple(below) + (most,)


def make_plan(heads, rows, blocks, levels, lengths, plan, choices, before_edge, after_edge):
    def clear(edge, carry):
        before_edge[edge] = 0
        after_edge[edge] = 0
        return carry

    lax.fori_loop(0, blocks + 1, clear, 0)

    def place(image, start):
        end = start + lengths[image]
        edge = (end - 1) // rows

        @pl.when(edge > start // rows)
        def _():
            before_edge[edge] = edge * rows - start
            after_edge[edge] = end - edge * rows

        return end

    lax.fori_loop(0, lengths.shape[0], place, 0)

    entry = lax.broadcasted_iota(jnp.int32, (8, 128), 1)
    for kind in (ODD, EVEN):
        limit = jnp.full((8, 128), levels[kind][-1], jnp.int32)
        for number, level in enumerate(levels[kind]):
            limit = jnp.where(entry == number, level, limit)

        def check(number, fits):
            edge = 2 * number + (1 if kind == ODD else 2)
            after = round_up(after_edge[edge])
            before = round_up(before_edge[edge])
            taken = jnp.zeros((8, 128), jnp.int32)
            for count in range(1, heads + 1):
                taken += jnp.where(after * count <= limit, 1, 0)
                taken += jnp.where(before * count <= limit, 1, 0)
            return jnp.minimum(fits, jnp.where(taken >= heads, 1, 0))

        last = len(levels[kind]) - 1
        chosen = jnp.int32(last)
        if last:
            edges = (blocks - (0 if kind == ODD else 1)) // 2
            fits = lax.fori_loop(0, edges, check, jnp.ones((8, 128), jnp.int32))
            chosen = jnp.min(jnp.where(fits == 1, entry, last))
        most_rows = jnp.int32(levels[kind][-1])
        for number, level in enumerate(levels[kind][:-1]):
            most_rows = jnp.where(chosen == number, level, most_rows)

        block = lax.axis_index("dp")
        lower = lax.rem(block, 2) == (0 if kind == ODD else 1)
        edge = jnp.where(lower, block + 1, block)
        before = before_edge[edge]
        after = after_edge[edge]
        most = jnp.int32(0)
        least = jnp.int32(heads)
        for count in range(1, heads + 1):
            most += jnp.where(round_up(after) * count <= most_rows, 1, 0)
            least -= jnp.where(round_up(before) * count <= most_rows, 1, 0)
        low = jnp.clip(jnp.int32(heads // 2), least, most)
        crossed = before > 0
        base = kind * FIELDS
        plan[base + BEFORE] = before
        plan[base + AFTER] = after
        plan[base + LOWER] = lower.astype(jnp.int32)
        plan[base + JOBS] = jnp.where(crossed, jnp.where(lower, low, heads - low), 0)
        plan[base + JOB_HEAD] = jnp.where(lower, 0, low)
        plan[base + SENT] = jnp.where(crossed, jnp.where(lower, heads - low, low), 0)
        plan[base + SENT_HEAD] = jnp.where(lower, low, 0)
        plan[base + LEVEL] = chosen
        choices[kind][0] = chosen


class Edge:
    def __init__(self, plan, kind, rows):
        read = lambda field: plan[kind * FIELDS + field]
        self.lower = read(LOWER) == 1
        self.jobs, self.job_head = read(JOBS), read(JOB_HEAD)
        self.sent, self.sent_head = read(SENT), read(SENT_HEAD)
        self.level = read(LEVEL)
        before, after = read(BEFORE), read(AFTER)
        self.before, self.after = before, after
        self.own_begin = jnp.where(self.lower, rows - before, 0)
        self.own_end = jnp.where(self.lower, rows, after)
        self.own_rows = round_up(jnp.where(self.lower, before, after))
        self.other_rows = round_up(jnp.where(self.lower, after, before))
        self.own = jnp.where(self.lower, rows - self.own_rows, 0)
        self.other = jnp.where(self.lower, 0, rows - self.other_rows)
        self.first_block = self.own_begin // BLOCK
        self.last_block = (self.own_end + BLOCK - 1) // BLOCK


def tiles(start, size):
    return pl.ds(pl.multiple_of(start, TILE), pl.multiple_of(size, TILE))


def lanes(head):
    return pl.ds(pl.multiple_of(head * HEAD_DIM, HEAD_DIM), HEAD_DIM)


def attention(query, key, value, grad, mask_columns, store, chunk):
    count = query.shape[0]
    key_t = key.T
    value_t = value.T
    across = (((1,), (1,)), ((), ()))
    chunks = [slice(first, first + chunk) for first in range(0, count, chunk)]
    scores = [
        lax.dot_general(key, query[cols], across, preferred_element_type=jnp.float32)
        for cols in chunks
    ]
    grad_probs = [
        lax.dot_general(value, grad[cols], across, preferred_element_type=jnp.float32)
        for cols in chunks
    ]
    probs_low = []
    grad_scores = []
    for number, cols in enumerate(chunks):
        masked = jnp.where(mask_columns(cols), scores[number], -1e30)
        top = jnp.max(masked, axis=0, keepdims=True)
        weights = jnp.exp2((masked - top) * (FACTOR * LOG2E))
        total = jnp.sum(weights, axis=0, keepdims=True)
        probs = weights * (1.0 / total)
        probs_low.append(probs.astype(jnp.bfloat16))
        result_t = jnp.dot(value_t, probs_low[-1], preferred_element_type=jnp.float32)
        weighted = probs * grad_probs[number]
        centre = jnp.sum(weighted, axis=0, keepdims=True)
        grad_scores.append((weighted - probs * centre).astype(jnp.bfloat16))
        grad_query_t = jnp.dot(key_t, grad_scores[-1], preferred_element_type=jnp.float32) * FACTOR
        store(0, cols, result_t.astype(jnp.bfloat16).T)
        store(1, cols, grad_query_t.astype(jnp.bfloat16).T)
    probs_low = jnp.concatenate(probs_low, axis=1)
    grad_scores = jnp.concatenate(grad_scores, axis=1)
    grad_value = jnp.dot(probs_low, grad, preferred_element_type=jnp.float32)
    store(3, slice(None), grad_value.astype(jnp.bfloat16))
    grad_key = jnp.dot(grad_scores, query, preferred_element_type=jnp.float32)
    store(2, slice(None), (grad_key * FACTOR).astype(jnp.bfloat16))


def local_kernel(lengths, query_ref, key_ref, value_ref, grad_ref, *rest):
    outs = rest[:4]
    image_rows = rest[4]
    count = query_ref.shape[0]

    @pl.when(pl.program_id(0) == 0)
    def _():
        position = lax.axis_index("dp") * count + lax.broadcasted_iota(jnp.int32, (8, count), 1)

        def place(image, carry):
            start, begin = carry
            return start + lengths[image], jnp.where(position >= start, start, begin)

        first = (jnp.int32(0), jnp.zeros((8, count), jnp.int32))
        _, begin = lax.fori_loop(0, lengths.shape[0], place, first)
        image_rows[...] = begin.astype(jnp.float32)

    image_col = image_rows[...].T[:, :1]

    def store(which, rows, part):
        outs[which][rows, :] = part

    attention(
        query_ref[...],
        key_ref[...],
        value_ref[...],
        grad_ref[...],
        lambda cols: image_col == image_rows[:1, cols],
        store,
        LOCAL_CHUNK,
    )


def local_attention(lengths, arrays):
    rows, width = arrays[0].shape
    heads = width // HEAD_DIM
    block = pl.BlockSpec((rows, HEAD_DIM), lambda head: (0, head))
    return pl.pallas_call(
        local_kernel,
        grid=(heads,),
        in_specs=[pl.BlockSpec(memory_space=pltpu.SMEM)] + [block] * 4,
        out_specs=[block] * 4,
        out_shape=[jax.ShapeDtypeStruct((rows, width), jnp.bfloat16)] * 4,
        scratch_shapes=[pltpu.VMEM((8, rows), jnp.float32)],
        compiler_params=pltpu.CompilerParams(vmem_limit_bytes=VMEM_LIMIT),
        cost_estimate=pl.CostEstimate(
            flops=12 * rows * rows * width, bytes_accessed=16 * rows * width, transcendentals=0
        ),
        name="local_images",
    )(lengths, *arrays)


START = lambda copy: copy.start()
WAIT = lambda copy: copy.wait()
ANYWHERE = pl.BlockSpec(memory_space=pl.ANY)
SCALARS = pl.BlockSpec(memory_space=pltpu.SMEM)


def pieces(levels):
    starts = (0,) + levels[:-1]
    return [(start, end - start) for start, end in zip(starts, levels)]


def piece_shapes(levels):
    return [jax.ShapeDtypeStruct((size, 4 * HEAD_DIM), jnp.bfloat16) for _, size in pieces(levels)]


def copy_pieces(levels, level, staged, offset, arrays, sems, out, action):
    for number, (start, size) in enumerate(pieces(levels)):
        inside = staged.at[pl.ds(offset + start, size)]
        outside = arrays[number]
        source, target = (inside, outside) if out else (outside, inside)

        @pl.when(True if number == 0 else level >= number)
        def _():
            action(pltpu.make_async_copy(source, target, sems.at[number]))


def pack_kernel(levels, blocks, lengths, query, key, value, grad, *rest):
    counts = [len(levels[ODD]), len(levels[EVEN])]
    plan, choices, rest = rest[0], rest[1:3], rest[3:]
    outs = rest[:counts[0]], rest[counts[0]:sum(counts)]
    before_edge, after_edge, held, *staged, sems, odd_sem, even_sem = rest[sum(counts):]
    rows, width = query.shape
    heads = width // HEAD_DIM
    loads = [
        pltpu.make_async_copy(array, held.at[which, pl.ds(0, rows)], sems.at[which])
        for which, array in enumerate((query, key, value, grad))
    ]
    for copy in loads:
        copy.start()
    make_plan(heads, rows, blocks, levels, lengths, plan, choices, before_edge, after_edge)

    def gather(edge, staged):
        steps = (edge.own_rows + BLOCK - 1) // BLOCK

        def one_head(slot, carry):
            def one_block(step, carry):
                source = pl.ds(pl.multiple_of(edge.own + step * BLOCK, TILE), BLOCK)
                target = pl.ds(pl.multiple_of(slot * edge.own_rows + step * BLOCK, TILE), BLOCK)
                for which in range(4):
                    staged[target, which * HEAD_DIM:(which + 1) * HEAD_DIM] = held[
                        which, source, lanes(edge.sent_head + slot)]
                return carry

            return lax.fori_loop(0, steps, one_block, carry)

        lax.fori_loop(0, edge.sent, one_head, 0)

    for copy in loads:
        copy.wait()
    moves = []
    for kind, sem in ((EVEN, even_sem), (ODD, odd_sem)):
        edge = Edge(plan, kind, rows)
        gather(edge, staged[kind])
        move = functools.partial(
            copy_pieces, levels[kind], edge.level, staged[kind], 0, outs[kind], sem, True)
        move(START)
        moves.append(move)
    for move in moves:
        move(WAIT)


def pack(lengths, arrays, levels, blocks):
    rows, width = arrays[0].shape
    counts = [len(levels[ODD]), len(levels[EVEN])]
    one = jax.ShapeDtypeStruct((1,), jnp.int32)
    plan, odd_level, even_level, *outs = pl.pallas_call(
        functools.partial(pack_kernel, levels, blocks),
        in_specs=[SCALARS] + [ANYWHERE] * 4,
        out_specs=[SCALARS] * 3 + [ANYWHERE] * sum(counts),
        out_shape=[jax.ShapeDtypeStruct((2 * FIELDS,), jnp.int32), one, one]
        + piece_shapes(levels[ODD]) + piece_shapes(levels[EVEN]),
        scratch_shapes=[
            pltpu.SMEM((blocks + 2,), jnp.int32),
            pltpu.SMEM((blocks + 2,), jnp.int32),
            pltpu.VMEM((4, rows + BLOCK, width), jnp.bfloat16),
            pltpu.VMEM((levels[ODD][-1] + BLOCK, 4 * HEAD_DIM), jnp.bfloat16),
            pltpu.VMEM((levels[EVEN][-1] + BLOCK, 4 * HEAD_DIM), jnp.bfloat16),
            pltpu.SemaphoreType.DMA((4,)),
            pltpu.SemaphoreType.DMA((counts[ODD],)),
            pltpu.SemaphoreType.DMA((counts[EVEN],)),
        ],
        compiler_params=pltpu.CompilerParams(vmem_limit_bytes=PACK_VMEM_LIMIT),
        name="pack",
    )(lengths, *arrays)
    return plan, (odd_level, even_level), (outs[:counts[0]], outs[counts[0]:])


def crossing_kernel(levels, kind, plan, query, key, value, grad, *rest):
    count = len(levels)
    received, back, kept = rest[:count], rest[count:2 * count], rest[2 * count]
    own, staged_in, staged_out, result, own_sem, in_sem, out_sem, kept_sem = rest[2 * count + 1:]
    rows, width = query.shape
    edge = Edge(plan, kind, rows)
    jobs = edge.jobs
    own_part = tiles(edge.own, edge.own_rows)
    margin = rows

    def load_own(action):
        for which, array in enumerate((query, key, value, grad)):
            action(pltpu.make_async_copy(
                array.at[own_part], own.at[which, own_part], own_sem.at[which]))

    def keep(job):
        buffer = lax.rem(job, 2)
        return pltpu.make_async_copy(
            result.at[buffer, own_part], kept.at[job, own_part], kept_sem.at[buffer])

    position = lax.broadcasted_iota(jnp.int32, (rows, HEAD_DIM), 0)
    in_own = (position >= edge.own_begin) & (position < edge.own_end)
    key_position = lax.broadcasted_iota(jnp.int32, (rows, 1), 0)
    in_image = (key_position < edge.after) | (key_position >= rows - edge.before)
    in_window = (position < edge.after) | (position >= rows - edge.before)

    def one_job(step, carry):
        job = jnp.where(edge.lower, step, jobs - 1 - step)
        buffer = lax.rem(job, 2)
        start = margin + job * edge.other_rows - edge.other
        window = pl.ds(pl.multiple_of(start, TILE), rows)

        @pl.when(step >= 2)
        def _():
            keep(job).wait()

        zero = jnp.zeros((rows, HEAD_DIM), jnp.bfloat16)
        operands = []
        for which in range(4):
            columns = slice(which * HEAD_DIM, (which + 1) * HEAD_DIM)
            operands.append(jnp.where(
                in_own,
                own[which, :, lanes(edge.job_head + job)],
                jnp.where(in_window, staged_in[window, columns], zero),
            ))

        def store(which, part_rows, part):
            result[buffer, part_rows, which * HEAD_DIM:(which + 1) * HEAD_DIM] = part

        attention(*operands, lambda cols: in_image, store, CROSSING_CHUNK)
        staged_out[window, :] = result[buffer]
        keep(job).start()
        return carry

    @pl.when(jobs > 0)
    def _():
        stage = functools.partial(
            copy_pieces, levels, edge.level, staged_in, margin, received, in_sem, False)
        send = functools.partial(
            copy_pieces, levels, edge.level, staged_out, margin, back, out_sem, True)
        stage(START)
        load_own(START)
        load_own(WAIT)
        stage(WAIT)
        lax.fori_loop(0, jobs, one_job, 0)
        send(START)

        @pl.when(jobs >= 2)
        def _():
            keep(1).wait()

        keep(0).wait()
        send(WAIT)


def crossing_images(kind, plan, arrays, received, levels):
    rows, width = arrays[0].shape
    heads = width // HEAD_DIM
    four = 4 * HEAD_DIM
    count = len(levels)
    staged = pltpu.VMEM((rows + levels[-1] + rows, four), jnp.bfloat16)
    outs = pl.pallas_call(
        functools.partial(crossing_kernel, levels, kind),
        in_specs=[SCALARS] + [ANYWHERE] * (4 + count),
        out_specs=[ANYWHERE] * (count + 1),
        out_shape=piece_shapes(levels)
        + [jax.ShapeDtypeStruct((heads, rows, four), jnp.bfloat16)],
        scratch_shapes=[
            pltpu.VMEM((4, rows, width), jnp.bfloat16),
            staged,
            staged,
            pltpu.VMEM((2, rows, four), jnp.bfloat16),
            pltpu.SemaphoreType.DMA((4,)),
            pltpu.SemaphoreType.DMA((count,)),
            pltpu.SemaphoreType.DMA((count,)),
            pltpu.SemaphoreType.DMA((2,)),
        ],
        compiler_params=pltpu.CompilerParams(vmem_limit_bytes=VMEM_LIMIT),
        name="odd_edge_images" if kind == ODD else "even_edge_images",
    )(plan, *arrays, *received)
    return outs[:count], outs[count]


def overlay(whole, which, edge, first_head, heads, source):
    def one_head(slot, carry):
        def one_block(block, carry):
            first = block * BLOCK
            part = pl.ds(pl.multiple_of(first, BLOCK), BLOCK)
            position = first + lax.broadcasted_iota(jnp.int32, (BLOCK, HEAD_DIM), 0)
            whole[which, part, lanes(first_head + slot)] = jnp.where(
                (position >= edge.own_begin) & (position < edge.own_end),
                source(slot, first),
                whole[which, part, lanes(first_head + slot)],
            )
            return carry

        return lax.fori_loop(edge.first_block, edge.last_block, one_block, carry)

    lax.fori_loop(0, heads, one_head, 0)


def returned_source(edge, staged, columns):
    def source(slot, first):
        start = BLOCK + slot * edge.own_rows + first - edge.own
        return staged[pl.ds(pl.multiple_of(start, TILE), BLOCK), columns]

    return source


def most_kernel(levels, plan, kept_odd, kept_even, *rest):
    count = len(levels)
    returned, local, outs = rest[:count], rest[count:count + 4], rest[count + 4:count + 8]
    whole, held, staged, whole_sem, held_sem, staged_sem, out_sem = rest[count + 8:]
    rows, width = local[0].shape
    heads = width // HEAD_DIM
    kept = (kept_odd, kept_even)
    edges = [Edge(plan, kind, rows) for kind in (ODD, EVEN)]

    def parts(action):
        for kind in (ODD, EVEN):
            edge = edges[kind]
            part = tiles(edge.own, edge.own_rows)
            for slot in range(heads):
                @pl.when(slot < edge.jobs)
                def _():
                    action(pltpu.make_async_copy(
                        kept[kind].at[slot, part], held.at[kind, slot, part],
                        held_sem.at[kind, slot]))

    loads = [
        pltpu.make_async_copy(local[which], whole.at[which], whole_sem.at[which])
        for which in range(4)
    ]
    saves = [
        pltpu.make_async_copy(whole.at[which], outs[which], out_sem.at[which])
        for which in range(4)
    ]
    stage = functools.partial(
        copy_pieces, levels, edges[EVEN].level, staged, BLOCK, returned, staged_sem, False)
    parts(START)
    stage(START)
    for copy in loads:
        copy.start()
    parts(WAIT)
    stage(WAIT)
    for which in range(4):
        columns = slice(which * HEAD_DIM, (which + 1) * HEAD_DIM)
        loads[which].wait()
        for kind in (ODD, EVEN):
            overlay(
                whole, which, edges[kind], edges[kind].job_head, edges[kind].jobs,
                lambda slot, first: held[
                    kind, slot, pl.ds(pl.multiple_of(first, BLOCK), BLOCK), columns])
        edge = edges[EVEN]
        overlay(whole, which, edge, edge.sent_head, edge.sent,
                returned_source(edge, staged, columns))
        saves[which].start()
    for copy in saves:
        copy.wait()


def merge_most(plan, kept_odd, kept_even, returned, local, levels):
    rows, width = local[0].shape
    heads = width // HEAD_DIM
    four = 4 * HEAD_DIM
    count = len(levels)
    return pl.pallas_call(
        functools.partial(most_kernel, levels),
        in_specs=[SCALARS] + [ANYWHERE] * (6 + count),
        out_specs=[ANYWHERE] * 4,
        out_shape=[jax.ShapeDtypeStruct((rows, width), jnp.bfloat16)] * 4,
        scratch_shapes=[
            pltpu.VMEM((4, rows, width), jnp.bfloat16),
            pltpu.VMEM((2, heads, rows, four), jnp.bfloat16),
            pltpu.VMEM((levels[-1] + 2 * BLOCK, four), jnp.bfloat16),
            pltpu.SemaphoreType.DMA((4,)),
            pltpu.SemaphoreType.DMA((2, heads)),
            pltpu.SemaphoreType.DMA((count,)),
            pltpu.SemaphoreType.DMA((4,)),
        ],
        compiler_params=pltpu.CompilerParams(vmem_limit_bytes=VMEM_LIMIT),
        cost_estimate=pl.CostEstimate(
            flops=0, bytes_accessed=32 * rows * width, transcendentals=0
        ),
        name="merge_most",
    )(plan, kept_odd, kept_even, *returned, *local)


def last_kernel(levels, plan, *rest):
    count = len(levels)
    returned, outs = rest[:count], rest[count + 4:count + 8]
    whole, staged, whole_sem, staged_sem = rest[count + 8:]
    rows = whole.shape[1]
    edge = Edge(plan, ODD, rows)
    part = pl.ds(
        pl.multiple_of(edge.first_block * BLOCK, BLOCK),
        pl.multiple_of((edge.last_block - edge.first_block) * BLOCK, BLOCK))

    def move(which, out):
        inside, outside = whole.at[which, part], outs[which].at[part]
        source, target = (inside, outside) if out else (outside, inside)
        return pltpu.make_async_copy(source, target, whole_sem.at[which])

    stage = functools.partial(
        copy_pieces, levels, edge.level, staged, BLOCK, returned, staged_sem, False)

    @pl.when(edge.sent > 0)
    def _():
        stage(START)
        for which in range(4):
            move(which, False).start()
        stage(WAIT)
        for which in range(4):
            columns = slice(which * HEAD_DIM, (which + 1) * HEAD_DIM)
            move(which, False).wait()
            overlay(whole, which, edge, edge.sent_head, edge.sent,
                    returned_source(edge, staged, columns))
            move(which, True).start()
        for which in range(4):
            move(which, True).wait()


def merge_last(plan, returned, outs, levels):
    rows, width = outs[0].shape
    count = len(levels)
    return pl.pallas_call(
        functools.partial(last_kernel, levels),
        in_specs=[SCALARS] + [ANYWHERE] * (count + 4),
        out_specs=[ANYWHERE] * 4,
        out_shape=[jax.ShapeDtypeStruct((rows, width), jnp.bfloat16)] * 4,
        input_output_aliases={1 + count + which: which for which in range(4)},
        scratch_shapes=[
            pltpu.VMEM((4, rows, width), jnp.bfloat16),
            pltpu.VMEM((levels[-1] + 2 * BLOCK, 4 * HEAD_DIM), jnp.bfloat16),
            pltpu.SemaphoreType.DMA((4,)),
            pltpu.SemaphoreType.DMA((count,)),
        ],
        compiler_params=pltpu.CompilerParams(vmem_limit_bytes=VMEM_LIMIT),
        name="merge_last",
    )(plan, *returned, *outs)


def swapped(value, kind):
    first = 0 if kind == ODD else 1
    pairs = [(block, block + 1) for block in range(first, lax.axis_size("dp") - 1, 2)]
    return lax.ppermute(value, "dp", pairs + [(after, before) for before, after in pairs])


def swap_further(level, arrays, kind):
    if not arrays:
        return []

    def send(used, arrays):
        return [
            swapped(array, kind) if number < used else jnp.zeros_like(array)
            for number, array in enumerate(arrays)
        ]

    branches = [functools.partial(send, used) for used in range(len(arrays) + 1)]
    return lax.switch(level[0], branches, list(arrays))


def body(queries, keys, values, out_grad, lengths):
    rows, width = queries.shape
    arrays = (queries, keys, values, out_grad)
    levels = [size_levels(kind, rows, width // HEAD_DIM) for kind in (ODD, EVEN)]
    plan, (odd_level, even_level), (odd, even) = pack(
        lengths, arrays, levels, lax.axis_size("dp"))
    even_first = swapped(even[0], EVEN)
    odd_first = swapped(odd[0], ODD)
    local = local_attention(lengths, arrays)
    even_first, even_level, local = lax.optimization_barrier((even_first, even_level, local))
    received = [even_first, *swap_further(even_level, even[1:], EVEN)]
    back_even, kept_even = crossing_images(EVEN, plan, arrays, received, levels[EVEN])
    odd_level, kept_even = lax.optimization_barrier((odd_level, kept_even))
    received = [odd_first, *swap_further(odd_level, odd[1:], ODD)]
    first, received = lax.optimization_barrier((back_even[0], received))
    back_first = swapped(first, EVEN)
    back_odd, kept_odd = crossing_images(ODD, plan, arrays, received, levels[ODD])
    odd_first = swapped(back_odd[0], ODD)
    even_level, kept_odd = lax.optimization_barrier((even_level, kept_odd))
    returned = [back_first, *swap_further(even_level, back_even[1:], EVEN)]
    outs = merge_most(plan, kept_odd, kept_even, returned, local, levels[EVEN])
    odd_level, outs = lax.optimization_barrier((odd_level, outs))
    returned = [odd_first, *swap_further(odd_level, back_odd[1:], ODD)]
    return tuple(merge_last(plan, returned, outs, levels[ODD]))


def solution(mesh):
    in_specs = (P("dp", "tensor"), P("dp", "tensor"), P("dp", "tensor"), P("dp", "tensor"), P())
    out_specs = (P("dp", "tensor"), P("dp", "tensor"), P("dp", "tensor"), P("dp", "tensor"))
    return jax.shard_map(body, mesh=mesh, in_specs=in_specs, out_specs=out_specs, check_vma=False)
```

```python
import functools
import math

import jax
import jax.numpy as jnp
from jax import lax
from jax.experimental import pallas as pl
from jax.experimental.pallas import tpu as pltpu
from jax.sharding import PartitionSpec as P

HEAD_DIM = 128
TILE = 16
BLOCK = 64
LOCAL_CHUNK = 256
CROSSING_CHUNK = 512
FACTOR = 1.0 / math.sqrt(HEAD_DIM)
LOG2E = 1.4426950408889634
VMEM_LIMIT = 32 * 1024 * 1024
PACK_VMEM_LIMIT = 60 * 1024 * 1024

FIELDS = 8
BEFORE, AFTER, LOWER, JOBS, JOB_HEAD, SENT, SENT_HEAD, LEVEL = range(FIELDS)
ODD, EVEN = 0, 1

LEVEL_UNITS = ((12,), (7, 12))


def round_up(value):
    return (value + (TILE - 1)) // TILE * TILE


def worst_case_rows(rows, heads):
    worst = 0
    for before in range(TILE, rows + 1, TILE):
        for after in range(TILE, rows + TILE - before + 1, TILE):
            needed = min(max(after * low, before * (heads - low)) for low in range(heads + 1))
            worst = max(worst, needed)
    return worst


def size_levels(kind, rows, heads):
    unit = rows * heads // 48
    most = worst_case_rows(rows, heads)
    below = sorted(level * unit for level in LEVEL_UNITS[kind] if level * unit < most)
    return tuple(below) + (most,)


def make_plan(heads, rows, blocks, levels, lengths, plan, choices, before_edge, after_edge):
    def clear(edge, carry):
        before_edge[edge] = 0
        after_edge[edge] = 0
        return carry

    lax.fori_loop(0, blocks + 1, clear, 0)

    def place(image, start):
        end = start + lengths[image]
        edge = (end - 1) // rows

        @pl.when(edge > start // rows)
        def _():
            before_edge[edge] = edge * rows - start
            after_edge[edge] = end - edge * rows

        return end

    lax.fori_loop(0, lengths.shape[0], place, 0)

    entry = lax.broadcasted_iota(jnp.int32, (8, 128), 1)
    for kind in (ODD, EVEN):
        limit = jnp.full((8, 128), levels[kind][-1], jnp.int32)
        for number, level in enumerate(levels[kind]):
            limit = jnp.where(entry == number, level, limit)

        def check(number, fits):
            edge = 2 * number + (1 if kind == ODD else 2)
            after = round_up(after_edge[edge])
            before = round_up(before_edge[edge])
            taken = jnp.zeros((8, 128), jnp.int32)
            for count in range(1, heads + 1):
                taken += jnp.where(after * count <= limit, 1, 0)
                taken += jnp.where(before * count <= limit, 1, 0)
            return jnp.minimum(fits, jnp.where(taken >= heads, 1, 0))

        last = len(levels[kind]) - 1
        chosen = jnp.int32(last)
        if last:
            edges = (blocks - (0 if kind == ODD else 1)) // 2
            fits = lax.fori_loop(0, edges, check, jnp.ones((8, 128), jnp.int32))
            chosen = jnp.min(jnp.where(fits == 1, entry, last))
        most_rows = jnp.int32(levels[kind][-1])
        for number, level in enumerate(levels[kind][:-1]):
            most_rows = jnp.where(chosen == number, level, most_rows)

        block = lax.axis_index("dp")
        lower = lax.rem(block, 2) == (0 if kind == ODD else 1)
        edge = jnp.where(lower, block + 1, block)
        before = before_edge[edge]
        after = after_edge[edge]
        most = jnp.int32(0)
        least = jnp.int32(heads)
        for count in range(1, heads + 1):
            most += jnp.where(round_up(after) * count <= most_rows, 1, 0)
            least -= jnp.where(round_up(before) * count <= most_rows, 1, 0)
        low = jnp.clip(jnp.int32(heads // 2), least, most)
        crossed = before > 0
        base = kind * FIELDS
        plan[base + BEFORE] = before
        plan[base + AFTER] = after
        plan[base + LOWER] = lower.astype(jnp.int32)
        plan[base + JOBS] = jnp.where(crossed, jnp.where(lower, low, heads - low), 0)
        plan[base + JOB_HEAD] = jnp.where(lower, 0, low)
        plan[base + SENT] = jnp.where(crossed, jnp.where(lower, heads - low, low), 0)
        plan[base + SENT_HEAD] = jnp.where(lower, low, 0)
        plan[base + LEVEL] = chosen
        choices[kind][0] = chosen


class Edge:
    def __init__(self, plan, kind, rows):
        read = lambda field: plan[kind * FIELDS + field]
        self.lower = read(LOWER) == 1
        self.jobs, self.job_head = read(JOBS), read(JOB_HEAD)
        self.sent, self.sent_head = read(SENT), read(SENT_HEAD)
        self.level = read(LEVEL)
        before, after = read(BEFORE), read(AFTER)
        self.before, self.after = before, after
        self.own_begin = jnp.where(self.lower, rows - before, 0)
        self.own_end = jnp.where(self.lower, rows, after)
        self.own_rows = round_up(jnp.where(self.lower, before, after))
        self.other_rows = round_up(jnp.where(self.lower, after, before))
        self.own = jnp.where(self.lower, rows - self.own_rows, 0)
        self.other = jnp.where(self.lower, 0, rows - self.other_rows)
        self.first_block = self.own_begin // BLOCK
        self.last_block = (self.own_end + BLOCK - 1) // BLOCK


def tiles(start, size):
    return pl.ds(pl.multiple_of(start, TILE), pl.multiple_of(size, TILE))


def lanes(head):
    return pl.ds(pl.multiple_of(head * HEAD_DIM, HEAD_DIM), HEAD_DIM)


def attention(query, key, value, grad, mask_columns, store, chunk):
    count = query.shape[0]
    key_t = key.T
    value_t = value.T
    across = (((1,), (1,)), ((), ()))
    chunks = [slice(first, first + chunk) for first in range(0, count, chunk)]
    scores = [
        lax.dot_general(key, query[cols], across, preferred_element_type=jnp.float32)
        for cols in chunks
    ]
    grad_probs = [
        lax.dot_general(value, grad[cols], across, preferred_element_type=jnp.float32)
        for cols in chunks
    ]
    probs_low = []
    grad_scores = []
    for number, cols in enumerate(chunks):
        masked = jnp.where(mask_columns(cols), scores[number], -1e30)
        top = jnp.max(masked, axis=0, keepdims=True)
        weights = jnp.exp2((masked - top) * (FACTOR * LOG2E))
        total = jnp.sum(weights, axis=0, keepdims=True)
        probs = weights * (1.0 / total)
        probs_low.append(probs.astype(jnp.bfloat16))
        result_t = jnp.dot(value_t, probs_low[-1], preferred_element_type=jnp.float32)
        weighted = probs * grad_probs[number]
        centre = jnp.sum(weighted, axis=0, keepdims=True)
        grad_scores.append((weighted - probs * centre).astype(jnp.bfloat16))
        grad_query_t = jnp.dot(key_t, grad_scores[-1], preferred_element_type=jnp.float32) * FACTOR
        store(0, cols, result_t.astype(jnp.bfloat16).T)
        store(1, cols, grad_query_t.astype(jnp.bfloat16).T)
    probs_low = jnp.concatenate(probs_low, axis=1)
    grad_scores = jnp.concatenate(grad_scores, axis=1)
    grad_value = jnp.dot(probs_low, grad, preferred_element_type=jnp.float32)
    store(3, slice(None), grad_value.astype(jnp.bfloat16))
    grad_key = jnp.dot(grad_scores, query, preferred_element_type=jnp.float32)
    store(2, slice(None), (grad_key * FACTOR).astype(jnp.bfloat16))


def local_kernel(lengths, query_ref, key_ref, value_ref, grad_ref, *rest):
    outs = rest[:4]
    image_rows = rest[4]
    count = query_ref.shape[0]

    @pl.when(pl.program_id(0) == 0)
    def _():
        position = lax.axis_index("dp") * count + lax.broadcasted_iota(jnp.int32, (8, count), 1)

        def place(image, carry):
            start, begin = carry
            return start + lengths[image], jnp.where(position >= start, start, begin)

        first = (jnp.int32(0), jnp.zeros((8, count), jnp.int32))
        _, begin = lax.fori_loop(0, lengths.shape[0], place, first)
        image_rows[...] = begin.astype(jnp.float32)

    image_col = image_rows[...].T[:, :1]

    def store(which, rows, part):
        outs[which][rows, :] = part

    attention(
        query_ref[...],
        key_ref[...],
        value_ref[...],
        grad_ref[...],
        lambda cols: image_col == image_rows[:1, cols],
        store,
        LOCAL_CHUNK,
    )


def local_attention(lengths, arrays):
    rows, width = arrays[0].shape
    heads = width // HEAD_DIM
    block = pl.BlockSpec((rows, HEAD_DIM), lambda head: (0, head))
    return pl.pallas_call(
        local_kernel,
        grid=(heads,),
        in_specs=[pl.BlockSpec(memory_space=pltpu.SMEM)] + [block] * 4,
        out_specs=[block] * 4,
        out_shape=[jax.ShapeDtypeStruct((rows, width), jnp.bfloat16)] * 4,
        scratch_shapes=[pltpu.VMEM((8, rows), jnp.float32)],
        compiler_params=pltpu.CompilerParams(vmem_limit_bytes=VMEM_LIMIT),
        cost_estimate=pl.CostEstimate(
            flops=12 * rows * rows * width, bytes_accessed=16 * rows * width, transcendentals=0
        ),
        name="local_images",
    )(lengths, *arrays)


START = lambda copy: copy.start()
WAIT = lambda copy: copy.wait()
ANYWHERE = pl.BlockSpec(memory_space=pl.ANY)
SCALARS = pl.BlockSpec(memory_space=pltpu.SMEM)


def pieces(levels):
    starts = (0,) + levels[:-1]
    return [(start, end - start) for start, end in zip(starts, levels)]


def piece_shapes(levels):
    return [jax.ShapeDtypeStruct((size, 4 * HEAD_DIM), jnp.bfloat16) for _, size in pieces(levels)]


def copy_pieces(levels, level, staged, offset, arrays, sems, out, action):
    for number, (start, size) in enumerate(pieces(levels)):
        inside = staged.at[pl.ds(offset + start, size)]
        outside = arrays[number]
        source, target = (inside, outside) if out else (outside, inside)

        @pl.when(True if number == 0 else level >= number)
        def _():
            action(pltpu.make_async_copy(source, target, sems.at[number]))


def pack_kernel(levels, blocks, lengths, query, key, value, grad, *rest):
    counts = [len(levels[ODD]), len(levels[EVEN])]
    plan, choices, rest = rest[0], rest[1:3], rest[3:]
    outs = rest[:counts[0]], rest[counts[0]:sum(counts)]
    before_edge, after_edge, held, *staged, sems, odd_sem, even_sem = rest[sum(counts):]
    rows, width = query.shape
    heads = width // HEAD_DIM
    loads = [
        pltpu.make_async_copy(array, held.at[which, pl.ds(0, rows)], sems.at[which])
        for which, array in enumerate((query, key, value, grad))
    ]
    for copy in loads:
        copy.start()
    make_plan(heads, rows, blocks, levels, lengths, plan, choices, before_edge, after_edge)

    def gather(edge, staged):
        steps = (edge.own_rows + BLOCK - 1) // BLOCK

        def one_head(slot, carry):
            def one_block(step, carry):
                source = pl.ds(pl.multiple_of(edge.own + step * BLOCK, TILE), BLOCK)
                target = pl.ds(pl.multiple_of(slot * edge.own_rows + step * BLOCK, TILE), BLOCK)
                for which in range(4):
                    staged[target, which * HEAD_DIM:(which + 1) * HEAD_DIM] = held[
                        which, source, lanes(edge.sent_head + slot)]
                return carry

            return lax.fori_loop(0, steps, one_block, carry)

        lax.fori_loop(0, edge.sent, one_head, 0)

    for copy in loads:
        copy.wait()
    moves = []
    for kind, sem in ((EVEN, even_sem), (ODD, odd_sem)):
        edge = Edge(plan, kind, rows)
        gather(edge, staged[kind])
        move = functools.partial(
            copy_pieces, levels[kind], edge.level, staged[kind], 0, outs[kind], sem, True)
        move(START)
        moves.append(move)
    for move in moves:
        move(WAIT)


def pack(lengths, arrays, levels, blocks):
    rows, width = arrays[0].shape
    counts = [len(levels[ODD]), len(levels[EVEN])]
    one = jax.ShapeDtypeStruct((1,), jnp.int32)
    plan, odd_level, even_level, *outs = pl.pallas_call(
        functools.partial(pack_kernel, levels, blocks),
        in_specs=[SCALARS] + [ANYWHERE] * 4,
        out_specs=[SCALARS] * 3 + [ANYWHERE] * sum(counts),
        out_shape=[jax.ShapeDtypeStruct((2 * FIELDS,), jnp.int32), one, one]
        + piece_shapes(levels[ODD]) + piece_shapes(levels[EVEN]),
        scratch_shapes=[
            pltpu.SMEM((blocks + 2,), jnp.int32),
            pltpu.SMEM((blocks + 2,), jnp.int32),
            pltpu.VMEM((4, rows + BLOCK, width), jnp.bfloat16),
            pltpu.VMEM((levels[ODD][-1] + BLOCK, 4 * HEAD_DIM), jnp.bfloat16),
            pltpu.VMEM((levels[EVEN][-1] + BLOCK, 4 * HEAD_DIM), jnp.bfloat16),
            pltpu.SemaphoreType.DMA((4,)),
            pltpu.SemaphoreType.DMA((counts[ODD],)),
            pltpu.SemaphoreType.DMA((counts[EVEN],)),
        ],
        compiler_params=pltpu.CompilerParams(vmem_limit_bytes=PACK_VMEM_LIMIT),
        name="pack",
    )(lengths, *arrays)
    return plan, (odd_level, even_level), (outs[:counts[0]], outs[counts[0]:])


def crossing_kernel(levels, kind, plan, query, key, value, grad, *rest):
    count = len(levels)
    received, back, kept = rest[:count], rest[count:2 * count], rest[2 * count]
    own, staged_in, staged_out, result, own_sem, in_sem, out_sem, kept_sem = rest[2 * count + 1:]
    rows, width = query.shape
    edge = Edge(plan, kind, rows)
    jobs = edge.jobs
    own_part = tiles(edge.own, edge.own_rows)
    margin = rows

    def load_own(action):
        for which, array in enumerate((query, key, value, grad)):
            action(pltpu.make_async_copy(
                array.at[own_part], own.at[which, own_part], own_sem.at[which]))

    def keep(job):
        buffer = lax.rem(job, 2)
        return pltpu.make_async_copy(
            result.at[buffer, own_part], kept.at[job, own_part], kept_sem.at[buffer])

    position = lax.broadcasted_iota(jnp.int32, (rows, HEAD_DIM), 0)
    in_own = (position >= edge.own_begin) & (position < edge.own_end)
    key_position = lax.broadcasted_iota(jnp.int32, (rows, 1), 0)
    in_image = (key_position < edge.after) | (key_position >= rows - edge.before)
    in_window = (position < edge.after) | (position >= rows - edge.before)

    def one_job(step, carry):
        job = jnp.where(edge.lower, step, jobs - 1 - step)
        buffer = lax.rem(job, 2)
        start = margin + job * edge.other_rows - edge.other
        window = pl.ds(pl.multiple_of(start, TILE), rows)

        @pl.when(step >= 2)
        def _():
            keep(job).wait()

        zero = jnp.zeros((rows, HEAD_DIM), jnp.bfloat16)
        operands = []
        for which in range(4):
            columns = slice(which * HEAD_DIM, (which + 1) * HEAD_DIM)
            operands.append(jnp.where(
                in_own,
                own[which, :, lanes(edge.job_head + job)],
                jnp.where(in_window, staged_in[window, columns], zero),
            ))

        def store(which, part_rows, part):
            result[buffer, part_rows, which * HEAD_DIM:(which + 1) * HEAD_DIM] = part

        attention(*operands, lambda cols: in_image, store, CROSSING_CHUNK)
        staged_out[window, :] = result[buffer]
        keep(job).start()
        return carry

    @pl.when(jobs > 0)
    def _():
        stage = functools.partial(
            copy_pieces, levels, edge.level, staged_in, margin, received, in_sem, False)
        send = functools.partial(
            copy_pieces, levels, edge.level, staged_out, margin, back, out_sem, True)
        stage(START)
        load_own(START)
        load_own(WAIT)
        stage(WAIT)
        lax.fori_loop(0, jobs, one_job, 0)
        send(START)

        @pl.when(jobs >= 2)
        def _():
            keep(1).wait()

        keep(0).wait()
        send(WAIT)


def crossing_images(kind, plan, arrays, received, levels):
    rows, width = arrays[0].shape
    heads = width // HEAD_DIM
    four = 4 * HEAD_DIM
    count = len(levels)
    staged = pltpu.VMEM((rows + levels[-1] + rows, four), jnp.bfloat16)
    outs = pl.pallas_call(
        functools.partial(crossing_kernel, levels, kind),
        in_specs=[SCALARS] + [ANYWHERE] * (4 + count),
        out_specs=[ANYWHERE] * (count + 1),
        out_shape=piece_shapes(levels)
        + [jax.ShapeDtypeStruct((heads, rows, four), jnp.bfloat16)],
        scratch_shapes=[
            pltpu.VMEM((4, rows, width), jnp.bfloat16),
            staged,
            staged,
            pltpu.VMEM((2, rows, four), jnp.bfloat16),
            pltpu.SemaphoreType.DMA((4,)),
            pltpu.SemaphoreType.DMA((count,)),
            pltpu.SemaphoreType.DMA((count,)),
            pltpu.SemaphoreType.DMA((2,)),
        ],
        compiler_params=pltpu.CompilerParams(vmem_limit_bytes=VMEM_LIMIT),
        name="odd_edge_images" if kind == ODD else "even_edge_images",
    )(plan, *arrays, *received)
    return outs[:count], outs[count]


def overlay(whole, which, edge, first_head, heads, source):
    def one_head(slot, carry):
        def one_block(block, carry):
            first = block * BLOCK
            part = pl.ds(pl.multiple_of(first, BLOCK), BLOCK)
            position = first + lax.broadcasted_iota(jnp.int32, (BLOCK, HEAD_DIM), 0)
            whole[which, part, lanes(first_head + slot)] = jnp.where(
                (position >= edge.own_begin) & (position < edge.own_end),
                source(slot, first),
                whole[which, part, lanes(first_head + slot)],
            )
            return carry

        return lax.fori_loop(edge.first_block, edge.last_block, one_block, carry)

    lax.fori_loop(0, heads, one_head, 0)


def returned_source(edge, staged, columns):
    def source(slot, first):
        start = BLOCK + slot * edge.own_rows + first - edge.own
        return staged[pl.ds(pl.multiple_of(start, TILE), BLOCK), columns]

    return source


def most_kernel(levels, plan, kept_odd, kept_even, *rest):
    count = len(levels)
    returned, local, outs = rest[:count], rest[count:count + 4], rest[count + 4:count + 8]
    whole, held, staged, whole_sem, held_sem, staged_sem, out_sem = rest[count + 8:]
    rows, width = local[0].shape
    heads = width // HEAD_DIM
    kept = (kept_odd, kept_even)
    edges = [Edge(plan, kind, rows) for kind in (ODD, EVEN)]

    def parts(action):
        for kind in (ODD, EVEN):
            edge = edges[kind]
            part = tiles(edge.own, edge.own_rows)
            for slot in range(heads):
                @pl.when(slot < edge.jobs)
                def _():
                    action(pltpu.make_async_copy(
                        kept[kind].at[slot, part], held.at[kind, slot, part],
                        held_sem.at[kind, slot]))

    loads = [
        pltpu.make_async_copy(local[which], whole.at[which], whole_sem.at[which])
        for which in range(4)
    ]
    saves = [
        pltpu.make_async_copy(whole.at[which], outs[which], out_sem.at[which])
        for which in range(4)
    ]
    stage = functools.partial(
        copy_pieces, levels, edges[EVEN].level, staged, BLOCK, returned, staged_sem, False)
    parts(START)
    stage(START)
    for copy in loads:
        copy.start()
    parts(WAIT)
    stage(WAIT)
    for which in range(4):
        columns = slice(which * HEAD_DIM, (which + 1) * HEAD_DIM)
        loads[which].wait()
        for kind in (ODD, EVEN):
            overlay(
                whole, which, edges[kind], edges[kind].job_head, edges[kind].jobs,
                lambda slot, first: held[
                    kind, slot, pl.ds(pl.multiple_of(first, BLOCK), BLOCK), columns])
        edge = edges[EVEN]
        overlay(whole, which, edge, edge.sent_head, edge.sent,
                returned_source(edge, staged, columns))
        saves[which].start()
    for copy in saves:
        copy.wait()


def merge_most(plan, kept_odd, kept_even, returned, local, levels):
    rows, width = local[0].shape
    heads = width // HEAD_DIM
    four = 4 * HEAD_DIM
    count = len(levels)
    return pl.pallas_call(
        functools.partial(most_kernel, levels),
        in_specs=[SCALARS] + [ANYWHERE] * (6 + count),
        out_specs=[ANYWHERE] * 4,
        out_shape=[jax.ShapeDtypeStruct((rows, width), jnp.bfloat16)] * 4,
        scratch_shapes=[
            pltpu.VMEM((4, rows, width), jnp.bfloat16),
            pltpu.VMEM((2, heads, rows, four), jnp.bfloat16),
            pltpu.VMEM((levels[-1] + 2 * BLOCK, four), jnp.bfloat16),
            pltpu.SemaphoreType.DMA((4,)),
            pltpu.SemaphoreType.DMA((2, heads)),
            pltpu.SemaphoreType.DMA((count,)),
            pltpu.SemaphoreType.DMA((4,)),
        ],
        compiler_params=pltpu.CompilerParams(vmem_limit_bytes=VMEM_LIMIT),
        cost_estimate=pl.CostEstimate(
            flops=0, bytes_accessed=32 * rows * width, transcendentals=0
        ),
        name="merge_most",
    )(plan, kept_odd, kept_even, *returned, *local)


def last_kernel(levels, plan, *rest):
    count = len(levels)
    returned, outs = rest[:count], rest[count + 4:count + 8]
    whole, staged, whole_sem, staged_sem = rest[count + 8:]
    rows = whole.shape[1]
    edge = Edge(plan, ODD, rows)
    part = pl.ds(
        pl.multiple_of(edge.first_block * BLOCK, BLOCK),
        pl.multiple_of((edge.last_block - edge.first_block) * BLOCK, BLOCK))

    def move(which, out):
        inside, outside = whole.at[which, part], outs[which].at[part]
        source, target = (inside, outside) if out else (outside, inside)
        return pltpu.make_async_copy(source, target, whole_sem.at[which])

    stage = functools.partial(
        copy_pieces, levels, edge.level, staged, BLOCK, returned, staged_sem, False)

    @pl.when(edge.sent > 0)
    def _():
        stage(START)
        for which in range(4):
            move(which, False).start()
        stage(WAIT)
        for which in range(4):
            columns = slice(which * HEAD_DIM, (which + 1) * HEAD_DIM)
            move(which, False).wait()
            overlay(whole, which, edge, edge.sent_head, edge.sent,
                    returned_source(edge, staged, columns))
            move(which, True).start()
        for which in range(4):
            move(which, True).wait()


def merge_last(plan, returned, outs, levels):
    rows, width = outs[0].shape
    count = len(levels)
    return pl.pallas_call(
        functools.partial(last_kernel, levels),
        in_specs=[SCALARS] + [ANYWHERE] * (count + 4),
        out_specs=[ANYWHERE] * 4,
        out_shape=[jax.ShapeDtypeStruct((rows, width), jnp.bfloat16)] * 4,
        input_output_aliases={1 + count + which: which for which in range(4)},
        scratch_shapes=[
            pltpu.VMEM((4, rows, width), jnp.bfloat16),
            pltpu.VMEM((levels[-1] + 2 * BLOCK, 4 * HEAD_DIM), jnp.bfloat16),
            pltpu.SemaphoreType.DMA((4,)),
            pltpu.SemaphoreType.DMA((count,)),
        ],
        compiler_params=pltpu.CompilerParams(vmem_limit_bytes=VMEM_LIMIT),
        name="merge_last",
    )(plan, *returned, *outs)


def swapped(value, kind):
    first = 0 if kind == ODD else 1
    pairs = [(block, block + 1) for block in range(first, lax.axis_size("dp") - 1, 2)]
    return lax.ppermute(value, "dp", pairs + [(after, before) for before, after in pairs])


def swap_further(level, arrays, kind):
    if not arrays:
        return []

    def send(used, arrays):
        return [
            swapped(array, kind) if number < used else jnp.zeros_like(array)
            for number, array in enumerate(arrays)
        ]

    branches = [functools.partial(send, used) for used in range(len(arrays) + 1)]
    return lax.switch(level[0], branches, list(arrays))


def body(queries, keys, values, out_grad, lengths):
    rows, width = queries.shape
    arrays = (queries, keys, values, out_grad)
    levels = [size_levels(kind, rows, width // HEAD_DIM) for kind in (ODD, EVEN)]
    plan, (odd_level, even_level), (odd, even) = pack(
        lengths, arrays, levels, lax.axis_size("dp"))
    even_first = swapped(even[0], EVEN)
    odd_first = swapped(odd[0], ODD)
    local = local_attention(lengths, arrays)
    even_first, even_level, local = lax.optimization_barrier((even_first, even_level, local))
    received = [even_first, *swap_further(even_level, even[1:], EVEN)]
    back_even, kept_even = crossing_images(EVEN, plan, arrays, received, levels[EVEN])
    odd_level, kept_even = lax.optimization_barrier((odd_level, kept_even))
    received = [odd_first, *swap_further(odd_level, odd[1:], ODD)]
    first, received = lax.optimization_barrier((back_even[0], received))
    back_first = swapped(first, EVEN)
    back_odd, kept_odd = crossing_images(ODD, plan, arrays, received, levels[ODD])
    odd_first = swapped(back_odd[0], ODD)
    even_level, kept_odd = lax.optimization_barrier((even_level, kept_odd))
    returned = [back_first, *swap_further(even_level, back_even[1:], EVEN)]
    outs = merge_most(plan, kept_odd, kept_even, returned, local, levels[EVEN])
    odd_level, outs = lax.optimization_barrier((odd_level, outs))
    returned = [odd_first, *swap_further(odd_level, back_odd[1:], ODD)]
    return tuple(merge_last(plan, returned, outs, levels[ODD]))


def solution(mesh):
    in_specs = (P("dp", "tensor"), P("dp", "tensor"), P("dp", "tensor"), P("dp", "tensor"), P())
    out_specs = (P("dp", "tensor"), P("dp", "tensor"), P("dp", "tensor"), P("dp", "tensor"))
    return jax.shard_map(body, mesh=mesh, in_specs=in_specs, out_specs=out_specs, check_vma=False)
```

```python
import functools
import math

import jax
import jax.numpy as jnp
from jax import lax
from jax.experimental import pallas as pl
from jax.experimental.pallas import tpu as pltpu
from jax.sharding import PartitionSpec as P

HEAD_DIM = 128
TILE = 16
BLOCK = 64
LOCAL_CHUNK = 256
CROSSING_CHUNK = 512
FACTOR = 1.0 / math.sqrt(HEAD_DIM)
LOG2E = 1.4426950408889634
VMEM_LIMIT = 32 * 1024 * 1024
PACK_VMEM_LIMIT = 60 * 1024 * 1024

FIELDS = 8
BEFORE, AFTER, LOWER, JOBS, JOB_HEAD, SENT, SENT_HEAD, LEVEL = range(FIELDS)
ODD, EVEN = 0, 1

LEVEL_UNITS = ((9, 12), (9, 12))


def round_up(value):
    return (value + (TILE - 1)) // TILE * TILE


def worst_case_rows(rows, heads):
    worst = 0
    for before in range(TILE, rows + 1, TILE):
        for after in range(TILE, rows + TILE - before + 1, TILE):
            needed = min(max(after * low, before * (heads - low)) for low in range(heads + 1))
            worst = max(worst, needed)
    return worst


def size_levels(kind, rows, heads):
    unit = rows * heads // 48
    most = worst_case_rows(rows, heads)
    below = sorted(level * unit for level in LEVEL_UNITS[kind] if level * unit < most)
    return tuple(below) + (most,)


def make_plan(heads, rows, blocks, levels, lengths, plan, choices, before_edge, after_edge):
    def clear(edge, carry):
        before_edge[edge] = 0
        after_edge[edge] = 0
        return carry

    lax.fori_loop(0, blocks + 1, clear, 0)

    def place(image, start):
        end = start + lengths[image]
        edge = (end - 1) // rows

        @pl.when(edge > start // rows)
        def _():
            before_edge[edge] = edge * rows - start
            after_edge[edge] = end - edge * rows

        return end

    lax.fori_loop(0, lengths.shape[0], place, 0)

    entry = lax.broadcasted_iota(jnp.int32, (8, 128), 1)
    for kind in (ODD, EVEN):
        limit = jnp.full((8, 128), levels[kind][-1], jnp.int32)
        for number, level in enumerate(levels[kind]):
            limit = jnp.where(entry == number, level, limit)

        def check(number, fits):
            edge = 2 * number + (1 if kind == ODD else 2)
            after = round_up(after_edge[edge])
            before = round_up(before_edge[edge])
            taken = jnp.zeros((8, 128), jnp.int32)
            for count in range(1, heads + 1):
                taken += jnp.where(after * count <= limit, 1, 0)
                taken += jnp.where(before * count <= limit, 1, 0)
            return jnp.minimum(fits, jnp.where(taken >= heads, 1, 0))

        last = len(levels[kind]) - 1
        chosen = jnp.int32(last)
        if last:
            edges = (blocks - (0 if kind == ODD else 1)) // 2
            fits = lax.fori_loop(0, edges, check, jnp.ones((8, 128), jnp.int32))
            chosen = jnp.min(jnp.where(fits == 1, entry, last))
        most_rows = jnp.int32(levels[kind][-1])
        for number, level in enumerate(levels[kind][:-1]):
            most_rows = jnp.where(chosen == number, level, most_rows)

        block = lax.axis_index("dp")
        lower = lax.rem(block, 2) == (0 if kind == ODD else 1)
        edge = jnp.where(lower, block + 1, block)
        before = before_edge[edge]
        after = after_edge[edge]
        most = jnp.int32(0)
        least = jnp.int32(heads)
        for count in range(1, heads + 1):
            most += jnp.where(round_up(after) * count <= most_rows, 1, 0)
            least -= jnp.where(round_up(before) * count <= most_rows, 1, 0)
        low = jnp.clip(jnp.int32(heads // 2), least, most)
        crossed = before > 0
        base = kind * FIELDS
        plan[base + BEFORE] = before
        plan[base + AFTER] = after
        plan[base + LOWER] = lower.astype(jnp.int32)
        plan[base + JOBS] = jnp.where(crossed, jnp.where(lower, low, heads - low), 0)
        plan[base + JOB_HEAD] = jnp.where(lower, 0, low)
        plan[base + SENT] = jnp.where(crossed, jnp.where(lower, heads - low, low), 0)
        plan[base + SENT_HEAD] = jnp.where(lower, low, 0)
        plan[base + LEVEL] = chosen
        choices[kind][0] = chosen


class Edge:
    def __init__(self, plan, kind, rows):
        read = lambda field: plan[kind * FIELDS + field]
        self.lower = read(LOWER) == 1
        self.jobs, self.job_head = read(JOBS), read(JOB_HEAD)
        self.sent, self.sent_head = read(SENT), read(SENT_HEAD)
        self.level = read(LEVEL)
        before, after = read(BEFORE), read(AFTER)
        self.before, self.after = before, after
        self.own_begin = jnp.where(self.lower, rows - before, 0)
        self.own_end = jnp.where(self.lower, rows, after)
        self.own_rows = round_up(jnp.where(self.lower, before, after))
        self.other_rows = round_up(jnp.where(self.lower, after, before))
        self.own = jnp.where(self.lower, rows - self.own_rows, 0)
        self.other = jnp.where(self.lower, 0, rows - self.other_rows)
        self.first_block = self.own_begin // BLOCK
        self.last_block = (self.own_end + BLOCK - 1) // BLOCK


def tiles(start, size):
    return pl.ds(pl.multiple_of(start, TILE), pl.multiple_of(size, TILE))


def lanes(head):
    return pl.ds(pl.multiple_of(head * HEAD_DIM, HEAD_DIM), HEAD_DIM)


def attention(query, key, value, grad, mask_columns, store, chunk):
    count = query.shape[0]
    key_t = key.T
    value_t = value.T
    across = (((1,), (1,)), ((), ()))
    chunks = [slice(first, first + chunk) for first in range(0, count, chunk)]
    scores = [
        lax.dot_general(key, query[cols], across, preferred_element_type=jnp.float32)
        for cols in chunks
    ]
    grad_probs = [
        lax.dot_general(value, grad[cols], across, preferred_element_type=jnp.float32)
        for cols in chunks
    ]
    probs_low = []
    grad_scores = []
    for number, cols in enumerate(chunks):
        masked = jnp.where(mask_columns(cols), scores[number], -1e30)
        top = jnp.max(masked, axis=0, keepdims=True)
        weights = jnp.exp2((masked - top) * (FACTOR * LOG2E))
        total = jnp.sum(weights, axis=0, keepdims=True)
        probs = weights * (1.0 / total)
        probs_low.append(probs.astype(jnp.bfloat16))
        result_t = jnp.dot(value_t, probs_low[-1], preferred_element_type=jnp.float32)
        weighted = probs * grad_probs[number]
        centre = jnp.sum(weighted, axis=0, keepdims=True)
        grad_scores.append((weighted - probs * centre).astype(jnp.bfloat16))
        grad_query_t = jnp.dot(key_t, grad_scores[-1], preferred_element_type=jnp.float32) * FACTOR
        store(0, cols, result_t.astype(jnp.bfloat16).T)
        store(1, cols, grad_query_t.astype(jnp.bfloat16).T)
    probs_low = jnp.concatenate(probs_low, axis=1)
    grad_scores = jnp.concatenate(grad_scores, axis=1)
    grad_value = jnp.dot(probs_low, grad, preferred_element_type=jnp.float32)
    store(3, slice(None), grad_value.astype(jnp.bfloat16))
    grad_key = jnp.dot(grad_scores, query, preferred_element_type=jnp.float32)
    store(2, slice(None), (grad_key * FACTOR).astype(jnp.bfloat16))


def local_kernel(lengths, query_ref, key_ref, value_ref, grad_ref, *rest):
    outs = rest[:4]
    image_rows = rest[4]
    count = query_ref.shape[0]

    @pl.when(pl.program_id(0) == 0)
    def _():
        position = lax.axis_index("dp") * count + lax.broadcasted_iota(jnp.int32, (8, count), 1)

        def place(image, carry):
            start, begin = carry
            return start + lengths[image], jnp.where(position >= start, start, begin)

        first = (jnp.int32(0), jnp.zeros((8, count), jnp.int32))
        _, begin = lax.fori_loop(0, lengths.shape[0], place, first)
        image_rows[...] = begin.astype(jnp.float32)

    image_col = image_rows[...].T[:, :1]

    def store(which, rows, part):
        outs[which][rows, :] = part

    attention(
        query_ref[...],
        key_ref[...],
        value_ref[...],
        grad_ref[...],
        lambda cols: image_col == image_rows[:1, cols],
        store,
        LOCAL_CHUNK,
    )


def local_attention(lengths, arrays):
    rows, width = arrays[0].shape
    heads = width // HEAD_DIM
    block = pl.BlockSpec((rows, HEAD_DIM), lambda head: (0, head))
    return pl.pallas_call(
        local_kernel,
        grid=(heads,),
        in_specs=[pl.BlockSpec(memory_space=pltpu.SMEM)] + [block] * 4,
        out_specs=[block] * 4,
        out_shape=[pltpu.HBM((rows, width), jnp.bfloat16)] * 4,
        scratch_shapes=[pltpu.VMEM((8, rows), jnp.float32)],
        compiler_params=pltpu.CompilerParams(vmem_limit_bytes=VMEM_LIMIT),
        cost_estimate=pl.CostEstimate(
            flops=12 * rows * rows * width, bytes_accessed=16 * rows * width, transcendentals=0
        ),
        name="local_images",
    )(lengths, *in_hbm(arrays))


START = lambda copy: copy.start()
WAIT = lambda copy: copy.wait()
ANYWHERE = pl.BlockSpec(memory_space=pl.ANY)
SCALARS = pl.BlockSpec(memory_space=pltpu.SMEM)


def in_hbm(arrays):
    return [pltpu.with_memory_space_constraint(array, pltpu.HBM) for array in arrays]


def pieces(levels):
    return [(0, levels[0])] + [(levels[0], level - levels[0]) for level in levels[1:]]


def piece_shapes(levels):
    return [pltpu.HBM((size, 4 * HEAD_DIM), jnp.bfloat16) for _, size in pieces(levels)]


def copy_pieces(levels, level, staged, offset, arrays, sems, out, action):
    for number, (start, size) in enumerate(pieces(levels)):
        inside = staged.at[pl.ds(offset + start, size)]
        outside = arrays[number]
        source, target = (inside, outside) if out else (outside, inside)

        @pl.when(True if number == 0 else level == number)
        def _():
            action(pltpu.make_async_copy(source, target, sems.at[number]))


def pack_kernel(levels, blocks, lengths, query, key, value, grad, *rest):
    counts = [len(levels[ODD]), len(levels[EVEN])]
    plan, choices, rest = rest[0], rest[1:3], rest[3:]
    outs = rest[:counts[0]], rest[counts[0]:sum(counts)]
    before_edge, after_edge, held, *staged, sems, odd_sem, even_sem = rest[sum(counts):]
    rows, width = query.shape
    heads = width // HEAD_DIM
    loads = [
        pltpu.make_async_copy(array, held.at[which, pl.ds(0, rows)], sems.at[which])
        for which, array in enumerate((query, key, value, grad))
    ]
    for copy in loads:
        copy.start()
    make_plan(heads, rows, blocks, levels, lengths, plan, choices, before_edge, after_edge)

    def gather(edge, staged):
        steps = (edge.own_rows + BLOCK - 1) // BLOCK

        def one_head(slot, carry):
            def one_block(step, carry):
                source = pl.ds(pl.multiple_of(edge.own + step * BLOCK, TILE), BLOCK)
                target = pl.ds(pl.multiple_of(slot * edge.own_rows + step * BLOCK, TILE), BLOCK)
                for which in range(4):
                    staged[target, which * HEAD_DIM:(which + 1) * HEAD_DIM] = held[
                        which, source, lanes(edge.sent_head + slot)]
                return carry

            return lax.fori_loop(0, steps, one_block, carry)

        lax.fori_loop(0, edge.sent, one_head, 0)

    for copy in loads:
        copy.wait()
    moves = []
    for kind, sem in ((EVEN, even_sem), (ODD, odd_sem)):
        edge = Edge(plan, kind, rows)
        gather(edge, staged[kind])
        move = functools.partial(
            copy_pieces, levels[kind], edge.level, staged[kind], 0, outs[kind], sem, True)
        move(START)
        moves.append(move)
    for move in moves:
        move(WAIT)


def pack(lengths, arrays, levels, blocks):
    rows, width = arrays[0].shape
    counts = [len(levels[ODD]), len(levels[EVEN])]
    one = jax.ShapeDtypeStruct((1,), jnp.int32)
    plan, odd_level, even_level, *outs = pl.pallas_call(
        functools.partial(pack_kernel, levels, blocks),
        in_specs=[SCALARS] + [ANYWHERE] * 4,
        out_specs=[SCALARS] * 3 + [ANYWHERE] * sum(counts),
        out_shape=[jax.ShapeDtypeStruct((2 * FIELDS,), jnp.int32), one, one]
        + piece_shapes(levels[ODD]) + piece_shapes(levels[EVEN]),
        scratch_shapes=[
            pltpu.SMEM((blocks + 2,), jnp.int32),
            pltpu.SMEM((blocks + 2,), jnp.int32),
            pltpu.VMEM((4, rows + BLOCK, width), jnp.bfloat16),
            pltpu.VMEM((levels[ODD][-1] + BLOCK, 4 * HEAD_DIM), jnp.bfloat16),
            pltpu.VMEM((levels[EVEN][-1] + BLOCK, 4 * HEAD_DIM), jnp.bfloat16),
            pltpu.SemaphoreType.DMA((4,)),
            pltpu.SemaphoreType.DMA((counts[ODD],)),
            pltpu.SemaphoreType.DMA((counts[EVEN],)),
        ],
        compiler_params=pltpu.CompilerParams(vmem_limit_bytes=PACK_VMEM_LIMIT),
        name="pack",
    )(lengths, *in_hbm(arrays))
    return plan, (odd_level, even_level), (outs[:counts[0]], outs[counts[0]:])


def crossing_kernel(levels, kind, plan, query, key, value, grad, *rest):
    count = len(levels)
    received, back, kept = rest[:count], rest[count:2 * count], rest[2 * count]
    own, staged_in, staged_out, result, own_sem, in_sem, out_sem, kept_sem = rest[2 * count + 1:]
    rows, width = query.shape
    edge = Edge(plan, kind, rows)
    jobs = edge.jobs
    own_part = tiles(edge.own, edge.own_rows)
    margin = rows

    def load_own(action):
        for which, array in enumerate((query, key, value, grad)):
            action(pltpu.make_async_copy(
                array.at[own_part], own.at[which, own_part], own_sem.at[which]))

    def keep(job):
        buffer = lax.rem(job, 2)
        return pltpu.make_async_copy(
            result.at[buffer, own_part], kept.at[job, own_part], kept_sem.at[buffer])

    position = lax.broadcasted_iota(jnp.int32, (rows, HEAD_DIM), 0)
    in_own = (position >= edge.own_begin) & (position < edge.own_end)
    key_position = lax.broadcasted_iota(jnp.int32, (rows, 1), 0)
    in_image = (key_position < edge.after) | (key_position >= rows - edge.before)
    in_window = (position < edge.after) | (position >= rows - edge.before)

    def one_job(step, carry):
        job = jnp.where(edge.lower, step, jobs - 1 - step)
        buffer = lax.rem(job, 2)
        start = margin + job * edge.other_rows - edge.other
        window = pl.ds(pl.multiple_of(start, TILE), rows)

        @pl.when(step >= 2)
        def _():
            keep(job).wait()

        zero = jnp.zeros((rows, HEAD_DIM), jnp.bfloat16)
        operands = []
        for which in range(4):
            columns = slice(which * HEAD_DIM, (which + 1) * HEAD_DIM)
            operands.append(jnp.where(
                in_own,
                own[which, :, lanes(edge.job_head + job)],
                jnp.where(in_window, staged_in[window, columns], zero),
            ))

        def store(which, part_rows, part):
            result[buffer, part_rows, which * HEAD_DIM:(which + 1) * HEAD_DIM] = part

        attention(*operands, lambda cols: in_image, store, CROSSING_CHUNK)
        staged_out[window, :] = result[buffer]
        keep(job).start()
        return carry

    @pl.when(jobs > 0)
    def _():
        stage = functools.partial(
            copy_pieces, levels, edge.level, staged_in, margin, received, in_sem, False)
        send = functools.partial(
            copy_pieces, levels, edge.level, staged_out, margin, back, out_sem, True)
        stage(START)
        load_own(START)
        load_own(WAIT)
        stage(WAIT)
        lax.fori_loop(0, jobs, one_job, 0)
        send(START)

        @pl.when(jobs >= 2)
        def _():
            keep(1).wait()

        keep(0).wait()
        send(WAIT)


def crossing_images(kind, plan, arrays, received, levels):
    rows, width = arrays[0].shape
    heads = width // HEAD_DIM
    four = 4 * HEAD_DIM
    count = len(levels)
    staged = pltpu.VMEM((rows + levels[-1] + rows, four), jnp.bfloat16)
    outs = pl.pallas_call(
        functools.partial(crossing_kernel, levels, kind),
        in_specs=[SCALARS] + [ANYWHERE] * (4 + count),
        out_specs=[ANYWHERE] * (count + 1),
        out_shape=piece_shapes(levels)
        + [pltpu.HBM((heads, rows, four), jnp.bfloat16)],
        scratch_shapes=[
            pltpu.VMEM((4, rows, width), jnp.bfloat16),
            staged,
            staged,
            pltpu.VMEM((2, rows, four), jnp.bfloat16),
            pltpu.SemaphoreType.DMA((4,)),
            pltpu.SemaphoreType.DMA((count,)),
            pltpu.SemaphoreType.DMA((count,)),
            pltpu.SemaphoreType.DMA((2,)),
        ],
        compiler_params=pltpu.CompilerParams(vmem_limit_bytes=VMEM_LIMIT),
        cost_estimate=pl.CostEstimate(
            flops=12 * rows * rows * width, bytes_accessed=16 * rows * width, transcendentals=0
        ),
        name="odd_edge_images" if kind == ODD else "even_edge_images",
    )(plan, *in_hbm(arrays), *received)
    return outs[:count], outs[count]


def overlay(whole, which, edge, first_head, heads, source):
    def one_head(slot, carry):
        def one_block(block, carry):
            first = block * BLOCK
            part = pl.ds(pl.multiple_of(first, BLOCK), BLOCK)
            position = first + lax.broadcasted_iota(jnp.int32, (BLOCK, HEAD_DIM), 0)
            whole[which, part, lanes(first_head + slot)] = jnp.where(
                (position >= edge.own_begin) & (position < edge.own_end),
                source(slot, first),
                whole[which, part, lanes(first_head + slot)],
            )
            return carry

        return lax.fori_loop(edge.first_block, edge.last_block, one_block, carry)

    lax.fori_loop(0, heads, one_head, 0)


def returned_source(edge, staged, columns):
    def source(slot, first):
        start = BLOCK + slot * edge.own_rows + first - edge.own
        return staged[pl.ds(pl.multiple_of(start, TILE), BLOCK), columns]

    return source


def keep_kernel(plan, kept_odd, kept_even, *rest):
    local, outs = rest[:4], rest[4:8]
    whole, held, whole_sem, held_sem, out_sem = rest[8:]
    rows, width = local[0].shape
    heads = width // HEAD_DIM
    kept = (kept_odd, kept_even)
    edges = [Edge(plan, kind, rows) for kind in (ODD, EVEN)]

    def parts(action):
        for kind in (ODD, EVEN):
            edge = edges[kind]
            part = tiles(edge.own, edge.own_rows)
            for slot in range(heads):
                @pl.when(slot < edge.jobs)
                def _():
                    action(pltpu.make_async_copy(
                        kept[kind].at[slot, part], held.at[kind, slot, part],
                        held_sem.at[kind, slot]))

    loads = [
        pltpu.make_async_copy(local[which], whole.at[which], whole_sem.at[which])
        for which in range(4)
    ]
    saves = [
        pltpu.make_async_copy(whole.at[which], outs[which], out_sem.at[which])
        for which in range(4)
    ]
    parts(START)
    for copy in loads:
        copy.start()
    parts(WAIT)
    for which in range(4):
        columns = slice(which * HEAD_DIM, (which + 1) * HEAD_DIM)
        loads[which].wait()
        for kind in (ODD, EVEN):
            overlay(
                whole, which, edges[kind], edges[kind].job_head, edges[kind].jobs,
                lambda slot, first: held[
                    kind, slot, pl.ds(pl.multiple_of(first, BLOCK), BLOCK), columns])
        saves[which].start()
    for copy in saves:
        copy.wait()


def merge_kept(plan, kept_odd, kept_even, local):
    rows, width = local[0].shape
    heads = width // HEAD_DIM
    return pl.pallas_call(
        keep_kernel,
        in_specs=[SCALARS] + [ANYWHERE] * 6,
        out_specs=[ANYWHERE] * 4,
        out_shape=[pltpu.HBM((rows, width), jnp.bfloat16)] * 4,
        scratch_shapes=[
            pltpu.VMEM((4, rows, width), jnp.bfloat16),
            pltpu.VMEM((2, heads, rows, 4 * HEAD_DIM), jnp.bfloat16),
            pltpu.SemaphoreType.DMA((4,)),
            pltpu.SemaphoreType.DMA((2, heads)),
            pltpu.SemaphoreType.DMA((4,)),
        ],
        compiler_params=pltpu.CompilerParams(vmem_limit_bytes=VMEM_LIMIT),
        cost_estimate=pl.CostEstimate(
            flops=0, bytes_accessed=32 * rows * width, transcendentals=0
        ),
        name="merge_kept",
    )(plan, *in_hbm([kept_odd, kept_even, *local]))


def return_kernel(levels, plan, *rest):
    counts = [len(levels[ODD]), len(levels[EVEN])]
    total = sum(counts)
    returned = rest[:counts[ODD]], rest[counts[ODD]:total]
    outs = rest[total + 4:total + 8]
    whole, odd_staged, even_staged, whole_sem, odd_sem, even_sem = rest[total + 8:]
    staged = odd_staged, even_staged
    rows = whole.shape[1]
    edges = [Edge(plan, kind, rows) for kind in (ODD, EVEN)]
    stages = [
        functools.partial(
            copy_pieces, levels[kind], edges[kind].level, staged[kind], BLOCK, returned[kind],
            sem, False)
        for kind, sem in ((ODD, odd_sem), (EVEN, even_sem))
    ]

    ends = []
    for edge, other in (edges, edges[::-1]):
        meets = jnp.logical_not(edge.lower) & (other.sent > 0)
        ends.append(jnp.where(
            meets, jnp.minimum(edge.last_block, other.first_block), edge.last_block))

    def move(kind, which, out, action):
        first, last = edges[kind].first_block, ends[kind]

        @pl.when((edges[kind].sent > 0) & (last > first))
        def _():
            part = pl.ds(
                pl.multiple_of(first * BLOCK, BLOCK), pl.multiple_of((last - first) * BLOCK, BLOCK))
            inside, outside = whole.at[which, part], outs[which].at[part]
            source, target = (inside, outside) if out else (outside, inside)
            action(pltpu.make_async_copy(source, target, whole_sem.at[kind, which]))

    for stage in stages:
        stage(START)
    for which in range(4):
        for kind in (ODD, EVEN):
            move(kind, which, False, START)
    for stage in stages:
        stage(WAIT)
    for which in range(4):
        columns = slice(which * HEAD_DIM, (which + 1) * HEAD_DIM)
        for kind in (ODD, EVEN):
            move(kind, which, False, WAIT)
        for kind in (ODD, EVEN):
            edge = edges[kind]
            overlay(whole, which, edge, edge.sent_head, edge.sent,
                    returned_source(edge, staged[kind], columns))
        for kind in (ODD, EVEN):
            move(kind, which, True, START)
    for which in range(4):
        for kind in (ODD, EVEN):
            move(kind, which, True, WAIT)


def merge_returned(plan, odd, even, outs, levels):
    rows, width = outs[0].shape
    counts = [len(levels[ODD]), len(levels[EVEN])]
    return pl.pallas_call(
        functools.partial(return_kernel, levels),
        in_specs=[SCALARS] + [ANYWHERE] * (sum(counts) + 4),
        out_specs=[ANYWHERE] * 4,
        out_shape=[pltpu.HBM((rows, width), jnp.bfloat16)] * 4,
        input_output_aliases={1 + sum(counts) + which: which for which in range(4)},
        scratch_shapes=[
            pltpu.VMEM((4, rows, width), jnp.bfloat16),
            pltpu.VMEM((levels[ODD][-1] + 2 * BLOCK, 4 * HEAD_DIM), jnp.bfloat16),
            pltpu.VMEM((levels[EVEN][-1] + 2 * BLOCK, 4 * HEAD_DIM), jnp.bfloat16),
            pltpu.SemaphoreType.DMA((2, 4)),
            pltpu.SemaphoreType.DMA((counts[ODD],)),
            pltpu.SemaphoreType.DMA((counts[EVEN],)),
        ],
        compiler_params=pltpu.CompilerParams(vmem_limit_bytes=VMEM_LIMIT),
        name="merge_returned",
    )(plan, *odd, *even, *in_hbm(outs))


def swapped(value, kind):
    first = 0 if kind == ODD else 1
    pairs = [(block, block + 1) for block in range(first, lax.axis_size("dp") - 1, 2)]
    return lax.ppermute(value, "dp", pairs + [(after, before) for before, after in pairs])


def swap_further(choices, odd, even):
    counts = [len(odd), len(even)]
    if not sum(counts):
        return [], []
    pairs = [(first, second) for first in range(counts[0] + 1) for second in range(counts[1] + 1)]

    def send(used, odd, even):
        return tuple(
            [
                swapped(array, kind) if number == used[kind] else jnp.zeros_like(array)
                for number, array in enumerate(arrays, start=1)
            ]
            for kind, arrays in ((ODD, odd), (EVEN, even))
        )

    index = 0
    for choice, count in zip(choices, counts):
        if count:
            index = index * (count + 1) + choice[0]
    branches = [functools.partial(send, pair) for pair in pairs]
    return lax.switch(index, branches, list(odd), list(even))


def body(queries, keys, values, out_grad, lengths):
    rows, width = queries.shape
    arrays = (queries, keys, values, out_grad)
    levels = [size_levels(kind, rows, width // HEAD_DIM) for kind in (ODD, EVEN)]
    plan, choices, (odd, even) = pack(lengths, arrays, levels, lax.axis_size("dp"))
    even_first = swapped(even[0], EVEN)
    odd_first = swapped(odd[0], ODD)
    local = local_attention(lengths, arrays)
    choices, local = lax.optimization_barrier((choices, local))
    _, more = swap_further(choices, [], even[1:])
    back_even, kept_even = crossing_images(EVEN, plan, arrays, [even_first, *more], levels[EVEN])
    choices, kept_even = lax.optimization_barrier((choices, kept_even))
    more, _ = swap_further(choices, odd[1:], [])
    received = [odd_first, *more]
    first, received = lax.optimization_barrier((back_even[0], received))
    even_first = swapped(first, EVEN)
    back_odd, kept_odd = crossing_images(ODD, plan, arrays, received, levels[ODD])
    odd_first = swapped(back_odd[0], ODD)
    outs = merge_kept(plan, kept_odd, kept_even, local)
    choices, outs = lax.optimization_barrier((choices, outs))
    more_odd, more_even = swap_further(choices, back_odd[1:], back_even[1:])
    return tuple(merge_returned(
        plan, [odd_first, *more_odd], [even_first, *more_even], outs, levels))


def solution(mesh):
    in_specs = (P("dp", "tensor"), P("dp", "tensor"), P("dp", "tensor"), P("dp", "tensor"), P())
    out_specs = (P("dp", "tensor"), P("dp", "tensor"), P("dp", "tensor"), P("dp", "tensor"))
    return jax.shard_map(body, mesh=mesh, in_specs=in_specs, out_specs=out_specs, check_vma=False)
```

```python
import functools
import math

import jax
import jax.numpy as jnp
from jax import lax
from jax.experimental import pallas as pl
from jax.experimental.pallas import tpu as pltpu
from jax.sharding import PartitionSpec as P

HEAD_DIM = 128
TILE = 16
BLOCK = 64
LOCAL_CHUNK = 256
CROSSING_CHUNK = 512
FACTOR = 1.0 / math.sqrt(HEAD_DIM)
LOG2E = 1.4426950408889634
VMEM_LIMIT = 32 * 1024 * 1024
PACK_VMEM_LIMIT = 60 * 1024 * 1024

FIELDS = 8
BEFORE, AFTER, LOWER, JOBS, JOB_HEAD, SENT, SENT_HEAD, LEVEL = range(FIELDS)
ODD, EVEN = 0, 1

LEVEL_UNITS = ((9, 11, 12), (9, 11, 12))


def round_up(value):
    return (value + (TILE - 1)) & -TILE


def blocks_of(value, size):
    if size & (size - 1):
        return value // size
    return lax.shift_right_logical(value, jnp.int32(size.bit_length() - 1))


def worst_case_rows(rows, heads):
    worst = 0
    for before in range(TILE, rows + 1, TILE):
        for after in range(TILE, rows + TILE - before + 1, TILE):
            needed = min(max(after * low, before * (heads - low)) for low in range(heads + 1))
            worst = max(worst, needed)
    return worst


def size_levels(kind, rows, heads):
    unit = rows * heads // 48
    most = worst_case_rows(rows, heads)
    below = sorted(int(level * unit) for level in LEVEL_UNITS[kind] if level * unit < most)
    return tuple(below) + (most,)


def make_plan(heads, rows, blocks, levels, lengths, plan, choices, before_edge, after_edge):
    def clear(edge, carry):
        before_edge[edge] = 0
        after_edge[edge] = 0
        return carry

    lax.fori_loop(0, blocks + 1, clear, 0)

    def place(image, start):
        end = start + lengths[image]
        edge = blocks_of(end - 1, rows)

        @pl.when(edge > blocks_of(start, rows))
        def _():
            before_edge[edge] = edge * rows - start
            after_edge[edge] = end - edge * rows

        return end

    lax.fori_loop(0, lengths.shape[0], place, 0)

    entry = lax.broadcasted_iota(jnp.int32, (8, 128), 1)
    for kind in (ODD, EVEN):
        limit = jnp.full((8, 128), levels[kind][-1], jnp.int32)
        for number, level in enumerate(levels[kind]):
            limit = jnp.where(entry == number, level, limit)

        def check(number, fits):
            edge = 2 * number + (1 if kind == ODD else 2)
            after = round_up(after_edge[edge])
            before = round_up(before_edge[edge])
            taken = jnp.zeros((8, 128), jnp.int32)
            for count in range(1, heads + 1):
                taken += jnp.where(after * count <= limit, 1, 0)
                taken += jnp.where(before * count <= limit, 1, 0)
            return jnp.minimum(fits, jnp.where(taken >= heads, 1, 0))

        last = len(levels[kind]) - 1
        chosen = jnp.int32(last)
        if last:
            edges = (blocks - (0 if kind == ODD else 1)) // 2
            fits = lax.fori_loop(0, edges, check, jnp.ones((8, 128), jnp.int32))
            chosen = jnp.min(jnp.where(fits == 1, entry, last))
        most_rows = jnp.int32(levels[kind][-1])
        for number, level in enumerate(levels[kind][:-1]):
            most_rows = jnp.where(chosen == number, level, most_rows)

        block = lax.axis_index("dp")
        lower = lax.rem(block, 2) == (0 if kind == ODD else 1)
        edge = jnp.where(lower, block + 1, block)
        before = before_edge[edge]
        after = after_edge[edge]
        most = jnp.int32(0)
        least = jnp.int32(heads)
        for count in range(1, heads + 1):
            most += jnp.where(round_up(after) * count <= most_rows, 1, 0)
            least -= jnp.where(round_up(before) * count <= most_rows, 1, 0)
        low = jnp.clip(jnp.int32(heads // 2), least, most)
        crossed = before > 0
        base = kind * FIELDS
        plan[base + BEFORE] = before
        plan[base + AFTER] = after
        plan[base + LOWER] = lower.astype(jnp.int32)
        plan[base + JOBS] = jnp.where(crossed, jnp.where(lower, low, heads - low), 0)
        plan[base + JOB_HEAD] = jnp.where(lower, 0, low)
        plan[base + SENT] = jnp.where(crossed, jnp.where(lower, heads - low, low), 0)
        plan[base + SENT_HEAD] = jnp.where(lower, low, 0)
        plan[base + LEVEL] = chosen
        choices[kind][0] = chosen


class Edge:
    def __init__(self, plan, kind, rows):
        read = lambda field: plan[kind * FIELDS + field]
        self.lower = read(LOWER) == 1
        self.jobs, self.job_head = read(JOBS), read(JOB_HEAD)
        self.sent, self.sent_head = read(SENT), read(SENT_HEAD)
        self.level = read(LEVEL)
        before, after = read(BEFORE), read(AFTER)
        self.before, self.after = before, after
        self.own_begin = jnp.where(self.lower, rows - before, 0)
        self.own_end = jnp.where(self.lower, rows, after)
        self.own_rows = round_up(jnp.where(self.lower, before, after))
        self.other_rows = round_up(jnp.where(self.lower, after, before))
        self.own = jnp.where(self.lower, rows - self.own_rows, 0)
        self.other = jnp.where(self.lower, 0, rows - self.other_rows)
        self.first_block = blocks_of(self.own_begin, BLOCK)
        self.last_block = blocks_of(self.own_end + BLOCK - 1, BLOCK)


def tiles(start, size):
    return pl.ds(pl.multiple_of(start, TILE), pl.multiple_of(size, TILE))


def lanes(head):
    return pl.ds(pl.multiple_of(head * HEAD_DIM, HEAD_DIM), HEAD_DIM)


def attention(query, key, value, grad, mask_columns, store, chunk):
    count = query.shape[0]
    key_t = key.T
    value_t = value.T
    across = (((1,), (1,)), ((), ()))
    chunks = [slice(first, first + chunk) for first in range(0, count, chunk)]
    scores = [
        lax.dot_general(key, query[cols], across, preferred_element_type=jnp.float32)
        for cols in chunks
    ]
    grad_probs = [
        lax.dot_general(value, grad[cols], across, preferred_element_type=jnp.float32)
        for cols in chunks
    ]
    probs_low = []
    grad_scores = []
    for number, cols in enumerate(chunks):
        masked = jnp.where(mask_columns(cols), scores[number], -1e30)
        top = jnp.max(masked, axis=0, keepdims=True)
        weights = jnp.exp2((masked - top) * (FACTOR * LOG2E))
        total = jnp.sum(weights, axis=0, keepdims=True)
        probs = weights * (1.0 / total)
        probs_low.append(probs.astype(jnp.bfloat16))
        result_t = jnp.dot(value_t, probs_low[-1], preferred_element_type=jnp.float32)
        weighted = probs * grad_probs[number]
        centre = jnp.sum(weighted, axis=0, keepdims=True)
        grad_scores.append((weighted - probs * centre).astype(jnp.bfloat16))
        grad_query_t = jnp.dot(key_t, grad_scores[-1], preferred_element_type=jnp.float32) * FACTOR
        store(0, cols, result_t.astype(jnp.bfloat16).T)
        store(1, cols, grad_query_t.astype(jnp.bfloat16).T)
    probs_low = jnp.concatenate(probs_low, axis=1)
    grad_scores = jnp.concatenate(grad_scores, axis=1)
    grad_value = jnp.dot(probs_low, grad, preferred_element_type=jnp.float32)
    store(3, slice(None), grad_value.astype(jnp.bfloat16))
    grad_key = jnp.dot(grad_scores, query, preferred_element_type=jnp.float32)
    store(2, slice(None), (grad_key * FACTOR).astype(jnp.bfloat16))


def local_kernel(lengths, query_ref, key_ref, value_ref, grad_ref, *rest):
    outs = rest[:4]
    image_rows = rest[4]
    count = query_ref.shape[0]

    @pl.when(pl.program_id(0) == 0)
    def _():
        position = lax.axis_index("dp") * count + lax.broadcasted_iota(jnp.int32, (8, count), 1)

        def place(image, carry):
            start, begin = carry
            return start + lengths[image], jnp.where(position >= start, start, begin)

        first = (jnp.int32(0), jnp.zeros((8, count), jnp.int32))
        _, begin = lax.fori_loop(0, lengths.shape[0], place, first)
        image_rows[...] = begin.astype(jnp.float32)

    image_col = image_rows[...].T[:, :1]

    def store(which, rows, part):
        outs[which][rows, :] = part

    attention(
        query_ref[...],
        key_ref[...],
        value_ref[...],
        grad_ref[...],
        lambda cols: image_col == image_rows[:1, cols],
        store,
        LOCAL_CHUNK,
    )


def local_attention(lengths, arrays):
    rows, width = arrays[0].shape
    heads = width // HEAD_DIM
    block = pl.BlockSpec((rows, HEAD_DIM), lambda head: (0, head))
    return pl.pallas_call(
        local_kernel,
        grid=(heads,),
        in_specs=[pl.BlockSpec(memory_space=pltpu.SMEM)] + [block] * 4,
        out_specs=[block] * 4,
        out_shape=[pltpu.HBM((rows, width), jnp.bfloat16)] * 4,
        scratch_shapes=[pltpu.VMEM((8, rows), jnp.float32)],
        compiler_params=pltpu.CompilerParams(vmem_limit_bytes=VMEM_LIMIT),
        cost_estimate=pl.CostEstimate(
            flops=12 * rows * rows * width, bytes_accessed=16 * rows * width, transcendentals=0
        ),
        name="local_images",
    )(lengths, *in_hbm(arrays))


START = lambda copy: copy.start()
WAIT = lambda copy: copy.wait()
ANYWHERE = pl.BlockSpec(memory_space=pl.ANY)
SCALARS = pl.BlockSpec(memory_space=pltpu.SMEM)


def in_hbm(arrays):
    return [pltpu.with_memory_space_constraint(array, pltpu.HBM) for array in arrays]


def pieces(levels):
    return [(0, levels[0])] + [(levels[0], level - levels[0]) for level in levels[1:]]


def piece_shapes(levels):
    return [pltpu.HBM((size, 4 * HEAD_DIM), jnp.bfloat16) for _, size in pieces(levels)]


def copy_pieces(levels, level, staged, offset, arrays, sems, out, action):
    for number, (start, size) in enumerate(pieces(levels)):
        inside = staged.at[pl.ds(offset + start, size)]
        outside = arrays[number]
        source, target = (inside, outside) if out else (outside, inside)

        @pl.when(True if number == 0 else level == number)
        def _():
            action(pltpu.make_async_copy(source, target, sems.at[number]))


def gather(edge, held, staged):
    steps = blocks_of(edge.own_rows + BLOCK - 1, BLOCK)

    def one_head(slot, carry):
        def one_block(step, carry):
            source = pl.ds(pl.multiple_of(edge.own + step * BLOCK, TILE), BLOCK)
            target = pl.ds(pl.multiple_of(slot * edge.own_rows + step * BLOCK, TILE), BLOCK)
            for which in range(4):
                staged[target, which * HEAD_DIM:(which + 1) * HEAD_DIM] = held[
                    which, source, lanes(edge.sent_head + slot)]
            return carry

        return lax.fori_loop(0, steps, one_block, carry)

    lax.fori_loop(0, edge.sent, one_head, 0)


def pack_even_kernel(levels, blocks, lengths, query, key, value, grad, *rest):
    count = len(levels[EVEN])
    plan, choices, outs = rest[0], rest[1:3], rest[3:3 + count]
    before_edge, after_edge, held, staged, load_sem, out_sem = rest[3 + count:]
    rows, width = query.shape
    loads = [
        pltpu.make_async_copy(array, held.at[which, pl.ds(0, rows)], load_sem.at[which])
        for which, array in enumerate((query, key, value, grad))
    ]
    for copy in loads:
        copy.start()
    make_plan(
        width // HEAD_DIM, rows, blocks, levels, lengths, plan, choices, before_edge, after_edge)
    for copy in loads:
        copy.wait()
    edge = Edge(plan, EVEN, rows)
    gather(edge, held, staged)
    move = functools.partial(
        copy_pieces, levels[EVEN], edge.level, staged, 0, outs, out_sem, True)
    move(START)
    move(WAIT)


def pack_odd_kernel(levels, plan, query, key, value, grad, *rest):
    count = len(levels)
    outs = rest[:count]
    held, staged, load_sem, out_sem = rest[count:]
    rows = query.shape[0]
    edge = Edge(plan, ODD, rows)
    part = tiles(edge.own, edge.own_rows)
    loads = [
        pltpu.make_async_copy(array.at[part], held.at[which, part], load_sem.at[which])
        for which, array in enumerate((query, key, value, grad))
    ]

    @pl.when(edge.sent > 0)
    def _():
        for copy in loads:
            copy.start()
        for copy in loads:
            copy.wait()
        gather(edge, held, staged)
        move = functools.partial(
            copy_pieces, levels, edge.level, staged, 0, outs, out_sem, True)
        move(START)
        move(WAIT)


def pack_scratch(rows, width, levels):
    return [
        pltpu.VMEM((4, rows + BLOCK, width), jnp.bfloat16),
        pltpu.VMEM((levels[-1] + BLOCK, 4 * HEAD_DIM), jnp.bfloat16),
        pltpu.SemaphoreType.DMA((4,)),
        pltpu.SemaphoreType.DMA((len(levels),)),
    ]


def pack_even(lengths, arrays, levels, blocks):
    rows, width = arrays[0].shape
    one = jax.ShapeDtypeStruct((1,), jnp.int32)
    plan, odd_level, even_level, *even = pl.pallas_call(
        functools.partial(pack_even_kernel, levels, blocks),
        in_specs=[SCALARS] + [ANYWHERE] * 4,
        out_specs=[SCALARS] * 3 + [ANYWHERE] * len(levels[EVEN]),
        out_shape=[jax.ShapeDtypeStruct((2 * FIELDS,), jnp.int32), one, one]
        + piece_shapes(levels[EVEN]),
        scratch_shapes=[
            pltpu.SMEM((blocks + 2,), jnp.int32),
            pltpu.SMEM((blocks + 2,), jnp.int32),
        ] + pack_scratch(rows, width, levels[EVEN]),
        compiler_params=pltpu.CompilerParams(vmem_limit_bytes=PACK_VMEM_LIMIT),
        name="pack_even",
    )(lengths, *in_hbm(arrays))
    return plan, (odd_level, even_level), even


def pack_odd(plan, arrays, levels):
    rows, width = arrays[0].shape
    return pl.pallas_call(
        functools.partial(pack_odd_kernel, levels),
        in_specs=[SCALARS] + [ANYWHERE] * 4,
        out_specs=[ANYWHERE] * len(levels),
        out_shape=piece_shapes(levels),
        scratch_shapes=pack_scratch(rows, width, levels),
        compiler_params=pltpu.CompilerParams(vmem_limit_bytes=VMEM_LIMIT),
        name="pack_odd",
    )(plan, *in_hbm(arrays))


def crossing_kernel(levels, kind, plan, query, key, value, grad, *rest):
    count = len(levels)
    received, back, kept = rest[:count], rest[count:2 * count], rest[2 * count]
    own, staged_in, staged_out, result, own_sem, in_sem, out_sem, kept_sem = rest[2 * count + 1:]
    rows, width = query.shape
    edge = Edge(plan, kind, rows)
    jobs = edge.jobs
    own_part = tiles(edge.own, edge.own_rows)
    margin = rows

    def load_own(action):
        for which, array in enumerate((query, key, value, grad)):
            action(pltpu.make_async_copy(
                array.at[own_part], own.at[which, own_part], own_sem.at[which]))

    def keep(job):
        buffer = lax.rem(job, 2)
        return pltpu.make_async_copy(
            result.at[buffer, own_part], kept.at[job, own_part], kept_sem.at[buffer])

    position = lax.broadcasted_iota(jnp.int32, (rows, HEAD_DIM), 0)
    in_own = (position >= edge.own_begin) & (position < edge.own_end)
    key_position = lax.broadcasted_iota(jnp.int32, (rows, 1), 0)
    in_image = (key_position < edge.after) | (key_position >= rows - edge.before)
    in_window = (position < edge.after) | (position >= rows - edge.before)

    def one_job(step, carry):
        job = jnp.where(edge.lower, step, jobs - 1 - step)
        buffer = lax.rem(job, 2)
        start = margin + job * edge.other_rows - edge.other
        window = pl.ds(pl.multiple_of(start, TILE), rows)

        @pl.when(step >= 2)
        def _():
            keep(job).wait()

        zero = jnp.zeros((rows, HEAD_DIM), jnp.bfloat16)
        operands = []
        for which in range(4):
            columns = slice(which * HEAD_DIM, (which + 1) * HEAD_DIM)
            operands.append(jnp.where(
                in_own,
                own[which, :, lanes(edge.job_head + job)],
                jnp.where(in_window, staged_in[window, columns], zero),
            ))

        def store(which, part_rows, part):
            result[buffer, part_rows, which * HEAD_DIM:(which + 1) * HEAD_DIM] = part

        attention(*operands, lambda cols: in_image, store, CROSSING_CHUNK)
        staged_out[window, :] = result[buffer]
        keep(job).start()
        return carry

    @pl.when(jobs > 0)
    def _():
        stage = functools.partial(
            copy_pieces, levels, edge.level, staged_in, margin, received, in_sem, False)
        send = functools.partial(
            copy_pieces, levels, edge.level, staged_out, margin, back, out_sem, True)
        stage(START)
        load_own(START)
        load_own(WAIT)
        stage(WAIT)
        lax.fori_loop(0, jobs, one_job, 0)
        send(START)

        @pl.when(jobs >= 2)
        def _():
            keep(1).wait()

        keep(0).wait()
        send(WAIT)


def crossing_images(kind, plan, arrays, received, levels):
    rows, width = arrays[0].shape
    heads = width // HEAD_DIM
    four = 4 * HEAD_DIM
    count = len(levels)
    staged = pltpu.VMEM((rows + levels[-1] + rows, four), jnp.bfloat16)
    outs = pl.pallas_call(
        functools.partial(crossing_kernel, levels, kind),
        in_specs=[SCALARS] + [ANYWHERE] * (4 + count),
        out_specs=[ANYWHERE] * (count + 1),
        out_shape=piece_shapes(levels)
        + [pltpu.HBM((heads, rows, four), jnp.bfloat16)],
        scratch_shapes=[
            pltpu.VMEM((4, rows, width), jnp.bfloat16),
            staged,
            staged,
            pltpu.VMEM((2, rows, four), jnp.bfloat16),
            pltpu.SemaphoreType.DMA((4,)),
            pltpu.SemaphoreType.DMA((count,)),
            pltpu.SemaphoreType.DMA((count,)),
            pltpu.SemaphoreType.DMA((2,)),
        ],
        compiler_params=pltpu.CompilerParams(vmem_limit_bytes=VMEM_LIMIT),
        cost_estimate=pl.CostEstimate(
            flops=12 * rows * rows * width, bytes_accessed=16 * rows * width, transcendentals=0
        ),
        name="odd_edge_images" if kind == ODD else "even_edge_images",
    )(plan, *in_hbm(arrays), *received)
    return outs[:count], outs[count]


def overlay(whole, which, edge, first_head, heads, source):
    def one_head(slot, carry):
        def one_block(block, carry):
            first = block * BLOCK
            part = pl.ds(pl.multiple_of(first, BLOCK), BLOCK)
            position = first + lax.broadcasted_iota(jnp.int32, (BLOCK, HEAD_DIM), 0)
            whole[which, part, lanes(first_head + slot)] = jnp.where(
                (position >= edge.own_begin) & (position < edge.own_end),
                source(slot, first),
                whole[which, part, lanes(first_head + slot)],
            )
            return carry

        return lax.fori_loop(edge.first_block, edge.last_block, one_block, carry)

    lax.fori_loop(0, heads, one_head, 0)


def returned_source(edge, staged, columns):
    def source(slot, first):
        start = BLOCK + slot * edge.own_rows + first - edge.own
        return staged[pl.ds(pl.multiple_of(start, TILE), BLOCK), columns]

    return source


def keep_kernel(plan, kept_odd, kept_even, *rest):
    local, outs = rest[:4], rest[4:8]
    whole, held, whole_sem, held_sem, out_sem = rest[8:]
    rows, width = local[0].shape
    heads = width // HEAD_DIM
    kept = (kept_odd, kept_even)
    edges = [Edge(plan, kind, rows) for kind in (ODD, EVEN)]

    def parts(action):
        for kind in (ODD, EVEN):
            edge = edges[kind]
            part = tiles(edge.own, edge.own_rows)
            for slot in range(heads):
                @pl.when(slot < edge.jobs)
                def _():
                    action(pltpu.make_async_copy(
                        kept[kind].at[slot, part], held.at[kind, slot, part],
                        held_sem.at[kind, slot]))

    loads = [
        pltpu.make_async_copy(local[which], whole.at[which], whole_sem.at[which])
        for which in range(4)
    ]
    saves = [
        pltpu.make_async_copy(whole.at[which], outs[which], out_sem.at[which])
        for which in range(4)
    ]
    parts(START)
    for copy in loads:
        copy.start()
    parts(WAIT)
    for which in range(4):
        columns = slice(which * HEAD_DIM, (which + 1) * HEAD_DIM)
        loads[which].wait()
        for kind in (ODD, EVEN):
            overlay(
                whole, which, edges[kind], edges[kind].job_head, edges[kind].jobs,
                lambda slot, first: held[
                    kind, slot, pl.ds(pl.multiple_of(first, BLOCK), BLOCK), columns])
        saves[which].start()
    for copy in saves:
        copy.wait()


def merge_kept(plan, kept_odd, kept_even, local):
    rows, width = local[0].shape
    heads = width // HEAD_DIM
    return pl.pallas_call(
        keep_kernel,
        in_specs=[SCALARS] + [ANYWHERE] * 6,
        out_specs=[ANYWHERE] * 4,
        out_shape=[pltpu.HBM((rows, width), jnp.bfloat16)] * 4,
        scratch_shapes=[
            pltpu.VMEM((4, rows, width), jnp.bfloat16),
            pltpu.VMEM((2, heads, rows, 4 * HEAD_DIM), jnp.bfloat16),
            pltpu.SemaphoreType.DMA((4,)),
            pltpu.SemaphoreType.DMA((2, heads)),
            pltpu.SemaphoreType.DMA((4,)),
        ],
        compiler_params=pltpu.CompilerParams(vmem_limit_bytes=VMEM_LIMIT),
        cost_estimate=pl.CostEstimate(
            flops=0, bytes_accessed=32 * rows * width, transcendentals=0
        ),
        name="merge_kept",
    )(plan, *in_hbm([kept_odd, kept_even, *local]))


def return_kernel(levels, plan, *rest):
    counts = [len(levels[ODD]), len(levels[EVEN])]
    total = sum(counts)
    returned = rest[:counts[ODD]], rest[counts[ODD]:total]
    outs = rest[total + 4:total + 8]
    whole, odd_staged, even_staged, whole_sem, odd_sem, even_sem = rest[total + 8:]
    staged = odd_staged, even_staged
    rows = whole.shape[1]
    edges = [Edge(plan, kind, rows) for kind in (ODD, EVEN)]
    stages = [
        functools.partial(
            copy_pieces, levels[kind], edges[kind].level, staged[kind], BLOCK, returned[kind],
            sem, False)
        for kind, sem in ((ODD, odd_sem), (EVEN, even_sem))
    ]

    ends = []
    for edge, other in (edges, edges[::-1]):
        meets = jnp.logical_not(edge.lower) & (other.sent > 0)
        ends.append(jnp.where(
            meets, jnp.minimum(edge.last_block, other.first_block), edge.last_block))

    def move(kind, which, out, action):
        first, last = edges[kind].first_block, ends[kind]

        @pl.when((edges[kind].sent > 0) & (last > first))
        def _():
            part = pl.ds(
                pl.multiple_of(first * BLOCK, BLOCK), pl.multiple_of((last - first) * BLOCK, BLOCK))
            inside, outside = whole.at[which, part], outs[which].at[part]
            source, target = (inside, outside) if out else (outside, inside)
            action(pltpu.make_async_copy(source, target, whole_sem.at[kind, which]))

    for stage in stages:
        stage(START)
    for which in range(4):
        for kind in (ODD, EVEN):
            move(kind, which, False, START)
    for stage in stages:
        stage(WAIT)
    for which in range(4):
        columns = slice(which * HEAD_DIM, (which + 1) * HEAD_DIM)
        for kind in (ODD, EVEN):
            move(kind, which, False, WAIT)
        for kind in (ODD, EVEN):
            edge = edges[kind]
            overlay(whole, which, edge, edge.sent_head, edge.sent,
                    returned_source(edge, staged[kind], columns))
        for kind in (ODD, EVEN):
            move(kind, which, True, START)
    for which in range(4):
        for kind in (ODD, EVEN):
            move(kind, which, True, WAIT)


def merge_returned(plan, odd, even, outs, levels):
    rows, width = outs[0].shape
    counts = [len(levels[ODD]), len(levels[EVEN])]
    return pl.pallas_call(
        functools.partial(return_kernel, levels),
        in_specs=[SCALARS] + [ANYWHERE] * (sum(counts) + 4),
        out_specs=[ANYWHERE] * 4,
        out_shape=[pltpu.HBM((rows, width), jnp.bfloat16)] * 4,
        input_output_aliases={1 + sum(counts) + which: which for which in range(4)},
        scratch_shapes=[
            pltpu.VMEM((4, rows, width), jnp.bfloat16),
            pltpu.VMEM((levels[ODD][-1] + 2 * BLOCK, 4 * HEAD_DIM), jnp.bfloat16),
            pltpu.VMEM((levels[EVEN][-1] + 2 * BLOCK, 4 * HEAD_DIM), jnp.bfloat16),
            pltpu.SemaphoreType.DMA((2, 4)),
            pltpu.SemaphoreType.DMA((counts[ODD],)),
            pltpu.SemaphoreType.DMA((counts[EVEN],)),
        ],
        compiler_params=pltpu.CompilerParams(vmem_limit_bytes=VMEM_LIMIT),
        name="merge_returned",
    )(plan, *odd, *even, *in_hbm(outs))


def swapped(value, kind):
    first = 0 if kind == ODD else 1
    pairs = [(block, block + 1) for block in range(first, lax.axis_size("dp") - 1, 2)]
    return lax.ppermute(value, "dp", pairs + [(after, before) for before, after in pairs])


def swap_further(choices, odd, even):
    counts = [len(odd), len(even)]
    if not sum(counts):
        return [], []
    pairs = [(first, second) for first in range(counts[0] + 1) for second in range(counts[1] + 1)]

    def send(used, odd, even):
        return tuple(
            [
                swapped(array, kind) if number == used[kind] else array
                for number, array in enumerate(arrays, start=1)
            ]
            for kind, arrays in ((ODD, odd), (EVEN, even))
        )

    index = 0
    for choice, count in zip(choices, counts):
        if count:
            index = index * (count + 1) + choice[0]
    branches = [functools.partial(send, pair) for pair in pairs]
    return lax.switch(index, branches, list(odd), list(even))


def body(queries, keys, values, out_grad, lengths):
    rows, width = queries.shape
    arrays = (queries, keys, values, out_grad)
    levels = [size_levels(kind, rows, width // HEAD_DIM) for kind in (ODD, EVEN)]
    plan, choices, even = pack_even(lengths, arrays, levels, lax.axis_size("dp"))
    even_first = swapped(even[0], EVEN)
    odd = pack_odd(plan, arrays, levels[ODD])
    odd_first = swapped(odd[0], ODD)
    local = local_attention(lengths, arrays)
    choices, local = lax.optimization_barrier((choices, local))
    _, more = swap_further(choices, [], even[1:])
    back_even, kept_even = crossing_images(EVEN, plan, arrays, [even_first, *more], levels[EVEN])
    choices, kept_even = lax.optimization_barrier((choices, kept_even))
    more, _ = swap_further(choices, odd[1:], [])
    received = [odd_first, *more]
    first, received = lax.optimization_barrier((back_even[0], received))
    even_first = swapped(first, EVEN)
    back_odd, kept_odd = crossing_images(ODD, plan, arrays, received, levels[ODD])
    odd_first = swapped(back_odd[0], ODD)
    outs = merge_kept(plan, kept_odd, kept_even, local)
    choices, outs = lax.optimization_barrier((choices, outs))
    more_odd, more_even = swap_further(choices, back_odd[1:], back_even[1:])
    return tuple(merge_returned(
        plan, [odd_first, *more_odd], [even_first, *more_even], outs, levels))


def solution(mesh):
    in_specs = (P("dp", "tensor"), P("dp", "tensor"), P("dp", "tensor"), P("dp", "tensor"), P())
    out_specs = (P("dp", "tensor"), P("dp", "tensor"), P("dp", "tensor"), P("dp", "tensor"))
    return jax.shard_map(body, mesh=mesh, in_specs=in_specs, out_specs=out_specs, check_vma=False)
```

```python
import functools
import math

import jax
import jax.numpy as jnp
from jax import lax
from jax.experimental import pallas as pl
from jax.experimental.pallas import tpu as pltpu
from jax.sharding import PartitionSpec as P

HEAD_DIM = 128
TILE = 16
BLOCK = 64
LOCAL_CHUNK = 256
CROSSING_CHUNK = 512
FACTOR = 1.0 / math.sqrt(HEAD_DIM)
LOG2E = 1.4426950408889634
VMEM_LIMIT = 32 * 1024 * 1024
PACK_VMEM_LIMIT = 60 * 1024 * 1024

SCHEDULED_LAST = pl.CostEstimate(flops=1, bytes_accessed=1, transcendentals=0)

FIELDS = 8
BEFORE, AFTER, LOWER, JOBS, JOB_HEAD, SENT, SENT_HEAD, LEVEL = range(FIELDS)
ODD, EVEN = 0, 1

LEVEL_UNITS = ((9, 11, 12), (9, 11, 12))


def round_up(value):
    return (value + (TILE - 1)) & -TILE


def blocks_of(value, size):
    if size & (size - 1):
        return value // size
    return lax.shift_right_logical(value, jnp.int32(size.bit_length() - 1))


def worst_case_rows(rows, heads):
    worst = 0
    for before in range(TILE, rows + 1, TILE):
        for after in range(TILE, rows + TILE - before + 1, TILE):
            needed = min(max(after * low, before * (heads - low)) for low in range(heads + 1))
            worst = max(worst, needed)
    return worst


def size_levels(kind, rows, heads):
    unit = rows * heads // 48
    most = worst_case_rows(rows, heads)
    below = sorted(int(level * unit) for level in LEVEL_UNITS[kind] if level * unit < most)
    return tuple(below) + (most,)


def make_plan(heads, rows, blocks, levels, lengths, plan, choices, before_edge, after_edge):
    def clear(edge, carry):
        before_edge[edge] = 0
        after_edge[edge] = 0
        return carry

    lax.fori_loop(0, blocks + 1, clear, 0)

    def place(image, start):
        end = start + lengths[image]
        edge = blocks_of(end - 1, rows)

        @pl.when(edge > blocks_of(start, rows))
        def _():
            before_edge[edge] = edge * rows - start
            after_edge[edge] = end - edge * rows

        return end

    lax.fori_loop(0, lengths.shape[0], place, 0)

    entry = lax.broadcasted_iota(jnp.int32, (8, 128), 1)
    for kind in (ODD, EVEN):
        limit = jnp.full((8, 128), levels[kind][-1], jnp.int32)
        for number, level in enumerate(levels[kind]):
            limit = jnp.where(entry == number, level, limit)

        def check(number, fits):
            edge = 2 * number + (1 if kind == ODD else 2)
            after = round_up(after_edge[edge])
            before = round_up(before_edge[edge])
            taken = jnp.zeros((8, 128), jnp.int32)
            for count in range(1, heads + 1):
                taken += jnp.where(after * count <= limit, 1, 0)
                taken += jnp.where(before * count <= limit, 1, 0)
            return jnp.minimum(fits, jnp.where(taken >= heads, 1, 0))

        last = len(levels[kind]) - 1
        chosen = jnp.int32(last)
        if last:
            edges = (blocks - (0 if kind == ODD else 1)) // 2
            fits = lax.fori_loop(0, edges, check, jnp.ones((8, 128), jnp.int32))
            chosen = jnp.min(jnp.where(fits == 1, entry, last))
        most_rows = jnp.int32(levels[kind][-1])
        for number, level in enumerate(levels[kind][:-1]):
            most_rows = jnp.where(chosen == number, level, most_rows)

        block = lax.axis_index("dp")
        lower = lax.rem(block, 2) == (0 if kind == ODD else 1)
        edge = jnp.where(lower, block + 1, block)
        before = before_edge[edge]
        after = after_edge[edge]
        most = jnp.int32(0)
        least = jnp.int32(heads)
        for count in range(1, heads + 1):
            most += jnp.where(round_up(after) * count <= most_rows, 1, 0)
            least -= jnp.where(round_up(before) * count <= most_rows, 1, 0)
        low = jnp.clip(jnp.int32(heads // 2), least, most)
        crossed = before > 0
        base = kind * FIELDS
        plan[base + BEFORE] = before
        plan[base + AFTER] = after
        plan[base + LOWER] = lower.astype(jnp.int32)
        plan[base + JOBS] = jnp.where(crossed, jnp.where(lower, low, heads - low), 0)
        plan[base + JOB_HEAD] = jnp.where(lower, 0, low)
        plan[base + SENT] = jnp.where(crossed, jnp.where(lower, heads - low, low), 0)
        plan[base + SENT_HEAD] = jnp.where(lower, low, 0)
        plan[base + LEVEL] = chosen
        choices[kind][0] = chosen


class Edge:
    def __init__(self, plan, kind, rows):
        read = lambda field: plan[kind * FIELDS + field]
        self.lower = read(LOWER) == 1
        self.jobs, self.job_head = read(JOBS), read(JOB_HEAD)
        self.sent, self.sent_head = read(SENT), read(SENT_HEAD)
        self.level = read(LEVEL)
        before, after = read(BEFORE), read(AFTER)
        self.before, self.after = before, after
        self.own_begin = jnp.where(self.lower, rows - before, 0)
        self.own_end = jnp.where(self.lower, rows, after)
        self.own_rows = round_up(jnp.where(self.lower, before, after))
        self.other_rows = round_up(jnp.where(self.lower, after, before))
        self.own = jnp.where(self.lower, rows - self.own_rows, 0)
        self.other = jnp.where(self.lower, 0, rows - self.other_rows)
        self.first_block = blocks_of(self.own_begin, BLOCK)
        self.last_block = blocks_of(self.own_end + BLOCK - 1, BLOCK)


def tiles(start, size):
    return pl.ds(pl.multiple_of(start, TILE), pl.multiple_of(size, TILE))


def lanes(head):
    return pl.ds(pl.multiple_of(head * HEAD_DIM, HEAD_DIM), HEAD_DIM)


def attention(query, key, value, grad, mask_columns, store, chunk):
    count = query.shape[0]
    key_t = key.T
    value_t = value.T
    across = (((1,), (1,)), ((), ()))
    chunks = [slice(first, first + chunk) for first in range(0, count, chunk)]
    scores = [
        lax.dot_general(key, query[cols], across, preferred_element_type=jnp.float32)
        for cols in chunks
    ]
    grad_probs = [
        lax.dot_general(value, grad[cols], across, preferred_element_type=jnp.float32)
        for cols in chunks
    ]
    probs_low = []
    grad_scores = []
    for number, cols in enumerate(chunks):
        masked = jnp.where(mask_columns(cols), scores[number], -1e30)
        top = jnp.max(masked, axis=0, keepdims=True)
        weights = jnp.exp2((masked - top) * (FACTOR * LOG2E))
        total = jnp.sum(weights, axis=0, keepdims=True)
        probs = weights * (1.0 / total)
        probs_low.append(probs.astype(jnp.bfloat16))
        result_t = jnp.dot(value_t, probs_low[-1], preferred_element_type=jnp.float32)
        weighted = probs * grad_probs[number]
        centre = jnp.sum(weighted, axis=0, keepdims=True)
        grad_scores.append((weighted - probs * centre).astype(jnp.bfloat16))
        grad_query_t = jnp.dot(key_t, grad_scores[-1], preferred_element_type=jnp.float32) * FACTOR
        store(0, cols, result_t.astype(jnp.bfloat16).T)
        store(1, cols, grad_query_t.astype(jnp.bfloat16).T)
    probs_low = jnp.concatenate(probs_low, axis=1)
    grad_scores = jnp.concatenate(grad_scores, axis=1)
    grad_value = jnp.dot(probs_low, grad, preferred_element_type=jnp.float32)
    store(3, slice(None), grad_value.astype(jnp.bfloat16))
    grad_key = jnp.dot(grad_scores, query, preferred_element_type=jnp.float32)
    store(2, slice(None), (grad_key * FACTOR).astype(jnp.bfloat16))


def local_kernel(lengths, query_ref, key_ref, value_ref, grad_ref, *rest):
    outs, image_rows = rest[-5:-1], rest[-1]
    count = query_ref.shape[0]

    @pl.when(pl.program_id(0) == 0)
    def _():
        position = lax.axis_index("dp") * count + lax.broadcasted_iota(jnp.int32, (8, count), 1)

        def place(image, carry):
            start, begin = carry
            return start + lengths[image], jnp.where(position >= start, start, begin)

        first = (jnp.int32(0), jnp.zeros((8, count), jnp.int32))
        _, begin = lax.fori_loop(0, lengths.shape[0], place, first)
        image_rows[...] = begin.astype(jnp.float32)

    image_col = image_rows[...].T[:, :1]

    def store(which, rows, part):
        outs[which][rows, :] = part

    attention(
        query_ref[...],
        key_ref[...],
        value_ref[...],
        grad_ref[...],
        lambda cols: image_col == image_rows[:1, cols],
        store,
        LOCAL_CHUNK,
    )


def local_attention(lengths, arrays, first_head, last_head, outs=()):
    rows, width = arrays[0].shape
    block = pl.BlockSpec((rows, HEAD_DIM), lambda step: (0, first_head + step))
    return pl.pallas_call(
        local_kernel,
        grid=(last_head - first_head,),
        in_specs=[SCALARS] + [block] * 4 + [ANYWHERE] * len(outs),
        out_specs=[block] * 4,
        out_shape=[pltpu.HBM((rows, width), jnp.bfloat16)] * 4,
        input_output_aliases={5 + which: which for which in range(len(outs))},
        scratch_shapes=[pltpu.VMEM((8, rows), jnp.float32)],
        compiler_params=pltpu.CompilerParams(vmem_limit_bytes=VMEM_LIMIT),
        cost_estimate=SCHEDULED_LAST,
        name="local_images",
    )(lengths, *in_hbm([*arrays, *outs]))


START = lambda copy: copy.start()
WAIT = lambda copy: copy.wait()
ANYWHERE = pl.BlockSpec(memory_space=pl.ANY)
SCALARS = pl.BlockSpec(memory_space=pltpu.SMEM)


def in_hbm(arrays):
    return [pltpu.with_memory_space_constraint(array, pltpu.HBM) for array in arrays]


def pieces(levels):
    return [(0, levels[0])] + [(levels[0], level - levels[0]) for level in levels[1:]]


def piece_shapes(levels):
    return [pltpu.HBM((size, 4 * HEAD_DIM), jnp.bfloat16) for _, size in pieces(levels)]


def copy_pieces(levels, level, staged, offset, arrays, sems, out, action):
    for number, (start, size) in enumerate(pieces(levels)):
        inside = staged.at[pl.ds(offset + start, size)]
        outside = arrays[number]
        source, target = (inside, outside) if out else (outside, inside)

        @pl.when(True if number == 0 else level == number)
        def _():
            action(pltpu.make_async_copy(source, target, sems.at[number]))


def gather(edge, held, staged):
    steps = blocks_of(edge.own_rows + BLOCK - 1, BLOCK)

    def one_head(slot, carry):
        def one_block(step, carry):
            source = pl.ds(pl.multiple_of(edge.own + step * BLOCK, TILE), BLOCK)
            target = pl.ds(pl.multiple_of(slot * edge.own_rows + step * BLOCK, TILE), BLOCK)
            for which in range(4):
                staged[target, which * HEAD_DIM:(which + 1) * HEAD_DIM] = held[
                    which, source, lanes(edge.sent_head + slot)]
            return carry

        return lax.fori_loop(0, steps, one_block, carry)

    lax.fori_loop(0, edge.sent, one_head, 0)


def pack_even_kernel(levels, blocks, lengths, query, key, value, grad, *rest):
    count = len(levels[EVEN])
    plan, choices, outs = rest[0], rest[1:3], rest[3:3 + count]
    before_edge, after_edge, held, staged, load_sem, out_sem = rest[3 + count:]
    rows, width = query.shape
    loads = [
        pltpu.make_async_copy(array, held.at[which, pl.ds(0, rows)], load_sem.at[which])
        for which, array in enumerate((query, key, value, grad))
    ]
    for copy in loads:
        copy.start()
    make_plan(
        width // HEAD_DIM, rows, blocks, levels, lengths, plan, choices, before_edge, after_edge)
    for copy in loads:
        copy.wait()
    edge = Edge(plan, EVEN, rows)
    gather(edge, held, staged)
    move = functools.partial(
        copy_pieces, levels[EVEN], edge.level, staged, 0, outs, out_sem, True)
    move(START)
    move(WAIT)


def pack_odd_kernel(levels, plan, query, key, value, grad, *rest):
    count = len(levels)
    outs = rest[:count]
    held, staged, load_sem, out_sem = rest[count:]
    rows = query.shape[0]
    edge = Edge(plan, ODD, rows)
    part = tiles(edge.own, edge.own_rows)
    loads = [
        pltpu.make_async_copy(array.at[part], held.at[which, part], load_sem.at[which])
        for which, array in enumerate((query, key, value, grad))
    ]

    @pl.when(edge.sent > 0)
    def _():
        for copy in loads:
            copy.start()
        for copy in loads:
            copy.wait()
        gather(edge, held, staged)
        move = functools.partial(
            copy_pieces, levels, edge.level, staged, 0, outs, out_sem, True)
        move(START)
        move(WAIT)


def pack_scratch(rows, width, levels):
    return [
        pltpu.VMEM((4, rows + BLOCK, width), jnp.bfloat16),
        pltpu.VMEM((levels[-1] + BLOCK, 4 * HEAD_DIM), jnp.bfloat16),
        pltpu.SemaphoreType.DMA((4,)),
        pltpu.SemaphoreType.DMA((len(levels),)),
    ]


def pack_even(lengths, arrays, levels, blocks):
    rows, width = arrays[0].shape
    one = jax.ShapeDtypeStruct((1,), jnp.int32)
    plan, odd_level, even_level, *even = pl.pallas_call(
        functools.partial(pack_even_kernel, levels, blocks),
        in_specs=[SCALARS] + [ANYWHERE] * 4,
        out_specs=[SCALARS] * 3 + [ANYWHERE] * len(levels[EVEN]),
        out_shape=[jax.ShapeDtypeStruct((2 * FIELDS,), jnp.int32), one, one]
        + piece_shapes(levels[EVEN]),
        scratch_shapes=[
            pltpu.SMEM((blocks + 2,), jnp.int32),
            pltpu.SMEM((blocks + 2,), jnp.int32),
        ] + pack_scratch(rows, width, levels[EVEN]),
        compiler_params=pltpu.CompilerParams(vmem_limit_bytes=PACK_VMEM_LIMIT),
        name="pack_even",
    )(lengths, *in_hbm(arrays))
    return plan, (odd_level, even_level), even


def pack_odd(plan, arrays, levels):
    rows, width = arrays[0].shape
    return pl.pallas_call(
        functools.partial(pack_odd_kernel, levels),
        in_specs=[SCALARS] + [ANYWHERE] * 4,
        out_specs=[ANYWHERE] * len(levels),
        out_shape=piece_shapes(levels),
        scratch_shapes=pack_scratch(rows, width, levels),
        compiler_params=pltpu.CompilerParams(vmem_limit_bytes=VMEM_LIMIT),
        name="pack_odd",
    )(plan, *in_hbm(arrays))


def crossing_kernel(levels, kind, plan, query, key, value, grad, *rest):
    count = len(levels)
    received, back, kept = rest[:count], rest[count:2 * count], rest[2 * count]
    own, staged_in, staged_out, result, own_sem, in_sem, out_sem, kept_sem = rest[2 * count + 1:]
    rows, width = query.shape
    edge = Edge(plan, kind, rows)
    jobs = edge.jobs
    own_part = tiles(edge.own, edge.own_rows)
    margin = rows

    def load_own(action):
        for which, array in enumerate((query, key, value, grad)):
            action(pltpu.make_async_copy(
                array.at[own_part], own.at[which, own_part], own_sem.at[which]))

    def keep(job):
        buffer = lax.rem(job, 2)
        return pltpu.make_async_copy(
            result.at[buffer, own_part], kept.at[job, own_part], kept_sem.at[buffer])

    position = lax.broadcasted_iota(jnp.int32, (rows, HEAD_DIM), 0)
    in_own = (position >= edge.own_begin) & (position < edge.own_end)
    key_position = lax.broadcasted_iota(jnp.int32, (rows, 1), 0)
    in_image = (key_position < edge.after) | (key_position >= rows - edge.before)
    in_window = (position < edge.after) | (position >= rows - edge.before)

    def one_job(step, carry):
        job = jnp.where(edge.lower, step, jobs - 1 - step)
        buffer = lax.rem(job, 2)
        start = margin + job * edge.other_rows - edge.other
        window = pl.ds(pl.multiple_of(start, TILE), rows)

        @pl.when(step >= 2)
        def _():
            keep(job).wait()

        zero = jnp.zeros((rows, HEAD_DIM), jnp.bfloat16)
        operands = []
        for which in range(4):
            columns = slice(which * HEAD_DIM, (which + 1) * HEAD_DIM)
            operands.append(jnp.where(
                in_own,
                own[which, :, lanes(edge.job_head + job)],
                jnp.where(in_window, staged_in[window, columns], zero),
            ))

        def store(which, part_rows, part):
            result[buffer, part_rows, which * HEAD_DIM:(which + 1) * HEAD_DIM] = part

        attention(*operands, lambda cols: in_image, store, CROSSING_CHUNK)
        staged_out[window, :] = result[buffer]
        keep(job).start()
        return carry

    @pl.when(jobs > 0)
    def _():
        stage = functools.partial(
            copy_pieces, levels, edge.level, staged_in, margin, received, in_sem, False)
        send = functools.partial(
            copy_pieces, levels, edge.level, staged_out, margin, back, out_sem, True)
        stage(START)
        load_own(START)
        load_own(WAIT)
        stage(WAIT)
        lax.fori_loop(0, jobs, one_job, 0)
        send(START)

        @pl.when(jobs >= 2)
        def _():
            keep(1).wait()

        keep(0).wait()
        send(WAIT)


def crossing_images(kind, plan, arrays, received, levels):
    rows, width = arrays[0].shape
    heads = width // HEAD_DIM
    four = 4 * HEAD_DIM
    count = len(levels)
    staged = pltpu.VMEM((rows + levels[-1] + rows, four), jnp.bfloat16)
    outs = pl.pallas_call(
        functools.partial(crossing_kernel, levels, kind),
        in_specs=[SCALARS] + [ANYWHERE] * (4 + count),
        out_specs=[ANYWHERE] * (count + 1),
        out_shape=piece_shapes(levels)
        + [pltpu.HBM((heads, rows, four), jnp.bfloat16)],
        scratch_shapes=[
            pltpu.VMEM((4, rows, width), jnp.bfloat16),
            staged,
            staged,
            pltpu.VMEM((2, rows, four), jnp.bfloat16),
            pltpu.SemaphoreType.DMA((4,)),
            pltpu.SemaphoreType.DMA((count,)),
            pltpu.SemaphoreType.DMA((count,)),
            pltpu.SemaphoreType.DMA((2,)),
        ],
        compiler_params=pltpu.CompilerParams(vmem_limit_bytes=VMEM_LIMIT),
        cost_estimate=pl.CostEstimate(
            flops=12 * rows * rows * width, bytes_accessed=16 * rows * width, transcendentals=0
        ),
        name="odd_edge_images" if kind == ODD else "even_edge_images",
    )(plan, *in_hbm(arrays), *received)
    return outs[:count], outs[count]


def overlay(whole, which, edge, first_head, heads, source):
    def one_head(slot, carry):
        def one_block(block, carry):
            first = block * BLOCK
            part = pl.ds(pl.multiple_of(first, BLOCK), BLOCK)
            position = first + lax.broadcasted_iota(jnp.int32, (BLOCK, HEAD_DIM), 0)
            whole[which, part, lanes(first_head + slot)] = jnp.where(
                (position >= edge.own_begin) & (position < edge.own_end),
                source(slot, first),
                whole[which, part, lanes(first_head + slot)],
            )
            return carry

        return lax.fori_loop(edge.first_block, edge.last_block, one_block, carry)

    lax.fori_loop(0, heads, one_head, 0)


def returned_source(edge, staged, columns):
    def source(slot, first):
        start = BLOCK + slot * edge.own_rows + first - edge.own
        return staged[pl.ds(pl.multiple_of(start, TILE), BLOCK), columns]

    return source


def keep_kernel(plan, kept_odd, kept_even, *rest):
    local, outs = rest[:4], rest[4:8]
    whole, held, whole_sem, held_sem, out_sem = rest[8:]
    rows, width = local[0].shape
    heads = width // HEAD_DIM
    kept = (kept_odd, kept_even)
    edges = [Edge(plan, kind, rows) for kind in (ODD, EVEN)]

    def parts(action):
        for kind in (ODD, EVEN):
            edge = edges[kind]
            part = tiles(edge.own, edge.own_rows)
            for slot in range(heads):
                @pl.when(slot < edge.jobs)
                def _():
                    action(pltpu.make_async_copy(
                        kept[kind].at[slot, part], held.at[kind, slot, part],
                        held_sem.at[kind, slot]))

    loads = [
        pltpu.make_async_copy(local[which], whole.at[which], whole_sem.at[which])
        for which in range(4)
    ]
    saves = [
        pltpu.make_async_copy(whole.at[which], outs[which], out_sem.at[which])
        for which in range(4)
    ]
    parts(START)
    for copy in loads:
        copy.start()
    parts(WAIT)
    for which in range(4):
        columns = slice(which * HEAD_DIM, (which + 1) * HEAD_DIM)
        loads[which].wait()
        for kind in (ODD, EVEN):
            overlay(
                whole, which, edges[kind], edges[kind].job_head, edges[kind].jobs,
                lambda slot, first: held[
                    kind, slot, pl.ds(pl.multiple_of(first, BLOCK), BLOCK), columns])
        saves[which].start()
    for copy in saves:
        copy.wait()


def merge_kept(plan, kept_odd, kept_even, local):
    rows, width = local[0].shape
    heads = width // HEAD_DIM
    return pl.pallas_call(
        keep_kernel,
        in_specs=[SCALARS] + [ANYWHERE] * 6,
        out_specs=[ANYWHERE] * 4,
        out_shape=[pltpu.HBM((rows, width), jnp.bfloat16)] * 4,
        scratch_shapes=[
            pltpu.VMEM((4, rows, width), jnp.bfloat16),
            pltpu.VMEM((2, heads, rows, 4 * HEAD_DIM), jnp.bfloat16),
            pltpu.SemaphoreType.DMA((4,)),
            pltpu.SemaphoreType.DMA((2, heads)),
            pltpu.SemaphoreType.DMA((4,)),
        ],
        compiler_params=pltpu.CompilerParams(vmem_limit_bytes=VMEM_LIMIT),
        cost_estimate=SCHEDULED_LAST,
        name="merge_kept",
    )(plan, *in_hbm([kept_odd, kept_even, *local]))


def return_kernel(levels, plan, *rest):
    counts = [len(levels[ODD]), len(levels[EVEN])]
    total = sum(counts)
    returned = rest[:counts[ODD]], rest[counts[ODD]:total]
    outs = rest[total + 4:total + 8]
    whole, odd_staged, even_staged, whole_sem, odd_sem, even_sem = rest[total + 8:]
    staged = odd_staged, even_staged
    rows = whole.shape[1]
    edges = [Edge(plan, kind, rows) for kind in (ODD, EVEN)]
    stages = [
        functools.partial(
            copy_pieces, levels[kind], edges[kind].level, staged[kind], BLOCK, returned[kind],
            sem, False)
        for kind, sem in ((ODD, odd_sem), (EVEN, even_sem))
    ]

    ends = []
    for edge, other in (edges, edges[::-1]):
        meets = jnp.logical_not(edge.lower) & (other.sent > 0)
        ends.append(jnp.where(
            meets, jnp.minimum(edge.last_block, other.first_block), edge.last_block))

    def move(kind, which, out, action):
        first, last = edges[kind].first_block, ends[kind]

        @pl.when((edges[kind].sent > 0) & (last > first))
        def _():
            part = pl.ds(
                pl.multiple_of(first * BLOCK, BLOCK), pl.multiple_of((last - first) * BLOCK, BLOCK))
            inside, outside = whole.at[which, part], outs[which].at[part]
            source, target = (inside, outside) if out else (outside, inside)
            action(pltpu.make_async_copy(source, target, whole_sem.at[kind, which]))

    for stage in stages:
        stage(START)
    for which in range(4):
        for kind in (ODD, EVEN):
            move(kind, which, False, START)
    for stage in stages:
        stage(WAIT)
    for which in range(4):
        columns = slice(which * HEAD_DIM, (which + 1) * HEAD_DIM)
        for kind in (ODD, EVEN):
            move(kind, which, False, WAIT)
        for kind in (ODD, EVEN):
            edge = edges[kind]
            overlay(whole, which, edge, edge.sent_head, edge.sent,
                    returned_source(edge, staged[kind], columns))
        for kind in (ODD, EVEN):
            move(kind, which, True, START)
    for which in range(4):
        for kind in (ODD, EVEN):
            move(kind, which, True, WAIT)


def merge_returned(plan, odd, even, outs, levels):
    rows, width = outs[0].shape
    counts = [len(levels[ODD]), len(levels[EVEN])]
    return pl.pallas_call(
        functools.partial(return_kernel, levels),
        in_specs=[SCALARS] + [ANYWHERE] * (sum(counts) + 4),
        out_specs=[ANYWHERE] * 4,
        out_shape=[pltpu.HBM((rows, width), jnp.bfloat16)] * 4,
        input_output_aliases={1 + sum(counts) + which: which for which in range(4)},
        scratch_shapes=[
            pltpu.VMEM((4, rows, width), jnp.bfloat16),
            pltpu.VMEM((levels[ODD][-1] + 2 * BLOCK, 4 * HEAD_DIM), jnp.bfloat16),
            pltpu.VMEM((levels[EVEN][-1] + 2 * BLOCK, 4 * HEAD_DIM), jnp.bfloat16),
            pltpu.SemaphoreType.DMA((2, 4)),
            pltpu.SemaphoreType.DMA((counts[ODD],)),
            pltpu.SemaphoreType.DMA((counts[EVEN],)),
        ],
        compiler_params=pltpu.CompilerParams(vmem_limit_bytes=VMEM_LIMIT),
        name="merge_returned",
    )(plan, *odd, *even, *in_hbm(outs))


def swapped(value, kind):
    first = 0 if kind == ODD else 1
    pairs = [(block, block + 1) for block in range(first, lax.axis_size("dp") - 1, 2)]
    return lax.ppermute(value, "dp", pairs + [(after, before) for before, after in pairs])


def swap_further(choices, odd, even):
    counts = [len(odd), len(even)]
    if not sum(counts):
        return [], []
    pairs = [(first, second) for first in range(counts[0] + 1) for second in range(counts[1] + 1)]

    def send(used, odd, even):
        return tuple(
            [
                swapped(array, kind) if number == used[kind] else array
                for number, array in enumerate(arrays, start=1)
            ]
            for kind, arrays in ((ODD, odd), (EVEN, even))
        )

    index = 0
    for choice, count in zip(choices, counts):
        if count:
            index = index * (count + 1) + choice[0]
    branches = [functools.partial(send, pair) for pair in pairs]
    return lax.switch(index, branches, list(odd), list(even))


def body(queries, keys, values, out_grad, lengths):
    rows, width = queries.shape
    arrays = (queries, keys, values, out_grad)
    levels = [size_levels(kind, rows, width // HEAD_DIM) for kind in (ODD, EVEN)]
    plan, choices, even = pack_even(lengths, arrays, levels, lax.axis_size("dp"))
    even_first = swapped(even[0], EVEN)
    odd = pack_odd(plan, arrays, levels[ODD])
    odd_first = swapped(odd[0], ODD)
    heads = width // HEAD_DIM
    local = local_attention(lengths, arrays, 0, heads // 2)
    choices, local = lax.optimization_barrier((choices, local))
    _, more = swap_further(choices, [], even[1:])
    back_even, kept_even = crossing_images(EVEN, plan, arrays, [even_first, *more], levels[EVEN])
    choices, kept_even = lax.optimization_barrier((choices, kept_even))
    more, _ = swap_further(choices, odd[1:], [])
    received = [odd_first, *more]
    first, received = lax.optimization_barrier((back_even[0], received))
    even_first = swapped(first, EVEN)
    back_odd, kept_odd = crossing_images(ODD, plan, arrays, received, levels[ODD])
    odd_first = swapped(back_odd[0], ODD)
    kept_odd, local = lax.optimization_barrier((kept_odd, local))
    local = local_attention(lengths, arrays, heads // 2, heads, local)
    outs = merge_kept(plan, kept_odd, kept_even, local)
    even_first, choices, outs = lax.optimization_barrier((even_first, choices, outs))
    more_odd, more_even = swap_further(choices, back_odd[1:], back_even[1:])
    return tuple(merge_returned(
        plan, [odd_first, *more_odd], [even_first, *more_even], outs, levels))


def solution(mesh):
    in_specs = (P("dp", "tensor"), P("dp", "tensor"), P("dp", "tensor"), P("dp", "tensor"), P())
    out_specs = (P("dp", "tensor"), P("dp", "tensor"), P("dp", "tensor"), P("dp", "tensor"))
    return jax.shard_map(body, mesh=mesh, in_specs=in_specs, out_specs=out_specs, check_vma=False)
```

```python
import functools
import math

import jax
import jax.numpy as jnp
from jax import lax
from jax.experimental import pallas as pl
from jax.experimental.pallas import tpu as pltpu
from jax.sharding import PartitionSpec as P

HEAD_DIM = 128
TILE = 16
BLOCK = 64
LOCAL_CHUNK = 256
CROSSING_CHUNK = 512
FACTOR = 1.0 / math.sqrt(HEAD_DIM)
LOG2E = 1.4426950408889634
VMEM_LIMIT = 32 * 1024 * 1024
PACK_VMEM_LIMIT = 60 * 1024 * 1024

SCHEDULED_LAST = pl.CostEstimate(flops=1, bytes_accessed=1, transcendentals=0)

FIELDS = 8
BEFORE, AFTER, LOWER, JOBS, JOB_HEAD, SENT, SENT_HEAD, LEVEL = range(FIELDS)
ODD, EVEN = 0, 1

LEVEL_UNITS = ((8, 10, 11, 12), (8, 10, 11, 12))


def round_up(value):
    return (value + (TILE - 1)) & -TILE


def blocks_of(value, size):
    if size & (size - 1):
        return value // size
    return lax.shift_right_logical(value, jnp.int32(size.bit_length() - 1))


def worst_case_rows(rows, heads):
    worst = 0
    for before in range(TILE, rows + 1, TILE):
        for after in range(TILE, rows + TILE - before + 1, TILE):
            needed = min(max(after * low, before * (heads - low)) for low in range(heads + 1))
            worst = max(worst, needed)
    return worst


def size_levels(kind, rows, heads):
    unit = rows * heads // 48
    most = worst_case_rows(rows, heads)
    below = sorted(int(level * unit) for level in LEVEL_UNITS[kind] if level * unit < most)
    return tuple(below) + (most,)


def find_crossings(rows, blocks, lengths, before_edge, after_edge):
    def clear(edge, carry):
        before_edge[edge] = 0
        after_edge[edge] = 0
        return carry

    lax.fori_loop(0, blocks + 1, clear, 0)

    def place(image, start):
        end = start + lengths[image]
        edge = blocks_of(end - 1, rows)

        @pl.when(edge > blocks_of(start, rows))
        def _():
            before_edge[edge] = edge * rows - start
            after_edge[edge] = end - edge * rows

        return end

    lax.fori_loop(0, lengths.shape[0], place, 0)


def own_edge(kind, before_edge, after_edge):
    block = lax.axis_index("dp")
    lower = lax.rem(block, 2) == (0 if kind == ODD else 1)
    edge = jnp.where(lower, block + 1, block)
    return lower, before_edge[edge], after_edge[edge]


def make_plan(heads, blocks, levels, plan, choices, before_edge, after_edge):
    entry = lax.broadcasted_iota(jnp.int32, (8, 128), 1)
    for kind in (ODD, EVEN):
        limit = jnp.full((8, 128), levels[kind][-1], jnp.int32)
        for number, level in enumerate(levels[kind]):
            limit = jnp.where(entry == number, level, limit)

        def check(number, fits):
            edge = 2 * number + (1 if kind == ODD else 2)
            after = round_up(after_edge[edge])
            before = round_up(before_edge[edge])
            taken = jnp.zeros((8, 128), jnp.int32)
            for count in range(1, heads + 1):
                taken += jnp.where(after * count <= limit, 1, 0)
                taken += jnp.where(before * count <= limit, 1, 0)
            return jnp.minimum(fits, jnp.where(taken >= heads, 1, 0))

        last = len(levels[kind]) - 1
        chosen = jnp.int32(last)
        if last:
            edges = (blocks - (0 if kind == ODD else 1)) // 2
            fits = lax.fori_loop(0, edges, check, jnp.ones((8, 128), jnp.int32))
            chosen = jnp.min(jnp.where(fits == 1, entry, last))
        most_rows = jnp.int32(levels[kind][-1])
        for number, level in enumerate(levels[kind][:-1]):
            most_rows = jnp.where(chosen == number, level, most_rows)

        lower, before, after = own_edge(kind, before_edge, after_edge)
        most = jnp.int32(0)
        least = jnp.int32(heads)
        for count in range(1, heads + 1):
            most += jnp.where(round_up(after) * count <= most_rows, 1, 0)
            least -= jnp.where(round_up(before) * count <= most_rows, 1, 0)
        low = jnp.clip(jnp.int32(heads // 2), least, most)
        crossed = before > 0
        base = kind * FIELDS
        plan[base + BEFORE] = before
        plan[base + AFTER] = after
        plan[base + LOWER] = lower.astype(jnp.int32)
        plan[base + JOBS] = jnp.where(crossed, jnp.where(lower, low, heads - low), 0)
        plan[base + JOB_HEAD] = jnp.where(lower, 0, low)
        plan[base + SENT] = jnp.where(crossed, jnp.where(lower, heads - low, low), 0)
        plan[base + SENT_HEAD] = jnp.where(lower, low, 0)
        plan[base + LEVEL] = chosen
        choices[kind][0] = chosen


class Edge:
    def __init__(self, plan, kind, rows):
        read = lambda field: plan[kind * FIELDS + field]
        self.lower = read(LOWER) == 1
        self.jobs, self.job_head = read(JOBS), read(JOB_HEAD)
        self.sent, self.sent_head = read(SENT), read(SENT_HEAD)
        self.level = read(LEVEL)
        before, after = read(BEFORE), read(AFTER)
        self.before, self.after = before, after
        self.own_begin = jnp.where(self.lower, rows - before, 0)
        self.own_end = jnp.where(self.lower, rows, after)
        self.own_rows = round_up(jnp.where(self.lower, before, after))
        self.other_rows = round_up(jnp.where(self.lower, after, before))
        self.own = jnp.where(self.lower, rows - self.own_rows, 0)
        self.other = jnp.where(self.lower, 0, rows - self.other_rows)
        self.first_block = blocks_of(self.own_begin, BLOCK)
        self.last_block = blocks_of(self.own_end + BLOCK - 1, BLOCK)


def tiles(start, size):
    return pl.ds(pl.multiple_of(start, TILE), pl.multiple_of(size, TILE))


def lanes(head):
    return pl.ds(pl.multiple_of(head * HEAD_DIM, HEAD_DIM), HEAD_DIM)


def attention(query, key, value, grad, mask_columns, store, chunk):
    count = query.shape[0]
    key_t = key.T
    value_t = value.T
    grad_t = grad.T
    across = (((1,), (1,)), ((), ()))
    chunks = [slice(first, first + chunk) for first in range(0, count, chunk)]
    scores = [
        lax.dot_general(key, query[cols], across, preferred_element_type=jnp.float32)
        for cols in chunks
    ]
    grad_probs = [
        lax.dot_general(value, grad[cols], across, preferred_element_type=jnp.float32)
        for cols in chunks
    ]
    probs_low = []
    grad_scores = []
    for number, cols in enumerate(chunks):
        masked = jnp.where(mask_columns(cols), scores[number], -1e30)
        top = jnp.max(masked, axis=0, keepdims=True)
        weights = jnp.exp2((masked - top) * (FACTOR * LOG2E))
        total = jnp.sum(weights, axis=0, keepdims=True)
        probs = weights * (1.0 / total)
        probs_low.append(probs.astype(jnp.bfloat16))
        result_t = jnp.dot(value_t, probs_low[-1], preferred_element_type=jnp.float32)
        result_t = result_t.astype(jnp.bfloat16)
        centre = jnp.sum(
            grad_t[:, cols].astype(jnp.float32) * result_t.astype(jnp.float32),
            axis=0,
            keepdims=True,
        )
        grad_scores.append((probs * (grad_probs[number] - centre)).astype(jnp.bfloat16))
        grad_query_t = jnp.dot(key_t, grad_scores[-1], preferred_element_type=jnp.float32) * FACTOR
        store(0, cols, result_t.T)
        store(1, cols, grad_query_t.astype(jnp.bfloat16).T)
    probs_low = jnp.concatenate(probs_low, axis=1)
    grad_scores = jnp.concatenate(grad_scores, axis=1)
    grad_value = jnp.dot(probs_low, grad, preferred_element_type=jnp.float32)
    store(3, slice(None), grad_value.astype(jnp.bfloat16))
    grad_key = jnp.dot(grad_scores, query, preferred_element_type=jnp.float32)
    store(2, slice(None), (grad_key * FACTOR).astype(jnp.bfloat16))


def local_kernel(lengths, query_ref, key_ref, value_ref, grad_ref, *rest):
    outs, image_rows = rest[-5:-1], rest[-1]
    count = query_ref.shape[0]

    @pl.when(pl.program_id(0) == 0)
    def _():
        position = lax.axis_index("dp") * count + lax.broadcasted_iota(jnp.int32, (8, count), 1)

        def place(image, carry):
            start, begin = carry
            return start + lengths[image], jnp.where(position >= start, start, begin)

        first = (jnp.int32(0), jnp.zeros((8, count), jnp.int32))
        _, begin = lax.fori_loop(0, lengths.shape[0], place, first)
        image_rows[...] = begin.astype(jnp.float32)

    image_col = image_rows[...].T[:, :1]

    def store(which, rows, part):
        outs[which][rows, :] = part

    attention(
        query_ref[...],
        key_ref[...],
        value_ref[...],
        grad_ref[...],
        lambda cols: image_col == image_rows[:1, cols],
        store,
        LOCAL_CHUNK,
    )


def local_attention(lengths, arrays, first_head, last_head, outs=()):
    rows, width = arrays[0].shape
    block = pl.BlockSpec((rows, HEAD_DIM), lambda step: (0, first_head + step))
    return pl.pallas_call(
        local_kernel,
        grid=(last_head - first_head,),
        in_specs=[SCALARS] + [block] * 4 + [ANYWHERE] * len(outs),
        out_specs=[block] * 4,
        out_shape=[pltpu.HBM((rows, width), jnp.bfloat16)] * 4,
        input_output_aliases={5 + which: which for which in range(len(outs))},
        scratch_shapes=[pltpu.VMEM((8, rows), jnp.float32)],
        compiler_params=pltpu.CompilerParams(vmem_limit_bytes=VMEM_LIMIT),
        cost_estimate=SCHEDULED_LAST,
        name="local_images",
    )(lengths, *in_hbm([*arrays, *outs]))


START = lambda copy: copy.start()
WAIT = lambda copy: copy.wait()
ANYWHERE = pl.BlockSpec(memory_space=pl.ANY)
SCALARS = pl.BlockSpec(memory_space=pltpu.SMEM)


def in_hbm(arrays):
    return [pltpu.with_memory_space_constraint(array, pltpu.HBM) for array in arrays]


def pieces(levels):
    return [(0, levels[0])] + [(levels[0], level - levels[0]) for level in levels[1:]]


def piece_shapes(levels):
    return [pltpu.HBM((size, 4 * HEAD_DIM), jnp.bfloat16) for _, size in pieces(levels)]


def copy_pieces(levels, level, staged, offset, arrays, sems, out, action, first=0):
    for number, (start, size) in enumerate(pieces(levels)):
        if number < first:
            continue
        inside = staged.at[pl.ds(offset + start, size)]
        outside = arrays[number]
        source, target = (inside, outside) if out else (outside, inside)

        @pl.when(True if number == 0 else level == number)
        def _():
            action(pltpu.make_async_copy(source, target, sems.at[number]))


def gather(edge, held, staged):
    steps = blocks_of(edge.own_rows + BLOCK - 1, BLOCK)

    def one_head(slot, carry):
        def one_block(step, carry):
            source = pl.ds(pl.multiple_of(edge.own + step * BLOCK, TILE), BLOCK)
            target = pl.ds(pl.multiple_of(slot * edge.own_rows + step * BLOCK, TILE), BLOCK)
            for which in range(4):
                staged[target, which * HEAD_DIM:(which + 1) * HEAD_DIM] = held[
                    which, source, lanes(edge.sent_head + slot)]
            return carry

        return lax.fori_loop(0, steps, one_block, carry)

    lax.fori_loop(0, edge.sent, one_head, 0)


def pack_even_kernel(levels, blocks, lengths, query, key, value, grad, *rest):
    count = len(levels[EVEN])
    plan, choices, outs = rest[0], rest[1:3], rest[3:3 + count]
    before_edge, after_edge, held, staged, load_sem, out_sem = rest[3 + count:]
    rows, width = query.shape
    find_crossings(rows, blocks, lengths, before_edge, after_edge)
    lower, before, after = own_edge(EVEN, before_edge, after_edge)
    own_rows = round_up(jnp.where(lower, before, after))
    part = tiles(jnp.where(lower, rows - own_rows, 0), own_rows)
    loads = [
        pltpu.make_async_copy(array.at[part], held.at[which, part], load_sem.at[which])
        for which, array in enumerate((query, key, value, grad))
    ]

    @pl.when(before > 0)
    def _():
        for copy in loads:
            copy.start()

    make_plan(width // HEAD_DIM, blocks, levels, plan, choices, before_edge, after_edge)

    @pl.when(before > 0)
    def _():
        for copy in loads:
            copy.wait()
        edge = Edge(plan, EVEN, rows)
        gather(edge, held, staged)
        send = functools.partial(
            copy_pieces, levels[EVEN], edge.level, staged, 0, outs, out_sem, True, first=1)
        send(START)
        outs[0][...] = staged[:outs[0].shape[0], :]
        send(WAIT)


def pack_odd_kernel(levels, plan, query, key, value, grad, *rest):
    count = len(levels)
    outs = rest[:count]
    held, staged, load_sem, out_sem = rest[count:]
    rows = query.shape[0]
    edge = Edge(plan, ODD, rows)
    part = tiles(edge.own, edge.own_rows)
    loads = [
        pltpu.make_async_copy(array.at[part], held.at[which, part], load_sem.at[which])
        for which, array in enumerate((query, key, value, grad))
    ]

    @pl.when(edge.sent > 0)
    def _():
        for copy in loads:
            copy.start()
        for copy in loads:
            copy.wait()
        gather(edge, held, staged)
        move = functools.partial(
            copy_pieces, levels, edge.level, staged, 0, outs, out_sem, True)
        move(START)
        move(WAIT)


def pack_scratch(rows, width, levels):
    return [
        pltpu.VMEM((4, rows + BLOCK, width), jnp.bfloat16),
        pltpu.VMEM((levels[-1] + BLOCK, 4 * HEAD_DIM), jnp.bfloat16),
        pltpu.SemaphoreType.DMA((4,)),
        pltpu.SemaphoreType.DMA((len(levels),)),
    ]


def pack_even(lengths, arrays, levels, blocks):
    rows, width = arrays[0].shape
    one = jax.ShapeDtypeStruct((1,), jnp.int32)
    plan, odd_level, even_level, *even = pl.pallas_call(
        functools.partial(pack_even_kernel, levels, blocks),
        in_specs=[SCALARS] + [ANYWHERE] * 4,
        out_specs=[SCALARS] * 3 + [pl.BlockSpec(memory_space=pltpu.VMEM)]
        + [ANYWHERE] * (len(levels[EVEN]) - 1),
        out_shape=[jax.ShapeDtypeStruct((2 * FIELDS,), jnp.int32), one, one]
        + [pltpu.VMEM((levels[EVEN][0], 4 * HEAD_DIM), jnp.bfloat16)]
        + piece_shapes(levels[EVEN])[1:],
        scratch_shapes=[
            pltpu.SMEM((blocks + 2,), jnp.int32),
            pltpu.SMEM((blocks + 2,), jnp.int32),
        ] + pack_scratch(rows, width, levels[EVEN]),
        compiler_params=pltpu.CompilerParams(vmem_limit_bytes=PACK_VMEM_LIMIT),
        name="pack_even",
    )(lengths, *in_hbm(arrays))
    return plan, (odd_level, even_level), even


def pack_odd(plan, arrays, levels):
    rows, width = arrays[0].shape
    return pl.pallas_call(
        functools.partial(pack_odd_kernel, levels),
        in_specs=[SCALARS] + [ANYWHERE] * 4,
        out_specs=[ANYWHERE] * len(levels),
        out_shape=piece_shapes(levels),
        scratch_shapes=pack_scratch(rows, width, levels),
        compiler_params=pltpu.CompilerParams(vmem_limit_bytes=VMEM_LIMIT),
        name="pack_odd",
    )(plan, *in_hbm(arrays))


def crossing_kernel(levels, kind, plan, query, key, value, grad, *rest):
    count = len(levels)
    received, back, kept = rest[:count], rest[count:2 * count], rest[2 * count]
    own, staged_in, staged_out, result, own_sem, in_sem, out_sem, kept_sem = rest[2 * count + 1:]
    rows, width = query.shape
    edge = Edge(plan, kind, rows)
    jobs = edge.jobs
    own_part = tiles(edge.own, edge.own_rows)
    margin = rows

    def load_own(action):
        for which, array in enumerate((query, key, value, grad)):
            action(pltpu.make_async_copy(
                array.at[own_part], own.at[which, own_part], own_sem.at[which]))

    def keep(job):
        buffer = lax.rem(job, 2)
        return pltpu.make_async_copy(
            result.at[buffer, own_part], kept.at[job, own_part], kept_sem.at[buffer])

    position = lax.broadcasted_iota(jnp.int32, (rows, HEAD_DIM), 0)
    in_own = (position >= edge.own_begin) & (position < edge.own_end)
    key_position = lax.broadcasted_iota(jnp.int32, (rows, 1), 0)
    in_image = (key_position < edge.after) | (key_position >= rows - edge.before)
    in_window = (position < edge.after) | (position >= rows - edge.before)

    def one_job(step, carry):
        job = jnp.where(edge.lower, step, jobs - 1 - step)
        buffer = lax.rem(job, 2)
        start = margin + job * edge.other_rows - edge.other
        window = pl.ds(pl.multiple_of(start, TILE), rows)

        @pl.when(step >= 2)
        def _():
            keep(job).wait()

        zero = jnp.zeros((rows, HEAD_DIM), jnp.bfloat16)
        operands = []
        for which in range(4):
            columns = slice(which * HEAD_DIM, (which + 1) * HEAD_DIM)
            operands.append(jnp.where(
                in_own,
                own[which, :, lanes(edge.job_head + job)],
                jnp.where(in_window, staged_in[window, columns], zero),
            ))

        def store(which, part_rows, part):
            result[buffer, part_rows, which * HEAD_DIM:(which + 1) * HEAD_DIM] = part

        attention(*operands, lambda cols: in_image, store, CROSSING_CHUNK)
        staged_out[window, :] = result[buffer]
        keep(job).start()
        return carry

    @pl.when(jobs > 0)
    def _():
        stage = functools.partial(
            copy_pieces, levels, edge.level, staged_in, margin, received, in_sem, False)
        send = functools.partial(
            copy_pieces, levels, edge.level, staged_out, margin, back, out_sem, True)
        stage(START)
        load_own(START)
        load_own(WAIT)
        stage(WAIT)
        lax.fori_loop(0, jobs, one_job, 0)
        send(START)

        @pl.when(jobs >= 2)
        def _():
            keep(1).wait()

        keep(0).wait()
        send(WAIT)


def crossing_images(kind, plan, arrays, received, levels):
    rows, width = arrays[0].shape
    heads = width // HEAD_DIM
    four = 4 * HEAD_DIM
    count = len(levels)
    staged = pltpu.VMEM((rows + levels[-1] + rows, four), jnp.bfloat16)
    outs = pl.pallas_call(
        functools.partial(crossing_kernel, levels, kind),
        in_specs=[SCALARS] + [ANYWHERE] * (4 + count),
        out_specs=[ANYWHERE] * (count + 1),
        out_shape=piece_shapes(levels)
        + [pltpu.HBM((heads, rows, four), jnp.bfloat16)],
        scratch_shapes=[
            pltpu.VMEM((4, rows, width), jnp.bfloat16),
            staged,
            staged,
            pltpu.VMEM((2, rows, four), jnp.bfloat16),
            pltpu.SemaphoreType.DMA((4,)),
            pltpu.SemaphoreType.DMA((count,)),
            pltpu.SemaphoreType.DMA((count,)),
            pltpu.SemaphoreType.DMA((2,)),
        ],
        compiler_params=pltpu.CompilerParams(vmem_limit_bytes=VMEM_LIMIT),
        cost_estimate=pl.CostEstimate(
            flops=12 * rows * rows * width, bytes_accessed=16 * rows * width, transcendentals=0
        ),
        name="odd_edge_images" if kind == ODD else "even_edge_images",
    )(plan, *in_hbm(arrays), *received)
    return outs[:count], outs[count]


def overlay(whole, which, edge, first_head, heads, source):
    mixed = jnp.where(edge.lower, edge.first_block, edge.last_block - 1)
    full = jnp.where(edge.lower, edge.first_block + 1, edge.first_block)

    def one_head(slot, carry):
        place = lanes(first_head + slot)

        def one_block(step, carry):
            first = (full + step) * BLOCK
            part = pl.ds(pl.multiple_of(first, BLOCK), BLOCK)
            whole[which, part, place] = source(slot, first)
            return carry

        first = mixed * BLOCK
        part = pl.ds(pl.multiple_of(first, BLOCK), BLOCK)
        position = first + lax.broadcasted_iota(jnp.int32, (BLOCK, HEAD_DIM), 0)
        whole[which, part, place] = jnp.where(
            (position >= edge.own_begin) & (position < edge.own_end),
            source(slot, first),
            whole[which, part, place],
        )
        return lax.fori_loop(0, edge.last_block - edge.first_block - 1, one_block, carry)

    lax.fori_loop(0, heads, one_head, 0)


def returned_source(edge, staged, columns):
    def source(slot, first):
        start = BLOCK + slot * edge.own_rows + first - edge.own
        return staged[pl.ds(pl.multiple_of(start, TILE), BLOCK), columns]

    return source


def keep_kernel(plan, kept_odd, kept_even, *rest):
    local, outs = rest[:4], rest[4:8]
    whole, held, whole_sem, held_sem, out_sem = rest[8:]
    rows, width = local[0].shape
    heads = width // HEAD_DIM
    kept = (kept_odd, kept_even)
    edges = [Edge(plan, kind, rows) for kind in (ODD, EVEN)]

    def parts(action):
        for kind in (ODD, EVEN):
            edge = edges[kind]
            part = tiles(edge.own, edge.own_rows)
            for slot in range(heads):
                @pl.when(slot < edge.jobs)
                def _():
                    action(pltpu.make_async_copy(
                        kept[kind].at[slot, part], held.at[kind, slot, part],
                        held_sem.at[kind, slot]))

    loads = [
        pltpu.make_async_copy(local[which], whole.at[which], whole_sem.at[which])
        for which in range(4)
    ]
    saves = [
        pltpu.make_async_copy(whole.at[which], outs[which], out_sem.at[which])
        for which in range(4)
    ]
    parts(START)
    for copy in loads:
        copy.start()
    parts(WAIT)
    for which in range(4):
        columns = slice(which * HEAD_DIM, (which + 1) * HEAD_DIM)
        loads[which].wait()
        for kind in (ODD, EVEN):
            overlay(
                whole, which, edges[kind], edges[kind].job_head, edges[kind].jobs,
                lambda slot, first: held[
                    kind, slot, pl.ds(pl.multiple_of(first, BLOCK), BLOCK), columns])
        saves[which].start()
    for copy in saves:
        copy.wait()


def merge_kept(plan, kept_odd, kept_even, local):
    rows, width = local[0].shape
    heads = width // HEAD_DIM
    return pl.pallas_call(
        keep_kernel,
        in_specs=[SCALARS] + [ANYWHERE] * 6,
        out_specs=[ANYWHERE] * 4,
        out_shape=[pltpu.HBM((rows, width), jnp.bfloat16)] * 4,
        scratch_shapes=[
            pltpu.VMEM((4, rows, width), jnp.bfloat16),
            pltpu.VMEM((2, heads, rows, 4 * HEAD_DIM), jnp.bfloat16),
            pltpu.SemaphoreType.DMA((4,)),
            pltpu.SemaphoreType.DMA((2, heads)),
            pltpu.SemaphoreType.DMA((4,)),
        ],
        compiler_params=pltpu.CompilerParams(vmem_limit_bytes=VMEM_LIMIT),
        cost_estimate=SCHEDULED_LAST,
        name="merge_kept",
    )(plan, *in_hbm([kept_odd, kept_even, *local]))


def return_kernel(levels, plan, *rest):
    counts = [len(levels[ODD]), len(levels[EVEN])]
    total = sum(counts)
    returned = rest[:counts[ODD]], rest[counts[ODD]:total]
    outs = rest[total + 4:total + 8]
    whole, odd_staged, even_staged, whole_sem, odd_sem, even_sem = rest[total + 8:]
    staged = odd_staged, even_staged
    rows = whole.shape[1]
    edges = [Edge(plan, kind, rows) for kind in (ODD, EVEN)]
    stages = [
        functools.partial(
            copy_pieces, levels[kind], edges[kind].level, staged[kind], BLOCK, returned[kind],
            sem, False)
        for kind, sem in ((ODD, odd_sem), (EVEN, even_sem))
    ]

    ends = []
    for edge, other in (edges, edges[::-1]):
        meets = jnp.logical_not(edge.lower) & (other.sent > 0)
        ends.append(jnp.where(
            meets, jnp.minimum(edge.last_block, other.first_block), edge.last_block))

    def move(kind, which, out, action):
        first, last = edges[kind].first_block, ends[kind]

        @pl.when((edges[kind].sent > 0) & (last > first))
        def _():
            part = pl.ds(
                pl.multiple_of(first * BLOCK, BLOCK), pl.multiple_of((last - first) * BLOCK, BLOCK))
            inside, outside = whole.at[which, part], outs[which].at[part]
            source, target = (inside, outside) if out else (outside, inside)
            action(pltpu.make_async_copy(source, target, whole_sem.at[kind, which]))

    for stage in stages:
        stage(START)
    for which in range(4):
        for kind in (ODD, EVEN):
            move(kind, which, False, START)
    for stage in stages:
        stage(WAIT)
    for which in range(4):
        columns = slice(which * HEAD_DIM, (which + 1) * HEAD_DIM)
        for kind in (ODD, EVEN):
            move(kind, which, False, WAIT)
        for kind in (ODD, EVEN):
            edge = edges[kind]
            overlay(whole, which, edge, edge.sent_head, edge.sent,
                    returned_source(edge, staged[kind], columns))
        for kind in (ODD, EVEN):
            move(kind, which, True, START)
    for which in range(4):
        for kind in (ODD, EVEN):
            move(kind, which, True, WAIT)


def merge_returned(plan, odd, even, outs, levels):
    rows, width = outs[0].shape
    counts = [len(levels[ODD]), len(levels[EVEN])]
    return pl.pallas_call(
        functools.partial(return_kernel, levels),
        in_specs=[SCALARS] + [ANYWHERE] * (sum(counts) + 4),
        out_specs=[ANYWHERE] * 4,
        out_shape=[pltpu.HBM((rows, width), jnp.bfloat16)] * 4,
        input_output_aliases={1 + sum(counts) + which: which for which in range(4)},
        scratch_shapes=[
            pltpu.VMEM((4, rows, width), jnp.bfloat16),
            pltpu.VMEM((levels[ODD][-1] + 2 * BLOCK, 4 * HEAD_DIM), jnp.bfloat16),
            pltpu.VMEM((levels[EVEN][-1] + 2 * BLOCK, 4 * HEAD_DIM), jnp.bfloat16),
            pltpu.SemaphoreType.DMA((2, 4)),
            pltpu.SemaphoreType.DMA((counts[ODD],)),
            pltpu.SemaphoreType.DMA((counts[EVEN],)),
        ],
        compiler_params=pltpu.CompilerParams(vmem_limit_bytes=VMEM_LIMIT),
        name="merge_returned",
    )(plan, *odd, *even, *in_hbm(outs))


def swapped(value, kind):
    first = 0 if kind == ODD else 1
    pairs = [(block, block + 1) for block in range(first, lax.axis_size("dp") - 1, 2)]
    return lax.ppermute(value, "dp", pairs + [(after, before) for before, after in pairs])


def swap_further(choices, odd, even):
    counts = [len(odd), len(even)]
    if not sum(counts):
        return [], []
    pairs = [(first, second) for first in range(counts[0] + 1) for second in range(counts[1] + 1)]

    def send(used, odd, even):
        return tuple(
            [
                swapped(array, kind) if number == used[kind] else array
                for number, array in enumerate(arrays, start=1)
            ]
            for kind, arrays in ((ODD, odd), (EVEN, even))
        )

    index = 0
    for choice, count in zip(choices, counts):
        if count:
            index = index * (count + 1) + choice[0]
    branches = [functools.partial(send, pair) for pair in pairs]
    return lax.switch(index, branches, list(odd), list(even))


def body(queries, keys, values, out_grad, lengths):
    rows, width = queries.shape
    arrays = (queries, keys, values, out_grad)
    levels = [size_levels(kind, rows, width // HEAD_DIM) for kind in (ODD, EVEN)]
    plan, choices, even = pack_even(lengths, arrays, levels, lax.axis_size("dp"))
    even_first = swapped(even[0], EVEN)
    odd = pack_odd(plan, arrays, levels[ODD])
    odd_first = swapped(odd[0], ODD)
    heads = width // HEAD_DIM
    local = local_attention(lengths, arrays, 0, heads // 2)
    choices, local = lax.optimization_barrier((choices, local))
    _, more = swap_further(choices, [], even[1:])
    back_even, kept_even = crossing_images(EVEN, plan, arrays, [even_first, *more], levels[EVEN])
    choices, kept_even = lax.optimization_barrier((choices, kept_even))
    more, _ = swap_further(choices, odd[1:], [])
    received = [odd_first, *more]
    first, received = lax.optimization_barrier((back_even[0], received))
    even_first = swapped(first, EVEN)
    back_odd, kept_odd = crossing_images(ODD, plan, arrays, received, levels[ODD])
    odd_first = swapped(back_odd[0], ODD)
    kept_odd, local = lax.optimization_barrier((kept_odd, local))
    local = local_attention(lengths, arrays, heads // 2, heads, local)
    outs = merge_kept(plan, kept_odd, kept_even, local)
    even_first, choices, outs = lax.optimization_barrier((even_first, choices, outs))
    more_odd, more_even = swap_further(choices, back_odd[1:], back_even[1:])
    return tuple(merge_returned(
        plan, [odd_first, *more_odd], [even_first, *more_even], outs, levels))


def solution(mesh):
    in_specs = (P("dp", "tensor"), P("dp", "tensor"), P("dp", "tensor"), P("dp", "tensor"), P())
    out_specs = (P("dp", "tensor"), P("dp", "tensor"), P("dp", "tensor"), P("dp", "tensor"))
    return jax.shard_map(body, mesh=mesh, in_specs=in_specs, out_specs=out_specs, check_vma=False)
```

```python
import functools
import math

import jax
import jax.numpy as jnp
from jax import lax
from jax.experimental import pallas as pl
from jax.experimental.pallas import tpu as pltpu
from jax.sharding import PartitionSpec as P

HEAD_DIM = 128
TILE = 16
BLOCK = 64
LOCAL_CHUNK = 256
CROSSING_CHUNK = 256
FACTOR = 1.0 / math.sqrt(HEAD_DIM)
LOG2E = 1.4426950408889634
VMEM_LIMIT = 32 * 1024 * 1024
PACK_VMEM_LIMIT = 60 * 1024 * 1024

SCHEDULED_LAST = pl.CostEstimate(flops=1, bytes_accessed=1, transcendentals=0)

FIELDS = 8
BEFORE, AFTER, LOWER, JOBS, JOB_HEAD, SENT, SENT_HEAD, LEVEL = range(FIELDS)
ODD, EVEN = 0, 1

LEVEL_UNITS = ((9, 10, 11, 12, 13), (9, 10, 11, 12, 13))


def round_up(value):
    return (value + (TILE - 1)) & -TILE


def blocks_of(value, size):
    if size & (size - 1):
        return value // size
    return lax.shift_right_logical(value, jnp.int32(size.bit_length() - 1))


def worst_case_rows(rows, heads):
    worst = 0
    for before in range(TILE, rows + 1, TILE):
        for after in range(TILE, rows + TILE - before + 1, TILE):
            needed = min(max(after * low, before * (heads - low)) for low in range(heads + 1))
            worst = max(worst, needed)
    return worst


def size_levels(kind, rows, heads):
    unit = rows * heads // 48
    most = worst_case_rows(rows, heads)
    below = sorted(int(level * unit) for level in LEVEL_UNITS[kind] if level * unit < most)
    return tuple(below) + (most,)


def find_crossings(rows, blocks, lengths, before_edge, after_edge):
    def clear(edge, carry):
        before_edge[edge] = 0
        after_edge[edge] = 0
        return carry

    lax.fori_loop(0, blocks + 1, clear, 0)

    def place(image, start):
        end = start + lengths[image]
        edge = blocks_of(end - 1, rows)

        @pl.when(edge > blocks_of(start, rows))
        def _():
            before_edge[edge] = edge * rows - start
            after_edge[edge] = end - edge * rows

        return end

    lax.fori_loop(0, lengths.shape[0], place, 0)


def own_edge(kind, before_edge, after_edge):
    block = lax.axis_index("dp")
    lower = lax.rem(block, 2) == (0 if kind == ODD else 1)
    edge = jnp.where(lower, block + 1, block)
    return lower, before_edge[edge], after_edge[edge]


def make_plan(heads, blocks, levels, plan, choices, before_edge, after_edge):
    entry = lax.broadcasted_iota(jnp.int32, (8, 128), 1)
    for kind in (ODD, EVEN):
        limit = jnp.full((8, 128), levels[kind][-1], jnp.int32)
        for number, level in enumerate(levels[kind]):
            limit = jnp.where(entry == number, level, limit)

        def check(number, fits):
            edge = 2 * number + (1 if kind == ODD else 2)
            after = round_up(after_edge[edge])
            before = round_up(before_edge[edge])
            taken = jnp.zeros((8, 128), jnp.int32)
            for count in range(1, heads + 1):
                taken += jnp.where(after * count <= limit, 1, 0)
                taken += jnp.where(before * count <= limit, 1, 0)
            return jnp.minimum(fits, jnp.where(taken >= heads, 1, 0))

        last = len(levels[kind]) - 1
        chosen = jnp.int32(last)
        if last:
            edges = (blocks - (0 if kind == ODD else 1)) // 2
            fits = lax.fori_loop(0, edges, check, jnp.ones((8, 128), jnp.int32))
            chosen = jnp.min(jnp.where(fits == 1, entry, last))
        most_rows = jnp.int32(levels[kind][-1])
        for number, level in enumerate(levels[kind][:-1]):
            most_rows = jnp.where(chosen == number, level, most_rows)

        lower, before, after = own_edge(kind, before_edge, after_edge)
        most = jnp.int32(0)
        least = jnp.int32(heads)
        for count in range(1, heads + 1):
            most += jnp.where(round_up(after) * count <= most_rows, 1, 0)
            least -= jnp.where(round_up(before) * count <= most_rows, 1, 0)
        low = jnp.clip(jnp.int32(heads // 2), least, most)
        crossed = before > 0
        base = kind * FIELDS
        plan[base + BEFORE] = before
        plan[base + AFTER] = after
        plan[base + LOWER] = lower.astype(jnp.int32)
        plan[base + JOBS] = jnp.where(crossed, jnp.where(lower, low, heads - low), 0)
        plan[base + JOB_HEAD] = jnp.where(lower, 0, low)
        plan[base + SENT] = jnp.where(crossed, jnp.where(lower, heads - low, low), 0)
        plan[base + SENT_HEAD] = jnp.where(lower, low, 0)
        plan[base + LEVEL] = chosen
        choices[kind][0] = chosen


class Edge:
    def __init__(self, plan, kind, rows):
        read = lambda field: plan[kind * FIELDS + field]
        self.lower = read(LOWER) == 1
        self.jobs, self.job_head = read(JOBS), read(JOB_HEAD)
        self.sent, self.sent_head = read(SENT), read(SENT_HEAD)
        self.level = read(LEVEL)
        before, after = read(BEFORE), read(AFTER)
        self.before, self.after = before, after
        self.own_begin = jnp.where(self.lower, rows - before, 0)
        self.own_end = jnp.where(self.lower, rows, after)
        self.own_rows = round_up(jnp.where(self.lower, before, after))
        self.other_rows = round_up(jnp.where(self.lower, after, before))
        self.own = jnp.where(self.lower, rows - self.own_rows, 0)
        self.other = jnp.where(self.lower, 0, rows - self.other_rows)
        self.first_block = blocks_of(self.own_begin, BLOCK)
        self.last_block = blocks_of(self.own_end + BLOCK - 1, BLOCK)


def tiles(start, size):
    return pl.ds(pl.multiple_of(start, TILE), pl.multiple_of(size, TILE))


def lanes(head):
    return pl.ds(pl.multiple_of(head * HEAD_DIM, HEAD_DIM), HEAD_DIM)


def attention(query, key, value, grad, mask_columns, store, chunk):
    count = query.shape[0]
    key_t = key.T
    value_t = value.T
    grad_t = grad.T
    across = (((1,), (1,)), ((), ()))
    chunks = [slice(first, first + chunk) for first in range(0, count, chunk)]
    scores = [
        lax.dot_general(key, query[cols], across, preferred_element_type=jnp.float32)
        for cols in chunks
    ]
    grad_probs = [
        lax.dot_general(value, grad[cols], across, preferred_element_type=jnp.float32)
        for cols in chunks
    ]
    probs_low = []
    grad_scores = []
    for number, cols in enumerate(chunks):
        masked = jnp.where(mask_columns(cols), scores[number], -1e30)
        top = jnp.max(masked, axis=0, keepdims=True)
        weights = jnp.exp2((masked - top) * (FACTOR * LOG2E))
        total = jnp.sum(weights, axis=0, keepdims=True)
        probs = weights * (1.0 / total)
        probs_low.append(probs.astype(jnp.bfloat16))
        result_t = jnp.dot(value_t, probs_low[-1], preferred_element_type=jnp.float32)
        result_t = result_t.astype(jnp.bfloat16)
        centre = jnp.sum(
            grad_t[:, cols].astype(jnp.float32) * result_t.astype(jnp.float32),
            axis=0,
            keepdims=True,
        )
        grad_scores.append((probs * (grad_probs[number] - centre)).astype(jnp.bfloat16))
        grad_query_t = jnp.dot(key_t, grad_scores[-1], preferred_element_type=jnp.float32) * FACTOR
        store(0, cols, result_t.T)
        store(1, cols, grad_query_t.astype(jnp.bfloat16).T)
    probs_low = jnp.concatenate(probs_low, axis=1)
    grad_scores = jnp.concatenate(grad_scores, axis=1)
    grad_value = jnp.dot(probs_low, grad, preferred_element_type=jnp.float32)
    store(3, slice(None), grad_value.astype(jnp.bfloat16))
    grad_key = jnp.dot(grad_scores, query, preferred_element_type=jnp.float32)
    store(2, slice(None), (grad_key * FACTOR).astype(jnp.bfloat16))


def local_kernel(lengths, query_ref, key_ref, value_ref, grad_ref, *rest):
    outs, image_rows = rest[-5:-1], rest[-1]
    count = query_ref.shape[0]

    @pl.when(pl.program_id(0) == 0)
    def _():
        position = lax.axis_index("dp") * count + lax.broadcasted_iota(jnp.int32, (8, count), 1)

        def place(image, carry):
            start, begin = carry
            return start + lengths[image], jnp.where(position >= start, start, begin)

        first = (jnp.int32(0), jnp.zeros((8, count), jnp.int32))
        _, begin = lax.fori_loop(0, lengths.shape[0], place, first)
        image_rows[...] = begin.astype(jnp.float32)

    image_col = image_rows[...].T[:, :1]

    def store(which, rows, part):
        outs[which][rows, :] = part

    attention(
        query_ref[...],
        key_ref[...],
        value_ref[...],
        grad_ref[...],
        lambda cols: image_col == image_rows[:1, cols],
        store,
        LOCAL_CHUNK,
    )


def local_attention(lengths, arrays, first_head, last_head, outs=()):
    rows, width = arrays[0].shape
    block = pl.BlockSpec((rows, HEAD_DIM), lambda step: (0, first_head + step))
    return pl.pallas_call(
        local_kernel,
        grid=(last_head - first_head,),
        in_specs=[SCALARS] + [block] * 4 + [ANYWHERE] * len(outs),
        out_specs=[block] * 4,
        out_shape=[pltpu.HBM((rows, width), jnp.bfloat16)] * 4,
        input_output_aliases={5 + which: which for which in range(len(outs))},
        scratch_shapes=[pltpu.VMEM((8, rows), jnp.float32)],
        compiler_params=pltpu.CompilerParams(vmem_limit_bytes=VMEM_LIMIT),
        cost_estimate=SCHEDULED_LAST,
        name="local_images",
    )(lengths, *in_hbm([*arrays, *outs]))


START = lambda copy: copy.start()
WAIT = lambda copy: copy.wait()
ANYWHERE = pl.BlockSpec(memory_space=pl.ANY)
SCALARS = pl.BlockSpec(memory_space=pltpu.SMEM)


def in_hbm(arrays):
    return [pltpu.with_memory_space_constraint(array, pltpu.HBM) for array in arrays]


def pieces(levels):
    return [(0, levels[0])] + [(levels[0], level - levels[0]) for level in levels[1:]]


def piece_shapes(levels):
    return [pltpu.HBM((size, 4 * HEAD_DIM), jnp.bfloat16) for _, size in pieces(levels)]


def copy_pieces(levels, level, staged, offset, arrays, sems, out, action, first=0):
    for number, (start, size) in enumerate(pieces(levels)):
        if number < first:
            continue
        inside = staged.at[pl.ds(offset + start, size)]
        outside = arrays[number]
        source, target = (inside, outside) if out else (outside, inside)

        @pl.when(True if number == 0 else level == number)
        def _():
            action(pltpu.make_async_copy(source, target, sems.at[number]))


def gather(edge, held, staged):
    steps = blocks_of(edge.own_rows + BLOCK - 1, BLOCK)

    def one_head(slot, carry):
        def one_block(step, carry):
            source = pl.ds(pl.multiple_of(edge.own + step * BLOCK, TILE), BLOCK)
            target = pl.ds(pl.multiple_of(slot * edge.own_rows + step * BLOCK, TILE), BLOCK)
            for which in range(4):
                staged[target, which * HEAD_DIM:(which + 1) * HEAD_DIM] = held[
                    which, source, lanes(edge.sent_head + slot)]
            return carry

        return lax.fori_loop(0, steps, one_block, carry)

    lax.fori_loop(0, edge.sent, one_head, 0)


def pack_even_kernel(levels, blocks, lengths, query, key, value, grad, *rest):
    count = len(levels[EVEN])
    plan, choices, outs = rest[0], rest[1:3], rest[3:3 + count]
    before_edge, after_edge, held, staged, load_sem, out_sem = rest[3 + count:]
    rows, width = query.shape
    find_crossings(rows, blocks, lengths, before_edge, after_edge)
    lower, before, after = own_edge(EVEN, before_edge, after_edge)
    own_rows = round_up(jnp.where(lower, before, after))
    part = tiles(jnp.where(lower, rows - own_rows, 0), own_rows)
    loads = [
        pltpu.make_async_copy(array.at[part], held.at[which, part], load_sem.at[which])
        for which, array in enumerate((query, key, value, grad))
    ]

    @pl.when(before > 0)
    def _():
        for copy in loads:
            copy.start()

    make_plan(width // HEAD_DIM, blocks, levels, plan, choices, before_edge, after_edge)

    @pl.when(before > 0)
    def _():
        for copy in loads:
            copy.wait()
        edge = Edge(plan, EVEN, rows)
        gather(edge, held, staged)
        send = functools.partial(
            copy_pieces, levels[EVEN], edge.level, staged, 0, outs, out_sem, True, first=1)
        send(START)
        outs[0][...] = staged[:outs[0].shape[0], :]
        send(WAIT)


def pack_odd_kernel(levels, plan, query, key, value, grad, *rest):
    count = len(levels)
    outs = rest[:count]
    held, staged, load_sem, out_sem = rest[count:]
    rows = query.shape[0]
    edge = Edge(plan, ODD, rows)
    part = tiles(edge.own, edge.own_rows)
    loads = [
        pltpu.make_async_copy(array.at[part], held.at[which, part], load_sem.at[which])
        for which, array in enumerate((query, key, value, grad))
    ]

    @pl.when(edge.sent > 0)
    def _():
        for copy in loads:
            copy.start()
        for copy in loads:
            copy.wait()
        gather(edge, held, staged)
        move = functools.partial(
            copy_pieces, levels, edge.level, staged, 0, outs, out_sem, True)
        move(START)
        move(WAIT)


def pack_scratch(rows, width, levels):
    return [
        pltpu.VMEM((4, rows + BLOCK, width), jnp.bfloat16),
        pltpu.VMEM((levels[-1] + BLOCK, 4 * HEAD_DIM), jnp.bfloat16),
        pltpu.SemaphoreType.DMA((4,)),
        pltpu.SemaphoreType.DMA((len(levels),)),
    ]


def pack_even(lengths, arrays, levels, blocks):
    rows, width = arrays[0].shape
    one = jax.ShapeDtypeStruct((1,), jnp.int32)
    plan, odd_level, even_level, *even = pl.pallas_call(
        functools.partial(pack_even_kernel, levels, blocks),
        in_specs=[SCALARS] + [ANYWHERE] * 4,
        out_specs=[SCALARS] * 3 + [pl.BlockSpec(memory_space=pltpu.VMEM)]
        + [ANYWHERE] * (len(levels[EVEN]) - 1),
        out_shape=[jax.ShapeDtypeStruct((2 * FIELDS,), jnp.int32), one, one]
        + [pltpu.VMEM((levels[EVEN][0], 4 * HEAD_DIM), jnp.bfloat16)]
        + piece_shapes(levels[EVEN])[1:],
        scratch_shapes=[
            pltpu.SMEM((blocks + 2,), jnp.int32),
            pltpu.SMEM((blocks + 2,), jnp.int32),
        ] + pack_scratch(rows, width, levels[EVEN]),
        compiler_params=pltpu.CompilerParams(vmem_limit_bytes=PACK_VMEM_LIMIT),
        name="pack_even",
    )(lengths, *in_hbm(arrays))
    return plan, (odd_level, even_level), even


def pack_odd(plan, arrays, levels):
    rows, width = arrays[0].shape
    return pl.pallas_call(
        functools.partial(pack_odd_kernel, levels),
        in_specs=[SCALARS] + [ANYWHERE] * 4,
        out_specs=[ANYWHERE] * len(levels),
        out_shape=piece_shapes(levels),
        scratch_shapes=pack_scratch(rows, width, levels),
        compiler_params=pltpu.CompilerParams(vmem_limit_bytes=VMEM_LIMIT),
        name="pack_odd",
    )(plan, *in_hbm(arrays))


def crossing_kernel(levels, kind, plan, query, key, value, grad, *rest):
    count = len(levels)
    received, back, kept = rest[:count], rest[count:2 * count], rest[2 * count]
    own, staged_in, staged_out, result, own_sem, in_sem, out_sem, kept_sem = rest[2 * count + 1:]
    rows, width = query.shape
    edge = Edge(plan, kind, rows)
    jobs = edge.jobs
    own_part = tiles(edge.own, edge.own_rows)
    margin = rows

    def load_own(action):
        for which, array in enumerate((query, key, value, grad)):
            action(pltpu.make_async_copy(
                array.at[own_part], own.at[which, own_part], own_sem.at[which]))

    def keep(job):
        buffer = lax.rem(job, 2)
        return pltpu.make_async_copy(
            result.at[buffer, own_part], kept.at[job, own_part], kept_sem.at[buffer])

    position = lax.broadcasted_iota(jnp.int32, (rows, HEAD_DIM), 0)
    in_own = (position >= edge.own_begin) & (position < edge.own_end)
    key_position = lax.broadcasted_iota(jnp.int32, (rows, 1), 0)
    in_image = (key_position < edge.after) | (key_position >= rows - edge.before)
    in_window = (position < edge.after) | (position >= rows - edge.before)

    def one_job(step, carry):
        job = jnp.where(edge.lower, step, jobs - 1 - step)
        buffer = lax.rem(job, 2)
        start = margin + job * edge.other_rows - edge.other
        window = pl.ds(pl.multiple_of(start, TILE), rows)

        @pl.when(step >= 2)
        def _():
            keep(job).wait()

        zero = jnp.zeros((rows, HEAD_DIM), jnp.bfloat16)
        operands = []
        for which in range(4):
            columns = slice(which * HEAD_DIM, (which + 1) * HEAD_DIM)
            operands.append(jnp.where(
                in_own,
                own[which, :, lanes(edge.job_head + job)],
                jnp.where(in_window, staged_in[window, columns], zero),
            ))

        def store(which, part_rows, part):
            result[buffer, part_rows, which * HEAD_DIM:(which + 1) * HEAD_DIM] = part

        attention(*operands, lambda cols: in_image, store, CROSSING_CHUNK)
        staged_out[window, :] = result[buffer]
        keep(job).start()
        return carry

    @pl.when(jobs > 0)
    def _():
        stage = functools.partial(
            copy_pieces, levels, edge.level, staged_in, margin, received, in_sem, False)
        send = functools.partial(
            copy_pieces, levels, edge.level, staged_out, margin, back, out_sem, True)
        stage(START)
        load_own(START)
        load_own(WAIT)
        stage(WAIT)
        lax.fori_loop(0, jobs, one_job, 0)
        send(START)

        @pl.when(jobs >= 2)
        def _():
            keep(1).wait()

        keep(0).wait()
        send(WAIT)


def crossing_images(kind, plan, arrays, received, levels):
    rows, width = arrays[0].shape
    heads = width // HEAD_DIM
    four = 4 * HEAD_DIM
    count = len(levels)
    staged = pltpu.VMEM((rows + levels[-1] + rows, four), jnp.bfloat16)
    outs = pl.pallas_call(
        functools.partial(crossing_kernel, levels, kind),
        in_specs=[SCALARS] + [ANYWHERE] * (4 + count),
        out_specs=[ANYWHERE] * (count + 1),
        out_shape=piece_shapes(levels)
        + [pltpu.HBM((heads, rows, four), jnp.bfloat16)],
        scratch_shapes=[
            pltpu.VMEM((4, rows, width), jnp.bfloat16),
            staged,
            staged,
            pltpu.VMEM((2, rows, four), jnp.bfloat16),
            pltpu.SemaphoreType.DMA((4,)),
            pltpu.SemaphoreType.DMA((count,)),
            pltpu.SemaphoreType.DMA((count,)),
            pltpu.SemaphoreType.DMA((2,)),
        ],
        compiler_params=pltpu.CompilerParams(vmem_limit_bytes=VMEM_LIMIT),
        cost_estimate=pl.CostEstimate(
            flops=12 * rows * rows * width, bytes_accessed=16 * rows * width, transcendentals=0
        ),
        name="odd_edge_images" if kind == ODD else "even_edge_images",
    )(plan, *in_hbm(arrays), *received)
    return outs[:count], outs[count]


def overlay(whole, which, edge, first_head, heads, source):
    mixed = jnp.where(edge.lower, edge.first_block, edge.last_block - 1)
    full = jnp.where(edge.lower, edge.first_block + 1, edge.first_block)

    def one_head(slot, carry):
        place = lanes(first_head + slot)

        def one_block(step, carry):
            first = (full + step) * BLOCK
            part = pl.ds(pl.multiple_of(first, BLOCK), BLOCK)
            whole[which, part, place] = source(slot, first)
            return carry

        first = mixed * BLOCK
        part = pl.ds(pl.multiple_of(first, BLOCK), BLOCK)
        position = first + lax.broadcasted_iota(jnp.int32, (BLOCK, HEAD_DIM), 0)
        whole[which, part, place] = jnp.where(
            (position >= edge.own_begin) & (position < edge.own_end),
            source(slot, first),
            whole[which, part, place],
        )
        return lax.fori_loop(0, edge.last_block - edge.first_block - 1, one_block, carry)

    lax.fori_loop(0, heads, one_head, 0)


def returned_source(edge, staged, columns):
    def source(slot, first):
        start = BLOCK + slot * edge.own_rows + first - edge.own
        return staged[pl.ds(pl.multiple_of(start, TILE), BLOCK), columns]

    return source


def keep_kernel(plan, kept_odd, kept_even, *rest):
    local, outs = rest[:4], rest[4:8]
    whole, held, whole_sem, held_sem, out_sem = rest[8:]
    rows, width = local[0].shape
    heads = width // HEAD_DIM
    kept = (kept_odd, kept_even)
    edges = [Edge(plan, kind, rows) for kind in (ODD, EVEN)]

    def parts(action):
        for kind in (ODD, EVEN):
            edge = edges[kind]
            part = tiles(edge.own, edge.own_rows)
            for slot in range(heads):
                @pl.when(slot < edge.jobs)
                def _():
                    action(pltpu.make_async_copy(
                        kept[kind].at[slot, part], held.at[kind, slot, part],
                        held_sem.at[kind, slot]))

    loads = [
        pltpu.make_async_copy(local[which], whole.at[which], whole_sem.at[which])
        for which in range(4)
    ]
    saves = [
        pltpu.make_async_copy(whole.at[which], outs[which], out_sem.at[which])
        for which in range(4)
    ]
    parts(START)
    for copy in loads:
        copy.start()
    parts(WAIT)
    for which in range(4):
        columns = slice(which * HEAD_DIM, (which + 1) * HEAD_DIM)
        loads[which].wait()
        for kind in (ODD, EVEN):
            overlay(
                whole, which, edges[kind], edges[kind].job_head, edges[kind].jobs,
                lambda slot, first: held[
                    kind, slot, pl.ds(pl.multiple_of(first, BLOCK), BLOCK), columns])
        saves[which].start()
    for copy in saves:
        copy.wait()


def merge_kept(plan, kept_odd, kept_even, local):
    rows, width = local[0].shape
    heads = width // HEAD_DIM
    return pl.pallas_call(
        keep_kernel,
        in_specs=[SCALARS] + [ANYWHERE] * 6,
        out_specs=[ANYWHERE] * 4,
        out_shape=[pltpu.HBM((rows, width), jnp.bfloat16)] * 4,
        scratch_shapes=[
            pltpu.VMEM((4, rows, width), jnp.bfloat16),
            pltpu.VMEM((2, heads, rows, 4 * HEAD_DIM), jnp.bfloat16),
            pltpu.SemaphoreType.DMA((4,)),
            pltpu.SemaphoreType.DMA((2, heads)),
            pltpu.SemaphoreType.DMA((4,)),
        ],
        compiler_params=pltpu.CompilerParams(vmem_limit_bytes=VMEM_LIMIT),
        cost_estimate=SCHEDULED_LAST,
        name="merge_kept",
    )(plan, *in_hbm([kept_odd, kept_even, *local]))


def return_kernel(levels, plan, *rest):
    counts = [len(levels[ODD]), len(levels[EVEN])]
    total = sum(counts)
    returned = rest[:counts[ODD]], rest[counts[ODD]:total]
    outs = rest[total + 4:total + 8]
    whole, odd_staged, even_staged, whole_sem, odd_sem, even_sem = rest[total + 8:]
    staged = odd_staged, even_staged
    rows = whole.shape[1]
    edges = [Edge(plan, kind, rows) for kind in (ODD, EVEN)]
    stages = [
        functools.partial(
            copy_pieces, levels[kind], edges[kind].level, staged[kind], BLOCK, returned[kind],
            sem, False)
        for kind, sem in ((ODD, odd_sem), (EVEN, even_sem))
    ]

    ends = []
    for edge, other in (edges, edges[::-1]):
        meets = jnp.logical_not(edge.lower) & (other.sent > 0)
        ends.append(jnp.where(
            meets, jnp.minimum(edge.last_block, other.first_block), edge.last_block))

    def move(kind, which, out, action):
        first, last = edges[kind].first_block, ends[kind]

        @pl.when((edges[kind].sent > 0) & (last > first))
        def _():
            part = pl.ds(
                pl.multiple_of(first * BLOCK, BLOCK), pl.multiple_of((last - first) * BLOCK, BLOCK))
            inside, outside = whole.at[which, part], outs[which].at[part]
            source, target = (inside, outside) if out else (outside, inside)
            action(pltpu.make_async_copy(source, target, whole_sem.at[kind, which]))

    for stage in stages:
        stage(START)
    for which in range(4):
        for kind in (ODD, EVEN):
            move(kind, which, False, START)
    for stage in stages:
        stage(WAIT)
    for which in range(4):
        columns = slice(which * HEAD_DIM, (which + 1) * HEAD_DIM)
        for kind in (ODD, EVEN):
            move(kind, which, False, WAIT)
        for kind in (ODD, EVEN):
            edge = edges[kind]
            overlay(whole, which, edge, edge.sent_head, edge.sent,
                    returned_source(edge, staged[kind], columns))
        for kind in (ODD, EVEN):
            move(kind, which, True, START)
    for which in range(4):
        for kind in (ODD, EVEN):
            move(kind, which, True, WAIT)


def merge_returned(plan, odd, even, outs, levels):
    rows, width = outs[0].shape
    counts = [len(levels[ODD]), len(levels[EVEN])]
    return pl.pallas_call(
        functools.partial(return_kernel, levels),
        in_specs=[SCALARS] + [ANYWHERE] * (sum(counts) + 4),
        out_specs=[ANYWHERE] * 4,
        out_shape=[pltpu.HBM((rows, width), jnp.bfloat16)] * 4,
        input_output_aliases={1 + sum(counts) + which: which for which in range(4)},
        scratch_shapes=[
            pltpu.VMEM((4, rows, width), jnp.bfloat16),
            pltpu.VMEM((levels[ODD][-1] + 2 * BLOCK, 4 * HEAD_DIM), jnp.bfloat16),
            pltpu.VMEM((levels[EVEN][-1] + 2 * BLOCK, 4 * HEAD_DIM), jnp.bfloat16),
            pltpu.SemaphoreType.DMA((2, 4)),
            pltpu.SemaphoreType.DMA((counts[ODD],)),
            pltpu.SemaphoreType.DMA((counts[EVEN],)),
        ],
        compiler_params=pltpu.CompilerParams(vmem_limit_bytes=VMEM_LIMIT),
        name="merge_returned",
    )(plan, *odd, *even, *in_hbm(outs))


def swapped(value, kind):
    first = 0 if kind == ODD else 1
    pairs = [(block, block + 1) for block in range(first, lax.axis_size("dp") - 1, 2)]
    return lax.ppermute(value, "dp", pairs + [(after, before) for before, after in pairs])


def swap_further(choices, odd, even):
    counts = [len(odd), len(even)]
    if not sum(counts):
        return [], []
    pairs = [(first, second) for first in range(counts[0] + 1) for second in range(counts[1] + 1)]

    def send(used, odd, even):
        return tuple(
            [
                swapped(array, kind) if number == used[kind] else array
                for number, array in enumerate(arrays, start=1)
            ]
            for kind, arrays in ((ODD, odd), (EVEN, even))
        )

    index = 0
    for choice, count in zip(choices, counts):
        if count:
            index = index * (count + 1) + choice[0]
    branches = [functools.partial(send, pair) for pair in pairs]
    return lax.switch(index, branches, list(odd), list(even))


def body(queries, keys, values, out_grad, lengths):
    rows, width = queries.shape
    arrays = (queries, keys, values, out_grad)
    levels = [size_levels(kind, rows, width // HEAD_DIM) for kind in (ODD, EVEN)]
    plan, choices, even = pack_even(lengths, arrays, levels, lax.axis_size("dp"))
    even_first = swapped(even[0], EVEN)
    odd = pack_odd(plan, arrays, levels[ODD])
    odd_first = swapped(odd[0], ODD)
    heads = width // HEAD_DIM
    local = local_attention(lengths, arrays, 0, heads // 2)
    choices, local = lax.optimization_barrier((choices, local))
    _, more = swap_further(choices, [], even[1:])
    back_even, kept_even = crossing_images(EVEN, plan, arrays, [even_first, *more], levels[EVEN])
    choices, kept_even = lax.optimization_barrier((choices, kept_even))
    more, _ = swap_further(choices, odd[1:], [])
    received = [odd_first, *more]
    first, received = lax.optimization_barrier((back_even[0], received))
    even_first = swapped(first, EVEN)
    back_odd, kept_odd = crossing_images(ODD, plan, arrays, received, levels[ODD])
    odd_first = swapped(back_odd[0], ODD)
    kept_odd, local = lax.optimization_barrier((kept_odd, local))
    local = local_attention(lengths, arrays, heads // 2, heads, local)
    outs = merge_kept(plan, kept_odd, kept_even, local)
    even_first, choices, outs = lax.optimization_barrier((even_first, choices, outs))
    more_odd, more_even = swap_further(choices, back_odd[1:], back_even[1:])
    return tuple(merge_returned(
        plan, [odd_first, *more_odd], [even_first, *more_even], outs, levels))


def solution(mesh):
    in_specs = (P("dp", "tensor"), P("dp", "tensor"), P("dp", "tensor"), P("dp", "tensor"), P())
    out_specs = (P("dp", "tensor"), P("dp", "tensor"), P("dp", "tensor"), P("dp", "tensor"))
    return jax.shard_map(body, mesh=mesh, in_specs=in_specs, out_specs=out_specs, check_vma=False)
```

```python
import functools
import math

import jax
import jax.numpy as jnp
from jax import lax
from jax.experimental import pallas as pl
from jax.experimental.pallas import tpu as pltpu
from jax.sharding import PartitionSpec as P

HEAD_DIM = 128
TILE = 16
BLOCK = 64
LOCAL_CHUNK = 256
CROSSING_CHUNK = 256
FACTOR = 1.0 / math.sqrt(HEAD_DIM)
LOG2E = 1.4426950408889634
VMEM_LIMIT = 32 * 1024 * 1024
PACK_VMEM_LIMIT = 60 * 1024 * 1024

SCHEDULED_LAST = pl.CostEstimate(flops=1, bytes_accessed=1, transcendentals=0)

FIELDS = 8
BEFORE, AFTER, LOWER, JOBS, JOB_HEAD, SENT, SENT_HEAD, LEVEL = range(FIELDS)
ODD, EVEN = 0, 1

LEVEL_UNITS = ((9, 10, 11, 12, 13), (9, 10, 11, 12, 13))


def round_up(value):
    return (value + (TILE - 1)) & -TILE


def blocks_of(value, size):
    if size & (size - 1):
        return value // size
    return lax.shift_right_logical(value, jnp.int32(size.bit_length() - 1))


def worst_case_rows(rows, heads):
    worst = 0
    for before in range(TILE, rows + 1, TILE):
        for after in range(TILE, rows + TILE - before + 1, TILE):
            needed = min(max(after * low, before * (heads - low)) for low in range(heads + 1))
            worst = max(worst, needed)
    return worst


def size_levels(kind, rows, heads):
    unit = rows * heads // 48
    most = worst_case_rows(rows, heads)
    below = sorted(int(level * unit) for level in LEVEL_UNITS[kind] if level * unit < most)
    return tuple(below) + (most,)


def find_crossings(rows, blocks, lengths, before_edge, after_edge):
    def clear(edge, carry):
        before_edge[edge] = 0
        after_edge[edge] = 0
        return carry

    lax.fori_loop(0, blocks + 1, clear, 0)

    def place(image, start):
        end = start + lengths[image]
        edge = blocks_of(end - 1, rows)

        @pl.when(edge > blocks_of(start, rows))
        def _():
            before_edge[edge] = edge * rows - start
            after_edge[edge] = end - edge * rows

        return end

    lax.fori_loop(0, lengths.shape[0], place, 0)


def own_edge(kind, before_edge, after_edge):
    block = lax.axis_index("dp")
    lower = lax.rem(block, 2) == (0 if kind == ODD else 1)
    edge = jnp.where(lower, block + 1, block)
    return lower, before_edge[edge], after_edge[edge]


def make_plan(heads, blocks, levels, plan, choices, before_edge, after_edge):
    entry = lax.broadcasted_iota(jnp.int32, (8, 128), 1)
    for kind in (ODD, EVEN):
        limit = jnp.full((8, 128), levels[kind][-1], jnp.int32)
        for number, level in enumerate(levels[kind]):
            limit = jnp.where(entry == number, level, limit)

        def check(number, fits):
            edge = 2 * number + (1 if kind == ODD else 2)
            after = round_up(after_edge[edge])
            before = round_up(before_edge[edge])
            taken = jnp.zeros((8, 128), jnp.int32)
            for count in range(1, heads + 1):
                taken += jnp.where(after * count <= limit, 1, 0)
                taken += jnp.where(before * count <= limit, 1, 0)
            return jnp.minimum(fits, jnp.where(taken >= heads, 1, 0))

        last = len(levels[kind]) - 1
        chosen = jnp.int32(last)
        if last:
            edges = (blocks - (0 if kind == ODD else 1)) // 2
            fits = lax.fori_loop(0, edges, check, jnp.ones((8, 128), jnp.int32))
            chosen = jnp.min(jnp.where(fits == 1, entry, last))
        most_rows = jnp.int32(levels[kind][-1])
        for number, level in enumerate(levels[kind][:-1]):
            most_rows = jnp.where(chosen == number, level, most_rows)

        lower, before, after = own_edge(kind, before_edge, after_edge)
        most = jnp.int32(0)
        least = jnp.int32(heads)
        for count in range(1, heads + 1):
            most += jnp.where(round_up(after) * count <= most_rows, 1, 0)
            least -= jnp.where(round_up(before) * count <= most_rows, 1, 0)
        low = jnp.clip(jnp.int32(heads // 2), least, most)
        crossed = before > 0
        base = kind * FIELDS
        plan[base + BEFORE] = before
        plan[base + AFTER] = after
        plan[base + LOWER] = lower.astype(jnp.int32)
        plan[base + JOBS] = jnp.where(crossed, jnp.where(lower, low, heads - low), 0)
        plan[base + JOB_HEAD] = jnp.where(lower, 0, low)
        plan[base + SENT] = jnp.where(crossed, jnp.where(lower, heads - low, low), 0)
        plan[base + SENT_HEAD] = jnp.where(lower, low, 0)
        plan[base + LEVEL] = chosen
        choices[kind][0] = chosen


class Edge:
    def __init__(self, plan, kind, rows):
        read = lambda field: plan[kind * FIELDS + field]
        self.lower = read(LOWER) == 1
        self.jobs, self.job_head = read(JOBS), read(JOB_HEAD)
        self.sent, self.sent_head = read(SENT), read(SENT_HEAD)
        self.level = read(LEVEL)
        before, after = read(BEFORE), read(AFTER)
        self.before, self.after = before, after
        self.own_begin = jnp.where(self.lower, rows - before, 0)
        self.own_end = jnp.where(self.lower, rows, after)
        self.own_rows = round_up(jnp.where(self.lower, before, after))
        self.other_rows = round_up(jnp.where(self.lower, after, before))
        self.own = jnp.where(self.lower, rows - self.own_rows, 0)
        self.other = jnp.where(self.lower, 0, rows - self.other_rows)
        self.first_block = blocks_of(self.own_begin, BLOCK)
        self.last_block = blocks_of(self.own_end + BLOCK - 1, BLOCK)


def tiles(start, size):
    return pl.ds(pl.multiple_of(start, TILE), pl.multiple_of(size, TILE))


def lanes(head):
    return pl.ds(pl.multiple_of(head * HEAD_DIM, HEAD_DIM), HEAD_DIM)


def attention(query, key, value, grad, mask_columns, store, chunk):
    count = query.shape[0]
    key_t = key.T
    value_t = value.T
    grad_t = grad.T
    across = (((1,), (1,)), ((), ()))
    chunks = [slice(first, first + chunk) for first in range(0, count, chunk)]
    scores = [
        lax.dot_general(key, query[cols], across, preferred_element_type=jnp.float32)
        for cols in chunks
    ]
    grad_probs = [
        lax.dot_general(value, grad[cols], across, preferred_element_type=jnp.float32)
        for cols in chunks
    ]
    probs_low = []
    grad_scores = []
    for number, cols in enumerate(chunks):
        masked = jnp.where(mask_columns(cols), scores[number], -1e30)
        top = jnp.max(masked, axis=0, keepdims=True)
        weights = jnp.exp2((masked - top) * (FACTOR * LOG2E))
        total = jnp.sum(weights, axis=0, keepdims=True)
        probs = weights * (1.0 / total)
        probs_low.append(probs.astype(jnp.bfloat16))
        result_t = jnp.dot(value_t, probs_low[-1], preferred_element_type=jnp.float32)
        result_t = result_t.astype(jnp.bfloat16)
        centre = jnp.sum(
            grad_t[:, cols].astype(jnp.float32) * result_t.astype(jnp.float32),
            axis=0,
            keepdims=True,
        )
        grad_scores.append((probs * (grad_probs[number] - centre)).astype(jnp.bfloat16))
        grad_query_t = jnp.dot(key_t, grad_scores[-1], preferred_element_type=jnp.float32) * FACTOR
        store(0, cols, result_t.T)
        store(1, cols, grad_query_t.astype(jnp.bfloat16).T)
    probs_low = jnp.concatenate(probs_low, axis=1)
    grad_scores = jnp.concatenate(grad_scores, axis=1)
    grad_value = jnp.dot(probs_low, grad, preferred_element_type=jnp.float32)
    store(3, slice(None), grad_value.astype(jnp.bfloat16))
    grad_key = jnp.dot(grad_scores, query, preferred_element_type=jnp.float32)
    store(2, slice(None), (grad_key * FACTOR).astype(jnp.bfloat16))


def local_kernel(lengths, query_ref, key_ref, value_ref, grad_ref, *rest):
    outs, image_rows = rest[-5:-1], rest[-1]
    count = query_ref.shape[0]

    @pl.when(pl.program_id(0) == 0)
    def _():
        position = lax.axis_index("dp") * count + lax.broadcasted_iota(jnp.int32, (8, count), 1)

        def place(image, carry):
            start, begin = carry
            return start + lengths[image], jnp.where(position >= start, start, begin)

        first = (jnp.int32(0), jnp.zeros((8, count), jnp.int32))
        _, begin = lax.fori_loop(0, lengths.shape[0], place, first)
        image_rows[...] = begin.astype(jnp.float32)

    image_col = image_rows[...].T[:, :1]

    def store(which, rows, part):
        outs[which][rows, :] = part

    attention(
        query_ref[...],
        key_ref[...],
        value_ref[...],
        grad_ref[...],
        lambda cols: image_col == image_rows[:1, cols],
        store,
        LOCAL_CHUNK,
    )


def local_attention(lengths, arrays, first_head, last_head, outs=()):
    rows, width = arrays[0].shape
    block = pl.BlockSpec((rows, HEAD_DIM), lambda step: (0, first_head + step))
    return pl.pallas_call(
        local_kernel,
        grid=(last_head - first_head,),
        in_specs=[SCALARS] + [block] * 4 + [ANYWHERE] * len(outs),
        out_specs=[block] * 4,
        out_shape=[pltpu.HBM((rows, width), jnp.bfloat16)] * 4,
        input_output_aliases={5 + which: which for which in range(len(outs))},
        scratch_shapes=[pltpu.VMEM((8, rows), jnp.float32)],
        compiler_params=pltpu.CompilerParams(vmem_limit_bytes=VMEM_LIMIT),
        cost_estimate=SCHEDULED_LAST,
        name="local_images",
    )(lengths, *in_hbm([*arrays, *outs]))


START = lambda copy: copy.start()
WAIT = lambda copy: copy.wait()
ANYWHERE = pl.BlockSpec(memory_space=pl.ANY)
SCALARS = pl.BlockSpec(memory_space=pltpu.SMEM)


def in_hbm(arrays):
    return [pltpu.with_memory_space_constraint(array, pltpu.HBM) for array in arrays]


def pieces(levels):
    return [(0, levels[0])] + [(levels[0], level - levels[0]) for level in levels[1:]]


def piece_shapes(levels):
    return [pltpu.HBM((size, 4 * HEAD_DIM), jnp.bfloat16) for _, size in pieces(levels)]


def copy_pieces(levels, level, staged, offset, arrays, sems, out, action, first=0):
    for number, (start, size) in enumerate(pieces(levels)):
        if number < first:
            continue
        inside = staged.at[pl.ds(offset + start, size)]
        outside = arrays[number]
        source, target = (inside, outside) if out else (outside, inside)

        @pl.when(True if number == 0 else level == number)
        def _():
            action(pltpu.make_async_copy(source, target, sems.at[number]))


def gather(edge, held, staged):
    steps = blocks_of(edge.own_rows + BLOCK - 1, BLOCK)

    def one_head(slot, carry):
        def one_block(step, carry):
            source = pl.ds(pl.multiple_of(edge.own + step * BLOCK, TILE), BLOCK)
            target = pl.ds(pl.multiple_of(slot * edge.own_rows + step * BLOCK, TILE), BLOCK)
            for which in range(4):
                staged[target, which * HEAD_DIM:(which + 1) * HEAD_DIM] = held[
                    which, source, lanes(edge.sent_head + slot)]
            return carry

        return lax.fori_loop(0, steps, one_block, carry)

    lax.fori_loop(0, edge.sent, one_head, 0)


def pack_even_kernel(levels, blocks, lengths, query, key, value, grad, *rest):
    count = len(levels[EVEN])
    plan, choices, outs = rest[0], rest[1:3], rest[3:3 + count]
    before_edge, after_edge, held, staged, load_sem, out_sem = rest[3 + count:]
    rows, width = query.shape
    find_crossings(rows, blocks, lengths, before_edge, after_edge)
    lower, before, after = own_edge(EVEN, before_edge, after_edge)
    own_rows = round_up(jnp.where(lower, before, after))
    part = tiles(jnp.where(lower, rows - own_rows, 0), own_rows)
    loads = [
        pltpu.make_async_copy(array.at[part], held.at[which, part], load_sem.at[which])
        for which, array in enumerate((query, key, value, grad))
    ]

    @pl.when(before > 0)
    def _():
        for copy in loads:
            copy.start()

    make_plan(width // HEAD_DIM, blocks, levels, plan, choices, before_edge, after_edge)

    @pl.when(before > 0)
    def _():
        for copy in loads:
            copy.wait()
        edge = Edge(plan, EVEN, rows)
        gather(edge, held, staged)
        send = functools.partial(
            copy_pieces, levels[EVEN], edge.level, staged, 0, outs, out_sem, True, first=1)
        send(START)
        outs[0][...] = staged[:outs[0].shape[0], :]
        send(WAIT)


def pack_odd_kernel(levels, plan, query, key, value, grad, *rest):
    count = len(levels)
    outs = rest[:count]
    held, staged, load_sem, out_sem = rest[count:]
    rows = query.shape[0]
    edge = Edge(plan, ODD, rows)
    part = tiles(edge.own, edge.own_rows)
    loads = [
        pltpu.make_async_copy(array.at[part], held.at[which, part], load_sem.at[which])
        for which, array in enumerate((query, key, value, grad))
    ]

    @pl.when(edge.sent > 0)
    def _():
        for copy in loads:
            copy.start()
        for copy in loads:
            copy.wait()
        gather(edge, held, staged)
        move = functools.partial(
            copy_pieces, levels, edge.level, staged, 0, outs, out_sem, True)
        move(START)
        move(WAIT)


def pack_scratch(rows, width, levels):
    return [
        pltpu.VMEM((4, rows + BLOCK, width), jnp.bfloat16),
        pltpu.VMEM((levels[-1] + BLOCK, 4 * HEAD_DIM), jnp.bfloat16),
        pltpu.SemaphoreType.DMA((4,)),
        pltpu.SemaphoreType.DMA((len(levels),)),
    ]


def pack_even(lengths, arrays, levels, blocks):
    rows, width = arrays[0].shape
    one = jax.ShapeDtypeStruct((1,), jnp.int32)
    plan, odd_level, even_level, *even = pl.pallas_call(
        functools.partial(pack_even_kernel, levels, blocks),
        in_specs=[SCALARS] + [ANYWHERE] * 4,
        out_specs=[SCALARS] * 3 + [pl.BlockSpec(memory_space=pltpu.VMEM)]
        + [ANYWHERE] * (len(levels[EVEN]) - 1),
        out_shape=[jax.ShapeDtypeStruct((2 * FIELDS,), jnp.int32), one, one]
        + [pltpu.VMEM((levels[EVEN][0], 4 * HEAD_DIM), jnp.bfloat16)]
        + piece_shapes(levels[EVEN])[1:],
        scratch_shapes=[
            pltpu.SMEM((blocks + 2,), jnp.int32),
            pltpu.SMEM((blocks + 2,), jnp.int32),
        ] + pack_scratch(rows, width, levels[EVEN]),
        compiler_params=pltpu.CompilerParams(vmem_limit_bytes=PACK_VMEM_LIMIT),
        name="pack_even",
    )(lengths, *in_hbm(arrays))
    return plan, (odd_level, even_level), even


def pack_odd(plan, arrays, levels):
    rows, width = arrays[0].shape
    return pl.pallas_call(
        functools.partial(pack_odd_kernel, levels),
        in_specs=[SCALARS] + [ANYWHERE] * 4,
        out_specs=[ANYWHERE] * len(levels),
        out_shape=piece_shapes(levels),
        scratch_shapes=pack_scratch(rows, width, levels),
        compiler_params=pltpu.CompilerParams(vmem_limit_bytes=VMEM_LIMIT),
        name="pack_odd",
    )(plan, *in_hbm(arrays))


def crossing_kernel(levels, kind, plan, query, key, value, grad, *rest):
    count = len(levels)
    received, back, kept = rest[:count], rest[count:2 * count], rest[2 * count]
    own, staged_in, staged_out, window, result, own_sem, in_sem, out_sem, kept_sem = rest[
        2 * count + 1:]
    rows, width = query.shape
    edge = Edge(plan, kind, rows)
    jobs = edge.jobs
    own_part = tiles(edge.own, edge.own_rows)
    margin = rows

    def load_own(action):
        for which, array in enumerate((query, key, value, grad)):
            action(pltpu.make_async_copy(
                array.at[own_part], own.at[which, own_part], own_sem.at[which]))

    def keep(job):
        buffer = lax.rem(job, 2)
        return pltpu.make_async_copy(
            result.at[buffer, own_part], kept.at[job, own_part], kept_sem.at[buffer])

    key_position = lax.broadcasted_iota(jnp.int32, (rows, 1), 0)
    in_image = (key_position < edge.after) | (key_position >= rows - edge.before)

    gap = blocks_of(edge.after, BLOCK)
    rest = blocks_of(rows - edge.before + BLOCK - 1, BLOCK)
    all_blocks = rows // BLOCK
    own_blocks = jnp.where(edge.lower, rest, 0), jnp.where(edge.lower, all_blocks, gap)
    other_blocks = jnp.where(edge.lower, 0, rest), jnp.where(edge.lower, gap, all_blocks)

    def fill_window(head, start):
        def part(block):
            return pl.ds(pl.multiple_of(block * BLOCK, BLOCK), BLOCK)

        def own_rows(which, block):
            return own[which, part(block), lanes(head)]

        def other_rows(which, block):
            packed = pl.ds(pl.multiple_of(start + block * BLOCK, TILE), BLOCK)
            return staged_in[packed, which * HEAD_DIM:(which + 1) * HEAD_DIM]

        def mixed_rows(which, block):
            position = block * BLOCK + lax.broadcasted_iota(jnp.int32, (BLOCK, HEAD_DIM), 0)
            in_own = (position >= edge.own_begin) & (position < edge.own_end)
            in_window = (position < edge.after) | (position >= rows - edge.before)
            zero = jnp.zeros((BLOCK, HEAD_DIM), jnp.bfloat16)
            return jnp.where(
                in_own,
                own_rows(which, block),
                jnp.where(in_window, other_rows(which, block), zero),
            )

        def fill(blocks, source):
            def one_block(block, carry):
                for which in range(4):
                    window[part(block), which * HEAD_DIM:(which + 1) * HEAD_DIM] = source(
                        which, block)
                return carry

            lax.fori_loop(*blocks, one_block, 0)

        fill(own_blocks, own_rows)
        fill(other_blocks, other_rows)
        fill((gap, rest), mixed_rows)

    def one_job(step, carry):
        job = jnp.where(edge.lower, step, jobs - 1 - step)
        buffer = lax.rem(job, 2)
        start = margin + job * edge.other_rows - edge.other
        fill_window(edge.job_head + job, start)

        @pl.when(step >= 2)
        def _():
            keep(job).wait()

        def store(which, part_rows, part):
            result[buffer, part_rows, which * HEAD_DIM:(which + 1) * HEAD_DIM] = part

        operands = [
            window[:, which * HEAD_DIM:(which + 1) * HEAD_DIM] for which in range(4)
        ]
        attention(*operands, lambda cols: in_image, store, CROSSING_CHUNK)
        staged_out[pl.ds(pl.multiple_of(start, TILE), rows), :] = result[buffer]
        keep(job).start()
        return carry

    @pl.when(jobs > 0)
    def _():
        stage = functools.partial(
            copy_pieces, levels, edge.level, staged_in, margin, received, in_sem, False)
        send = functools.partial(
            copy_pieces, levels, edge.level, staged_out, margin, back, out_sem, True)
        stage(START)
        load_own(START)
        load_own(WAIT)
        stage(WAIT)
        lax.fori_loop(0, jobs, one_job, 0)
        send(START)

        @pl.when(jobs >= 2)
        def _():
            keep(1).wait()

        keep(0).wait()
        send(WAIT)


def crossing_images(kind, plan, arrays, received, levels):
    rows, width = arrays[0].shape
    heads = width // HEAD_DIM
    four = 4 * HEAD_DIM
    count = len(levels)
    staged = pltpu.VMEM((rows + levels[-1] + rows, four), jnp.bfloat16)
    outs = pl.pallas_call(
        functools.partial(crossing_kernel, levels, kind),
        in_specs=[SCALARS] + [ANYWHERE] * (4 + count),
        out_specs=[ANYWHERE] * (count + 1),
        out_shape=piece_shapes(levels)
        + [pltpu.HBM((heads, rows, four), jnp.bfloat16)],
        scratch_shapes=[
            pltpu.VMEM((4, rows, width), jnp.bfloat16),
            staged,
            staged,
            pltpu.VMEM((rows, four), jnp.bfloat16),
            pltpu.VMEM((2, rows, four), jnp.bfloat16),
            pltpu.SemaphoreType.DMA((4,)),
            pltpu.SemaphoreType.DMA((count,)),
            pltpu.SemaphoreType.DMA((count,)),
            pltpu.SemaphoreType.DMA((2,)),
        ],
        compiler_params=pltpu.CompilerParams(vmem_limit_bytes=VMEM_LIMIT),
        cost_estimate=pl.CostEstimate(
            flops=12 * rows * rows * width, bytes_accessed=16 * rows * width, transcendentals=0
        ),
        name="odd_edge_images" if kind == ODD else "even_edge_images",
    )(plan, *in_hbm(arrays), *received)
    return outs[:count], outs[count]


def overlay(whole, which, edge, first_head, heads, source):
    mixed = jnp.where(edge.lower, edge.first_block, edge.last_block - 1)
    full = jnp.where(edge.lower, edge.first_block + 1, edge.first_block)

    def one_head(slot, carry):
        place = lanes(first_head + slot)

        def one_block(step, carry):
            first = (full + step) * BLOCK
            part = pl.ds(pl.multiple_of(first, BLOCK), BLOCK)
            whole[which, part, place] = source(slot, first)
            return carry

        first = mixed * BLOCK
        part = pl.ds(pl.multiple_of(first, BLOCK), BLOCK)
        position = first + lax.broadcasted_iota(jnp.int32, (BLOCK, HEAD_DIM), 0)
        whole[which, part, place] = jnp.where(
            (position >= edge.own_begin) & (position < edge.own_end),
            source(slot, first),
            whole[which, part, place],
        )
        return lax.fori_loop(0, edge.last_block - edge.first_block - 1, one_block, carry)

    lax.fori_loop(0, heads, one_head, 0)


def returned_source(edge, staged, columns):
    def source(slot, first):
        start = BLOCK + slot * edge.own_rows + first - edge.own
        return staged[pl.ds(pl.multiple_of(start, TILE), BLOCK), columns]

    return source


def keep_kernel(plan, kept_odd, kept_even, *rest):
    local, outs = rest[:4], rest[4:8]
    whole, held, whole_sem, held_sem, out_sem = rest[8:]
    rows, width = local[0].shape
    heads = width // HEAD_DIM
    kept = (kept_odd, kept_even)
    edges = [Edge(plan, kind, rows) for kind in (ODD, EVEN)]

    def parts(action):
        for kind in (ODD, EVEN):
            edge = edges[kind]
            part = tiles(edge.own, edge.own_rows)
            for slot in range(heads):
                @pl.when(slot < edge.jobs)
                def _():
                    action(pltpu.make_async_copy(
                        kept[kind].at[slot, part], held.at[kind, slot, part],
                        held_sem.at[kind, slot]))

    loads = [
        pltpu.make_async_copy(local[which], whole.at[which], whole_sem.at[which])
        for which in range(4)
    ]
    saves = [
        pltpu.make_async_copy(whole.at[which], outs[which], out_sem.at[which])
        for which in range(4)
    ]
    parts(START)
    for copy in loads:
        copy.start()
    parts(WAIT)
    for which in range(4):
        columns = slice(which * HEAD_DIM, (which + 1) * HEAD_DIM)
        loads[which].wait()
        for kind in (ODD, EVEN):
            overlay(
                whole, which, edges[kind], edges[kind].job_head, edges[kind].jobs,
                lambda slot, first: held[
                    kind, slot, pl.ds(pl.multiple_of(first, BLOCK), BLOCK), columns])
        saves[which].start()
    for copy in saves:
        copy.wait()


def merge_kept(plan, kept_odd, kept_even, local):
    rows, width = local[0].shape
    heads = width // HEAD_DIM
    return pl.pallas_call(
        keep_kernel,
        in_specs=[SCALARS] + [ANYWHERE] * 6,
        out_specs=[ANYWHERE] * 4,
        out_shape=[pltpu.HBM((rows, width), jnp.bfloat16)] * 4,
        scratch_shapes=[
            pltpu.VMEM((4, rows, width), jnp.bfloat16),
            pltpu.VMEM((2, heads, rows, 4 * HEAD_DIM), jnp.bfloat16),
            pltpu.SemaphoreType.DMA((4,)),
            pltpu.SemaphoreType.DMA((2, heads)),
            pltpu.SemaphoreType.DMA((4,)),
        ],
        compiler_params=pltpu.CompilerParams(vmem_limit_bytes=VMEM_LIMIT),
        cost_estimate=SCHEDULED_LAST,
        name="merge_kept",
    )(plan, *in_hbm([kept_odd, kept_even, *local]))


def return_kernel(levels, plan, *rest):
    counts = [len(levels[ODD]), len(levels[EVEN])]
    total = sum(counts)
    returned = rest[:counts[ODD]], rest[counts[ODD]:total]
    outs = rest[total + 4:total + 8]
    whole, odd_staged, even_staged, whole_sem, odd_sem, even_sem = rest[total + 8:]
    staged = odd_staged, even_staged
    rows = whole.shape[1]
    edges = [Edge(plan, kind, rows) for kind in (ODD, EVEN)]
    stages = [
        functools.partial(
            copy_pieces, levels[kind], edges[kind].level, staged[kind], BLOCK, returned[kind],
            sem, False)
        for kind, sem in ((ODD, odd_sem), (EVEN, even_sem))
    ]

    ends = []
    for edge, other in (edges, edges[::-1]):
        meets = jnp.logical_not(edge.lower) & (other.sent > 0)
        ends.append(jnp.where(
            meets, jnp.minimum(edge.last_block, other.first_block), edge.last_block))

    def move(kind, which, out, action):
        first, last = edges[kind].first_block, ends[kind]

        @pl.when((edges[kind].sent > 0) & (last > first))
        def _():
            part = pl.ds(
                pl.multiple_of(first * BLOCK, BLOCK), pl.multiple_of((last - first) * BLOCK, BLOCK))
            inside, outside = whole.at[which, part], outs[which].at[part]
            source, target = (inside, outside) if out else (outside, inside)
            action(pltpu.make_async_copy(source, target, whole_sem.at[kind, which]))

    for stage in stages:
        stage(START)
    for which in range(4):
        for kind in (ODD, EVEN):
            move(kind, which, False, START)
    for stage in stages:
        stage(WAIT)
    for which in range(4):
        columns = slice(which * HEAD_DIM, (which + 1) * HEAD_DIM)
        for kind in (ODD, EVEN):
            move(kind, which, False, WAIT)
        for kind in (ODD, EVEN):
            edge = edges[kind]
            overlay(whole, which, edge, edge.sent_head, edge.sent,
                    returned_source(edge, staged[kind], columns))
        for kind in (ODD, EVEN):
            move(kind, which, True, START)
    for which in range(4):
        for kind in (ODD, EVEN):
            move(kind, which, True, WAIT)


def merge_returned(plan, odd, even, outs, levels):
    rows, width = outs[0].shape
    counts = [len(levels[ODD]), len(levels[EVEN])]
    return pl.pallas_call(
        functools.partial(return_kernel, levels),
        in_specs=[SCALARS] + [ANYWHERE] * (sum(counts) + 4),
        out_specs=[ANYWHERE] * 4,
        out_shape=[pltpu.HBM((rows, width), jnp.bfloat16)] * 4,
        input_output_aliases={1 + sum(counts) + which: which for which in range(4)},
        scratch_shapes=[
            pltpu.VMEM((4, rows, width), jnp.bfloat16),
            pltpu.VMEM((levels[ODD][-1] + 2 * BLOCK, 4 * HEAD_DIM), jnp.bfloat16),
            pltpu.VMEM((levels[EVEN][-1] + 2 * BLOCK, 4 * HEAD_DIM), jnp.bfloat16),
            pltpu.SemaphoreType.DMA((2, 4)),
            pltpu.SemaphoreType.DMA((counts[ODD],)),
            pltpu.SemaphoreType.DMA((counts[EVEN],)),
        ],
        compiler_params=pltpu.CompilerParams(vmem_limit_bytes=VMEM_LIMIT),
        name="merge_returned",
    )(plan, *odd, *even, *in_hbm(outs))


def swapped(value, kind):
    first = 0 if kind == ODD else 1
    pairs = [(block, block + 1) for block in range(first, lax.axis_size("dp") - 1, 2)]
    return lax.ppermute(value, "dp", pairs + [(after, before) for before, after in pairs])


def swap_further(choices, odd, even):
    counts = [len(odd), len(even)]
    if not sum(counts):
        return [], []
    pairs = [(first, second) for first in range(counts[0] + 1) for second in range(counts[1] + 1)]

    def send(used, odd, even):
        return tuple(
            [
                swapped(array, kind) if number == used[kind] else array
                for number, array in enumerate(arrays, start=1)
            ]
            for kind, arrays in ((ODD, odd), (EVEN, even))
        )

    index = 0
    for choice, count in zip(choices, counts):
        if count:
            index = index * (count + 1) + choice[0]
    branches = [functools.partial(send, pair) for pair in pairs]
    return lax.switch(index, branches, list(odd), list(even))


def body(queries, keys, values, out_grad, lengths):
    rows, width = queries.shape
    arrays = (queries, keys, values, out_grad)
    levels = [size_levels(kind, rows, width // HEAD_DIM) for kind in (ODD, EVEN)]
    plan, choices, even = pack_even(lengths, arrays, levels, lax.axis_size("dp"))
    even_first = swapped(even[0], EVEN)
    odd = pack_odd(plan, arrays, levels[ODD])
    odd_first = swapped(odd[0], ODD)
    heads = width // HEAD_DIM
    local = local_attention(lengths, arrays, 0, heads // 2)
    choices, local = lax.optimization_barrier((choices, local))
    _, more = swap_further(choices, [], even[1:])
    back_even, kept_even = crossing_images(EVEN, plan, arrays, [even_first, *more], levels[EVEN])
    choices, kept_even = lax.optimization_barrier((choices, kept_even))
    more, _ = swap_further(choices, odd[1:], [])
    received = [odd_first, *more]
    first, received = lax.optimization_barrier((back_even[0], received))
    even_first = swapped(first, EVEN)
    back_odd, kept_odd = crossing_images(ODD, plan, arrays, received, levels[ODD])
    odd_first = swapped(back_odd[0], ODD)
    kept_odd, local = lax.optimization_barrier((kept_odd, local))
    local = local_attention(lengths, arrays, heads // 2, heads, local)
    outs = merge_kept(plan, kept_odd, kept_even, local)
    even_first, choices, outs = lax.optimization_barrier((even_first, choices, outs))
    more_odd, more_even = swap_further(choices, back_odd[1:], back_even[1:])
    return tuple(merge_returned(
        plan, [odd_first, *more_odd], [even_first, *more_even], outs, levels))


def solution(mesh):
    in_specs = (P("dp", "tensor"), P("dp", "tensor"), P("dp", "tensor"), P("dp", "tensor"), P())
    out_specs = (P("dp", "tensor"), P("dp", "tensor"), P("dp", "tensor"), P("dp", "tensor"))
    return jax.shard_map(body, mesh=mesh, in_specs=in_specs, out_specs=out_specs, check_vma=False)
```

```python
import functools
import math

import jax
import jax.numpy as jnp
from jax import lax
from jax.experimental import pallas as pl
from jax.experimental.pallas import tpu as pltpu
from jax.sharding import PartitionSpec as P

HEAD_DIM = 128
TILE = 16
BLOCK = 64
LOCAL_CHUNK = 256
CROSSING_CHUNK = 256
FACTOR = 1.0 / math.sqrt(HEAD_DIM)
LOG2E = 1.4426950408889634
VMEM_LIMIT = 32 * 1024 * 1024
PACK_VMEM_LIMIT = 60 * 1024 * 1024

SCHEDULED_LAST = pl.CostEstimate(flops=1, bytes_accessed=1, transcendentals=0)

FIELDS = 8
BEFORE, AFTER, LOWER, JOBS, JOB_HEAD, SENT, SENT_HEAD, LEVEL = range(FIELDS)
ODD, EVEN = 0, 1

LEVEL_UNITS = ((9, 10, 11, 12, 13), (9, 10, 11, 12, 13))


def round_up(value):
    return (value + (TILE - 1)) & -TILE


def blocks_of(value, size):
    if size & (size - 1):
        return value // size
    return lax.shift_right_logical(value, jnp.int32(size.bit_length() - 1))


def worst_case_rows(rows, heads):
    worst = 0
    for before in range(TILE, rows + 1, TILE):
        for after in range(TILE, rows + TILE - before + 1, TILE):
            needed = min(max(after * low, before * (heads - low)) for low in range(heads + 1))
            worst = max(worst, needed)
    return worst


def size_levels(kind, rows, heads):
    unit = rows * heads // 48
    most = worst_case_rows(rows, heads)
    below = sorted(int(level * unit) for level in LEVEL_UNITS[kind] if level * unit < most)
    return tuple(below) + (most,)


def find_crossings(rows, blocks, lengths, before_edge, after_edge):
    def clear(edge, carry):
        before_edge[edge] = 0
        after_edge[edge] = 0
        return carry

    lax.fori_loop(0, blocks + 1, clear, 0)

    def place(image, start):
        end = start + lengths[image]
        edge = blocks_of(end - 1, rows)

        @pl.when(edge > blocks_of(start, rows))
        def _():
            before_edge[edge] = edge * rows - start
            after_edge[edge] = end - edge * rows

        return end

    lax.fori_loop(0, lengths.shape[0], place, 0)


def own_edge(kind, before_edge, after_edge):
    block = lax.axis_index("dp")
    lower = lax.rem(block, 2) == (0 if kind == ODD else 1)
    edge = jnp.where(lower, block + 1, block)
    return lower, before_edge[edge], after_edge[edge]


def make_plan(heads, blocks, levels, plan, choices, before_edge, after_edge):
    entry = lax.broadcasted_iota(jnp.int32, (8, 128), 1)
    for kind in (ODD, EVEN):
        limit = jnp.full((8, 128), levels[kind][-1], jnp.int32)
        for number, level in enumerate(levels[kind]):
            limit = jnp.where(entry == number, level, limit)

        def check(number, fits):
            edge = 2 * number + (1 if kind == ODD else 2)
            after = round_up(after_edge[edge])
            before = round_up(before_edge[edge])
            taken = jnp.zeros((8, 128), jnp.int32)
            for count in range(1, heads + 1):
                taken += jnp.where(after * count <= limit, 1, 0)
                taken += jnp.where(before * count <= limit, 1, 0)
            return jnp.minimum(fits, jnp.where(taken >= heads, 1, 0))

        last = len(levels[kind]) - 1
        chosen = jnp.int32(last)
        if last:
            edges = (blocks - (0 if kind == ODD else 1)) // 2
            fits = lax.fori_loop(0, edges, check, jnp.ones((8, 128), jnp.int32))
            chosen = jnp.min(jnp.where(fits == 1, entry, last))
        most_rows = jnp.int32(levels[kind][-1])
        for number, level in enumerate(levels[kind][:-1]):
            most_rows = jnp.where(chosen == number, level, most_rows)

        lower, before, after = own_edge(kind, before_edge, after_edge)
        most = jnp.int32(0)
        least = jnp.int32(heads)
        for count in range(1, heads + 1):
            most += jnp.where(round_up(after) * count <= most_rows, 1, 0)
            least -= jnp.where(round_up(before) * count <= most_rows, 1, 0)
        low = jnp.clip(jnp.int32(heads // 2), least, most)
        crossed = before > 0
        base = kind * FIELDS
        plan[base + BEFORE] = before
        plan[base + AFTER] = after
        plan[base + LOWER] = lower.astype(jnp.int32)
        plan[base + JOBS] = jnp.where(crossed, jnp.where(lower, low, heads - low), 0)
        plan[base + JOB_HEAD] = jnp.where(lower, 0, low)
        plan[base + SENT] = jnp.where(crossed, jnp.where(lower, heads - low, low), 0)
        plan[base + SENT_HEAD] = jnp.where(lower, low, 0)
        plan[base + LEVEL] = chosen
        choices[kind][0] = chosen


class Edge:
    def __init__(self, plan, kind, rows):
        read = lambda field: plan[kind * FIELDS + field]
        self.lower = read(LOWER) == 1
        self.jobs, self.job_head = read(JOBS), read(JOB_HEAD)
        self.sent, self.sent_head = read(SENT), read(SENT_HEAD)
        self.level = read(LEVEL)
        before, after = read(BEFORE), read(AFTER)
        self.before, self.after = before, after
        self.own_begin = jnp.where(self.lower, rows - before, 0)
        self.own_end = jnp.where(self.lower, rows, after)
        self.own_rows = round_up(jnp.where(self.lower, before, after))
        self.other_rows = round_up(jnp.where(self.lower, after, before))
        self.own = jnp.where(self.lower, rows - self.own_rows, 0)
        self.other = jnp.where(self.lower, 0, rows - self.other_rows)
        self.first_block = blocks_of(self.own_begin, BLOCK)
        self.last_block = blocks_of(self.own_end + BLOCK - 1, BLOCK)


def tiles(start, size):
    return pl.ds(pl.multiple_of(start, TILE), pl.multiple_of(size, TILE))


def lanes(head):
    return pl.ds(pl.multiple_of(head * HEAD_DIM, HEAD_DIM), HEAD_DIM)


def attention(query, key, value, grad, mask_columns, store, chunk):
    count = query.shape[0]
    key_t = key.T
    value_t = value.T
    grad_t = grad.T
    across = (((1,), (1,)), ((), ()))
    chunks = [slice(first, first + chunk) for first in range(0, count, chunk)]
    scores = [
        lax.dot_general(key, query[cols], across, preferred_element_type=jnp.float32)
        for cols in chunks
    ]
    grad_probs = [
        lax.dot_general(value, grad[cols], across, preferred_element_type=jnp.float32)
        for cols in chunks
    ]
    probs_low = []
    grad_scores = []
    for number, cols in enumerate(chunks):
        masked = jnp.where(mask_columns(cols), scores[number], -1e30)
        top = jnp.max(masked, axis=0, keepdims=True)
        weights = jnp.exp2((masked - top) * (FACTOR * LOG2E))
        total = jnp.sum(weights, axis=0, keepdims=True)
        probs = weights * (1.0 / total)
        probs_low.append(probs.astype(jnp.bfloat16))
        result_t = jnp.dot(value_t, probs_low[-1], preferred_element_type=jnp.float32)
        result_t = result_t.astype(jnp.bfloat16)
        centre = jnp.sum(
            grad_t[:, cols].astype(jnp.float32) * result_t.astype(jnp.float32),
            axis=0,
            keepdims=True,
        )
        grad_scores.append((probs * (grad_probs[number] - centre)).astype(jnp.bfloat16))
        grad_query_t = jnp.dot(key_t, grad_scores[-1], preferred_element_type=jnp.float32) * FACTOR
        store(0, cols, result_t.T)
        store(1, cols, grad_query_t.astype(jnp.bfloat16).T)
    probs_low = jnp.concatenate(probs_low, axis=1)
    grad_scores = jnp.concatenate(grad_scores, axis=1)
    grad_value = jnp.dot(probs_low, grad, preferred_element_type=jnp.float32)
    store(3, slice(None), grad_value.astype(jnp.bfloat16))
    grad_key = jnp.dot(grad_scores, query, preferred_element_type=jnp.float32)
    store(2, slice(None), (grad_key * FACTOR).astype(jnp.bfloat16))


def find_images(lengths, image_rows):
    count = image_rows.shape[1]
    position = lax.axis_index("dp") * count + lax.broadcasted_iota(jnp.int32, (8, count), 1)

    def place(image, carry):
        start, begin = carry
        return start + lengths[image], jnp.where(position >= start, start, begin)

    first = (jnp.int32(0), jnp.zeros((8, count), jnp.int32))
    _, begin = lax.fori_loop(0, lengths.shape[0], place, first)
    image_rows[...] = begin.astype(jnp.float32)


def local_head(operands, image_rows, outs):
    image_col = image_rows[...].T[:, :1]

    def store(which, rows, part):
        outs[which][rows, :] = part

    attention(
        *(operand[...] for operand in operands),
        lambda cols: image_col == image_rows[:1, cols],
        store,
        LOCAL_CHUNK,
    )


def local_kernel(lengths, *rest):
    operands, outs, image_rows = rest[:4], rest[4:8], rest[8]

    @pl.when(pl.program_id(0) == 0)
    def _():
        find_images(lengths, image_rows)

    local_head(operands, image_rows, outs)


def local_attention(lengths, arrays, heads):
    rows, width = arrays[0].shape
    block = pl.BlockSpec((rows, HEAD_DIM), lambda head: (0, head))
    return pl.pallas_call(
        local_kernel,
        grid=(heads,),
        in_specs=[SCALARS] + [block] * 4,
        out_specs=[block] * 4,
        out_shape=[pltpu.HBM((rows, width), jnp.bfloat16)] * 4,
        scratch_shapes=[pltpu.VMEM((8, rows), jnp.float32)],
        compiler_params=pltpu.CompilerParams(vmem_limit_bytes=VMEM_LIMIT),
        cost_estimate=SCHEDULED_LAST,
        name="local_images",
    )(lengths, *in_hbm(arrays))


START = lambda copy: copy.start()
WAIT = lambda copy: copy.wait()
ANYWHERE = pl.BlockSpec(memory_space=pl.ANY)
SCALARS = pl.BlockSpec(memory_space=pltpu.SMEM)


def in_hbm(arrays):
    return [pltpu.with_memory_space_constraint(array, pltpu.HBM) for array in arrays]


def pieces(levels):
    return [(0, levels[0])] + [(levels[0], level - levels[0]) for level in levels[1:]]


def piece_shapes(levels):
    return [pltpu.HBM((size, 4 * HEAD_DIM), jnp.bfloat16) for _, size in pieces(levels)]


def copy_pieces(levels, level, staged, offset, arrays, sems, out, action, first=0):
    for number, (start, size) in enumerate(pieces(levels)):
        if number < first:
            continue
        inside = staged.at[pl.ds(offset + start, size)]
        outside = arrays[number]
        source, target = (inside, outside) if out else (outside, inside)

        @pl.when(True if number == 0 else level == number)
        def _():
            action(pltpu.make_async_copy(source, target, sems.at[number]))


def gather(edge, held, staged):
    steps = blocks_of(edge.own_rows + BLOCK - 1, BLOCK)

    def one_head(slot, carry):
        def one_block(step, carry):
            source = pl.ds(pl.multiple_of(edge.own + step * BLOCK, TILE), BLOCK)
            target = pl.ds(pl.multiple_of(slot * edge.own_rows + step * BLOCK, TILE), BLOCK)
            for which in range(4):
                staged[target, which * HEAD_DIM:(which + 1) * HEAD_DIM] = held[
                    which, source, lanes(edge.sent_head + slot)]
            return carry

        return lax.fori_loop(0, steps, one_block, carry)

    lax.fori_loop(0, edge.sent, one_head, 0)


def pack_even_kernel(levels, blocks, lengths, query, key, value, grad, *rest):
    count = len(levels[EVEN])
    plan, choices, outs = rest[0], rest[1:3], rest[3:3 + count]
    before_edge, after_edge, held, staged, load_sem, out_sem = rest[3 + count:]
    rows, width = query.shape
    find_crossings(rows, blocks, lengths, before_edge, after_edge)
    lower, before, after = own_edge(EVEN, before_edge, after_edge)
    own_rows = round_up(jnp.where(lower, before, after))
    part = tiles(jnp.where(lower, rows - own_rows, 0), own_rows)
    loads = [
        pltpu.make_async_copy(array.at[part], held.at[which, part], load_sem.at[which])
        for which, array in enumerate((query, key, value, grad))
    ]

    @pl.when(before > 0)
    def _():
        for copy in loads:
            copy.start()

    make_plan(width // HEAD_DIM, blocks, levels, plan, choices, before_edge, after_edge)

    @pl.when(before > 0)
    def _():
        for copy in loads:
            copy.wait()
        edge = Edge(plan, EVEN, rows)
        gather(edge, held, staged)
        send = functools.partial(
            copy_pieces, levels[EVEN], edge.level, staged, 0, outs, out_sem, True, first=1)
        send(START)
        outs[0][...] = staged[:outs[0].shape[0], :]
        send(WAIT)


def pack_odd_kernel(levels, plan, query, key, value, grad, *rest):
    count = len(levels)
    outs = rest[:count]
    held, staged, load_sem, out_sem = rest[count:]
    rows = query.shape[0]
    edge = Edge(plan, ODD, rows)
    part = tiles(edge.own, edge.own_rows)
    loads = [
        pltpu.make_async_copy(array.at[part], held.at[which, part], load_sem.at[which])
        for which, array in enumerate((query, key, value, grad))
    ]

    @pl.when(edge.sent > 0)
    def _():
        for copy in loads:
            copy.start()
        for copy in loads:
            copy.wait()
        gather(edge, held, staged)
        move = functools.partial(
            copy_pieces, levels, edge.level, staged, 0, outs, out_sem, True)
        move(START)
        move(WAIT)


def pack_scratch(rows, width, levels):
    return [
        pltpu.VMEM((4, rows + BLOCK, width), jnp.bfloat16),
        pltpu.VMEM((levels[-1] + BLOCK, 4 * HEAD_DIM), jnp.bfloat16),
        pltpu.SemaphoreType.DMA((4,)),
        pltpu.SemaphoreType.DMA((len(levels),)),
    ]


def pack_even(lengths, arrays, levels, blocks):
    rows, width = arrays[0].shape
    one = jax.ShapeDtypeStruct((1,), jnp.int32)
    plan, odd_level, even_level, *even = pl.pallas_call(
        functools.partial(pack_even_kernel, levels, blocks),
        in_specs=[SCALARS] + [ANYWHERE] * 4,
        out_specs=[SCALARS] * 3 + [pl.BlockSpec(memory_space=pltpu.VMEM)]
        + [ANYWHERE] * (len(levels[EVEN]) - 1),
        out_shape=[jax.ShapeDtypeStruct((2 * FIELDS,), jnp.int32), one, one]
        + [pltpu.VMEM((levels[EVEN][0], 4 * HEAD_DIM), jnp.bfloat16)]
        + piece_shapes(levels[EVEN])[1:],
        scratch_shapes=[
            pltpu.SMEM((blocks + 2,), jnp.int32),
            pltpu.SMEM((blocks + 2,), jnp.int32),
        ] + pack_scratch(rows, width, levels[EVEN]),
        compiler_params=pltpu.CompilerParams(vmem_limit_bytes=PACK_VMEM_LIMIT),
        name="pack_even",
    )(lengths, *in_hbm(arrays))
    return plan, (odd_level, even_level), even


def pack_odd(plan, arrays, levels):
    rows, width = arrays[0].shape
    return pl.pallas_call(
        functools.partial(pack_odd_kernel, levels),
        in_specs=[SCALARS] + [ANYWHERE] * 4,
        out_specs=[ANYWHERE] * len(levels),
        out_shape=piece_shapes(levels),
        scratch_shapes=pack_scratch(rows, width, levels),
        compiler_params=pltpu.CompilerParams(vmem_limit_bytes=VMEM_LIMIT),
        name="pack_odd",
    )(plan, *in_hbm(arrays))


def crossing_kernel(levels, kind, plan, query, key, value, grad, *rest):
    count = len(levels)
    received, back, kept = rest[:count], rest[count:2 * count], rest[2 * count]
    own, staged_in, staged_out, result, own_sem, in_sem, out_sem, kept_sem = rest[2 * count + 1:]
    rows, width = query.shape
    edge = Edge(plan, kind, rows)
    jobs = edge.jobs
    own_part = tiles(edge.own, edge.own_rows)
    margin = rows

    def load_own(action):
        for which, array in enumerate((query, key, value, grad)):
            action(pltpu.make_async_copy(
                array.at[own_part], own.at[which, own_part], own_sem.at[which]))

    def keep(job):
        buffer = lax.rem(job, 2)
        return pltpu.make_async_copy(
            result.at[buffer, own_part], kept.at[job, own_part], kept_sem.at[buffer])

    position = lax.broadcasted_iota(jnp.int32, (rows, HEAD_DIM), 0)
    in_own = (position >= edge.own_begin) & (position < edge.own_end)
    key_position = lax.broadcasted_iota(jnp.int32, (rows, 1), 0)
    in_image = (key_position < edge.after) | (key_position >= rows - edge.before)
    in_window = (position < edge.after) | (position >= rows - edge.before)

    def one_job(step, carry):
        job = jnp.where(edge.lower, step, jobs - 1 - step)
        buffer = lax.rem(job, 2)
        start = margin + job * edge.other_rows - edge.other
        window = pl.ds(pl.multiple_of(start, TILE), rows)

        @pl.when(step >= 2)
        def _():
            keep(job).wait()

        zero = jnp.zeros((rows, HEAD_DIM), jnp.bfloat16)
        operands = []
        for which in range(4):
            columns = slice(which * HEAD_DIM, (which + 1) * HEAD_DIM)
            operands.append(jnp.where(
                in_own,
                own[which, :, lanes(edge.job_head + job)],
                jnp.where(in_window, staged_in[window, columns], zero),
            ))

        def store(which, part_rows, part):
            result[buffer, part_rows, which * HEAD_DIM:(which + 1) * HEAD_DIM] = part

        attention(*operands, lambda cols: in_image, store, CROSSING_CHUNK)
        staged_out[window, :] = result[buffer]
        keep(job).start()
        return carry

    @pl.when(jobs > 0)
    def _():
        stage = functools.partial(
            copy_pieces, levels, edge.level, staged_in, margin, received, in_sem, False)
        send = functools.partial(
            copy_pieces, levels, edge.level, staged_out, margin, back, out_sem, True)
        stage(START)
        load_own(START)
        load_own(WAIT)
        stage(WAIT)
        lax.fori_loop(0, jobs, one_job, 0)
        send(START)

        @pl.when(jobs >= 2)
        def _():
            keep(1).wait()

        keep(0).wait()
        send(WAIT)


def crossing_images(kind, plan, arrays, received, levels):
    rows, width = arrays[0].shape
    heads = width // HEAD_DIM
    four = 4 * HEAD_DIM
    count = len(levels)
    staged = pltpu.VMEM((rows + levels[-1] + rows, four), jnp.bfloat16)
    outs = pl.pallas_call(
        functools.partial(crossing_kernel, levels, kind),
        in_specs=[SCALARS] + [ANYWHERE] * (4 + count),
        out_specs=[ANYWHERE] * (count + 1),
        out_shape=piece_shapes(levels)
        + [pltpu.HBM((heads, rows, four), jnp.bfloat16)],
        scratch_shapes=[
            pltpu.VMEM((4, rows, width), jnp.bfloat16),
            staged,
            staged,
            pltpu.VMEM((2, rows, four), jnp.bfloat16),
            pltpu.SemaphoreType.DMA((4,)),
            pltpu.SemaphoreType.DMA((count,)),
            pltpu.SemaphoreType.DMA((count,)),
            pltpu.SemaphoreType.DMA((2,)),
        ],
        compiler_params=pltpu.CompilerParams(vmem_limit_bytes=VMEM_LIMIT),
        cost_estimate=pl.CostEstimate(
            flops=12 * rows * rows * width, bytes_accessed=16 * rows * width, transcendentals=0
        ),
        name="odd_edge_images" if kind == ODD else "even_edge_images",
    )(plan, *in_hbm(arrays), *received)
    return outs[:count], outs[count]


def overlay(whole, which, edge, first_head, heads, source):
    mixed = jnp.where(edge.lower, edge.first_block, edge.last_block - 1)
    full = jnp.where(edge.lower, edge.first_block + 1, edge.first_block)

    def one_head(slot, carry):
        place = lanes(first_head + slot)

        def one_block(step, carry):
            first = (full + step) * BLOCK
            part = pl.ds(pl.multiple_of(first, BLOCK), BLOCK)
            whole[which, part, place] = source(slot, first)
            return carry

        first = mixed * BLOCK
        part = pl.ds(pl.multiple_of(first, BLOCK), BLOCK)
        position = first + lax.broadcasted_iota(jnp.int32, (BLOCK, HEAD_DIM), 0)
        whole[which, part, place] = jnp.where(
            (position >= edge.own_begin) & (position < edge.own_end),
            source(slot, first),
            whole[which, part, place],
        )
        return lax.fori_loop(0, edge.last_block - edge.first_block - 1, one_block, carry)

    lax.fori_loop(0, heads, one_head, 0)


def returned_source(edge, staged, columns):
    def source(slot, first):
        start = BLOCK + slot * edge.own_rows + first - edge.own
        return staged[pl.ds(pl.multiple_of(start, TILE), BLOCK), columns]

    return source


def rest_kernel(done, plan, lengths, *rest):
    operands, before, kept = rest[:4], rest[4:8], rest[8:10]
    outs = rest[10:14]
    image_rows, held, held_sem = rest[14:]
    head = pl.program_id(0)
    rows = image_rows.shape[1]
    edges = [Edge(plan, kind, rows) for kind in (ODD, EVEN)]

    def kept_copy(kind, slot):
        part = tiles(edges[kind].own, edges[kind].own_rows)
        return pltpu.make_async_copy(
            kept[kind].at[slot, part], held.at[kind, slot, part], held_sem.at[kind, slot])

    @pl.when(head == 0)
    def _():
        for kind in (ODD, EVEN):
            def start(slot, carry):
                kept_copy(kind, slot).start()
                return carry

            lax.fori_loop(0, edges[kind].jobs, start, 0)

        find_images(lengths, image_rows)

    @pl.when(head < done)
    def _():
        for old, out in zip(before, outs):
            out[...] = old[...]

    @pl.when(head >= done)
    def _():
        local_head(operands, image_rows, outs)

    for kind in (ODD, EVEN):
        edge = edges[kind]
        slot = head - edge.job_head

        @pl.when((slot >= 0) & (slot < edge.jobs))
        def _():
            kept_copy(kind, slot).wait()

            def one_block(block, carry):
                first = block * BLOCK
                part = pl.ds(pl.multiple_of(first, BLOCK), BLOCK)
                position = first + lax.broadcasted_iota(jnp.int32, (BLOCK, HEAD_DIM), 0)
                wanted = (position >= edge.own_begin) & (position < edge.own_end)
                for which, out in enumerate(outs):
                    columns = slice(which * HEAD_DIM, (which + 1) * HEAD_DIM)
                    out[part, :] = jnp.where(wanted, held[kind, slot, part, columns], out[part, :])
                return carry

            lax.fori_loop(edge.first_block, edge.last_block, one_block, 0)


def rest_of_images(plan, lengths, arrays, done, local, kept_odd, kept_even):
    rows, width = arrays[0].shape
    heads = width // HEAD_DIM
    todo = pl.BlockSpec((rows, HEAD_DIM), lambda head: (0, jnp.maximum(head, done)))
    old = pl.BlockSpec((rows, HEAD_DIM), lambda head: (0, jnp.minimum(head, done - 1)))
    return pl.pallas_call(
        functools.partial(rest_kernel, done),
        grid=(heads,),
        in_specs=[SCALARS] * 2 + [todo] * 4 + [old] * 4 + [ANYWHERE] * 2,
        out_specs=[pl.BlockSpec((rows, HEAD_DIM), lambda head: (0, head))] * 4,
        out_shape=[pltpu.HBM((rows, width), jnp.bfloat16)] * 4,
        scratch_shapes=[
            pltpu.VMEM((8, rows), jnp.float32),
            pltpu.VMEM((2, heads, rows, 4 * HEAD_DIM), jnp.bfloat16),
            pltpu.SemaphoreType.DMA((2, heads)),
        ],
        compiler_params=pltpu.CompilerParams(vmem_limit_bytes=VMEM_LIMIT),
        cost_estimate=SCHEDULED_LAST,
        name="rest_of_images",
    )(plan, lengths, *in_hbm([*arrays, *local, kept_odd, kept_even]))


def return_kernel(levels, plan, *rest):
    counts = [len(levels[ODD]), len(levels[EVEN])]
    total = sum(counts)
    returned = rest[:counts[ODD]], rest[counts[ODD]:total]
    outs = rest[total + 4:total + 8]
    whole, odd_staged, even_staged, whole_sem, odd_sem, even_sem = rest[total + 8:]
    staged = odd_staged, even_staged
    rows = whole.shape[1]
    edges = [Edge(plan, kind, rows) for kind in (ODD, EVEN)]
    stages = [
        functools.partial(
            copy_pieces, levels[kind], edges[kind].level, staged[kind], BLOCK, returned[kind],
            sem, False)
        for kind, sem in ((ODD, odd_sem), (EVEN, even_sem))
    ]

    ends = []
    for edge, other in (edges, edges[::-1]):
        meets = jnp.logical_not(edge.lower) & (other.sent > 0)
        ends.append(jnp.where(
            meets, jnp.minimum(edge.last_block, other.first_block), edge.last_block))

    def move(kind, which, out, action):
        first, last = edges[kind].first_block, ends[kind]

        @pl.when((edges[kind].sent > 0) & (last > first))
        def _():
            part = pl.ds(
                pl.multiple_of(first * BLOCK, BLOCK), pl.multiple_of((last - first) * BLOCK, BLOCK))
            inside, outside = whole.at[which, part], outs[which].at[part]
            source, target = (inside, outside) if out else (outside, inside)
            action(pltpu.make_async_copy(source, target, whole_sem.at[kind, which]))

    for stage in stages:
        stage(START)
    for which in range(4):
        for kind in (ODD, EVEN):
            move(kind, which, False, START)
    for stage in stages:
        stage(WAIT)
    for which in range(4):
        columns = slice(which * HEAD_DIM, (which + 1) * HEAD_DIM)
        for kind in (ODD, EVEN):
            move(kind, which, False, WAIT)
        for kind in (ODD, EVEN):
            edge = edges[kind]
            overlay(whole, which, edge, edge.sent_head, edge.sent,
                    returned_source(edge, staged[kind], columns))
        for kind in (ODD, EVEN):
            move(kind, which, True, START)
    for which in range(4):
        for kind in (ODD, EVEN):
            move(kind, which, True, WAIT)


def merge_returned(plan, odd, even, outs, levels):
    rows, width = outs[0].shape
    counts = [len(levels[ODD]), len(levels[EVEN])]
    return pl.pallas_call(
        functools.partial(return_kernel, levels),
        in_specs=[SCALARS] + [ANYWHERE] * (sum(counts) + 4),
        out_specs=[ANYWHERE] * 4,
        out_shape=[pltpu.HBM((rows, width), jnp.bfloat16)] * 4,
        input_output_aliases={1 + sum(counts) + which: which for which in range(4)},
        scratch_shapes=[
            pltpu.VMEM((4, rows, width), jnp.bfloat16),
            pltpu.VMEM((levels[ODD][-1] + 2 * BLOCK, 4 * HEAD_DIM), jnp.bfloat16),
            pltpu.VMEM((levels[EVEN][-1] + 2 * BLOCK, 4 * HEAD_DIM), jnp.bfloat16),
            pltpu.SemaphoreType.DMA((2, 4)),
            pltpu.SemaphoreType.DMA((counts[ODD],)),
            pltpu.SemaphoreType.DMA((counts[EVEN],)),
        ],
        compiler_params=pltpu.CompilerParams(vmem_limit_bytes=VMEM_LIMIT),
        name="merge_returned",
    )(plan, *odd, *even, *in_hbm(outs))


def swapped(value, kind):
    first = 0 if kind == ODD else 1
    pairs = [(block, block + 1) for block in range(first, lax.axis_size("dp") - 1, 2)]
    return lax.ppermute(value, "dp", pairs + [(after, before) for before, after in pairs])


def swap_further(choices, odd, even):
    counts = [len(odd), len(even)]
    if not sum(counts):
        return [], []
    pairs = [(first, second) for first in range(counts[0] + 1) for second in range(counts[1] + 1)]

    def send(used, odd, even):
        return tuple(
            [
                swapped(array, kind) if number == used[kind] else array
                for number, array in enumerate(arrays, start=1)
            ]
            for kind, arrays in ((ODD, odd), (EVEN, even))
        )

    index = 0
    for choice, count in zip(choices, counts):
        if count:
            index = index * (count + 1) + choice[0]
    branches = [functools.partial(send, pair) for pair in pairs]
    return lax.switch(index, branches, list(odd), list(even))


def body(queries, keys, values, out_grad, lengths):
    rows, width = queries.shape
    arrays = (queries, keys, values, out_grad)
    levels = [size_levels(kind, rows, width // HEAD_DIM) for kind in (ODD, EVEN)]
    plan, choices, even = pack_even(lengths, arrays, levels, lax.axis_size("dp"))
    even_first = swapped(even[0], EVEN)
    odd = pack_odd(plan, arrays, levels[ODD])
    odd_first = swapped(odd[0], ODD)
    done = width // HEAD_DIM // 2
    local = local_attention(lengths, arrays, done)
    choices, local = lax.optimization_barrier((choices, local))
    _, more = swap_further(choices, [], even[1:])
    back_even, kept_even = crossing_images(EVEN, plan, arrays, [even_first, *more], levels[EVEN])
    choices, kept_even = lax.optimization_barrier((choices, kept_even))
    more, _ = swap_further(choices, odd[1:], [])
    received = [odd_first, *more]
    first, received = lax.optimization_barrier((back_even[0], received))
    even_first = swapped(first, EVEN)
    back_odd, kept_odd = crossing_images(ODD, plan, arrays, received, levels[ODD])
    odd_first = swapped(back_odd[0], ODD)
    kept_odd, local = lax.optimization_barrier((kept_odd, local))
    outs = rest_of_images(plan, lengths, arrays, done, local, kept_odd, kept_even)
    even_first, choices, outs = lax.optimization_barrier((even_first, choices, outs))
    more_odd, more_even = swap_further(choices, back_odd[1:], back_even[1:])
    return tuple(merge_returned(
        plan, [odd_first, *more_odd], [even_first, *more_even], outs, levels))


def solution(mesh):
    in_specs = (P("dp", "tensor"), P("dp", "tensor"), P("dp", "tensor"), P("dp", "tensor"), P())
    out_specs = (P("dp", "tensor"), P("dp", "tensor"), P("dp", "tensor"), P("dp", "tensor"))
    return jax.shard_map(body, mesh=mesh, in_specs=in_specs, out_specs=out_specs, check_vma=False)
```

```python
import functools
import math

import jax
import jax.numpy as jnp
from jax import lax
from jax.experimental import pallas as pl
from jax.experimental.pallas import tpu as pltpu
from jax.sharding import PartitionSpec as P

HEAD_DIM = 128
TILE = 16
BLOCK = 64
LOCAL_CHUNK = 256
CROSSING_CHUNK = 256
FACTOR = 1.0 / math.sqrt(HEAD_DIM)
LOG2E = 1.4426950408889634
VMEM_LIMIT = 32 * 1024 * 1024
PACK_VMEM_LIMIT = 60 * 1024 * 1024

SCHEDULED_LAST = pl.CostEstimate(flops=1, bytes_accessed=1, transcendentals=0)

FIELDS = 8
BEFORE, AFTER, LOWER, JOBS, JOB_HEAD, SENT, SENT_HEAD, LEVEL = range(FIELDS)
ODD, EVEN = 0, 1

LEVEL_UNITS = ((9, 10, 11, 12, 13), (9, 10, 11, 12, 13))


def round_up(value):
    return (value + (TILE - 1)) & -TILE


def blocks_of(value, size):
    if size & (size - 1):
        return value // size
    return lax.shift_right_logical(value, jnp.int32(size.bit_length() - 1))


def worst_case_rows(rows, heads):
    worst = 0
    for before in range(TILE, rows + 1, TILE):
        for after in range(TILE, rows + TILE - before + 1, TILE):
            needed = min(max(after * low, before * (heads - low)) for low in range(heads + 1))
            worst = max(worst, needed)
    return worst


def size_levels(kind, rows, heads):
    unit = rows * heads // 48
    most = worst_case_rows(rows, heads)
    below = sorted(int(level * unit) for level in LEVEL_UNITS[kind] if level * unit < most)
    return tuple(below) + (most,)


def find_crossings(rows, blocks, lengths, before_edge, after_edge):
    def clear(edge, carry):
        before_edge[edge] = 0
        after_edge[edge] = 0
        return carry

    lax.fori_loop(0, blocks + 1, clear, 0)

    def place(image, start):
        end = start + lengths[image]
        edge = blocks_of(end - 1, rows)

        @pl.when(edge > blocks_of(start, rows))
        def _():
            before_edge[edge] = edge * rows - start
            after_edge[edge] = end - edge * rows

        return end

    lax.fori_loop(0, lengths.shape[0], place, 0)


def own_edge(kind, before_edge, after_edge):
    block = lax.axis_index("dp")
    lower = lax.rem(block, 2) == (0 if kind == ODD else 1)
    edge = jnp.where(lower, block + 1, block)
    return lower, before_edge[edge], after_edge[edge]


def make_plan(heads, blocks, levels, plan, choices, before_edge, after_edge):
    entry = lax.broadcasted_iota(jnp.int32, (8, 128), 1)
    for kind in (ODD, EVEN):
        limit = jnp.full((8, 128), levels[kind][-1], jnp.int32)
        for number, level in enumerate(levels[kind]):
            limit = jnp.where(entry == number, level, limit)

        def check(number, fits):
            edge = 2 * number + (1 if kind == ODD else 2)
            after = round_up(after_edge[edge])
            before = round_up(before_edge[edge])
            taken = jnp.zeros((8, 128), jnp.int32)
            for count in range(1, heads + 1):
                taken += jnp.where(after * count <= limit, 1, 0)
                taken += jnp.where(before * count <= limit, 1, 0)
            return jnp.minimum(fits, jnp.where(taken >= heads, 1, 0))

        last = len(levels[kind]) - 1
        chosen = jnp.int32(last)
        if last:
            edges = (blocks - (0 if kind == ODD else 1)) // 2
            fits = lax.fori_loop(0, edges, check, jnp.ones((8, 128), jnp.int32))
            chosen = jnp.min(jnp.where(fits == 1, entry, last))
        most_rows = jnp.int32(levels[kind][-1])
        for number, level in enumerate(levels[kind][:-1]):
            most_rows = jnp.where(chosen == number, level, most_rows)

        lower, before, after = own_edge(kind, before_edge, after_edge)
        most = jnp.int32(0)
        least = jnp.int32(heads)
        for count in range(1, heads + 1):
            most += jnp.where(round_up(after) * count <= most_rows, 1, 0)
            least -= jnp.where(round_up(before) * count <= most_rows, 1, 0)
        low = jnp.clip(jnp.int32(heads // 2), least, most)
        crossed = before > 0
        base = kind * FIELDS
        plan[base + BEFORE] = before
        plan[base + AFTER] = after
        plan[base + LOWER] = lower.astype(jnp.int32)
        plan[base + JOBS] = jnp.where(crossed, jnp.where(lower, low, heads - low), 0)
        plan[base + JOB_HEAD] = jnp.where(lower, 0, low)
        plan[base + SENT] = jnp.where(crossed, jnp.where(lower, heads - low, low), 0)
        plan[base + SENT_HEAD] = jnp.where(lower, low, 0)
        plan[base + LEVEL] = chosen
        choices[kind][0] = chosen


class Edge:
    def __init__(self, plan, kind, rows):
        read = lambda field: plan[kind * FIELDS + field]
        self.lower = read(LOWER) == 1
        self.jobs, self.job_head = read(JOBS), read(JOB_HEAD)
        self.sent, self.sent_head = read(SENT), read(SENT_HEAD)
        self.level = read(LEVEL)
        before, after = read(BEFORE), read(AFTER)
        self.before, self.after = before, after
        self.own_begin = jnp.where(self.lower, rows - before, 0)
        self.own_end = jnp.where(self.lower, rows, after)
        self.own_rows = round_up(jnp.where(self.lower, before, after))
        self.other_rows = round_up(jnp.where(self.lower, after, before))
        self.own = jnp.where(self.lower, rows - self.own_rows, 0)
        self.other = jnp.where(self.lower, 0, rows - self.other_rows)
        self.first_block = blocks_of(self.own_begin, BLOCK)
        self.last_block = blocks_of(self.own_end + BLOCK - 1, BLOCK)


def tiles(start, size):
    return pl.ds(pl.multiple_of(start, TILE), pl.multiple_of(size, TILE))


def lanes(head):
    return pl.ds(pl.multiple_of(head * HEAD_DIM, HEAD_DIM), HEAD_DIM)


def attention(query, key, value, grad, masked, store, chunk):
    count = query.shape[0]
    key_t = key.T
    value_t = value.T
    grad_t = grad.T
    across = (((1,), (1,)), ((), ()))
    chunks = [slice(first, first + chunk) for first in range(0, count, chunk)]
    scores = [
        lax.dot_general(key, query[cols], across, preferred_element_type=jnp.float32)
        for cols in chunks
    ]
    grad_probs = [
        lax.dot_general(value, grad[cols], across, preferred_element_type=jnp.float32)
        for cols in chunks
    ]
    probs_low = []
    grad_scores = []
    for number, cols in enumerate(chunks):
        seen = masked(scores[number], cols)
        top = jnp.max(seen, axis=0, keepdims=True)
        weights = jnp.exp2((seen - top) * (FACTOR * LOG2E))
        total = jnp.sum(weights, axis=0, keepdims=True)
        probs = weights * (1.0 / total)
        probs_low.append(probs.astype(jnp.bfloat16))
        result_t = jnp.dot(value_t, probs_low[-1], preferred_element_type=jnp.float32)
        result_t = result_t.astype(jnp.bfloat16)
        centre = jnp.sum(
            grad_t[:, cols].astype(jnp.float32) * result_t.astype(jnp.float32),
            axis=0,
            keepdims=True,
        )
        grad_scores.append((probs * (grad_probs[number] - centre)).astype(jnp.bfloat16))
        grad_query_t = jnp.dot(key_t, grad_scores[-1], preferred_element_type=jnp.float32) * FACTOR
        store(0, cols, result_t.T)
        store(1, cols, grad_query_t.astype(jnp.bfloat16).T)
    probs_low = jnp.concatenate(probs_low, axis=1)
    grad_scores = jnp.concatenate(grad_scores, axis=1)
    grad_value = jnp.dot(probs_low, grad, preferred_element_type=jnp.float32)
    store(3, slice(None), grad_value.astype(jnp.bfloat16))
    grad_key = jnp.dot(grad_scores, query, preferred_element_type=jnp.float32)
    store(2, slice(None), (grad_key * FACTOR).astype(jnp.bfloat16))


def repeated(columns, count):
    return jnp.concatenate([columns] * (count // columns.shape[1]), axis=1)


def find_images(lengths, image_rows, image_cols):
    count = image_rows.shape[1]
    position = lax.axis_index("dp") * count + lax.broadcasted_iota(jnp.int32, (8, count), 1)

    def place(image, carry):
        start, begin = carry
        return start + lengths[image], jnp.where(position >= start, start, begin)

    first = (jnp.int32(0), jnp.zeros((8, count), jnp.int32))
    _, begin = lax.fori_loop(0, lengths.shape[0], place, first)
    begin = begin.astype(jnp.float32)
    image_rows[...] = begin
    image_cols[...] = jnp.broadcast_to(begin.T[:, :1], image_cols.shape)


def local_head(operands, image_rows, image_cols, outs):
    def store(which, rows, part):
        outs[which][rows, :] = part

    attention(
        *(operand[...] for operand in operands),
        lambda scores, cols: jnp.where(
            repeated(image_cols[...], scores.shape[1]) == image_rows[:1, cols], scores, -1e30),
        store,
        LOCAL_CHUNK,
    )


def local_kernel(lengths, *rest):
    operands, outs = rest[:4], rest[4:8]
    image_rows, image_cols = rest[8:]

    @pl.when(pl.program_id(0) == 0)
    def _():
        find_images(lengths, image_rows, image_cols)

    local_head(operands, image_rows, image_cols, outs)


def local_attention(lengths, arrays, heads):
    rows, width = arrays[0].shape
    block = pl.BlockSpec((rows, HEAD_DIM), lambda head: (0, head))
    return pl.pallas_call(
        local_kernel,
        grid=(heads,),
        in_specs=[SCALARS] + [block] * 4,
        out_specs=[block] * 4,
        out_shape=[pltpu.HBM((rows, width), jnp.bfloat16)] * 4,
        scratch_shapes=[
            pltpu.VMEM((8, rows), jnp.float32),
            pltpu.VMEM((rows, HEAD_DIM), jnp.float32),
        ],
        compiler_params=pltpu.CompilerParams(vmem_limit_bytes=VMEM_LIMIT),
        cost_estimate=SCHEDULED_LAST,
        name="local_images",
    )(lengths, *in_hbm(arrays))


START = lambda copy: copy.start()
WAIT = lambda copy: copy.wait()
ANYWHERE = pl.BlockSpec(memory_space=pl.ANY)
SCALARS = pl.BlockSpec(memory_space=pltpu.SMEM)


def in_hbm(arrays):
    return [pltpu.with_memory_space_constraint(array, pltpu.HBM) for array in arrays]


def pieces(levels):
    return [(0, levels[0])] + [(levels[0], level - levels[0]) for level in levels[1:]]


def piece_shapes(levels):
    return [pltpu.HBM((size, 4 * HEAD_DIM), jnp.bfloat16) for _, size in pieces(levels)]


def copy_pieces(levels, level, staged, offset, arrays, sems, out, action, first=0):
    for number, (start, size) in enumerate(pieces(levels)):
        if number < first:
            continue
        inside = staged.at[pl.ds(offset + start, size)]
        outside = arrays[number]
        source, target = (inside, outside) if out else (outside, inside)

        @pl.when(True if number == 0 else level == number)
        def _():
            action(pltpu.make_async_copy(source, target, sems.at[number]))


def gather(edge, held, staged):
    steps = blocks_of(edge.own_rows + BLOCK - 1, BLOCK)

    def one_head(slot, carry):
        def one_block(step, carry):
            source = pl.ds(pl.multiple_of(edge.own + step * BLOCK, TILE), BLOCK)
            target = pl.ds(pl.multiple_of(slot * edge.own_rows + step * BLOCK, TILE), BLOCK)
            for which in range(4):
                staged[target, which * HEAD_DIM:(which + 1) * HEAD_DIM] = held[
                    which, source, lanes(edge.sent_head + slot)]
            return carry

        return lax.fori_loop(0, steps, one_block, carry)

    lax.fori_loop(0, edge.sent, one_head, 0)


def pack_even_kernel(levels, blocks, lengths, query, key, value, grad, *rest):
    count = len(levels[EVEN])
    plan, choices, outs = rest[0], rest[1:3], rest[3:3 + count]
    before_edge, after_edge, held, staged, load_sem, out_sem = rest[3 + count:]
    rows, width = query.shape
    find_crossings(rows, blocks, lengths, before_edge, after_edge)
    lower, before, after = own_edge(EVEN, before_edge, after_edge)
    own_rows = round_up(jnp.where(lower, before, after))
    part = tiles(jnp.where(lower, rows - own_rows, 0), own_rows)
    loads = [
        pltpu.make_async_copy(array.at[part], held.at[which, part], load_sem.at[which])
        for which, array in enumerate((query, key, value, grad))
    ]

    @pl.when(before > 0)
    def _():
        for copy in loads:
            copy.start()

    make_plan(width // HEAD_DIM, blocks, levels, plan, choices, before_edge, after_edge)

    @pl.when(before > 0)
    def _():
        for copy in loads:
            copy.wait()
        edge = Edge(plan, EVEN, rows)
        gather(edge, held, staged)
        send = functools.partial(
            copy_pieces, levels[EVEN], edge.level, staged, 0, outs, out_sem, True, first=1)
        send(START)
        outs[0][...] = staged[:outs[0].shape[0], :]
        send(WAIT)


def pack_odd_kernel(levels, plan, query, key, value, grad, *rest):
    count = len(levels)
    outs = rest[:count]
    held, staged, load_sem, out_sem = rest[count:]
    rows = query.shape[0]
    edge = Edge(plan, ODD, rows)
    part = tiles(edge.own, edge.own_rows)
    loads = [
        pltpu.make_async_copy(array.at[part], held.at[which, part], load_sem.at[which])
        for which, array in enumerate((query, key, value, grad))
    ]

    @pl.when(edge.sent > 0)
    def _():
        for copy in loads:
            copy.start()
        for copy in loads:
            copy.wait()
        gather(edge, held, staged)
        move = functools.partial(
            copy_pieces, levels, edge.level, staged, 0, outs, out_sem, True)
        move(START)
        move(WAIT)


def pack_scratch(rows, width, levels):
    return [
        pltpu.VMEM((4, rows + BLOCK, width), jnp.bfloat16),
        pltpu.VMEM((levels[-1] + BLOCK, 4 * HEAD_DIM), jnp.bfloat16),
        pltpu.SemaphoreType.DMA((4,)),
        pltpu.SemaphoreType.DMA((len(levels),)),
    ]


def pack_even(lengths, arrays, levels, blocks):
    rows, width = arrays[0].shape
    one = jax.ShapeDtypeStruct((1,), jnp.int32)
    plan, odd_level, even_level, *even = pl.pallas_call(
        functools.partial(pack_even_kernel, levels, blocks),
        in_specs=[SCALARS] + [ANYWHERE] * 4,
        out_specs=[SCALARS] * 3 + [pl.BlockSpec(memory_space=pltpu.VMEM)]
        + [ANYWHERE] * (len(levels[EVEN]) - 1),
        out_shape=[jax.ShapeDtypeStruct((2 * FIELDS,), jnp.int32), one, one]
        + [pltpu.VMEM((levels[EVEN][0], 4 * HEAD_DIM), jnp.bfloat16)]
        + piece_shapes(levels[EVEN])[1:],
        scratch_shapes=[
            pltpu.SMEM((blocks + 2,), jnp.int32),
            pltpu.SMEM((blocks + 2,), jnp.int32),
        ] + pack_scratch(rows, width, levels[EVEN]),
        compiler_params=pltpu.CompilerParams(vmem_limit_bytes=PACK_VMEM_LIMIT),
        name="pack_even",
    )(lengths, *in_hbm(arrays))
    return plan, (odd_level, even_level), even


def pack_odd(plan, arrays, levels):
    rows, width = arrays[0].shape
    return pl.pallas_call(
        functools.partial(pack_odd_kernel, levels),
        in_specs=[SCALARS] + [ANYWHERE] * 4,
        out_specs=[ANYWHERE] * len(levels),
        out_shape=piece_shapes(levels),
        scratch_shapes=pack_scratch(rows, width, levels),
        compiler_params=pltpu.CompilerParams(vmem_limit_bytes=VMEM_LIMIT),
        name="pack_odd",
    )(plan, *in_hbm(arrays))


def crossing_kernel(levels, kind, plan, query, key, value, grad, *rest):
    count = len(levels)
    received, back, kept = rest[:count], rest[count:2 * count], rest[2 * count]
    (own, staged_in, staged_out, window, result, unseen, own_sem, in_sem, out_sem,
     kept_sem) = rest[2 * count + 1:]
    rows, width = query.shape
    edge = Edge(plan, kind, rows)
    jobs = edge.jobs
    own_part = tiles(edge.own, edge.own_rows)
    margin = rows

    def load_own(action):
        for which, array in enumerate((query, key, value, grad)):
            action(pltpu.make_async_copy(
                array.at[own_part], own.at[which, own_part], own_sem.at[which]))

    def keep(job):
        buffer = lax.rem(job, 2)
        return pltpu.make_async_copy(
            result.at[buffer, own_part], kept.at[job, own_part], kept_sem.at[buffer])

    gap = blocks_of(edge.after, BLOCK)
    rest = blocks_of(rows - edge.before + BLOCK - 1, BLOCK)
    all_blocks = rows // BLOCK
    own_blocks = jnp.where(edge.lower, rest, 0), jnp.where(edge.lower, all_blocks, gap)
    other_blocks = jnp.where(edge.lower, 0, rest), jnp.where(edge.lower, gap, all_blocks)

    def fill_window(head, start):
        def part(block):
            return pl.ds(pl.multiple_of(block * BLOCK, BLOCK), BLOCK)

        def own_rows(which, block):
            return own[which, part(block), lanes(head)]

        def other_rows(which, block):
            packed = pl.ds(pl.multiple_of(start + block * BLOCK, TILE), BLOCK)
            return staged_in[packed, which * HEAD_DIM:(which + 1) * HEAD_DIM]

        def mixed_rows(which, block):
            position = block * BLOCK + lax.broadcasted_iota(jnp.int32, (BLOCK, HEAD_DIM), 0)
            in_own = (position >= edge.own_begin) & (position < edge.own_end)
            in_window = (position < edge.after) | (position >= rows - edge.before)
            zero = jnp.zeros((BLOCK, HEAD_DIM), jnp.bfloat16)
            return jnp.where(
                in_own,
                own_rows(which, block),
                jnp.where(in_window, other_rows(which, block), zero),
            )

        def fill(blocks, source):
            def one_block(block, carry):
                for which in range(4):
                    window[part(block), which * HEAD_DIM:(which + 1) * HEAD_DIM] = source(
                        which, block)
                return carry

            lax.fori_loop(*blocks, one_block, 0)

        fill(own_blocks, own_rows)
        fill(other_blocks, other_rows)
        fill((gap, rest), mixed_rows)

    def one_job(step, carry):
        job = jnp.where(edge.lower, step, jobs - 1 - step)
        buffer = lax.rem(job, 2)
        start = margin + job * edge.other_rows - edge.other
        fill_window(edge.job_head + job, start)

        @pl.when(step >= 2)
        def _():
            keep(job).wait()

        def store(which, part_rows, part):
            result[buffer, part_rows, which * HEAD_DIM:(which + 1) * HEAD_DIM] = part

        operands = [
            window[:, which * HEAD_DIM:(which + 1) * HEAD_DIM] for which in range(4)
        ]
        attention(
            *operands,
            lambda scores, cols: scores + repeated(unseen[...], scores.shape[1]),
            store,
            CROSSING_CHUNK,
        )
        staged_out[pl.ds(pl.multiple_of(start, TILE), rows), :] = result[buffer]
        keep(job).start()
        return carry

    @pl.when(jobs > 0)
    def _():
        stage = functools.partial(
            copy_pieces, levels, edge.level, staged_in, margin, received, in_sem, False)
        send = functools.partial(
            copy_pieces, levels, edge.level, staged_out, margin, back, out_sem, True)
        stage(START)
        load_own(START)
        position = lax.broadcasted_iota(jnp.int32, (rows, HEAD_DIM), 0)
        in_image = (position < edge.after) | (position >= rows - edge.before)
        unseen[...] = jnp.where(in_image, 0.0, -1e30)
        load_own(WAIT)
        stage(WAIT)
        lax.fori_loop(0, jobs, one_job, 0)
        send(START)

        @pl.when(jobs >= 2)
        def _():
            keep(1).wait()

        keep(0).wait()
        send(WAIT)


def crossing_images(kind, plan, arrays, received, levels):
    rows, width = arrays[0].shape
    heads = width // HEAD_DIM
    four = 4 * HEAD_DIM
    count = len(levels)
    staged = pltpu.VMEM((rows + levels[-1] + rows, four), jnp.bfloat16)
    outs = pl.pallas_call(
        functools.partial(crossing_kernel, levels, kind),
        in_specs=[SCALARS] + [ANYWHERE] * (4 + count),
        out_specs=[ANYWHERE] * (count + 1),
        out_shape=piece_shapes(levels)
        + [pltpu.HBM((heads, rows, four), jnp.bfloat16)],
        scratch_shapes=[
            pltpu.VMEM((4, rows, width), jnp.bfloat16),
            staged,
            staged,
            pltpu.VMEM((rows, four), jnp.bfloat16),
            pltpu.VMEM((2, rows, four), jnp.bfloat16),
            pltpu.VMEM((rows, HEAD_DIM), jnp.float32),
            pltpu.SemaphoreType.DMA((4,)),
            pltpu.SemaphoreType.DMA((count,)),
            pltpu.SemaphoreType.DMA((count,)),
            pltpu.SemaphoreType.DMA((2,)),
        ],
        compiler_params=pltpu.CompilerParams(vmem_limit_bytes=VMEM_LIMIT),
        cost_estimate=pl.CostEstimate(
            flops=12 * rows * rows * width, bytes_accessed=16 * rows * width, transcendentals=0
        ),
        name="odd_edge_images" if kind == ODD else "even_edge_images",
    )(plan, *in_hbm(arrays), *received)
    return outs[:count], outs[count]


def overlay(whole, which, edge, first_head, heads, source):
    mixed = jnp.where(edge.lower, edge.first_block, edge.last_block - 1)
    full = jnp.where(edge.lower, edge.first_block + 1, edge.first_block)

    def one_head(slot, carry):
        place = lanes(first_head + slot)

        def one_block(step, carry):
            first = (full + step) * BLOCK
            part = pl.ds(pl.multiple_of(first, BLOCK), BLOCK)
            whole[which, part, place] = source(slot, first)
            return carry

        first = mixed * BLOCK
        part = pl.ds(pl.multiple_of(first, BLOCK), BLOCK)
        position = first + lax.broadcasted_iota(jnp.int32, (BLOCK, HEAD_DIM), 0)
        whole[which, part, place] = jnp.where(
            (position >= edge.own_begin) & (position < edge.own_end),
            source(slot, first),
            whole[which, part, place],
        )
        return lax.fori_loop(0, edge.last_block - edge.first_block - 1, one_block, carry)

    lax.fori_loop(0, heads, one_head, 0)


def returned_source(edge, staged, columns):
    def source(slot, first):
        start = BLOCK + slot * edge.own_rows + first - edge.own
        return staged[pl.ds(pl.multiple_of(start, TILE), BLOCK), columns]

    return source


def rest_kernel(done, plan, lengths, *rest):
    operands, before, kept = rest[:4], rest[4:8], rest[8:10]
    outs = rest[10:14]
    image_rows, image_cols, held, held_sem = rest[14:]
    head = pl.program_id(0)
    rows = image_rows.shape[1]
    edges = [Edge(plan, kind, rows) for kind in (ODD, EVEN)]

    def kept_copy(kind, slot):
        part = tiles(edges[kind].own, edges[kind].own_rows)
        return pltpu.make_async_copy(
            kept[kind].at[slot, part], held.at[kind, slot, part], held_sem.at[kind, slot])

    @pl.when(head == 0)
    def _():
        for kind in (ODD, EVEN):
            def start(slot, carry):
                kept_copy(kind, slot).start()
                return carry

            lax.fori_loop(0, edges[kind].jobs, start, 0)

        find_images(lengths, image_rows, image_cols)

    @pl.when(head < done)
    def _():
        for old, out in zip(before, outs):
            out[...] = old[...]

    @pl.when(head >= done)
    def _():
        local_head(operands, image_rows, image_cols, outs)

    for kind in (ODD, EVEN):
        edge = edges[kind]
        slot = head - edge.job_head

        @pl.when((slot >= 0) & (slot < edge.jobs))
        def _():
            kept_copy(kind, slot).wait()

            def one_block(block, carry):
                first = block * BLOCK
                part = pl.ds(pl.multiple_of(first, BLOCK), BLOCK)
                position = first + lax.broadcasted_iota(jnp.int32, (BLOCK, HEAD_DIM), 0)
                wanted = (position >= edge.own_begin) & (position < edge.own_end)
                for which, out in enumerate(outs):
                    columns = slice(which * HEAD_DIM, (which + 1) * HEAD_DIM)
                    out[part, :] = jnp.where(wanted, held[kind, slot, part, columns], out[part, :])
                return carry

            lax.fori_loop(edge.first_block, edge.last_block, one_block, 0)


def rest_of_images(plan, lengths, arrays, done, local, kept_odd, kept_even):
    rows, width = arrays[0].shape
    heads = width // HEAD_DIM
    todo = pl.BlockSpec((rows, HEAD_DIM), lambda head: (0, jnp.maximum(head, done)))
    old = pl.BlockSpec((rows, HEAD_DIM), lambda head: (0, jnp.minimum(head, done - 1)))
    return pl.pallas_call(
        functools.partial(rest_kernel, done),
        grid=(heads,),
        in_specs=[SCALARS] * 2 + [todo] * 4 + [old] * 4 + [ANYWHERE] * 2,
        out_specs=[pl.BlockSpec((rows, HEAD_DIM), lambda head: (0, head))] * 4,
        out_shape=[pltpu.HBM((rows, width), jnp.bfloat16)] * 4,
        scratch_shapes=[
            pltpu.VMEM((8, rows), jnp.float32),
            pltpu.VMEM((rows, HEAD_DIM), jnp.float32),
            pltpu.VMEM((2, heads, rows, 4 * HEAD_DIM), jnp.bfloat16),
            pltpu.SemaphoreType.DMA((2, heads)),
        ],
        compiler_params=pltpu.CompilerParams(vmem_limit_bytes=VMEM_LIMIT),
        cost_estimate=SCHEDULED_LAST,
        name="rest_of_images",
    )(plan, lengths, *in_hbm([*arrays, *local, kept_odd, kept_even]))


def return_kernel(levels, plan, *rest):
    counts = [len(levels[ODD]), len(levels[EVEN])]
    total = sum(counts)
    returned = rest[:counts[ODD]], rest[counts[ODD]:total]
    outs = rest[total + 4:total + 8]
    whole, odd_staged, even_staged, whole_sem, odd_sem, even_sem = rest[total + 8:]
    staged = odd_staged, even_staged
    rows = whole.shape[1]
    edges = [Edge(plan, kind, rows) for kind in (ODD, EVEN)]
    stages = [
        functools.partial(
            copy_pieces, levels[kind], edges[kind].level, staged[kind], BLOCK, returned[kind],
            sem, False)
        for kind, sem in ((ODD, odd_sem), (EVEN, even_sem))
    ]

    ends = []
    for edge, other in (edges, edges[::-1]):
        meets = jnp.logical_not(edge.lower) & (other.sent > 0)
        ends.append(jnp.where(
            meets, jnp.minimum(edge.last_block, other.first_block), edge.last_block))

    def move(kind, which, out, action):
        first, last = edges[kind].first_block, ends[kind]

        @pl.when((edges[kind].sent > 0) & (last > first))
        def _():
            part = pl.ds(
                pl.multiple_of(first * BLOCK, BLOCK), pl.multiple_of((last - first) * BLOCK, BLOCK))
            inside, outside = whole.at[which, part], outs[which].at[part]
            source, target = (inside, outside) if out else (outside, inside)
            action(pltpu.make_async_copy(source, target, whole_sem.at[kind, which]))

    for stage in stages:
        stage(START)
    for which in range(4):
        for kind in (ODD, EVEN):
            move(kind, which, False, START)
    for stage in stages:
        stage(WAIT)
    for which in range(4):
        columns = slice(which * HEAD_DIM, (which + 1) * HEAD_DIM)
        for kind in (ODD, EVEN):
            move(kind, which, False, WAIT)
        for kind in (ODD, EVEN):
            edge = edges[kind]
            overlay(whole, which, edge, edge.sent_head, edge.sent,
                    returned_source(edge, staged[kind], columns))
        for kind in (ODD, EVEN):
            move(kind, which, True, START)
    for which in range(4):
        for kind in (ODD, EVEN):
            move(kind, which, True, WAIT)


def merge_returned(plan, odd, even, outs, levels):
    rows, width = outs[0].shape
    counts = [len(levels[ODD]), len(levels[EVEN])]
    return pl.pallas_call(
        functools.partial(return_kernel, levels),
        in_specs=[SCALARS] + [ANYWHERE] * (sum(counts) + 4),
        out_specs=[ANYWHERE] * 4,
        out_shape=[pltpu.HBM((rows, width), jnp.bfloat16)] * 4,
        input_output_aliases={1 + sum(counts) + which: which for which in range(4)},
        scratch_shapes=[
            pltpu.VMEM((4, rows, width), jnp.bfloat16),
            pltpu.VMEM((levels[ODD][-1] + 2 * BLOCK, 4 * HEAD_DIM), jnp.bfloat16),
            pltpu.VMEM((levels[EVEN][-1] + 2 * BLOCK, 4 * HEAD_DIM), jnp.bfloat16),
            pltpu.SemaphoreType.DMA((2, 4)),
            pltpu.SemaphoreType.DMA((counts[ODD],)),
            pltpu.SemaphoreType.DMA((counts[EVEN],)),
        ],
        compiler_params=pltpu.CompilerParams(vmem_limit_bytes=VMEM_LIMIT),
        name="merge_returned",
    )(plan, *odd, *even, *in_hbm(outs))


def swapped(value, kind):
    first = 0 if kind == ODD else 1
    pairs = [(block, block + 1) for block in range(first, lax.axis_size("dp") - 1, 2)]
    return lax.ppermute(value, "dp", pairs + [(after, before) for before, after in pairs])


def swap_further(choices, odd, even):
    counts = [len(odd), len(even)]
    if not sum(counts):
        return [], []
    pairs = [(first, second) for first in range(counts[0] + 1) for second in range(counts[1] + 1)]

    def send(used, odd, even):
        return tuple(
            [
                swapped(array, kind) if number == used[kind] else array
                for number, array in enumerate(arrays, start=1)
            ]
            for kind, arrays in ((ODD, odd), (EVEN, even))
        )

    index = 0
    for choice, count in zip(choices, counts):
        if count:
            index = index * (count + 1) + choice[0]
    branches = [functools.partial(send, pair) for pair in pairs]
    return lax.switch(index, branches, list(odd), list(even))


def body(queries, keys, values, out_grad, lengths):
    rows, width = queries.shape
    arrays = (queries, keys, values, out_grad)
    levels = [size_levels(kind, rows, width // HEAD_DIM) for kind in (ODD, EVEN)]
    plan, choices, even = pack_even(lengths, arrays, levels, lax.axis_size("dp"))
    even_first = swapped(even[0], EVEN)
    odd = pack_odd(plan, arrays, levels[ODD])
    odd_first = swapped(odd[0], ODD)
    done = width // HEAD_DIM // 2
    local = local_attention(lengths, arrays, done)
    choices, local = lax.optimization_barrier((choices, local))
    _, more = swap_further(choices, [], even[1:])
    back_even, kept_even = crossing_images(EVEN, plan, arrays, [even_first, *more], levels[EVEN])
    choices, kept_even = lax.optimization_barrier((choices, kept_even))
    more, _ = swap_further(choices, odd[1:], [])
    received = [odd_first, *more]
    first, received = lax.optimization_barrier((back_even[0], received))
    even_first = swapped(first, EVEN)
    back_odd, kept_odd = crossing_images(ODD, plan, arrays, received, levels[ODD])
    odd_first = swapped(back_odd[0], ODD)
    kept_odd, local = lax.optimization_barrier((kept_odd, local))
    outs = rest_of_images(plan, lengths, arrays, done, local, kept_odd, kept_even)
    even_first, choices, outs = lax.optimization_barrier((even_first, choices, outs))
    more_odd, more_even = swap_further(choices, back_odd[1:], back_even[1:])
    return tuple(merge_returned(
        plan, [odd_first, *more_odd], [even_first, *more_even], outs, levels))


def solution(mesh):
    in_specs = (P("dp", "tensor"), P("dp", "tensor"), P("dp", "tensor"), P("dp", "tensor"), P())
    out_specs = (P("dp", "tensor"), P("dp", "tensor"), P("dp", "tensor"), P("dp", "tensor"))
    return jax.shard_map(body, mesh=mesh, in_specs=in_specs, out_specs=out_specs, check_vma=False)
```

```python
import functools
import math

import jax
import jax.numpy as jnp
from jax import lax
from jax.experimental import pallas as pl
from jax.experimental.pallas import tpu as pltpu
from jax.sharding import PartitionSpec as P

HEAD_DIM = 128
TILE = 16
BLOCK = 64
LOCAL_CHUNK = 256
CROSSING_CHUNK = 256
FACTOR = 1.0 / math.sqrt(HEAD_DIM)
LOG2E = 1.4426950408889634
VMEM_LIMIT = 32 * 1024 * 1024
PACK_VMEM_LIMIT = 60 * 1024 * 1024

SCHEDULED_LAST = pl.CostEstimate(flops=1, bytes_accessed=1, transcendentals=0)

FIELDS = 8
BEFORE, AFTER, LOWER, JOBS, JOB_HEAD, SENT, SENT_HEAD, LEVEL = range(FIELDS)
ODD, EVEN = 0, 1

LEVEL_UNITS = ((9, 10, 11, 12, 13), (9, 10, 11, 12, 13))


def round_up(value):
    return (value + (TILE - 1)) & -TILE


def blocks_of(value, size):
    if size & (size - 1):
        return value // size
    return lax.shift_right_logical(value, jnp.int32(size.bit_length() - 1))


def worst_case_rows(rows, heads):
    worst = 0
    for before in range(TILE, rows + 1, TILE):
        for after in range(TILE, rows + TILE - before + 1, TILE):
            needed = min(max(after * low, before * (heads - low)) for low in range(heads + 1))
            worst = max(worst, needed)
    return worst


def size_levels(kind, rows, heads):
    unit = rows * heads // 48
    most = worst_case_rows(rows, heads)
    below = sorted(int(level * unit) for level in LEVEL_UNITS[kind] if level * unit < most)
    return tuple(below) + (most,)


def find_crossings(rows, blocks, lengths, before_edge, after_edge):
    def clear(edge, carry):
        before_edge[edge] = 0
        after_edge[edge] = 0
        return carry

    lax.fori_loop(0, blocks + 1, clear, 0)

    def place(image, start):
        end = start + lengths[image]
        edge = blocks_of(end - 1, rows)

        @pl.when(edge > blocks_of(start, rows))
        def _():
            before_edge[edge] = edge * rows - start
            after_edge[edge] = end - edge * rows

        return end

    lax.fori_loop(0, lengths.shape[0], place, 0)


def own_edge(kind, before_edge, after_edge):
    block = lax.axis_index("dp")
    lower = lax.rem(block, 2) == (0 if kind == ODD else 1)
    edge = jnp.where(lower, block + 1, block)
    return lower, before_edge[edge], after_edge[edge]


def make_plan(heads, blocks, levels, plan, choices, before_edge, after_edge):
    entry = lax.broadcasted_iota(jnp.int32, (8, 128), 1)
    for kind in (ODD, EVEN):
        limit = jnp.full((8, 128), levels[kind][-1], jnp.int32)
        for number, level in enumerate(levels[kind]):
            limit = jnp.where(entry == number, level, limit)

        def check(number, fits):
            edge = 2 * number + (1 if kind == ODD else 2)
            after = round_up(after_edge[edge])
            before = round_up(before_edge[edge])
            taken = jnp.zeros((8, 128), jnp.int32)
            for count in range(1, heads + 1):
                taken += jnp.where(after * count <= limit, 1, 0)
                taken += jnp.where(before * count <= limit, 1, 0)
            return jnp.minimum(fits, jnp.where(taken >= heads, 1, 0))

        last = len(levels[kind]) - 1
        chosen = jnp.int32(last)
        if last:
            edges = (blocks - (0 if kind == ODD else 1)) // 2
            fits = lax.fori_loop(0, edges, check, jnp.ones((8, 128), jnp.int32))
            chosen = jnp.min(jnp.where(fits == 1, entry, last))
        most_rows = jnp.int32(levels[kind][-1])
        for number, level in enumerate(levels[kind][:-1]):
            most_rows = jnp.where(chosen == number, level, most_rows)

        lower, before, after = own_edge(kind, before_edge, after_edge)
        most = jnp.int32(0)
        least = jnp.int32(heads)
        for count in range(1, heads + 1):
            most += jnp.where(round_up(after) * count <= most_rows, 1, 0)
            least -= jnp.where(round_up(before) * count <= most_rows, 1, 0)
        low = jnp.clip(jnp.int32(heads // 2), least, most)
        crossed = before > 0
        base = kind * FIELDS
        plan[base + BEFORE] = before
        plan[base + AFTER] = after
        plan[base + LOWER] = lower.astype(jnp.int32)
        plan[base + JOBS] = jnp.where(crossed, jnp.where(lower, low, heads - low), 0)
        plan[base + JOB_HEAD] = jnp.where(lower, 0, low)
        plan[base + SENT] = jnp.where(crossed, jnp.where(lower, heads - low, low), 0)
        plan[base + SENT_HEAD] = jnp.where(lower, low, 0)
        plan[base + LEVEL] = chosen
        choices[kind][0] = chosen


class Edge:
    def __init__(self, plan, kind, rows):
        read = lambda field: plan[kind * FIELDS + field]
        self.lower = read(LOWER) == 1
        self.jobs, self.job_head = read(JOBS), read(JOB_HEAD)
        self.sent, self.sent_head = read(SENT), read(SENT_HEAD)
        self.level = read(LEVEL)
        before, after = read(BEFORE), read(AFTER)
        self.before, self.after = before, after
        self.own_begin = jnp.where(self.lower, rows - before, 0)
        self.own_end = jnp.where(self.lower, rows, after)
        self.own_rows = round_up(jnp.where(self.lower, before, after))
        self.other_rows = round_up(jnp.where(self.lower, after, before))
        self.own = jnp.where(self.lower, rows - self.own_rows, 0)
        self.other = jnp.where(self.lower, 0, rows - self.other_rows)
        self.first_block = blocks_of(self.own_begin, BLOCK)
        self.last_block = blocks_of(self.own_end + BLOCK - 1, BLOCK)


def tiles(start, size):
    return pl.ds(pl.multiple_of(start, TILE), pl.multiple_of(size, TILE))


def lanes(head):
    return pl.ds(pl.multiple_of(head * HEAD_DIM, HEAD_DIM), HEAD_DIM)


def attention(query, key, value, grad, mask_columns, store, chunk):
    count = query.shape[0]
    key_t = key.T
    value_t = value.T
    grad_t = grad.T
    across = (((1,), (1,)), ((), ()))
    chunks = [slice(first, first + chunk) for first in range(0, count, chunk)]
    scores = [
        lax.dot_general(key, query[cols], across, preferred_element_type=jnp.float32)
        for cols in chunks
    ]
    grad_probs = [
        lax.dot_general(value, grad[cols], across, preferred_element_type=jnp.float32)
        for cols in chunks
    ]
    weights_low = []
    scaled_grads = []
    grad_scores = []
    for number, cols in enumerate(chunks):
        masked = jnp.where(mask_columns(cols), scores[number], -1e30)
        top = jnp.max(masked, axis=0, keepdims=True)
        weights = jnp.exp2((masked - top) * (FACTOR * LOG2E))
        weights_low.append(weights.astype(jnp.bfloat16))
        share = 1.0 / jnp.sum(weights, axis=0, keepdims=True)
        result_t = jnp.dot(value_t, weights_low[-1], preferred_element_type=jnp.float32)
        result_t = (result_t * share).astype(jnp.bfloat16)
        centre = jnp.sum(
            grad_t[:, cols].astype(jnp.float32) * result_t.astype(jnp.float32),
            axis=0,
            keepdims=True,
        )
        grad_scores.append(
            (weights * ((grad_probs[number] - centre) * share)).astype(jnp.bfloat16))
        grad_query_t = jnp.dot(key_t, grad_scores[-1], preferred_element_type=jnp.float32) * FACTOR
        store(0, cols, result_t.T)
        store(1, cols, grad_query_t.astype(jnp.bfloat16).T)
        share_column = jnp.broadcast_to(share, (8, chunk)).T[:, :1]
        scaled_grads.append((grad[cols].astype(jnp.float32) * share_column).astype(jnp.bfloat16))
    weights_low = jnp.concatenate(weights_low, axis=1)
    scaled_grads = jnp.concatenate(scaled_grads, axis=0)
    grad_scores = jnp.concatenate(grad_scores, axis=1)
    grad_value = jnp.dot(weights_low, scaled_grads, preferred_element_type=jnp.float32)
    store(3, slice(None), grad_value.astype(jnp.bfloat16))
    grad_key = jnp.dot(grad_scores, query, preferred_element_type=jnp.float32)
    store(2, slice(None), (grad_key * FACTOR).astype(jnp.bfloat16))


def find_images(lengths, image_rows):
    count = image_rows.shape[1]
    position = lax.axis_index("dp") * count + lax.broadcasted_iota(jnp.int32, (8, count), 1)

    def place(image, carry):
        start, begin = carry
        return start + lengths[image], jnp.where(position >= start, start, begin)

    first = (jnp.int32(0), jnp.zeros((8, count), jnp.int32))
    _, begin = lax.fori_loop(0, lengths.shape[0], place, first)
    image_rows[...] = begin.astype(jnp.float32)


def local_head(operands, image_rows, outs):
    image_col = image_rows[...].T[:, :1]

    def store(which, rows, part):
        outs[which][rows, :] = part

    attention(
        *(operand[...] for operand in operands),
        lambda cols: image_col == image_rows[:1, cols],
        store,
        LOCAL_CHUNK,
    )


def local_kernel(lengths, *rest):
    operands, outs, image_rows = rest[:4], rest[4:8], rest[8]

    @pl.when(pl.program_id(0) == 0)
    def _():
        find_images(lengths, image_rows)

    local_head(operands, image_rows, outs)


def local_attention(lengths, arrays, heads):
    rows, width = arrays[0].shape
    block = pl.BlockSpec((rows, HEAD_DIM), lambda head: (0, head))
    return pl.pallas_call(
        local_kernel,
        grid=(heads,),
        in_specs=[SCALARS] + [block] * 4,
        out_specs=[block] * 4,
        out_shape=[pltpu.HBM((rows, width), jnp.bfloat16)] * 4,
        scratch_shapes=[pltpu.VMEM((8, rows), jnp.float32)],
        compiler_params=pltpu.CompilerParams(vmem_limit_bytes=VMEM_LIMIT),
        cost_estimate=SCHEDULED_LAST,
        name="local_images",
    )(lengths, *in_hbm(arrays))


START = lambda copy: copy.start()
WAIT = lambda copy: copy.wait()
ANYWHERE = pl.BlockSpec(memory_space=pl.ANY)
SCALARS = pl.BlockSpec(memory_space=pltpu.SMEM)


def in_hbm(arrays):
    return [pltpu.with_memory_space_constraint(array, pltpu.HBM) for array in arrays]


def pieces(levels):
    return [(0, levels[0])] + [(levels[0], level - levels[0]) for level in levels[1:]]


def piece_shapes(levels):
    return [pltpu.HBM((size, 4 * HEAD_DIM), jnp.bfloat16) for _, size in pieces(levels)]


def copy_pieces(levels, level, staged, offset, arrays, sems, out, action, first=0):
    for number, (start, size) in enumerate(pieces(levels)):
        if number < first:
            continue
        inside = staged.at[pl.ds(offset + start, size)]
        outside = arrays[number]
        source, target = (inside, outside) if out else (outside, inside)

        @pl.when(True if number == 0 else level == number)
        def _():
            action(pltpu.make_async_copy(source, target, sems.at[number]))


def gather(edge, held, staged):
    steps = blocks_of(edge.own_rows + BLOCK - 1, BLOCK)

    def one_head(slot, carry):
        def one_block(step, carry):
            source = pl.ds(pl.multiple_of(edge.own + step * BLOCK, TILE), BLOCK)
            target = pl.ds(pl.multiple_of(slot * edge.own_rows + step * BLOCK, TILE), BLOCK)
            for which in range(4):
                staged[target, which * HEAD_DIM:(which + 1) * HEAD_DIM] = held[
                    which, source, lanes(edge.sent_head + slot)]
            return carry

        return lax.fori_loop(0, steps, one_block, carry)

    lax.fori_loop(0, edge.sent, one_head, 0)


def pack_even_kernel(levels, blocks, lengths, query, key, value, grad, *rest):
    count = len(levels[EVEN])
    plan, choices, outs = rest[0], rest[1:3], rest[3:3 + count]
    before_edge, after_edge, held, staged, load_sem, out_sem = rest[3 + count:]
    rows, width = query.shape
    find_crossings(rows, blocks, lengths, before_edge, after_edge)
    lower, before, after = own_edge(EVEN, before_edge, after_edge)
    own_rows = round_up(jnp.where(lower, before, after))
    part = tiles(jnp.where(lower, rows - own_rows, 0), own_rows)
    loads = [
        pltpu.make_async_copy(array.at[part], held.at[which, part], load_sem.at[which])
        for which, array in enumerate((query, key, value, grad))
    ]

    @pl.when(before > 0)
    def _():
        for copy in loads:
            copy.start()

    make_plan(width // HEAD_DIM, blocks, levels, plan, choices, before_edge, after_edge)

    @pl.when(before > 0)
    def _():
        for copy in loads:
            copy.wait()
        edge = Edge(plan, EVEN, rows)
        gather(edge, held, staged)
        send = functools.partial(
            copy_pieces, levels[EVEN], edge.level, staged, 0, outs, out_sem, True, first=1)
        send(START)
        outs[0][...] = staged[:outs[0].shape[0], :]
        send(WAIT)


def pack_odd_kernel(levels, plan, query, key, value, grad, *rest):
    count = len(levels)
    outs = rest[:count]
    held, staged, load_sem, out_sem = rest[count:]
    rows = query.shape[0]
    edge = Edge(plan, ODD, rows)
    part = tiles(edge.own, edge.own_rows)
    loads = [
        pltpu.make_async_copy(array.at[part], held.at[which, part], load_sem.at[which])
        for which, array in enumerate((query, key, value, grad))
    ]

    @pl.when(edge.sent > 0)
    def _():
        for copy in loads:
            copy.start()
        for copy in loads:
            copy.wait()
        gather(edge, held, staged)
        move = functools.partial(
            copy_pieces, levels, edge.level, staged, 0, outs, out_sem, True)
        move(START)
        move(WAIT)


def pack_scratch(rows, width, levels):
    return [
        pltpu.VMEM((4, rows + BLOCK, width), jnp.bfloat16),
        pltpu.VMEM((levels[-1] + BLOCK, 4 * HEAD_DIM), jnp.bfloat16),
        pltpu.SemaphoreType.DMA((4,)),
        pltpu.SemaphoreType.DMA((len(levels),)),
    ]


def pack_even(lengths, arrays, levels, blocks):
    rows, width = arrays[0].shape
    one = jax.ShapeDtypeStruct((1,), jnp.int32)
    plan, odd_level, even_level, *even = pl.pallas_call(
        functools.partial(pack_even_kernel, levels, blocks),
        in_specs=[SCALARS] + [ANYWHERE] * 4,
        out_specs=[SCALARS] * 3 + [pl.BlockSpec(memory_space=pltpu.VMEM)]
        + [ANYWHERE] * (len(levels[EVEN]) - 1),
        out_shape=[jax.ShapeDtypeStruct((2 * FIELDS,), jnp.int32), one, one]
        + [pltpu.VMEM((levels[EVEN][0], 4 * HEAD_DIM), jnp.bfloat16)]
        + piece_shapes(levels[EVEN])[1:],
        scratch_shapes=[
            pltpu.SMEM((blocks + 2,), jnp.int32),
            pltpu.SMEM((blocks + 2,), jnp.int32),
        ] + pack_scratch(rows, width, levels[EVEN]),
        compiler_params=pltpu.CompilerParams(vmem_limit_bytes=PACK_VMEM_LIMIT),
        name="pack_even",
    )(lengths, *in_hbm(arrays))
    return plan, (odd_level, even_level), even


def pack_odd(plan, arrays, levels):
    rows, width = arrays[0].shape
    return pl.pallas_call(
        functools.partial(pack_odd_kernel, levels),
        in_specs=[SCALARS] + [ANYWHERE] * 4,
        out_specs=[ANYWHERE] * len(levels),
        out_shape=piece_shapes(levels),
        scratch_shapes=pack_scratch(rows, width, levels),
        compiler_params=pltpu.CompilerParams(vmem_limit_bytes=VMEM_LIMIT),
        name="pack_odd",
    )(plan, *in_hbm(arrays))


def crossing_kernel(levels, kind, plan, query, key, value, grad, *rest):
    count = len(levels)
    received, back, kept = rest[:count], rest[count:2 * count], rest[2 * count]
    own, staged_in, staged_out, result, own_sem, in_sem, out_sem, kept_sem = rest[2 * count + 1:]
    rows, width = query.shape
    edge = Edge(plan, kind, rows)
    jobs = edge.jobs
    own_part = tiles(edge.own, edge.own_rows)
    margin = rows

    def load_own(action):
        for which, array in enumerate((query, key, value, grad)):
            action(pltpu.make_async_copy(
                array.at[own_part], own.at[which, own_part], own_sem.at[which]))

    def keep(job):
        buffer = lax.rem(job, 2)
        return pltpu.make_async_copy(
            result.at[buffer, own_part], kept.at[job, own_part], kept_sem.at[buffer])

    position = lax.broadcasted_iota(jnp.int32, (rows, HEAD_DIM), 0)
    in_own = (position >= edge.own_begin) & (position < edge.own_end)
    key_position = lax.broadcasted_iota(jnp.int32, (rows, 1), 0)
    in_image = (key_position < edge.after) | (key_position >= rows - edge.before)
    in_window = (position < edge.after) | (position >= rows - edge.before)

    def one_job(step, carry):
        job = jnp.where(edge.lower, step, jobs - 1 - step)
        buffer = lax.rem(job, 2)
        start = margin + job * edge.other_rows - edge.other
        window = pl.ds(pl.multiple_of(start, TILE), rows)

        @pl.when(step >= 2)
        def _():
            keep(job).wait()

        zero = jnp.zeros((rows, HEAD_DIM), jnp.bfloat16)
        operands = []
        for which in range(4):
            columns = slice(which * HEAD_DIM, (which + 1) * HEAD_DIM)
            operands.append(jnp.where(
                in_own,
                own[which, :, lanes(edge.job_head + job)],
                jnp.where(in_window, staged_in[window, columns], zero),
            ))

        def store(which, part_rows, part):
            result[buffer, part_rows, which * HEAD_DIM:(which + 1) * HEAD_DIM] = part

        attention(*operands, lambda cols: in_image, store, CROSSING_CHUNK)
        staged_out[window, :] = result[buffer]
        keep(job).start()
        return carry

    @pl.when(jobs > 0)
    def _():
        stage = functools.partial(
            copy_pieces, levels, edge.level, staged_in, margin, received, in_sem, False)
        send = functools.partial(
            copy_pieces, levels, edge.level, staged_out, margin, back, out_sem, True)
        stage(START)
        load_own(START)
        load_own(WAIT)
        stage(WAIT)
        lax.fori_loop(0, jobs, one_job, 0)
        send(START)

        @pl.when(jobs >= 2)
        def _():
            keep(1).wait()

        keep(0).wait()
        send(WAIT)


def crossing_images(kind, plan, arrays, received, levels):
    rows, width = arrays[0].shape
    heads = width // HEAD_DIM
    four = 4 * HEAD_DIM
    count = len(levels)
    staged = pltpu.VMEM((rows + levels[-1] + rows, four), jnp.bfloat16)
    outs = pl.pallas_call(
        functools.partial(crossing_kernel, levels, kind),
        in_specs=[SCALARS] + [ANYWHERE] * (4 + count),
        out_specs=[ANYWHERE] * (count + 1),
        out_shape=piece_shapes(levels)
        + [pltpu.HBM((heads, rows, four), jnp.bfloat16)],
        scratch_shapes=[
            pltpu.VMEM((4, rows, width), jnp.bfloat16),
            staged,
            staged,
            pltpu.VMEM((2, rows, four), jnp.bfloat16),
            pltpu.SemaphoreType.DMA((4,)),
            pltpu.SemaphoreType.DMA((count,)),
            pltpu.SemaphoreType.DMA((count,)),
            pltpu.SemaphoreType.DMA((2,)),
        ],
        compiler_params=pltpu.CompilerParams(vmem_limit_bytes=VMEM_LIMIT),
        cost_estimate=pl.CostEstimate(
            flops=12 * rows * rows * width, bytes_accessed=16 * rows * width, transcendentals=0
        ),
        name="odd_edge_images" if kind == ODD else "even_edge_images",
    )(plan, *in_hbm(arrays), *received)
    return outs[:count], outs[count]


def overlay(whole, which, edge, first_head, heads, source):
    mixed = jnp.where(edge.lower, edge.first_block, edge.last_block - 1)
    full = jnp.where(edge.lower, edge.first_block + 1, edge.first_block)

    def one_head(slot, carry):
        place = lanes(first_head + slot)

        def one_block(step, carry):
            first = (full + step) * BLOCK
            part = pl.ds(pl.multiple_of(first, BLOCK), BLOCK)
            whole[which, part, place] = source(slot, first)
            return carry

        first = mixed * BLOCK
        part = pl.ds(pl.multiple_of(first, BLOCK), BLOCK)
        position = first + lax.broadcasted_iota(jnp.int32, (BLOCK, HEAD_DIM), 0)
        whole[which, part, place] = jnp.where(
            (position >= edge.own_begin) & (position < edge.own_end),
            source(slot, first),
            whole[which, part, place],
        )
        return lax.fori_loop(0, edge.last_block - edge.first_block - 1, one_block, carry)

    lax.fori_loop(0, heads, one_head, 0)


def returned_source(edge, staged, columns):
    def source(slot, first):
        start = BLOCK + slot * edge.own_rows + first - edge.own
        return staged[pl.ds(pl.multiple_of(start, TILE), BLOCK), columns]

    return source


def rest_kernel(done, plan, lengths, *rest):
    operands, before, kept = rest[:4], rest[4:8], rest[8:10]
    outs = rest[10:14]
    image_rows, held, held_sem = rest[14:]
    head = pl.program_id(0)
    rows = image_rows.shape[1]
    edges = [Edge(plan, kind, rows) for kind in (ODD, EVEN)]

    def kept_copy(kind, slot):
        part = tiles(edges[kind].own, edges[kind].own_rows)
        return pltpu.make_async_copy(
            kept[kind].at[slot, part], held.at[kind, slot, part], held_sem.at[kind, slot])

    @pl.when(head == 0)
    def _():
        for kind in (ODD, EVEN):
            def start(slot, carry):
                kept_copy(kind, slot).start()
                return carry

            lax.fori_loop(0, edges[kind].jobs, start, 0)

        find_images(lengths, image_rows)

    @pl.when(head < done)
    def _():
        for old, out in zip(before, outs):
            out[...] = old[...]

    @pl.when(head >= done)
    def _():
        local_head(operands, image_rows, outs)

    for kind in (ODD, EVEN):
        edge = edges[kind]
        slot = head - edge.job_head

        @pl.when((slot >= 0) & (slot < edge.jobs))
        def _():
            kept_copy(kind, slot).wait()

            def one_block(block, carry):
                first = block * BLOCK
                part = pl.ds(pl.multiple_of(first, BLOCK), BLOCK)
                position = first + lax.broadcasted_iota(jnp.int32, (BLOCK, HEAD_DIM), 0)
                wanted = (position >= edge.own_begin) & (position < edge.own_end)
                for which, out in enumerate(outs):
                    columns = slice(which * HEAD_DIM, (which + 1) * HEAD_DIM)
                    out[part, :] = jnp.where(wanted, held[kind, slot, part, columns], out[part, :])
                return carry

            lax.fori_loop(edge.first_block, edge.last_block, one_block, 0)


def rest_of_images(plan, lengths, arrays, done, local, kept_odd, kept_even):
    rows, width = arrays[0].shape
    heads = width // HEAD_DIM
    todo = pl.BlockSpec((rows, HEAD_DIM), lambda head: (0, jnp.maximum(head, done)))
    old = pl.BlockSpec((rows, HEAD_DIM), lambda head: (0, jnp.minimum(head, done - 1)))
    return pl.pallas_call(
        functools.partial(rest_kernel, done),
        grid=(heads,),
        in_specs=[SCALARS] * 2 + [todo] * 4 + [old] * 4 + [ANYWHERE] * 2,
        out_specs=[pl.BlockSpec((rows, HEAD_DIM), lambda head: (0, head))] * 4,
        out_shape=[pltpu.HBM((rows, width), jnp.bfloat16)] * 4,
        scratch_shapes=[
            pltpu.VMEM((8, rows), jnp.float32),
            pltpu.VMEM((2, heads, rows, 4 * HEAD_DIM), jnp.bfloat16),
            pltpu.SemaphoreType.DMA((2, heads)),
        ],
        compiler_params=pltpu.CompilerParams(vmem_limit_bytes=VMEM_LIMIT),
        cost_estimate=SCHEDULED_LAST,
        name="rest_of_images",
    )(plan, lengths, *in_hbm([*arrays, *local, kept_odd, kept_even]))


def return_kernel(levels, plan, *rest):
    counts = [len(levels[ODD]), len(levels[EVEN])]
    total = sum(counts)
    returned = rest[:counts[ODD]], rest[counts[ODD]:total]
    outs = rest[total + 4:total + 8]
    whole, odd_staged, even_staged, whole_sem, odd_sem, even_sem = rest[total + 8:]
    staged = odd_staged, even_staged
    rows = whole.shape[1]
    edges = [Edge(plan, kind, rows) for kind in (ODD, EVEN)]
    stages = [
        functools.partial(
            copy_pieces, levels[kind], edges[kind].level, staged[kind], BLOCK, returned[kind],
            sem, False)
        for kind, sem in ((ODD, odd_sem), (EVEN, even_sem))
    ]

    ends = []
    for edge, other in (edges, edges[::-1]):
        meets = jnp.logical_not(edge.lower) & (other.sent > 0)
        ends.append(jnp.where(
            meets, jnp.minimum(edge.last_block, other.first_block), edge.last_block))

    def move(kind, which, out, action):
        first, last = edges[kind].first_block, ends[kind]

        @pl.when((edges[kind].sent > 0) & (last > first))
        def _():
            part = pl.ds(
                pl.multiple_of(first * BLOCK, BLOCK), pl.multiple_of((last - first) * BLOCK, BLOCK))
            inside, outside = whole.at[which, part], outs[which].at[part]
            source, target = (inside, outside) if out else (outside, inside)
            action(pltpu.make_async_copy(source, target, whole_sem.at[kind, which]))

    for stage in stages:
        stage(START)
    for which in range(4):
        for kind in (ODD, EVEN):
            move(kind, which, False, START)
    for stage in stages:
        stage(WAIT)
    for which in range(4):
        columns = slice(which * HEAD_DIM, (which + 1) * HEAD_DIM)
        for kind in (ODD, EVEN):
            move(kind, which, False, WAIT)
        for kind in (ODD, EVEN):
            edge = edges[kind]
            overlay(whole, which, edge, edge.sent_head, edge.sent,
                    returned_source(edge, staged[kind], columns))
        for kind in (ODD, EVEN):
            move(kind, which, True, START)
    for which in range(4):
        for kind in (ODD, EVEN):
            move(kind, which, True, WAIT)


def merge_returned(plan, odd, even, outs, levels):
    rows, width = outs[0].shape
    counts = [len(levels[ODD]), len(levels[EVEN])]
    return pl.pallas_call(
        functools.partial(return_kernel, levels),
        in_specs=[SCALARS] + [ANYWHERE] * (sum(counts) + 4),
        out_specs=[ANYWHERE] * 4,
        out_shape=[pltpu.HBM((rows, width), jnp.bfloat16)] * 4,
        input_output_aliases={1 + sum(counts) + which: which for which in range(4)},
        scratch_shapes=[
            pltpu.VMEM((4, rows, width), jnp.bfloat16),
            pltpu.VMEM((levels[ODD][-1] + 2 * BLOCK, 4 * HEAD_DIM), jnp.bfloat16),
            pltpu.VMEM((levels[EVEN][-1] + 2 * BLOCK, 4 * HEAD_DIM), jnp.bfloat16),
            pltpu.SemaphoreType.DMA((2, 4)),
            pltpu.SemaphoreType.DMA((counts[ODD],)),
            pltpu.SemaphoreType.DMA((counts[EVEN],)),
        ],
        compiler_params=pltpu.CompilerParams(vmem_limit_bytes=VMEM_LIMIT),
        name="merge_returned",
    )(plan, *odd, *even, *in_hbm(outs))


def swapped(value, kind):
    first = 0 if kind == ODD else 1
    pairs = [(block, block + 1) for block in range(first, lax.axis_size("dp") - 1, 2)]
    return lax.ppermute(value, "dp", pairs + [(after, before) for before, after in pairs])


def swap_further(choices, odd, even):
    counts = [len(odd), len(even)]
    if not sum(counts):
        return [], []
    pairs = [(first, second) for first in range(counts[0] + 1) for second in range(counts[1] + 1)]

    def send(used, odd, even):
        return tuple(
            [
                swapped(array, kind) if number == used[kind] else array
                for number, array in enumerate(arrays, start=1)
            ]
            for kind, arrays in ((ODD, odd), (EVEN, even))
        )

    index = 0
    for choice, count in zip(choices, counts):
        if count:
            index = index * (count + 1) + choice[0]
    branches = [functools.partial(send, pair) for pair in pairs]
    return lax.switch(index, branches, list(odd), list(even))


def body(queries, keys, values, out_grad, lengths):
    rows, width = queries.shape
    arrays = (queries, keys, values, out_grad)
    levels = [size_levels(kind, rows, width // HEAD_DIM) for kind in (ODD, EVEN)]
    plan, choices, even = pack_even(lengths, arrays, levels, lax.axis_size("dp"))
    even_first = swapped(even[0], EVEN)
    odd = pack_odd(plan, arrays, levels[ODD])
    odd_first = swapped(odd[0], ODD)
    done = width // HEAD_DIM // 2
    local = local_attention(lengths, arrays, done)
    choices, local = lax.optimization_barrier((choices, local))
    _, more = swap_further(choices, [], even[1:])
    back_even, kept_even = crossing_images(EVEN, plan, arrays, [even_first, *more], levels[EVEN])
    choices, kept_even = lax.optimization_barrier((choices, kept_even))
    more, _ = swap_further(choices, odd[1:], [])
    received = [odd_first, *more]
    first, received = lax.optimization_barrier((back_even[0], received))
    even_first = swapped(first, EVEN)
    back_odd, kept_odd = crossing_images(ODD, plan, arrays, received, levels[ODD])
    odd_first = swapped(back_odd[0], ODD)
    kept_odd, local = lax.optimization_barrier((kept_odd, local))
    outs = rest_of_images(plan, lengths, arrays, done, local, kept_odd, kept_even)
    even_first, choices, outs = lax.optimization_barrier((even_first, choices, outs))
    more_odd, more_even = swap_further(choices, back_odd[1:], back_even[1:])
    return tuple(merge_returned(
        plan, [odd_first, *more_odd], [even_first, *more_even], outs, levels))


def solution(mesh):
    in_specs = (P("dp", "tensor"), P("dp", "tensor"), P("dp", "tensor"), P("dp", "tensor"), P())
    out_specs = (P("dp", "tensor"), P("dp", "tensor"), P("dp", "tensor"), P("dp", "tensor"))
    return jax.shard_map(body, mesh=mesh, in_specs=in_specs, out_specs=out_specs, check_vma=False)
```

```python
import functools
import math

import jax
import jax.numpy as jnp
from jax import lax
from jax.experimental import pallas as pl
from jax.experimental.pallas import tpu as pltpu
from jax.sharding import PartitionSpec as P

HEAD_DIM = 128
TILE = 16
BLOCK = 64
LOCAL_CHUNK = 256
CROSSING_CHUNK = 256
FACTOR = 1.0 / math.sqrt(HEAD_DIM)
LOG2E = 1.4426950408889634
VMEM_LIMIT = 32 * 1024 * 1024
PACK_VMEM_LIMIT = 60 * 1024 * 1024

SCHEDULED_LAST = pl.CostEstimate(flops=1, bytes_accessed=1, transcendentals=0)

FIELDS = 8
BEFORE, AFTER, LOWER, JOBS, JOB_HEAD, SENT, SENT_HEAD, LEVEL = range(FIELDS)
ODD, EVEN = 0, 1

LEVEL_UNITS = ((9, 10, 11, 12, 13), (9, 10, 11, 12, 13))


def round_up(value):
    return (value + (TILE - 1)) & -TILE


def blocks_of(value, size):
    if size & (size - 1):
        return value // size
    return lax.shift_right_logical(value, jnp.int32(size.bit_length() - 1))


def worst_case_rows(rows, heads):
    worst = 0
    for before in range(TILE, rows + 1, TILE):
        for after in range(TILE, rows + TILE - before + 1, TILE):
            needed = min(max(after * low, before * (heads - low)) for low in range(heads + 1))
            worst = max(worst, needed)
    return worst


def size_levels(kind, rows, heads):
    unit = rows * heads // 48
    most = worst_case_rows(rows, heads)
    below = sorted(int(level * unit) for level in LEVEL_UNITS[kind] if level * unit < most)
    return tuple(below) + (most,)


def find_crossings(rows, blocks, lengths, before_edge, after_edge):
    def clear(edge, carry):
        before_edge[edge] = 0
        after_edge[edge] = 0
        return carry

    lax.fori_loop(0, blocks + 1, clear, 0)

    def place(image, start):
        end = start + lengths[image]
        edge = blocks_of(end - 1, rows)

        @pl.when(edge > blocks_of(start, rows))
        def _():
            before_edge[edge] = edge * rows - start
            after_edge[edge] = end - edge * rows

        return end

    lax.fori_loop(0, lengths.shape[0], place, 0)


def own_edge(kind, before_edge, after_edge):
    block = lax.axis_index("dp")
    lower = lax.rem(block, 2) == (0 if kind == ODD else 1)
    edge = jnp.where(lower, block + 1, block)
    return lower, before_edge[edge], after_edge[edge]


def make_plan(heads, blocks, levels, plan, choices, before_edge, after_edge):
    entry = lax.broadcasted_iota(jnp.int32, (8, 128), 1)
    for kind in (ODD, EVEN):
        limit = jnp.full((8, 128), levels[kind][-1], jnp.int32)
        for number, level in enumerate(levels[kind]):
            limit = jnp.where(entry == number, level, limit)

        def check(number, fits):
            edge = 2 * number + (1 if kind == ODD else 2)
            after = round_up(after_edge[edge])
            before = round_up(before_edge[edge])
            taken = jnp.zeros((8, 128), jnp.int32)
            for count in range(1, heads + 1):
                taken += jnp.where(after * count <= limit, 1, 0)
                taken += jnp.where(before * count <= limit, 1, 0)
            return jnp.minimum(fits, jnp.where(taken >= heads, 1, 0))

        last = len(levels[kind]) - 1
        chosen = jnp.int32(last)
        if last:
            edges = (blocks - (0 if kind == ODD else 1)) // 2
            fits = lax.fori_loop(0, edges, check, jnp.ones((8, 128), jnp.int32))
            chosen = jnp.min(jnp.where(fits == 1, entry, last))
        most_rows = jnp.int32(levels[kind][-1])
        for number, level in enumerate(levels[kind][:-1]):
            most_rows = jnp.where(chosen == number, level, most_rows)

        lower, before, after = own_edge(kind, before_edge, after_edge)
        most = jnp.int32(0)
        least = jnp.int32(heads)
        for count in range(1, heads + 1):
            most += jnp.where(round_up(after) * count <= most_rows, 1, 0)
            least -= jnp.where(round_up(before) * count <= most_rows, 1, 0)
        low = jnp.clip(jnp.int32(heads // 2), least, most)
        crossed = before > 0
        base = kind * FIELDS
        plan[base + BEFORE] = before
        plan[base + AFTER] = after
        plan[base + LOWER] = lower.astype(jnp.int32)
        plan[base + JOBS] = jnp.where(crossed, jnp.where(lower, low, heads - low), 0)
        plan[base + JOB_HEAD] = jnp.where(lower, 0, low)
        plan[base + SENT] = jnp.where(crossed, jnp.where(lower, heads - low, low), 0)
        plan[base + SENT_HEAD] = jnp.where(lower, low, 0)
        plan[base + LEVEL] = chosen
        choices[kind][0] = chosen


class Edge:
    def __init__(self, plan, kind, rows):
        read = lambda field: plan[kind * FIELDS + field]
        self.lower = read(LOWER) == 1
        self.jobs, self.job_head = read(JOBS), read(JOB_HEAD)
        self.sent, self.sent_head = read(SENT), read(SENT_HEAD)
        self.level = read(LEVEL)
        before, after = read(BEFORE), read(AFTER)
        self.before, self.after = before, after
        self.own_begin = jnp.where(self.lower, rows - before, 0)
        self.own_end = jnp.where(self.lower, rows, after)
        self.own_rows = round_up(jnp.where(self.lower, before, after))
        self.other_rows = round_up(jnp.where(self.lower, after, before))
        self.own = jnp.where(self.lower, rows - self.own_rows, 0)
        self.other = jnp.where(self.lower, 0, rows - self.other_rows)
        self.first_block = blocks_of(self.own_begin, BLOCK)
        self.last_block = blocks_of(self.own_end + BLOCK - 1, BLOCK)


def tiles(start, size):
    return pl.ds(pl.multiple_of(start, TILE), pl.multiple_of(size, TILE))


def lanes(head):
    return pl.ds(pl.multiple_of(head * HEAD_DIM, HEAD_DIM), HEAD_DIM)


def attention(query, key, value, grad, mask_columns, store, chunk):
    count = query.shape[0]
    key_t = key.T
    value_t = value.T
    grad_t = grad.T
    across = (((1,), (1,)), ((), ()))
    chunks = [slice(first, first + chunk) for first in range(0, count, chunk)]
    scores = [
        lax.dot_general(key, query[cols], across, preferred_element_type=jnp.float32)
        for cols in chunks
    ]
    grad_probs = [
        lax.dot_general(value, grad[cols], across, preferred_element_type=jnp.float32)
        for cols in chunks
    ]
    probs_low = []
    grad_scores = []
    for number, cols in enumerate(chunks):
        masked = jnp.where(mask_columns(cols), scores[number], -1e30)
        top = jnp.max(masked, axis=0, keepdims=True)
        weights = jnp.exp2((masked - top) * (FACTOR * LOG2E))
        total = jnp.sum(weights, axis=0, keepdims=True)
        probs = weights * (1.0 / total)
        probs_low.append(probs.astype(jnp.bfloat16))
        result_t = jnp.dot(value_t, probs_low[-1], preferred_element_type=jnp.float32)
        result_t = result_t.astype(jnp.bfloat16)
        centre = jnp.sum(
            grad_t[:, cols].astype(jnp.float32) * result_t.astype(jnp.float32),
            axis=0,
            keepdims=True,
        )
        grad_scores.append((probs * (grad_probs[number] - centre)).astype(jnp.bfloat16))
        grad_query_t = jnp.dot(key_t, grad_scores[-1], preferred_element_type=jnp.float32) * FACTOR
        store(0, cols, result_t.T)
        store(1, cols, grad_query_t.astype(jnp.bfloat16).T)
    probs_low = jnp.concatenate(probs_low, axis=1)
    grad_scores = jnp.concatenate(grad_scores, axis=1)
    grad_value = jnp.dot(probs_low, grad, preferred_element_type=jnp.float32)
    store(3, slice(None), grad_value.astype(jnp.bfloat16))
    grad_key = jnp.dot(grad_scores, query, preferred_element_type=jnp.float32)
    store(2, slice(None), (grad_key * FACTOR).astype(jnp.bfloat16))


def find_images(lengths, image_rows):
    count = image_rows.shape[1]
    position = lax.axis_index("dp") * count + lax.broadcasted_iota(jnp.int32, (8, count), 1)

    def place(image, carry):
        start, begin = carry
        return start + lengths[image], jnp.where(position >= start, start, begin)

    first = (jnp.int32(0), jnp.zeros((8, count), jnp.int32))
    _, begin = lax.fori_loop(0, lengths.shape[0], place, first)
    image_rows[...] = begin.astype(jnp.float32)


def local_head(operands, image_rows, outs):
    image_col = image_rows[...].T[:, :1]

    def store(which, rows, part):
        outs[which][rows, :] = part

    attention(
        *(operand[...] for operand in operands),
        lambda cols: image_col == image_rows[:1, cols],
        store,
        LOCAL_CHUNK,
    )


def local_kernel(lengths, *rest):
    operands, outs, image_rows = rest[:4], rest[4:8], rest[8]

    @pl.when(pl.program_id(0) == 0)
    def _():
        find_images(lengths, image_rows)

    local_head(operands, image_rows, outs)


def local_attention(lengths, arrays, heads):
    rows, width = arrays[0].shape
    block = pl.BlockSpec((rows, HEAD_DIM), lambda head: (0, head))
    return pl.pallas_call(
        local_kernel,
        grid=(heads,),
        in_specs=[SCALARS] + [block] * 4,
        out_specs=[block] * 4,
        out_shape=[pltpu.HBM((rows, width), jnp.bfloat16)] * 4,
        scratch_shapes=[pltpu.VMEM((8, rows), jnp.float32)],
        compiler_params=pltpu.CompilerParams(vmem_limit_bytes=VMEM_LIMIT),
        cost_estimate=SCHEDULED_LAST,
        name="local_images",
    )(lengths, *in_hbm(arrays))


START = lambda copy: copy.start()
WAIT = lambda copy: copy.wait()
ANYWHERE = pl.BlockSpec(memory_space=pl.ANY)
SCALARS = pl.BlockSpec(memory_space=pltpu.SMEM)


def in_hbm(arrays):
    return [pltpu.with_memory_space_constraint(array, pltpu.HBM) for array in arrays]


def pieces(levels):
    return [(0, levels[0])] + [(levels[0], level - levels[0]) for level in levels[1:]]


def piece_shapes(levels):
    return [pltpu.HBM((size, 4 * HEAD_DIM), jnp.bfloat16) for _, size in pieces(levels)]


def copy_pieces(levels, level, staged, offset, arrays, sems, out, action, first=0):
    for number, (start, size) in enumerate(pieces(levels)):
        if number < first:
            continue
        inside = staged.at[pl.ds(offset + start, size)]
        outside = arrays[number]
        source, target = (inside, outside) if out else (outside, inside)

        @pl.when(True if number == 0 else level == number)
        def _():
            action(pltpu.make_async_copy(source, target, sems.at[number]))


def gather(edge, held, staged):
    steps = blocks_of(edge.own_rows + BLOCK - 1, BLOCK)

    def one_head(slot, carry):
        def one_block(step, carry):
            source = pl.ds(pl.multiple_of(edge.own + step * BLOCK, TILE), BLOCK)
            target = pl.ds(pl.multiple_of(slot * edge.own_rows + step * BLOCK, TILE), BLOCK)
            for which in range(4):
                staged[target, which * HEAD_DIM:(which + 1) * HEAD_DIM] = held[
                    which, source, lanes(edge.sent_head + slot)]
            return carry

        return lax.fori_loop(0, steps, one_block, carry)

    lax.fori_loop(0, edge.sent, one_head, 0)


def pack_even_kernel(levels, blocks, lengths, query, key, value, grad, *rest):
    count = len(levels[EVEN])
    plan, choices, outs = rest[0], rest[1:3], rest[3:3 + count]
    before_edge, after_edge, held, staged, load_sem, out_sem = rest[3 + count:]
    rows, width = query.shape
    find_crossings(rows, blocks, lengths, before_edge, after_edge)
    lower, before, after = own_edge(EVEN, before_edge, after_edge)
    own_rows = round_up(jnp.where(lower, before, after))
    part = tiles(jnp.where(lower, rows - own_rows, 0), own_rows)
    loads = [
        pltpu.make_async_copy(array.at[part], held.at[which, part], load_sem.at[which])
        for which, array in enumerate((query, key, value, grad))
    ]

    @pl.when(before > 0)
    def _():
        for copy in loads:
            copy.start()

    make_plan(width // HEAD_DIM, blocks, levels, plan, choices, before_edge, after_edge)

    @pl.when(before > 0)
    def _():
        for copy in loads:
            copy.wait()
        edge = Edge(plan, EVEN, rows)
        gather(edge, held, staged)
        send = functools.partial(
            copy_pieces, levels[EVEN], edge.level, staged, 0, outs, out_sem, True, first=1)
        send(START)
        outs[0][...] = staged[:outs[0].shape[0], :]
        send(WAIT)


def pack_odd_kernel(levels, plan, query, key, value, grad, *rest):
    count = len(levels)
    outs = rest[:count]
    held, staged, load_sem, out_sem = rest[count:]
    rows = query.shape[0]
    edge = Edge(plan, ODD, rows)
    part = tiles(edge.own, edge.own_rows)
    loads = [
        pltpu.make_async_copy(array.at[part], held.at[which, part], load_sem.at[which])
        for which, array in enumerate((query, key, value, grad))
    ]

    @pl.when(edge.sent > 0)
    def _():
        for copy in loads:
            copy.start()
        for copy in loads:
            copy.wait()
        gather(edge, held, staged)
        move = functools.partial(
            copy_pieces, levels, edge.level, staged, 0, outs, out_sem, True)
        move(START)
        move(WAIT)


def pack_scratch(rows, width, levels):
    return [
        pltpu.VMEM((4, rows + BLOCK, width), jnp.bfloat16),
        pltpu.VMEM((levels[-1] + BLOCK, 4 * HEAD_DIM), jnp.bfloat16),
        pltpu.SemaphoreType.DMA((4,)),
        pltpu.SemaphoreType.DMA((len(levels),)),
    ]


def pack_even(lengths, arrays, levels, blocks):
    rows, width = arrays[0].shape
    one = jax.ShapeDtypeStruct((1,), jnp.int32)
    plan, odd_level, even_level, *even = pl.pallas_call(
        functools.partial(pack_even_kernel, levels, blocks),
        in_specs=[SCALARS] + [ANYWHERE] * 4,
        out_specs=[SCALARS] * 3 + [pl.BlockSpec(memory_space=pltpu.VMEM)]
        + [ANYWHERE] * (len(levels[EVEN]) - 1),
        out_shape=[jax.ShapeDtypeStruct((2 * FIELDS,), jnp.int32), one, one]
        + [pltpu.VMEM((levels[EVEN][0], 4 * HEAD_DIM), jnp.bfloat16)]
        + piece_shapes(levels[EVEN])[1:],
        scratch_shapes=[
            pltpu.SMEM((blocks + 2,), jnp.int32),
            pltpu.SMEM((blocks + 2,), jnp.int32),
        ] + pack_scratch(rows, width, levels[EVEN]),
        compiler_params=pltpu.CompilerParams(vmem_limit_bytes=PACK_VMEM_LIMIT),
        name="pack_even",
    )(lengths, *in_hbm(arrays))
    return plan, (odd_level, even_level), even


def pack_odd(plan, arrays, levels):
    rows, width = arrays[0].shape
    return pl.pallas_call(
        functools.partial(pack_odd_kernel, levels),
        in_specs=[SCALARS] + [ANYWHERE] * 4,
        out_specs=[ANYWHERE] * len(levels),
        out_shape=piece_shapes(levels),
        scratch_shapes=pack_scratch(rows, width, levels),
        compiler_params=pltpu.CompilerParams(vmem_limit_bytes=VMEM_LIMIT),
        name="pack_odd",
    )(plan, *in_hbm(arrays))


def crossing_kernel(levels, kind, plan, query, key, value, grad, *rest):
    count = len(levels)
    received, back, kept = rest[:count], rest[count:2 * count], rest[2 * count]
    own, staged_in, staged_out, result, own_sem, in_sem, out_sem, kept_sem = rest[2 * count + 1:]
    rows, width = query.shape
    edge = Edge(plan, kind, rows)
    jobs = edge.jobs
    own_part = tiles(edge.own, edge.own_rows)
    margin = rows

    def load_own(action):
        for which, array in enumerate((query, key, value, grad)):
            action(pltpu.make_async_copy(
                array.at[own_part], own.at[which, own_part], own_sem.at[which]))

    def keep(job):
        buffer = lax.rem(job, 2)
        return pltpu.make_async_copy(
            result.at[buffer, own_part], kept.at[job, own_part], kept_sem.at[buffer])

    position = lax.broadcasted_iota(jnp.int32, (rows, HEAD_DIM), 0)
    in_own = (position >= edge.own_begin) & (position < edge.own_end)
    key_position = lax.broadcasted_iota(jnp.int32, (rows, 1), 0)
    in_image = (key_position < edge.after) | (key_position >= rows - edge.before)
    in_window = (position < edge.after) | (position >= rows - edge.before)

    def one_job(step, carry):
        job = jnp.where(edge.lower, step, jobs - 1 - step)
        buffer = lax.rem(job, 2)
        start = margin + job * edge.other_rows - edge.other
        window = pl.ds(pl.multiple_of(start, TILE), rows)

        @pl.when(step >= 2)
        def _():
            keep(job).wait()

        zero = jnp.zeros((rows, HEAD_DIM), jnp.bfloat16)
        operands = []
        for which in range(4):
            columns = slice(which * HEAD_DIM, (which + 1) * HEAD_DIM)
            operands.append(jnp.where(
                in_own,
                own[which, :, lanes(edge.job_head + job)],
                jnp.where(in_window, staged_in[window, columns], zero),
            ))

        def store(which, part_rows, part):
            result[buffer, part_rows, which * HEAD_DIM:(which + 1) * HEAD_DIM] = part

        attention(*operands, lambda cols: in_image, store, CROSSING_CHUNK)
        staged_out[window, :] = result[buffer]
        keep(job).start()
        return carry

    @pl.when(jobs > 0)
    def _():
        stage = functools.partial(
            copy_pieces, levels, edge.level, staged_in, margin, received, in_sem, False)
        send = functools.partial(
            copy_pieces, levels, edge.level, staged_out, margin, back, out_sem, True)
        stage(START)
        load_own(START)
        load_own(WAIT)
        stage(WAIT)
        lax.fori_loop(0, jobs, one_job, 0)
        send(START)

        @pl.when(jobs >= 2)
        def _():
            keep(1).wait()

        keep(0).wait()
        send(WAIT)


def crossing_images(kind, plan, arrays, received, levels):
    rows, width = arrays[0].shape
    heads = width // HEAD_DIM
    four = 4 * HEAD_DIM
    count = len(levels)
    staged = pltpu.VMEM((rows + levels[-1] + rows, four), jnp.bfloat16)
    outs = pl.pallas_call(
        functools.partial(crossing_kernel, levels, kind),
        in_specs=[SCALARS] + [ANYWHERE] * (4 + count),
        out_specs=[ANYWHERE] * (count + 1),
        out_shape=piece_shapes(levels)
        + [pltpu.HBM((heads, rows, four), jnp.bfloat16)],
        scratch_shapes=[
            pltpu.VMEM((4, rows, width), jnp.bfloat16),
            staged,
            staged,
            pltpu.VMEM((2, rows, four), jnp.bfloat16),
            pltpu.SemaphoreType.DMA((4,)),
            pltpu.SemaphoreType.DMA((count,)),
            pltpu.SemaphoreType.DMA((count,)),
            pltpu.SemaphoreType.DMA((2,)),
        ],
        compiler_params=pltpu.CompilerParams(vmem_limit_bytes=VMEM_LIMIT),
        cost_estimate=pl.CostEstimate(
            flops=12 * rows * rows * width, bytes_accessed=16 * rows * width, transcendentals=0
        ),
        name="odd_edge_images" if kind == ODD else "even_edge_images",
    )(plan, *in_hbm(arrays), *received)
    return outs[:count], outs[count]


def overlay(whole, which, edge, first_head, heads, source):
    mixed = jnp.where(edge.lower, edge.first_block, edge.last_block - 1)
    full = jnp.where(edge.lower, edge.first_block + 1, edge.first_block)

    def one_head(slot, carry):
        place = lanes(first_head + slot)

        def one_block(step, carry):
            first = (full + step) * BLOCK
            part = pl.ds(pl.multiple_of(first, BLOCK), BLOCK)
            whole[which, part, place] = source(slot, first)
            return carry

        first = mixed * BLOCK
        part = pl.ds(pl.multiple_of(first, BLOCK), BLOCK)
        position = first + lax.broadcasted_iota(jnp.int32, (BLOCK, HEAD_DIM), 0)
        whole[which, part, place] = jnp.where(
            (position >= edge.own_begin) & (position < edge.own_end),
            source(slot, first),
            whole[which, part, place],
        )
        return lax.fori_loop(0, edge.last_block - edge.first_block - 1, one_block, carry)

    lax.fori_loop(0, heads, one_head, 0)


def returned_source(edge, staged, columns):
    def source(slot, first):
        start = BLOCK + slot * edge.own_rows + first - edge.own
        return staged[pl.ds(pl.multiple_of(start, TILE), BLOCK), columns]

    return source


def rest_kernel(done, plan, lengths, *rest):
    operands, before, kept = rest[:4], rest[4:8], rest[8:10]
    outs = rest[10:14]
    image_rows, held, held_sem = rest[14:]
    head = pl.program_id(0)
    rows = image_rows.shape[1]
    edges = [Edge(plan, kind, rows) for kind in (ODD, EVEN)]

    def kept_copy(kind, slot):
        part = tiles(edges[kind].own, edges[kind].own_rows)
        return pltpu.make_async_copy(
            kept[kind].at[slot, part], held.at[kind, slot, part], held_sem.at[kind, slot])

    @pl.when(head == 0)
    def _():
        for kind in (ODD, EVEN):
            def start(slot, carry):
                kept_copy(kind, slot).start()
                return carry

            lax.fori_loop(0, edges[kind].jobs, start, 0)

        find_images(lengths, image_rows)

    @pl.when(head < done)
    def _():
        for old, out in zip(before, outs):
            out[...] = old[...]

    @pl.when(head >= done)
    def _():
        local_head(operands, image_rows, outs)

    for kind in (ODD, EVEN):
        edge = edges[kind]
        slot = head - edge.job_head

        @pl.when((slot >= 0) & (slot < edge.jobs))
        def _():
            kept_copy(kind, slot).wait()

            def one_block(block, carry):
                first = block * BLOCK
                part = pl.ds(pl.multiple_of(first, BLOCK), BLOCK)
                position = first + lax.broadcasted_iota(jnp.int32, (BLOCK, HEAD_DIM), 0)
                wanted = (position >= edge.own_begin) & (position < edge.own_end)
                for which, out in enumerate(outs):
                    columns = slice(which * HEAD_DIM, (which + 1) * HEAD_DIM)
                    out[part, :] = jnp.where(wanted, held[kind, slot, part, columns], out[part, :])
                return carry

            lax.fori_loop(edge.first_block, edge.last_block, one_block, 0)


def rest_of_images(plan, lengths, arrays, done, local, kept_odd, kept_even):
    rows, width = arrays[0].shape
    heads = width // HEAD_DIM
    todo = pl.BlockSpec((rows, HEAD_DIM), lambda head: (0, jnp.maximum(head, done)))
    old = pl.BlockSpec((rows, HEAD_DIM), lambda head: (0, jnp.minimum(head, done - 1)))
    return pl.pallas_call(
        functools.partial(rest_kernel, done),
        grid=(heads,),
        in_specs=[SCALARS] * 2 + [todo] * 4 + [old] * 4 + [ANYWHERE] * 2,
        out_specs=[pl.BlockSpec((rows, HEAD_DIM), lambda head: (0, head))] * 4,
        out_shape=[pltpu.HBM((rows, width), jnp.bfloat16)] * 4,
        scratch_shapes=[
            pltpu.VMEM((8, rows), jnp.float32),
            pltpu.VMEM((2, heads, rows, 4 * HEAD_DIM), jnp.bfloat16),
            pltpu.SemaphoreType.DMA((2, heads)),
        ],
        compiler_params=pltpu.CompilerParams(vmem_limit_bytes=VMEM_LIMIT),
        cost_estimate=SCHEDULED_LAST,
        name="rest_of_images",
    )(plan, lengths, *in_hbm([*arrays, *local, kept_odd, kept_even]))


def return_kernel(levels, plan, *rest):
    counts = [len(levels[ODD]), len(levels[EVEN])]
    total = sum(counts)
    returned = rest[:counts[ODD]], rest[counts[ODD]:total]
    outs = rest[total + 4:total + 8]
    whole, odd_staged, even_staged, whole_sem, odd_sem, even_sem = rest[total + 8:]
    staged = odd_staged, even_staged
    rows = whole.shape[1]
    edges = [Edge(plan, kind, rows) for kind in (ODD, EVEN)]
    stages = [
        functools.partial(
            copy_pieces, levels[kind], edges[kind].level, staged[kind], BLOCK, returned[kind],
            sem, False)
        for kind, sem in ((ODD, odd_sem), (EVEN, even_sem))
    ]

    ends = []
    for edge, other in (edges, edges[::-1]):
        meets = jnp.logical_not(edge.lower) & (other.sent > 0)
        ends.append(jnp.where(
            meets, jnp.minimum(edge.last_block, other.first_block), edge.last_block))

    def move(kind, which, out, action):
        first, last = edges[kind].first_block, ends[kind]

        @pl.when((edges[kind].sent > 0) & (last > first))
        def _():
            part = pl.ds(
                pl.multiple_of(first * BLOCK, BLOCK), pl.multiple_of((last - first) * BLOCK, BLOCK))
            inside, outside = whole.at[which, part], outs[which].at[part]
            source, target = (inside, outside) if out else (outside, inside)
            action(pltpu.make_async_copy(source, target, whole_sem.at[kind, which]))

    for stage in stages:
        stage(START)
    for which in range(4):
        for kind in (ODD, EVEN):
            move(kind, which, False, START)
    for stage in stages:
        stage(WAIT)
    for which in range(4):
        columns = slice(which * HEAD_DIM, (which + 1) * HEAD_DIM)
        for kind in (ODD, EVEN):
            move(kind, which, False, WAIT)
        for kind in (ODD, EVEN):
            edge = edges[kind]
            overlay(whole, which, edge, edge.sent_head, edge.sent,
                    returned_source(edge, staged[kind], columns))
        for kind in (ODD, EVEN):
            move(kind, which, True, START)
    for which in range(4):
        for kind in (ODD, EVEN):
            move(kind, which, True, WAIT)


def merge_returned(plan, odd, even, outs, levels):
    rows, width = outs[0].shape
    counts = [len(levels[ODD]), len(levels[EVEN])]
    return pl.pallas_call(
        functools.partial(return_kernel, levels),
        in_specs=[SCALARS] + [ANYWHERE] * (sum(counts) + 4),
        out_specs=[ANYWHERE] * 4,
        out_shape=[pltpu.HBM((rows, width), jnp.bfloat16)] * 4,
        input_output_aliases={1 + sum(counts) + which: which for which in range(4)},
        scratch_shapes=[
            pltpu.VMEM((4, rows, width), jnp.bfloat16),
            pltpu.VMEM((levels[ODD][-1] + 2 * BLOCK, 4 * HEAD_DIM), jnp.bfloat16),
            pltpu.VMEM((levels[EVEN][-1] + 2 * BLOCK, 4 * HEAD_DIM), jnp.bfloat16),
            pltpu.SemaphoreType.DMA((2, 4)),
            pltpu.SemaphoreType.DMA((counts[ODD],)),
            pltpu.SemaphoreType.DMA((counts[EVEN],)),
        ],
        compiler_params=pltpu.CompilerParams(vmem_limit_bytes=VMEM_LIMIT),
        name="merge_returned",
    )(plan, *odd, *even, *in_hbm(outs))


def swapped(value, kind):
    first = 0 if kind == ODD else 1
    pairs = [(block, block + 1) for block in range(first, lax.axis_size("dp") - 1, 2)]
    return lax.ppermute(value, "dp", pairs + [(after, before) for before, after in pairs])


def swap_further(choices, odd, even):
    counts = [len(odd), len(even)]
    if not sum(counts):
        return [], []
    pairs = [(first, second) for first in range(counts[0] + 1) for second in range(counts[1] + 1)]

    def send(used, odd, even):
        return tuple(
            [
                swapped(array, kind) if number == used[kind] else array
                for number, array in enumerate(arrays, start=1)
            ]
            for kind, arrays in ((ODD, odd), (EVEN, even))
        )

    index = 0
    for choice, count in zip(choices, counts):
        if count:
            index = index * (count + 1) + choice[0]
    branches = [functools.partial(send, pair) for pair in pairs]
    return lax.switch(index, branches, list(odd), list(even))


def body(queries, keys, values, out_grad, lengths):
    rows, width = queries.shape
    arrays = (queries, keys, values, out_grad)
    levels = [size_levels(kind, rows, width // HEAD_DIM) for kind in (ODD, EVEN)]
    plan, choices, even = pack_even(lengths, arrays, levels, lax.axis_size("dp"))
    even_first = swapped(even[0], EVEN)
    odd = pack_odd(plan, arrays, levels[ODD])
    odd_first = swapped(odd[0], ODD)
    done = width // HEAD_DIM // 2 + 1
    local = local_attention(lengths, arrays, done)
    choices, local = lax.optimization_barrier((choices, local))
    _, more = swap_further(choices, [], even[1:])
    back_even, kept_even = crossing_images(EVEN, plan, arrays, [even_first, *more], levels[EVEN])
    choices, kept_even = lax.optimization_barrier((choices, kept_even))
    more, _ = swap_further(choices, odd[1:], [])
    received = [odd_first, *more]
    first, received = lax.optimization_barrier((back_even[0], received))
    even_first = swapped(first, EVEN)
    back_odd, kept_odd = crossing_images(ODD, plan, arrays, received, levels[ODD])
    odd_first = swapped(back_odd[0], ODD)
    kept_odd, local = lax.optimization_barrier((kept_odd, local))
    outs = rest_of_images(plan, lengths, arrays, done, local, kept_odd, kept_even)
    even_first, choices, outs = lax.optimization_barrier((even_first, choices, outs))
    more_odd, more_even = swap_further(choices, back_odd[1:], back_even[1:])
    return tuple(merge_returned(
        plan, [odd_first, *more_odd], [even_first, *more_even], outs, levels))


def solution(mesh):
    in_specs = (P("dp", "tensor"), P("dp", "tensor"), P("dp", "tensor"), P("dp", "tensor"), P())
    out_specs = (P("dp", "tensor"), P("dp", "tensor"), P("dp", "tensor"), P("dp", "tensor"))
    return jax.shard_map(body, mesh=mesh, in_specs=in_specs, out_specs=out_specs, check_vma=False)
```

```python
import functools
import math

import jax
import jax.numpy as jnp
from jax import lax
from jax.experimental import pallas as pl
from jax.experimental.pallas import tpu as pltpu
from jax.sharding import PartitionSpec as P

HEAD_DIM = 128
TILE = 16
BLOCK = 64
LOCAL_CHUNK = 256
CROSSING_CHUNK = 256
FACTOR = 1.0 / math.sqrt(HEAD_DIM)
LOG2E = 1.4426950408889634
VMEM_LIMIT = 32 * 1024 * 1024
PACK_VMEM_LIMIT = 60 * 1024 * 1024

SCHEDULED_LAST = pl.CostEstimate(flops=1, bytes_accessed=1, transcendentals=0)

FIELDS = 8
BEFORE, AFTER, LOWER, JOBS, JOB_HEAD, SENT, SENT_HEAD, LEVEL = range(FIELDS)
ODD, EVEN = 0, 1

LEVEL_UNITS = ((9, 10, 11, 12, 13), (9, 10, 11, 12, 13))


def round_up(value):
    return (value + (TILE - 1)) & -TILE


def blocks_of(value, size):
    if size & (size - 1):
        return value // size
    return lax.shift_right_logical(value, jnp.int32(size.bit_length() - 1))


def worst_case_rows(rows, heads):
    worst = 0
    for before in range(TILE, rows + 1, TILE):
        for after in range(TILE, rows + TILE - before + 1, TILE):
            needed = min(max(after * low, before * (heads - low)) for low in range(heads + 1))
            worst = max(worst, needed)
    return worst


def size_levels(kind, rows, heads):
    unit = rows * heads // 48
    most = worst_case_rows(rows, heads)
    below = sorted(int(level * unit) for level in LEVEL_UNITS[kind] if level * unit < most)
    return tuple(below) + (most,)


def find_crossings(rows, blocks, lengths, before_edge, after_edge):
    def clear(edge, carry):
        before_edge[edge] = 0
        after_edge[edge] = 0
        return carry

    lax.fori_loop(0, blocks + 1, clear, 0)

    def place(image, start):
        end = start + lengths[image]
        edge = blocks_of(end - 1, rows)

        @pl.when(edge > blocks_of(start, rows))
        def _():
            before_edge[edge] = edge * rows - start
            after_edge[edge] = end - edge * rows

        return end

    lax.fori_loop(0, lengths.shape[0], place, 0)


def own_edge(kind, before_edge, after_edge):
    block = lax.axis_index("dp")
    lower = lax.rem(block, 2) == (0 if kind == ODD else 1)
    edge = jnp.where(lower, block + 1, block)
    return lower, before_edge[edge], after_edge[edge]


def make_plan(heads, blocks, levels, plan, choices, before_edge, after_edge):
    entry = lax.broadcasted_iota(jnp.int32, (8, 128), 1)
    for kind in (ODD, EVEN):
        limit = jnp.full((8, 128), levels[kind][-1], jnp.int32)
        for number, level in enumerate(levels[kind]):
            limit = jnp.where(entry == number, level, limit)

        def check(number, fits):
            edge = 2 * number + (1 if kind == ODD else 2)
            after = round_up(after_edge[edge])
            before = round_up(before_edge[edge])
            taken = jnp.zeros((8, 128), jnp.int32)
            for count in range(1, heads + 1):
                taken += jnp.where(after * count <= limit, 1, 0)
                taken += jnp.where(before * count <= limit, 1, 0)
            return jnp.minimum(fits, jnp.where(taken >= heads, 1, 0))

        last = len(levels[kind]) - 1
        chosen = jnp.int32(last)
        if last:
            edges = (blocks - (0 if kind == ODD else 1)) // 2
            fits = lax.fori_loop(0, edges, check, jnp.ones((8, 128), jnp.int32))
            chosen = jnp.min(jnp.where(fits == 1, entry, last))
        most_rows = jnp.int32(levels[kind][-1])
        for number, level in enumerate(levels[kind][:-1]):
            most_rows = jnp.where(chosen == number, level, most_rows)

        lower, before, after = own_edge(kind, before_edge, after_edge)
        most = jnp.int32(0)
        least = jnp.int32(heads)
        for count in range(1, heads + 1):
            most += jnp.where(round_up(after) * count <= most_rows, 1, 0)
            least -= jnp.where(round_up(before) * count <= most_rows, 1, 0)
        low = jnp.clip(jnp.int32(heads // 2), least, most)
        crossed = before > 0
        base = kind * FIELDS
        plan[base + BEFORE] = before
        plan[base + AFTER] = after
        plan[base + LOWER] = lower.astype(jnp.int32)
        plan[base + JOBS] = jnp.where(crossed, jnp.where(lower, low, heads - low), 0)
        plan[base + JOB_HEAD] = jnp.where(lower, 0, low)
        plan[base + SENT] = jnp.where(crossed, jnp.where(lower, heads - low, low), 0)
        plan[base + SENT_HEAD] = jnp.where(lower, low, 0)
        plan[base + LEVEL] = chosen
        choices[kind][0] = chosen


class Edge:
    def __init__(self, plan, kind, rows):
        read = lambda field: plan[kind * FIELDS + field]
        self.lower = read(LOWER) == 1
        self.jobs, self.job_head = read(JOBS), read(JOB_HEAD)
        self.sent, self.sent_head = read(SENT), read(SENT_HEAD)
        self.level = read(LEVEL)
        before, after = read(BEFORE), read(AFTER)
        self.before, self.after = before, after
        self.own_begin = jnp.where(self.lower, rows - before, 0)
        self.own_end = jnp.where(self.lower, rows, after)
        self.own_rows = round_up(jnp.where(self.lower, before, after))
        self.other_rows = round_up(jnp.where(self.lower, after, before))
        self.own = jnp.where(self.lower, rows - self.own_rows, 0)
        self.other = jnp.where(self.lower, 0, rows - self.other_rows)
        self.first_block = blocks_of(self.own_begin, BLOCK)
        self.last_block = blocks_of(self.own_end + BLOCK - 1, BLOCK)


def tiles(start, size):
    return pl.ds(pl.multiple_of(start, TILE), pl.multiple_of(size, TILE))


def lanes(head):
    return pl.ds(pl.multiple_of(head * HEAD_DIM, HEAD_DIM), HEAD_DIM)


def attention(query, key, value, grad, mask_columns, store, chunk):
    count = query.shape[0]
    key_t = key.T
    value_t = value.T
    grad_t = grad.T
    across = (((1,), (1,)), ((), ()))
    chunks = [slice(first, first + chunk) for first in range(0, count, chunk)]
    scores = [
        lax.dot_general(key, query[cols], across, preferred_element_type=jnp.float32)
        for cols in chunks
    ]
    grad_probs = [
        lax.dot_general(value, grad[cols], across, preferred_element_type=jnp.float32)
        for cols in chunks
    ]
    probs_low = []
    grad_scores = []
    for number, cols in enumerate(chunks):
        masked = jnp.where(mask_columns(cols), scores[number], -1e30)
        top = jnp.max(masked, axis=0, keepdims=True)
        weights = jnp.exp2((masked - top) * (FACTOR * LOG2E))
        total = jnp.sum(weights, axis=0, keepdims=True)
        probs = weights * (1.0 / total)
        probs_low.append(probs.astype(jnp.bfloat16))
        result_t = jnp.dot(value_t, probs_low[-1], preferred_element_type=jnp.float32)
        result_t = result_t.astype(jnp.bfloat16)
        centre = jnp.sum(
            grad_t[:, cols].astype(jnp.float32) * result_t.astype(jnp.float32),
            axis=0,
            keepdims=True,
        )
        grad_scores.append((probs * (grad_probs[number] - centre)).astype(jnp.bfloat16))
        grad_query_t = jnp.dot(key_t, grad_scores[-1], preferred_element_type=jnp.float32) * FACTOR
        store(0, cols, result_t.T)
        store(1, cols, grad_query_t.astype(jnp.bfloat16).T)
    probs_low = jnp.concatenate(probs_low, axis=1)
    grad_scores = jnp.concatenate(grad_scores, axis=1)
    grad_value = jnp.dot(probs_low, grad, preferred_element_type=jnp.float32)
    store(3, slice(None), grad_value.astype(jnp.bfloat16))
    grad_key = jnp.dot(grad_scores, query, preferred_element_type=jnp.float32)
    store(2, slice(None), (grad_key * FACTOR).astype(jnp.bfloat16))


def find_images(lengths, image_rows):
    count = image_rows.shape[1]
    position = lax.axis_index("dp") * count + lax.broadcasted_iota(jnp.int32, (8, count), 1)

    def place(image, carry):
        start, begin = carry
        return start + lengths[image], jnp.where(position >= start, start, begin)

    first = (jnp.int32(0), jnp.zeros((8, count), jnp.int32))
    _, begin = lax.fori_loop(0, lengths.shape[0], place, first)
    image_rows[...] = begin.astype(jnp.float32)


def local_head(operands, image_rows, outs):
    image_col = image_rows[...].T[:, :1]

    def store(which, rows, part):
        outs[which][rows, :] = part

    attention(
        *(operand[...] for operand in operands),
        lambda cols: image_col == image_rows[:1, cols],
        store,
        LOCAL_CHUNK,
    )


def local_kernel(lengths, *rest):
    operands, outs, image_rows = rest[:4], rest[4:8], rest[8]

    @pl.when(pl.program_id(0) == 0)
    def _():
        find_images(lengths, image_rows)

    local_head(operands, image_rows, outs)


def local_attention(lengths, arrays, heads):
    rows, width = arrays[0].shape
    block = pl.BlockSpec((rows, HEAD_DIM), lambda head: (0, head))
    return pl.pallas_call(
        local_kernel,
        grid=(heads,),
        in_specs=[SCALARS] + [block] * 4,
        out_specs=[block] * 4,
        out_shape=[pltpu.HBM((rows, width), jnp.bfloat16)] * 4,
        scratch_shapes=[pltpu.VMEM((8, rows), jnp.float32)],
        compiler_params=pltpu.CompilerParams(vmem_limit_bytes=VMEM_LIMIT),
        cost_estimate=SCHEDULED_LAST,
        name="local_images",
    )(lengths, *in_hbm(arrays))


START = lambda copy: copy.start()
WAIT = lambda copy: copy.wait()
ANYWHERE = pl.BlockSpec(memory_space=pl.ANY)
SCALARS = pl.BlockSpec(memory_space=pltpu.SMEM)


def in_hbm(arrays):
    return [pltpu.with_memory_space_constraint(array, pltpu.HBM) for array in arrays]


def pieces(levels):
    return [(0, levels[0])] + [(levels[0], level - levels[0]) for level in levels[1:]]


def piece_shapes(levels):
    return [pltpu.HBM((size, 4 * HEAD_DIM), jnp.bfloat16) for _, size in pieces(levels)]


def copy_pieces(levels, level, used, staged, offset, arrays, sems, out, action, first=0):
    for number, (start, size) in enumerate(pieces(levels)):
        if number < first:
            continue
        taken = jnp.clip(used - start, 0, size)
        inside = staged.at[tiles(offset + start, taken)]
        outside = arrays[number].at[tiles(0, taken)]
        source, target = (inside, outside) if out else (outside, inside)

        @pl.when((taken > 0) & (True if number == 0 else level == number))
        def _():
            action(pltpu.make_async_copy(source, target, sems.at[number]))


def gather(edge, held, staged):
    steps = blocks_of(edge.own_rows + BLOCK - 1, BLOCK)

    def one_head(slot, carry):
        def one_block(step, carry):
            source = pl.ds(pl.multiple_of(edge.own + step * BLOCK, TILE), BLOCK)
            target = pl.ds(pl.multiple_of(slot * edge.own_rows + step * BLOCK, TILE), BLOCK)
            for which in range(4):
                staged[target, which * HEAD_DIM:(which + 1) * HEAD_DIM] = held[
                    which, source, lanes(edge.sent_head + slot)]
            return carry

        return lax.fori_loop(0, steps, one_block, carry)

    lax.fori_loop(0, edge.sent, one_head, 0)


def pack_even_kernel(levels, blocks, lengths, query, key, value, grad, *rest):
    count = len(levels[EVEN])
    plan, choices, outs = rest[0], rest[1:3], rest[3:3 + count]
    before_edge, after_edge, held, staged, load_sem, out_sem, far_sem = rest[3 + count:]
    rows, width = query.shape
    half = rows // 2
    block = lax.axis_index("dp")
    near = tiles(jnp.where(lax.rem(block, 2) == 1, rows - half, 0), half)
    operands = (query, key, value, grad)

    def load(part, sem):
        return [
            pltpu.make_async_copy(array.at[part], held.at[which, part], sem.at[which])
            for which, array in enumerate(operands)
        ]

    near_loads = load(near, load_sem)
    for copy in near_loads:
        copy.start()
    find_crossings(rows, blocks, lengths, before_edge, after_edge)
    lower, before, after = own_edge(EVEN, before_edge, after_edge)
    own_rows = round_up(jnp.where(lower, before, after))
    far_rows = jnp.maximum(own_rows - half, 0)
    far_loads = load(tiles(jnp.where(lower, rows - half - far_rows, half), far_rows), far_sem)

    @pl.when(far_rows > 0)
    def _():
        for copy in far_loads:
            copy.start()

    make_plan(width // HEAD_DIM, blocks, levels, plan, choices, before_edge, after_edge)
    for copy in near_loads:
        copy.wait()

    @pl.when(far_rows > 0)
    def _():
        for copy in far_loads:
            copy.wait()

    @pl.when(before > 0)
    def _():
        edge = Edge(plan, EVEN, rows)
        gather(edge, held, staged)
        send = functools.partial(
            copy_pieces, levels[EVEN], edge.level, edge.sent * edge.own_rows, staged, 0, outs,
            out_sem, True, first=1)
        send(START)
        outs[0][...] = staged[:outs[0].shape[0], :]
        send(WAIT)


def pack_odd_kernel(levels, plan, query, key, value, grad, *rest):
    count = len(levels)
    outs = rest[:count]
    held, staged, load_sem, out_sem = rest[count:]
    rows = query.shape[0]
    edge = Edge(plan, ODD, rows)
    part = tiles(edge.own, edge.own_rows)
    loads = [
        pltpu.make_async_copy(array.at[part], held.at[which, part], load_sem.at[which])
        for which, array in enumerate((query, key, value, grad))
    ]

    @pl.when(edge.sent > 0)
    def _():
        for copy in loads:
            copy.start()
        for copy in loads:
            copy.wait()
        gather(edge, held, staged)
        move = functools.partial(
            copy_pieces, levels, edge.level, edge.sent * edge.own_rows, staged, 0, outs,
            out_sem, True)
        move(START)
        move(WAIT)


def pack_scratch(rows, width, levels):
    return [
        pltpu.VMEM((4, rows + BLOCK, width), jnp.bfloat16),
        pltpu.VMEM((levels[-1] + BLOCK, 4 * HEAD_DIM), jnp.bfloat16),
        pltpu.SemaphoreType.DMA((4,)),
        pltpu.SemaphoreType.DMA((len(levels),)),
    ]


def pack_even(lengths, arrays, levels, blocks):
    rows, width = arrays[0].shape
    one = jax.ShapeDtypeStruct((1,), jnp.int32)
    plan, odd_level, even_level, *even = pl.pallas_call(
        functools.partial(pack_even_kernel, levels, blocks),
        in_specs=[SCALARS] + [ANYWHERE] * 4,
        out_specs=[SCALARS] * 3 + [pl.BlockSpec(memory_space=pltpu.VMEM)]
        + [ANYWHERE] * (len(levels[EVEN]) - 1),
        out_shape=[jax.ShapeDtypeStruct((2 * FIELDS,), jnp.int32), one, one]
        + [pltpu.VMEM((levels[EVEN][0], 4 * HEAD_DIM), jnp.bfloat16)]
        + piece_shapes(levels[EVEN])[1:],
        scratch_shapes=[
            pltpu.SMEM((blocks + 2,), jnp.int32),
            pltpu.SMEM((blocks + 2,), jnp.int32),
        ] + pack_scratch(rows, width, levels[EVEN]) + [pltpu.SemaphoreType.DMA((4,))],
        compiler_params=pltpu.CompilerParams(vmem_limit_bytes=PACK_VMEM_LIMIT),
        name="pack_even",
    )(lengths, *in_hbm(arrays))
    return plan, (odd_level, even_level), even


def pack_odd(plan, arrays, levels):
    rows, width = arrays[0].shape
    return pl.pallas_call(
        functools.partial(pack_odd_kernel, levels),
        in_specs=[SCALARS] + [ANYWHERE] * 4,
        out_specs=[ANYWHERE] * len(levels),
        out_shape=piece_shapes(levels),
        scratch_shapes=pack_scratch(rows, width, levels),
        compiler_params=pltpu.CompilerParams(vmem_limit_bytes=VMEM_LIMIT),
        name="pack_odd",
    )(plan, *in_hbm(arrays))


def crossing_kernel(levels, kind, plan, query, key, value, grad, *rest):
    count = len(levels)
    received, back, kept = rest[:count], rest[count:2 * count], rest[2 * count]
    own, staged_in, staged_out, result, own_sem, in_sem, out_sem, kept_sem = rest[2 * count + 1:]
    rows, width = query.shape
    edge = Edge(plan, kind, rows)
    jobs = edge.jobs
    own_part = tiles(edge.own, edge.own_rows)
    margin = rows

    def load_own(action):
        for which, array in enumerate((query, key, value, grad)):
            action(pltpu.make_async_copy(
                array.at[own_part], own.at[which, own_part], own_sem.at[which]))

    def keep(job):
        buffer = lax.rem(job, 2)
        return pltpu.make_async_copy(
            result.at[buffer, own_part], kept.at[job, own_part], kept_sem.at[buffer])

    position = lax.broadcasted_iota(jnp.int32, (rows, HEAD_DIM), 0)
    in_own = (position >= edge.own_begin) & (position < edge.own_end)
    key_position = lax.broadcasted_iota(jnp.int32, (rows, 1), 0)
    in_image = (key_position < edge.after) | (key_position >= rows - edge.before)
    in_window = (position < edge.after) | (position >= rows - edge.before)

    def one_job(step, carry):
        job = jnp.where(edge.lower, step, jobs - 1 - step)
        buffer = lax.rem(job, 2)
        start = margin + job * edge.other_rows - edge.other
        window = pl.ds(pl.multiple_of(start, TILE), rows)

        @pl.when(step >= 2)
        def _():
            keep(job).wait()

        zero = jnp.zeros((rows, HEAD_DIM), jnp.bfloat16)
        operands = []
        for which in range(4):
            columns = slice(which * HEAD_DIM, (which + 1) * HEAD_DIM)
            operands.append(jnp.where(
                in_own,
                own[which, :, lanes(edge.job_head + job)],
                jnp.where(in_window, staged_in[window, columns], zero),
            ))

        def store(which, part_rows, part):
            result[buffer, part_rows, which * HEAD_DIM:(which + 1) * HEAD_DIM] = part

        attention(*operands, lambda cols: in_image, store, CROSSING_CHUNK)
        staged_out[window, :] = result[buffer]
        keep(job).start()
        return carry

    @pl.when(jobs > 0)
    def _():
        stage = functools.partial(
            copy_pieces, levels, edge.level, jobs * edge.other_rows, staged_in, margin, received,
            in_sem, False)
        send = functools.partial(
            copy_pieces, levels, edge.level, jobs * edge.other_rows, staged_out, margin, back,
            out_sem, True)
        stage(START)
        load_own(START)
        load_own(WAIT)
        stage(WAIT)
        lax.fori_loop(0, jobs, one_job, 0)
        send(START)

        @pl.when(jobs >= 2)
        def _():
            keep(1).wait()

        keep(0).wait()
        send(WAIT)


def crossing_images(kind, plan, arrays, received, levels):
    rows, width = arrays[0].shape
    heads = width // HEAD_DIM
    four = 4 * HEAD_DIM
    count = len(levels)
    staged = pltpu.VMEM((rows + levels[-1] + rows, four), jnp.bfloat16)
    outs = pl.pallas_call(
        functools.partial(crossing_kernel, levels, kind),
        in_specs=[SCALARS] + [ANYWHERE] * (4 + count),
        out_specs=[ANYWHERE] * (count + 1),
        out_shape=piece_shapes(levels)
        + [pltpu.HBM((heads, rows, four), jnp.bfloat16)],
        scratch_shapes=[
            pltpu.VMEM((4, rows, width), jnp.bfloat16),
            staged,
            staged,
            pltpu.VMEM((2, rows, four), jnp.bfloat16),
            pltpu.SemaphoreType.DMA((4,)),
            pltpu.SemaphoreType.DMA((count,)),
            pltpu.SemaphoreType.DMA((count,)),
            pltpu.SemaphoreType.DMA((2,)),
        ],
        compiler_params=pltpu.CompilerParams(vmem_limit_bytes=VMEM_LIMIT),
        cost_estimate=pl.CostEstimate(
            flops=12 * rows * rows * width, bytes_accessed=16 * rows * width, transcendentals=0
        ),
        name="odd_edge_images" if kind == ODD else "even_edge_images",
    )(plan, *in_hbm(arrays), *received)
    return outs[:count], outs[count]


def overlay(whole, which, edge, first_head, heads, source):
    mixed = jnp.where(edge.lower, edge.first_block, edge.last_block - 1)
    full = jnp.where(edge.lower, edge.first_block + 1, edge.first_block)

    def one_head(slot, carry):
        place = lanes(first_head + slot)

        def one_block(step, carry):
            first = (full + step) * BLOCK
            part = pl.ds(pl.multiple_of(first, BLOCK), BLOCK)
            whole[which, part, place] = source(slot, first)
            return carry

        first = mixed * BLOCK
        part = pl.ds(pl.multiple_of(first, BLOCK), BLOCK)
        position = first + lax.broadcasted_iota(jnp.int32, (BLOCK, HEAD_DIM), 0)
        whole[which, part, place] = jnp.where(
            (position >= edge.own_begin) & (position < edge.own_end),
            source(slot, first),
            whole[which, part, place],
        )
        return lax.fori_loop(0, edge.last_block - edge.first_block - 1, one_block, carry)

    lax.fori_loop(0, heads, one_head, 0)


def returned_source(edge, staged, columns):
    def source(slot, first):
        start = BLOCK + slot * edge.own_rows + first - edge.own
        return staged[pl.ds(pl.multiple_of(start, TILE), BLOCK), columns]

    return source


def rest_kernel(done, plan, lengths, *rest):
    operands, before, kept = rest[:4], rest[4:8], rest[8:10]
    outs = rest[10:14]
    image_rows, held, held_sem = rest[14:]
    head = pl.program_id(0)
    rows = image_rows.shape[1]
    edges = [Edge(plan, kind, rows) for kind in (ODD, EVEN)]

    def kept_copy(kind, slot):
        part = tiles(edges[kind].own, edges[kind].own_rows)
        return pltpu.make_async_copy(
            kept[kind].at[slot, part], held.at[kind, slot, part], held_sem.at[kind, slot])

    @pl.when(head == 0)
    def _():
        for kind in (ODD, EVEN):
            def start(slot, carry):
                kept_copy(kind, slot).start()
                return carry

            lax.fori_loop(0, edges[kind].jobs, start, 0)

        find_images(lengths, image_rows)

    @pl.when(head < done)
    def _():
        for old, out in zip(before, outs):
            out[...] = old[...]

    @pl.when(head >= done)
    def _():
        local_head(operands, image_rows, outs)

    for kind in (ODD, EVEN):
        edge = edges[kind]
        slot = head - edge.job_head

        @pl.when((slot >= 0) & (slot < edge.jobs))
        def _():
            kept_copy(kind, slot).wait()

            def one_block(block, carry):
                first = block * BLOCK
                part = pl.ds(pl.multiple_of(first, BLOCK), BLOCK)
                position = first + lax.broadcasted_iota(jnp.int32, (BLOCK, HEAD_DIM), 0)
                wanted = (position >= edge.own_begin) & (position < edge.own_end)
                for which, out in enumerate(outs):
                    columns = slice(which * HEAD_DIM, (which + 1) * HEAD_DIM)
                    out[part, :] = jnp.where(wanted, held[kind, slot, part, columns], out[part, :])
                return carry

            lax.fori_loop(edge.first_block, edge.last_block, one_block, 0)


def rest_of_images(plan, lengths, arrays, done, local, kept_odd, kept_even):
    rows, width = arrays[0].shape
    heads = width // HEAD_DIM
    todo = pl.BlockSpec((rows, HEAD_DIM), lambda head: (0, jnp.maximum(head, done)))
    old = pl.BlockSpec((rows, HEAD_DIM), lambda head: (0, jnp.minimum(head, done - 1)))
    return pl.pallas_call(
        functools.partial(rest_kernel, done),
        grid=(heads,),
        in_specs=[SCALARS] * 2 + [todo] * 4 + [old] * 4 + [ANYWHERE] * 2,
        out_specs=[pl.BlockSpec((rows, HEAD_DIM), lambda head: (0, head))] * 4,
        out_shape=[pltpu.HBM((rows, width), jnp.bfloat16)] * 4,
        scratch_shapes=[
            pltpu.VMEM((8, rows), jnp.float32),
            pltpu.VMEM((2, heads, rows, 4 * HEAD_DIM), jnp.bfloat16),
            pltpu.SemaphoreType.DMA((2, heads)),
        ],
        compiler_params=pltpu.CompilerParams(vmem_limit_bytes=VMEM_LIMIT),
        cost_estimate=SCHEDULED_LAST,
        name="rest_of_images",
    )(plan, lengths, *in_hbm([*arrays, *local, kept_odd, kept_even]))


def return_kernel(levels, plan, *rest):
    counts = [len(levels[ODD]), len(levels[EVEN])]
    total = sum(counts)
    returned = rest[:counts[ODD]], rest[counts[ODD]:total]
    outs = rest[total + 4:total + 8]
    whole, odd_staged, even_staged, whole_sem, odd_sem, even_sem = rest[total + 8:]
    staged = odd_staged, even_staged
    rows = whole.shape[1]
    edges = [Edge(plan, kind, rows) for kind in (ODD, EVEN)]
    stages = [
        functools.partial(
            copy_pieces, levels[kind], edges[kind].level, edges[kind].sent * edges[kind].own_rows,
            staged[kind], BLOCK, returned[kind], sem, False)
        for kind, sem in ((ODD, odd_sem), (EVEN, even_sem))
    ]

    ends = []
    for edge, other in (edges, edges[::-1]):
        meets = jnp.logical_not(edge.lower) & (other.sent > 0)
        ends.append(jnp.where(
            meets, jnp.minimum(edge.last_block, other.first_block), edge.last_block))

    def move(kind, which, out, action):
        first, last = edges[kind].first_block, ends[kind]

        @pl.when((edges[kind].sent > 0) & (last > first))
        def _():
            part = pl.ds(
                pl.multiple_of(first * BLOCK, BLOCK), pl.multiple_of((last - first) * BLOCK, BLOCK))
            inside, outside = whole.at[which, part], outs[which].at[part]
            source, target = (inside, outside) if out else (outside, inside)
            action(pltpu.make_async_copy(source, target, whole_sem.at[kind, which]))

    for stage in stages:
        stage(START)
    for which in range(4):
        for kind in (ODD, EVEN):
            move(kind, which, False, START)
    for stage in stages:
        stage(WAIT)
    for which in range(4):
        columns = slice(which * HEAD_DIM, (which + 1) * HEAD_DIM)
        for kind in (ODD, EVEN):
            move(kind, which, False, WAIT)
        for kind in (ODD, EVEN):
            edge = edges[kind]
            overlay(whole, which, edge, edge.sent_head, edge.sent,
                    returned_source(edge, staged[kind], columns))
        for kind in (ODD, EVEN):
            move(kind, which, True, START)
    for which in range(4):
        for kind in (ODD, EVEN):
            move(kind, which, True, WAIT)


def merge_returned(plan, odd, even, outs, levels):
    rows, width = outs[0].shape
    counts = [len(levels[ODD]), len(levels[EVEN])]
    return pl.pallas_call(
        functools.partial(return_kernel, levels),
        in_specs=[SCALARS] + [ANYWHERE] * (sum(counts) + 4),
        out_specs=[ANYWHERE] * 4,
        out_shape=[pltpu.HBM((rows, width), jnp.bfloat16)] * 4,
        input_output_aliases={1 + sum(counts) + which: which for which in range(4)},
        scratch_shapes=[
            pltpu.VMEM((4, rows, width), jnp.bfloat16),
            pltpu.VMEM((levels[ODD][-1] + 2 * BLOCK, 4 * HEAD_DIM), jnp.bfloat16),
            pltpu.VMEM((levels[EVEN][-1] + 2 * BLOCK, 4 * HEAD_DIM), jnp.bfloat16),
            pltpu.SemaphoreType.DMA((2, 4)),
            pltpu.SemaphoreType.DMA((counts[ODD],)),
            pltpu.SemaphoreType.DMA((counts[EVEN],)),
        ],
        compiler_params=pltpu.CompilerParams(vmem_limit_bytes=VMEM_LIMIT),
        name="merge_returned",
    )(plan, *odd, *even, *in_hbm(outs))


def swapped(value, kind):
    first = 0 if kind == ODD else 1
    pairs = [(block, block + 1) for block in range(first, lax.axis_size("dp") - 1, 2)]
    return lax.ppermute(value, "dp", pairs + [(after, before) for before, after in pairs])


def swap_further(choices, odd, even):
    counts = [len(odd), len(even)]
    if not sum(counts):
        return [], []
    pairs = [(first, second) for first in range(counts[0] + 1) for second in range(counts[1] + 1)]

    def send(used, odd, even):
        return tuple(
            [
                swapped(array, kind) if number == used[kind] else array
                for number, array in enumerate(arrays, start=1)
            ]
            for kind, arrays in ((ODD, odd), (EVEN, even))
        )

    index = 0
    for choice, count in zip(choices, counts):
        if count:
            index = index * (count + 1) + choice[0]
    branches = [functools.partial(send, pair) for pair in pairs]
    return lax.switch(index, branches, list(odd), list(even))


def body(queries, keys, values, out_grad, lengths):
    rows, width = queries.shape
    arrays = (queries, keys, values, out_grad)
    levels = [size_levels(kind, rows, width // HEAD_DIM) for kind in (ODD, EVEN)]
    plan, choices, even = pack_even(lengths, arrays, levels, lax.axis_size("dp"))
    even_first = swapped(even[0], EVEN)
    odd = pack_odd(plan, arrays, levels[ODD])
    odd_first = swapped(odd[0], ODD)
    done = width // HEAD_DIM // 2
    local = local_attention(lengths, arrays, done)
    choices, local = lax.optimization_barrier((choices, local))
    _, more = swap_further(choices, [], even[1:])
    back_even, kept_even = crossing_images(EVEN, plan, arrays, [even_first, *more], levels[EVEN])
    choices, kept_even = lax.optimization_barrier((choices, kept_even))
    more, _ = swap_further(choices, odd[1:], [])
    received = [odd_first, *more]
    first, received = lax.optimization_barrier((back_even[0], received))
    even_first = swapped(first, EVEN)
    back_odd, kept_odd = crossing_images(ODD, plan, arrays, received, levels[ODD])
    odd_first = swapped(back_odd[0], ODD)
    kept_odd, local = lax.optimization_barrier((kept_odd, local))
    outs = rest_of_images(plan, lengths, arrays, done, local, kept_odd, kept_even)
    even_first, choices, outs = lax.optimization_barrier((even_first, choices, outs))
    more_odd, more_even = swap_further(choices, back_odd[1:], back_even[1:])
    return tuple(merge_returned(
        plan, [odd_first, *more_odd], [even_first, *more_even], outs, levels))


def solution(mesh):
    in_specs = (P("dp", "tensor"), P("dp", "tensor"), P("dp", "tensor"), P("dp", "tensor"), P())
    out_specs = (P("dp", "tensor"), P("dp", "tensor"), P("dp", "tensor"), P("dp", "tensor"))
    return jax.shard_map(body, mesh=mesh, in_specs=in_specs, out_specs=out_specs, check_vma=False)
```

```python
import functools
import math

import jax
import jax.numpy as jnp
from jax import lax
from jax.experimental import pallas as pl
from jax.experimental.pallas import tpu as pltpu
from jax.sharding import PartitionSpec as P

HEAD_DIM = 128
TILE = 16
BLOCK = 64
LOCAL_CHUNK = 256
CROSSING_CHUNK = 128
FACTOR = 1.0 / math.sqrt(HEAD_DIM)
LOG2E = 1.4426950408889634
VMEM_LIMIT = 32 * 1024 * 1024
PACK_VMEM_LIMIT = 60 * 1024 * 1024

SCHEDULED_LAST = pl.CostEstimate(flops=1, bytes_accessed=1, transcendentals=0)

FIELDS = 8
BEFORE, AFTER, LOWER, JOBS, JOB_HEAD, SENT, SENT_HEAD, LEVEL = range(FIELDS)
ODD, EVEN = 0, 1

LEVEL_UNITS = ((9, 10, 11, 12, 13), (9, 10, 11, 12, 13))


def round_up(value):
    return (value + (TILE - 1)) & -TILE


def blocks_of(value, size):
    if size & (size - 1):
        return value // size
    return lax.shift_right_logical(value, jnp.int32(size.bit_length() - 1))


def worst_case_rows(rows, heads):
    worst = 0
    for before in range(TILE, rows + 1, TILE):
        for after in range(TILE, rows + TILE - before + 1, TILE):
            needed = min(max(after * low, before * (heads - low)) for low in range(heads + 1))
            worst = max(worst, needed)
    return worst


def size_levels(kind, rows, heads):
    unit = rows * heads // 48
    most = worst_case_rows(rows, heads)
    below = sorted(int(level * unit) for level in LEVEL_UNITS[kind] if level * unit < most)
    return tuple(below) + (most,)


def find_crossings(rows, blocks, lengths, before_edge, after_edge):
    def clear(edge, carry):
        before_edge[edge] = 0
        after_edge[edge] = 0
        return carry

    lax.fori_loop(0, blocks + 1, clear, 0)

    def place(image, start):
        end = start + lengths[image]
        edge = blocks_of(end - 1, rows)

        @pl.when(edge > blocks_of(start, rows))
        def _():
            before_edge[edge] = edge * rows - start
            after_edge[edge] = end - edge * rows

        return end

    lax.fori_loop(0, lengths.shape[0], place, 0)


def own_edge(kind, before_edge, after_edge):
    block = lax.axis_index("dp")
    lower = lax.rem(block, 2) == (0 if kind == ODD else 1)
    edge = jnp.where(lower, block + 1, block)
    return lower, before_edge[edge], after_edge[edge]


def make_plan(heads, blocks, levels, plan, choices, before_edge, after_edge):
    entry = lax.broadcasted_iota(jnp.int32, (8, 128), 1)
    for kind in (ODD, EVEN):
        limit = jnp.full((8, 128), levels[kind][-1], jnp.int32)
        for number, level in enumerate(levels[kind]):
            limit = jnp.where(entry == number, level, limit)

        def check(number, fits):
            edge = 2 * number + (1 if kind == ODD else 2)
            after = round_up(after_edge[edge])
            before = round_up(before_edge[edge])
            taken = jnp.zeros((8, 128), jnp.int32)
            for count in range(1, heads + 1):
                taken += jnp.where(after * count <= limit, 1, 0)
                taken += jnp.where(before * count <= limit, 1, 0)
            return jnp.minimum(fits, jnp.where(taken >= heads, 1, 0))

        last = len(levels[kind]) - 1
        chosen = jnp.int32(last)
        if last:
            edges = (blocks - (0 if kind == ODD else 1)) // 2
            fits = lax.fori_loop(0, edges, check, jnp.ones((8, 128), jnp.int32))
            chosen = jnp.min(jnp.where(fits == 1, entry, last))
        most_rows = jnp.int32(levels[kind][-1])
        for number, level in enumerate(levels[kind][:-1]):
            most_rows = jnp.where(chosen == number, level, most_rows)

        lower, before, after = own_edge(kind, before_edge, after_edge)
        most = jnp.int32(0)
        least = jnp.int32(heads)
        for count in range(1, heads + 1):
            most += jnp.where(round_up(after) * count <= most_rows, 1, 0)
            least -= jnp.where(round_up(before) * count <= most_rows, 1, 0)
        low = jnp.clip(jnp.int32(heads // 2), least, most)
        crossed = before > 0
        base = kind * FIELDS
        plan[base + BEFORE] = before
        plan[base + AFTER] = after
        plan[base + LOWER] = lower.astype(jnp.int32)
        plan[base + JOBS] = jnp.where(crossed, jnp.where(lower, low, heads - low), 0)
        plan[base + JOB_HEAD] = jnp.where(lower, 0, low)
        plan[base + SENT] = jnp.where(crossed, jnp.where(lower, heads - low, low), 0)
        plan[base + SENT_HEAD] = jnp.where(lower, low, 0)
        plan[base + LEVEL] = chosen
        choices[kind][0] = chosen


class Edge:
    def __init__(self, plan, kind, rows):
        read = lambda field: plan[kind * FIELDS + field]
        self.lower = read(LOWER) == 1
        self.jobs, self.job_head = read(JOBS), read(JOB_HEAD)
        self.sent, self.sent_head = read(SENT), read(SENT_HEAD)
        self.level = read(LEVEL)
        before, after = read(BEFORE), read(AFTER)
        self.before, self.after = before, after
        self.own_begin = jnp.where(self.lower, rows - before, 0)
        self.own_end = jnp.where(self.lower, rows, after)
        self.own_rows = round_up(jnp.where(self.lower, before, after))
        self.other_rows = round_up(jnp.where(self.lower, after, before))
        self.own = jnp.where(self.lower, rows - self.own_rows, 0)
        self.other = jnp.where(self.lower, 0, rows - self.other_rows)
        self.first_block = blocks_of(self.own_begin, BLOCK)
        self.last_block = blocks_of(self.own_end + BLOCK - 1, BLOCK)


def tiles(start, size):
    return pl.ds(pl.multiple_of(start, TILE), pl.multiple_of(size, TILE))


def lanes(head):
    return pl.ds(pl.multiple_of(head * HEAD_DIM, HEAD_DIM), HEAD_DIM)


def attention(query, key, value, grad, mask_columns, store, chunk):
    count = query.shape[0]
    key_t = key.T
    value_t = value.T
    grad_t = grad.T
    across = (((1,), (1,)), ((), ()))
    chunks = [slice(first, first + chunk) for first in range(0, count, chunk)]
    scores = [
        lax.dot_general(key, query[cols], across, preferred_element_type=jnp.float32)
        for cols in chunks
    ]
    grad_probs = [
        lax.dot_general(value, grad[cols], across, preferred_element_type=jnp.float32)
        for cols in chunks
    ]
    probs_low = []
    grad_scores = []
    for number, cols in enumerate(chunks):
        masked = jnp.where(mask_columns(cols), scores[number], -1e30)
        top = jnp.max(masked, axis=0, keepdims=True)
        weights = jnp.exp2((masked - top) * (FACTOR * LOG2E))
        total = jnp.sum(weights, axis=0, keepdims=True)
        probs = weights * (1.0 / total)
        probs_low.append(probs.astype(jnp.bfloat16))
        result_t = jnp.dot(value_t, probs_low[-1], preferred_element_type=jnp.float32)
        result_t = result_t.astype(jnp.bfloat16)
        centre = jnp.sum(
            grad_t[:, cols].astype(jnp.float32) * result_t.astype(jnp.float32),
            axis=0,
            keepdims=True,
        )
        grad_scores.append((probs * (grad_probs[number] - centre)).astype(jnp.bfloat16))
        grad_query_t = jnp.dot(key_t, grad_scores[-1], preferred_element_type=jnp.float32) * FACTOR
        store(0, cols, result_t.T)
        store(1, cols, grad_query_t.astype(jnp.bfloat16).T)
    probs_low = jnp.concatenate(probs_low, axis=1)
    grad_scores = jnp.concatenate(grad_scores, axis=1)
    grad_value = jnp.dot(probs_low, grad, preferred_element_type=jnp.float32)
    store(3, slice(None), grad_value.astype(jnp.bfloat16))
    grad_key = jnp.dot(grad_scores, query, preferred_element_type=jnp.float32)
    store(2, slice(None), (grad_key * FACTOR).astype(jnp.bfloat16))


def find_images(lengths, image_rows):
    count = image_rows.shape[1]
    position = lax.axis_index("dp") * count + lax.broadcasted_iota(jnp.int32, (8, count), 1)

    def place(image, carry):
        start, begin = carry
        return start + lengths[image], jnp.where(position >= start, start, begin)

    first = (jnp.int32(0), jnp.zeros((8, count), jnp.int32))
    _, begin = lax.fori_loop(0, lengths.shape[0], place, first)
    image_rows[...] = begin.astype(jnp.float32)


def local_head(operands, image_rows, outs):
    image_col = image_rows[...].T[:, :1]

    def store(which, rows, part):
        outs[which][rows, :] = part

    attention(
        *(operand[...] for operand in operands),
        lambda cols: image_col == image_rows[:1, cols],
        store,
        LOCAL_CHUNK,
    )


def local_kernel(lengths, *rest):
    operands, outs, image_rows = rest[:4], rest[4:8], rest[8]

    @pl.when(pl.program_id(0) == 0)
    def _():
        find_images(lengths, image_rows)

    local_head(operands, image_rows, outs)


def local_attention(lengths, arrays, heads):
    rows, width = arrays[0].shape
    block = pl.BlockSpec((rows, HEAD_DIM), lambda head: (0, head))
    return pl.pallas_call(
        local_kernel,
        grid=(heads,),
        in_specs=[SCALARS] + [block] * 4,
        out_specs=[block] * 4,
        out_shape=[pltpu.HBM((rows, width), jnp.bfloat16)] * 4,
        scratch_shapes=[pltpu.VMEM((8, rows), jnp.float32)],
        compiler_params=pltpu.CompilerParams(vmem_limit_bytes=VMEM_LIMIT),
        cost_estimate=SCHEDULED_LAST,
        name="local_images",
    )(lengths, *in_hbm(arrays))


START = lambda copy: copy.start()
WAIT = lambda copy: copy.wait()
ANYWHERE = pl.BlockSpec(memory_space=pl.ANY)
SCALARS = pl.BlockSpec(memory_space=pltpu.SMEM)


def in_hbm(arrays):
    return [pltpu.with_memory_space_constraint(array, pltpu.HBM) for array in arrays]


def pieces(levels):
    return [(0, levels[0])] + [(levels[0], level - levels[0]) for level in levels[1:]]


def piece_shapes(levels):
    return [pltpu.HBM((size, 4 * HEAD_DIM), jnp.bfloat16) for _, size in pieces(levels)]


def copy_pieces(levels, level, used, staged, offset, arrays, sems, out, action, first=0):
    for number, (start, size) in enumerate(pieces(levels)):
        if number < first:
            continue
        taken = jnp.clip(used - start, 0, size)
        inside = staged.at[tiles(offset + start, taken)]
        outside = arrays[number].at[tiles(0, taken)]
        source, target = (inside, outside) if out else (outside, inside)

        @pl.when((taken > 0) & (True if number == 0 else level == number))
        def _():
            action(pltpu.make_async_copy(source, target, sems.at[number]))


def gather(edge, held, staged):
    steps = blocks_of(edge.own_rows + BLOCK - 1, BLOCK)

    def one_head(slot, carry):
        def one_block(step, carry):
            source = pl.ds(pl.multiple_of(edge.own + step * BLOCK, TILE), BLOCK)
            target = pl.ds(pl.multiple_of(slot * edge.own_rows + step * BLOCK, TILE), BLOCK)
            for which in range(4):
                staged[target, which * HEAD_DIM:(which + 1) * HEAD_DIM] = held[
                    which, source, lanes(edge.sent_head + slot)]
            return carry

        return lax.fori_loop(0, steps, one_block, carry)

    lax.fori_loop(0, edge.sent, one_head, 0)


def pack_even_kernel(levels, blocks, lengths, query, key, value, grad, *rest):
    count = len(levels[EVEN])
    plan, choices, outs = rest[0], rest[1:3], rest[3:3 + count]
    before_edge, after_edge, held, staged, load_sem, out_sem, far_sem = rest[3 + count:]
    rows, width = query.shape
    half = rows // 2
    block = lax.axis_index("dp")
    near = tiles(jnp.where(lax.rem(block, 2) == 1, rows - half, 0), half)
    operands = (query, key, value, grad)

    def load(part, sem):
        return [
            pltpu.make_async_copy(array.at[part], held.at[which, part], sem.at[which])
            for which, array in enumerate(operands)
        ]

    near_loads = load(near, load_sem)
    for copy in near_loads:
        copy.start()
    find_crossings(rows, blocks, lengths, before_edge, after_edge)
    lower, before, after = own_edge(EVEN, before_edge, after_edge)
    own_rows = round_up(jnp.where(lower, before, after))
    far_rows = jnp.maximum(own_rows - half, 0)
    far_loads = load(tiles(jnp.where(lower, rows - half - far_rows, half), far_rows), far_sem)

    @pl.when(far_rows > 0)
    def _():
        for copy in far_loads:
            copy.start()

    make_plan(width // HEAD_DIM, blocks, levels, plan, choices, before_edge, after_edge)
    for copy in near_loads:
        copy.wait()

    @pl.when(far_rows > 0)
    def _():
        for copy in far_loads:
            copy.wait()

    @pl.when(before > 0)
    def _():
        edge = Edge(plan, EVEN, rows)
        gather(edge, held, staged)
        send = functools.partial(
            copy_pieces, levels[EVEN], edge.level, edge.sent * edge.own_rows, staged, 0, outs,
            out_sem, True, first=1)
        send(START)
        outs[0][...] = staged[:outs[0].shape[0], :]
        send(WAIT)


def pack_odd_kernel(levels, plan, query, key, value, grad, *rest):
    count = len(levels)
    outs = rest[:count]
    held, staged, load_sem, out_sem = rest[count:]
    rows = query.shape[0]
    edge = Edge(plan, ODD, rows)
    part = tiles(edge.own, edge.own_rows)
    loads = [
        pltpu.make_async_copy(array.at[part], held.at[which, part], load_sem.at[which])
        for which, array in enumerate((query, key, value, grad))
    ]

    @pl.when(edge.sent > 0)
    def _():
        for copy in loads:
            copy.start()
        for copy in loads:
            copy.wait()
        gather(edge, held, staged)
        move = functools.partial(
            copy_pieces, levels, edge.level, edge.sent * edge.own_rows, staged, 0, outs,
            out_sem, True)
        move(START)
        move(WAIT)


def pack_scratch(rows, width, levels):
    return [
        pltpu.VMEM((4, rows + BLOCK, width), jnp.bfloat16),
        pltpu.VMEM((levels[-1] + BLOCK, 4 * HEAD_DIM), jnp.bfloat16),
        pltpu.SemaphoreType.DMA((4,)),
        pltpu.SemaphoreType.DMA((len(levels),)),
    ]


def pack_even(lengths, arrays, levels, blocks):
    rows, width = arrays[0].shape
    one = jax.ShapeDtypeStruct((1,), jnp.int32)
    plan, odd_level, even_level, *even = pl.pallas_call(
        functools.partial(pack_even_kernel, levels, blocks),
        in_specs=[SCALARS] + [ANYWHERE] * 4,
        out_specs=[SCALARS] * 3 + [pl.BlockSpec(memory_space=pltpu.VMEM)]
        + [ANYWHERE] * (len(levels[EVEN]) - 1),
        out_shape=[jax.ShapeDtypeStruct((2 * FIELDS,), jnp.int32), one, one]
        + [pltpu.VMEM((levels[EVEN][0], 4 * HEAD_DIM), jnp.bfloat16)]
        + piece_shapes(levels[EVEN])[1:],
        scratch_shapes=[
            pltpu.SMEM((blocks + 2,), jnp.int32),
            pltpu.SMEM((blocks + 2,), jnp.int32),
        ] + pack_scratch(rows, width, levels[EVEN]) + [pltpu.SemaphoreType.DMA((4,))],
        compiler_params=pltpu.CompilerParams(vmem_limit_bytes=PACK_VMEM_LIMIT),
        name="pack_even",
    )(lengths, *in_hbm(arrays))
    return plan, (odd_level, even_level), even


def pack_odd(plan, arrays, levels):
    rows, width = arrays[0].shape
    return pl.pallas_call(
        functools.partial(pack_odd_kernel, levels),
        in_specs=[SCALARS] + [ANYWHERE] * 4,
        out_specs=[ANYWHERE] * len(levels),
        out_shape=piece_shapes(levels),
        scratch_shapes=pack_scratch(rows, width, levels),
        compiler_params=pltpu.CompilerParams(vmem_limit_bytes=VMEM_LIMIT),
        name="pack_odd",
    )(plan, *in_hbm(arrays))


def crossing_kernel(levels, kind, plan, query, key, value, grad, *rest):
    count = len(levels)
    received, back, kept = rest[:count], rest[count:2 * count], rest[2 * count]
    own, staged_in, staged_out, result, own_sem, in_sem, out_sem, kept_sem = rest[2 * count + 1:]
    rows, width = query.shape
    edge = Edge(plan, kind, rows)
    jobs = edge.jobs
    own_part = tiles(edge.own, edge.own_rows)
    margin = rows

    def load_own(action):
        for which, array in enumerate((query, key, value, grad)):
            action(pltpu.make_async_copy(
                array.at[own_part], own.at[which, own_part], own_sem.at[which]))

    def keep(job):
        buffer = lax.rem(job, 2)
        return pltpu.make_async_copy(
            result.at[buffer, own_part], kept.at[job, own_part], kept_sem.at[buffer])

    position = lax.broadcasted_iota(jnp.int32, (rows, HEAD_DIM), 0)
    in_own = (position >= edge.own_begin) & (position < edge.own_end)
    key_position = lax.broadcasted_iota(jnp.int32, (rows, 1), 0)
    in_image = (key_position < edge.after) | (key_position >= rows - edge.before)
    in_window = (position < edge.after) | (position >= rows - edge.before)

    def one_job(step, carry):
        job = jnp.where(edge.lower, step, jobs - 1 - step)
        buffer = lax.rem(job, 2)
        start = margin + job * edge.other_rows - edge.other
        window = pl.ds(pl.multiple_of(start, TILE), rows)

        @pl.when(step >= 2)
        def _():
            keep(job).wait()

        zero = jnp.zeros((rows, HEAD_DIM), jnp.bfloat16)
        operands = []
        for which in range(4):
            columns = slice(which * HEAD_DIM, (which + 1) * HEAD_DIM)
            operands.append(jnp.where(
                in_own,
                own[which, :, lanes(edge.job_head + job)],
                jnp.where(in_window, staged_in[window, columns], zero),
            ))

        def store(which, part_rows, part):
            result[buffer, part_rows, which * HEAD_DIM:(which + 1) * HEAD_DIM] = part

        attention(*operands, lambda cols: in_image, store, CROSSING_CHUNK)
        staged_out[window, :] = result[buffer]
        keep(job).start()
        return carry

    @pl.when(jobs > 0)
    def _():
        stage = functools.partial(
            copy_pieces, levels, edge.level, jobs * edge.other_rows, staged_in, margin, received,
            in_sem, False)
        send = functools.partial(
            copy_pieces, levels, edge.level, jobs * edge.other_rows, staged_out, margin, back,
            out_sem, True)
        stage(START)
        load_own(START)
        load_own(WAIT)
        stage(WAIT)
        lax.fori_loop(0, jobs, one_job, 0)
        send(START)

        @pl.when(jobs >= 2)
        def _():
            keep(1).wait()

        keep(0).wait()
        send(WAIT)


def crossing_images(kind, plan, arrays, received, levels):
    rows, width = arrays[0].shape
    heads = width // HEAD_DIM
    four = 4 * HEAD_DIM
    count = len(levels)
    staged = pltpu.VMEM((rows + levels[-1] + rows, four), jnp.bfloat16)
    outs = pl.pallas_call(
        functools.partial(crossing_kernel, levels, kind),
        in_specs=[SCALARS] + [ANYWHERE] * (4 + count),
        out_specs=[ANYWHERE] * (count + 1),
        out_shape=piece_shapes(levels)
        + [pltpu.HBM((heads, rows, four), jnp.bfloat16)],
        scratch_shapes=[
            pltpu.VMEM((4, rows, width), jnp.bfloat16),
            staged,
            staged,
            pltpu.VMEM((2, rows, four), jnp.bfloat16),
            pltpu.SemaphoreType.DMA((4,)),
            pltpu.SemaphoreType.DMA((count,)),
            pltpu.SemaphoreType.DMA((count,)),
            pltpu.SemaphoreType.DMA((2,)),
        ],
        compiler_params=pltpu.CompilerParams(vmem_limit_bytes=VMEM_LIMIT),
        cost_estimate=pl.CostEstimate(
            flops=12 * rows * rows * width, bytes_accessed=16 * rows * width, transcendentals=0
        ),
        name="odd_edge_images" if kind == ODD else "even_edge_images",
    )(plan, *in_hbm(arrays), *received)
    return outs[:count], outs[count]


def overlay(whole, which, edge, first_head, heads, source):
    mixed = jnp.where(edge.lower, edge.first_block, edge.last_block - 1)
    full = jnp.where(edge.lower, edge.first_block + 1, edge.first_block)

    def one_head(slot, carry):
        place = lanes(first_head + slot)

        def one_block(step, carry):
            first = (full + step) * BLOCK
            part = pl.ds(pl.multiple_of(first, BLOCK), BLOCK)
            whole[which, part, place] = source(slot, first)
            return carry

        first = mixed * BLOCK
        part = pl.ds(pl.multiple_of(first, BLOCK), BLOCK)
        position = first + lax.broadcasted_iota(jnp.int32, (BLOCK, HEAD_DIM), 0)
        whole[which, part, place] = jnp.where(
            (position >= edge.own_begin) & (position < edge.own_end),
            source(slot, first),
            whole[which, part, place],
        )
        return lax.fori_loop(0, edge.last_block - edge.first_block - 1, one_block, carry)

    lax.fori_loop(0, heads, one_head, 0)


def returned_source(edge, staged, columns):
    def source(slot, first):
        start = BLOCK + slot * edge.own_rows + first - edge.own
        return staged[pl.ds(pl.multiple_of(start, TILE), BLOCK), columns]

    return source


def rest_kernel(done, plan, lengths, *rest):
    operands, before, kept = rest[:4], rest[4:8], rest[8:10]
    outs = rest[10:14]
    image_rows, held, held_sem = rest[14:]
    head = pl.program_id(0)
    rows = image_rows.shape[1]
    edges = [Edge(plan, kind, rows) for kind in (ODD, EVEN)]

    def kept_copy(kind, slot):
        part = tiles(edges[kind].own, edges[kind].own_rows)
        return pltpu.make_async_copy(
            kept[kind].at[slot, part], held.at[kind, slot, part], held_sem.at[kind, slot])

    @pl.when(head == 0)
    def _():
        for kind in (ODD, EVEN):
            def start(slot, carry):
                kept_copy(kind, slot).start()
                return carry

            lax.fori_loop(0, edges[kind].jobs, start, 0)

        find_images(lengths, image_rows)

    @pl.when(head < done)
    def _():
        for old, out in zip(before, outs):
            out[...] = old[...]

    @pl.when(head >= done)
    def _():
        local_head(operands, image_rows, outs)

    for kind in (ODD, EVEN):
        edge = edges[kind]
        slot = head - edge.job_head

        @pl.when((slot >= 0) & (slot < edge.jobs))
        def _():
            kept_copy(kind, slot).wait()

            def one_block(block, carry):
                first = block * BLOCK
                part = pl.ds(pl.multiple_of(first, BLOCK), BLOCK)
                position = first + lax.broadcasted_iota(jnp.int32, (BLOCK, HEAD_DIM), 0)
                wanted = (position >= edge.own_begin) & (position < edge.own_end)
                for which, out in enumerate(outs):
                    columns = slice(which * HEAD_DIM, (which + 1) * HEAD_DIM)
                    out[part, :] = jnp.where(wanted, held[kind, slot, part, columns], out[part, :])
                return carry

            lax.fori_loop(edge.first_block, edge.last_block, one_block, 0)


def rest_of_images(plan, lengths, arrays, done, local, kept_odd, kept_even):
    rows, width = arrays[0].shape
    heads = width // HEAD_DIM
    todo = pl.BlockSpec((rows, HEAD_DIM), lambda head: (0, jnp.maximum(head, done)))
    old = pl.BlockSpec((rows, HEAD_DIM), lambda head: (0, jnp.minimum(head, done - 1)))
    return pl.pallas_call(
        functools.partial(rest_kernel, done),
        grid=(heads,),
        in_specs=[SCALARS] * 2 + [todo] * 4 + [old] * 4 + [ANYWHERE] * 2,
        out_specs=[pl.BlockSpec((rows, HEAD_DIM), lambda head: (0, head))] * 4,
        out_shape=[pltpu.HBM((rows, width), jnp.bfloat16)] * 4,
        scratch_shapes=[
            pltpu.VMEM((8, rows), jnp.float32),
            pltpu.VMEM((2, heads, rows, 4 * HEAD_DIM), jnp.bfloat16),
            pltpu.SemaphoreType.DMA((2, heads)),
        ],
        compiler_params=pltpu.CompilerParams(vmem_limit_bytes=VMEM_LIMIT),
        cost_estimate=SCHEDULED_LAST,
        name="rest_of_images",
    )(plan, lengths, *in_hbm([*arrays, *local, kept_odd, kept_even]))


def return_kernel(levels, plan, *rest):
    counts = [len(levels[ODD]), len(levels[EVEN])]
    total = sum(counts)
    returned = rest[:counts[ODD]], rest[counts[ODD]:total]
    outs = rest[total + 4:total + 8]
    whole, odd_staged, even_staged, whole_sem, odd_sem, even_sem = rest[total + 8:]
    staged = odd_staged, even_staged
    rows = whole.shape[1]
    edges = [Edge(plan, kind, rows) for kind in (ODD, EVEN)]
    stages = [
        functools.partial(
            copy_pieces, levels[kind], edges[kind].level, edges[kind].sent * edges[kind].own_rows,
            staged[kind], BLOCK, returned[kind], sem, False)
        for kind, sem in ((ODD, odd_sem), (EVEN, even_sem))
    ]

    ends = []
    for edge, other in (edges, edges[::-1]):
        meets = jnp.logical_not(edge.lower) & (other.sent > 0)
        ends.append(jnp.where(
            meets, jnp.minimum(edge.last_block, other.first_block), edge.last_block))

    def move(kind, which, out, action):
        first, last = edges[kind].first_block, ends[kind]

        @pl.when((edges[kind].sent > 0) & (last > first))
        def _():
            part = pl.ds(
                pl.multiple_of(first * BLOCK, BLOCK), pl.multiple_of((last - first) * BLOCK, BLOCK))
            inside, outside = whole.at[which, part], outs[which].at[part]
            source, target = (inside, outside) if out else (outside, inside)
            action(pltpu.make_async_copy(source, target, whole_sem.at[kind, which]))

    for stage in stages:
        stage(START)
    for which in range(4):
        for kind in (ODD, EVEN):
            move(kind, which, False, START)
    for stage in stages:
        stage(WAIT)
    for which in range(4):
        columns = slice(which * HEAD_DIM, (which + 1) * HEAD_DIM)
        for kind in (ODD, EVEN):
            move(kind, which, False, WAIT)
        for kind in (ODD, EVEN):
            edge = edges[kind]
            overlay(whole, which, edge, edge.sent_head, edge.sent,
                    returned_source(edge, staged[kind], columns))
        for kind in (ODD, EVEN):
            move(kind, which, True, START)
    for which in range(4):
        for kind in (ODD, EVEN):
            move(kind, which, True, WAIT)


def merge_returned(plan, odd, even, outs, levels):
    rows, width = outs[0].shape
    counts = [len(levels[ODD]), len(levels[EVEN])]
    return pl.pallas_call(
        functools.partial(return_kernel, levels),
        in_specs=[SCALARS] + [ANYWHERE] * (sum(counts) + 4),
        out_specs=[ANYWHERE] * 4,
        out_shape=[pltpu.HBM((rows, width), jnp.bfloat16)] * 4,
        input_output_aliases={1 + sum(counts) + which: which for which in range(4)},
        scratch_shapes=[
            pltpu.VMEM((4, rows, width), jnp.bfloat16),
            pltpu.VMEM((levels[ODD][-1] + 2 * BLOCK, 4 * HEAD_DIM), jnp.bfloat16),
            pltpu.VMEM((levels[EVEN][-1] + 2 * BLOCK, 4 * HEAD_DIM), jnp.bfloat16),
            pltpu.SemaphoreType.DMA((2, 4)),
            pltpu.SemaphoreType.DMA((counts[ODD],)),
            pltpu.SemaphoreType.DMA((counts[EVEN],)),
        ],
        compiler_params=pltpu.CompilerParams(vmem_limit_bytes=VMEM_LIMIT),
        name="merge_returned",
    )(plan, *odd, *even, *in_hbm(outs))


def swapped(value, kind):
    first = 0 if kind == ODD else 1
    pairs = [(block, block + 1) for block in range(first, lax.axis_size("dp") - 1, 2)]
    return lax.ppermute(value, "dp", pairs + [(after, before) for before, after in pairs])


def swap_further(choices, odd, even):
    counts = [len(odd), len(even)]
    if not sum(counts):
        return [], []
    pairs = [(first, second) for first in range(counts[0] + 1) for second in range(counts[1] + 1)]

    def send(used, odd, even):
        return tuple(
            [
                swapped(array, kind) if number == used[kind] else array
                for number, array in enumerate(arrays, start=1)
            ]
            for kind, arrays in ((ODD, odd), (EVEN, even))
        )

    index = 0
    for choice, count in zip(choices, counts):
        if count:
            index = index * (count + 1) + choice[0]
    branches = [functools.partial(send, pair) for pair in pairs]
    return lax.switch(index, branches, list(odd), list(even))


def body(queries, keys, values, out_grad, lengths):
    rows, width = queries.shape
    arrays = (queries, keys, values, out_grad)
    levels = [size_levels(kind, rows, width // HEAD_DIM) for kind in (ODD, EVEN)]
    plan, choices, even = pack_even(lengths, arrays, levels, lax.axis_size("dp"))
    even_first = swapped(even[0], EVEN)
    odd = pack_odd(plan, arrays, levels[ODD])
    odd_first = swapped(odd[0], ODD)
    done = width // HEAD_DIM // 2
    local = local_attention(lengths, arrays, done)
    choices, local = lax.optimization_barrier((choices, local))
    _, more = swap_further(choices, [], even[1:])
    back_even, kept_even = crossing_images(EVEN, plan, arrays, [even_first, *more], levels[EVEN])
    choices, kept_even = lax.optimization_barrier((choices, kept_even))
    more, _ = swap_further(choices, odd[1:], [])
    received = [odd_first, *more]
    first, received = lax.optimization_barrier((back_even[0], received))
    even_first = swapped(first, EVEN)
    back_odd, kept_odd = crossing_images(ODD, plan, arrays, received, levels[ODD])
    odd_first = swapped(back_odd[0], ODD)
    kept_odd, local = lax.optimization_barrier((kept_odd, local))
    outs = rest_of_images(plan, lengths, arrays, done, local, kept_odd, kept_even)
    even_first, choices, outs = lax.optimization_barrier((even_first, choices, outs))
    more_odd, more_even = swap_further(choices, back_odd[1:], back_even[1:])
    return tuple(merge_returned(
        plan, [odd_first, *more_odd], [even_first, *more_even], outs, levels))


def solution(mesh):
    in_specs = (P("dp", "tensor"), P("dp", "tensor"), P("dp", "tensor"), P("dp", "tensor"), P())
    out_specs = (P("dp", "tensor"), P("dp", "tensor"), P("dp", "tensor"), P("dp", "tensor"))
    return jax.shard_map(body, mesh=mesh, in_specs=in_specs, out_specs=out_specs, check_vma=False)
```

```python
import functools
import math

import jax
import jax.numpy as jnp
from jax import lax
from jax.experimental import pallas as pl
from jax.experimental.pallas import tpu as pltpu
from jax.sharding import PartitionSpec as P

HEAD_DIM = 128
TILE = 16
BLOCK = 64
LOCAL_CHUNK = 256
CROSSING_CHUNK = 512
FACTOR = 1.0 / math.sqrt(HEAD_DIM)
LOG2E = 1.4426950408889634
VMEM_LIMIT = 32 * 1024 * 1024
PACK_VMEM_LIMIT = 60 * 1024 * 1024

SCHEDULED_LAST = pl.CostEstimate(flops=1, bytes_accessed=1, transcendentals=0)

FIELDS = 8
BEFORE, AFTER, LOWER, JOBS, JOB_HEAD, SENT, SENT_HEAD, LEVEL = range(FIELDS)
ODD, EVEN = 0, 1

LEVEL_UNITS = ((9, 10, 11, 12, 13), (9, 10, 11, 12, 13))


def round_up(value):
    return (value + (TILE - 1)) & -TILE


def blocks_of(value, size):
    if size & (size - 1):
        return value // size
    return lax.shift_right_logical(value, jnp.int32(size.bit_length() - 1))


def worst_case_rows(rows, heads):
    worst = 0
    for before in range(TILE, rows + 1, TILE):
        for after in range(TILE, rows + TILE - before + 1, TILE):
            needed = min(max(after * low, before * (heads - low)) for low in range(heads + 1))
            worst = max(worst, needed)
    return worst


def size_levels(kind, rows, heads):
    unit = rows * heads // 48
    most = worst_case_rows(rows, heads)
    below = sorted(int(level * unit) for level in LEVEL_UNITS[kind] if level * unit < most)
    return tuple(below) + (most,)


def find_crossings(rows, blocks, lengths, before_edge, after_edge):
    def clear(edge, carry):
        before_edge[edge] = 0
        after_edge[edge] = 0
        return carry

    lax.fori_loop(0, blocks + 1, clear, 0)

    def place(image, start):
        end = start + lengths[image]
        edge = blocks_of(end - 1, rows)

        @pl.when(edge > blocks_of(start, rows))
        def _():
            before_edge[edge] = edge * rows - start
            after_edge[edge] = end - edge * rows

        return end

    lax.fori_loop(0, lengths.shape[0], place, 0)


def own_edge(kind, before_edge, after_edge):
    block = lax.axis_index("dp")
    lower = lax.rem(block, 2) == (0 if kind == ODD else 1)
    edge = jnp.where(lower, block + 1, block)
    return lower, before_edge[edge], after_edge[edge]


def make_plan(heads, blocks, levels, plan, choices, before_edge, after_edge):
    entry = lax.broadcasted_iota(jnp.int32, (8, 128), 1)
    for kind in (ODD, EVEN):
        limit = jnp.full((8, 128), levels[kind][-1], jnp.int32)
        for number, level in enumerate(levels[kind]):
            limit = jnp.where(entry == number, level, limit)

        def check(number, fits):
            edge = 2 * number + (1 if kind == ODD else 2)
            after = round_up(after_edge[edge])
            before = round_up(before_edge[edge])
            taken = jnp.zeros((8, 128), jnp.int32)
            for count in range(1, heads + 1):
                taken += jnp.where(after * count <= limit, 1, 0)
                taken += jnp.where(before * count <= limit, 1, 0)
            return jnp.minimum(fits, jnp.where(taken >= heads, 1, 0))

        last = len(levels[kind]) - 1
        chosen = jnp.int32(last)
        if last:
            edges = (blocks - (0 if kind == ODD else 1)) // 2
            fits = lax.fori_loop(0, edges, check, jnp.ones((8, 128), jnp.int32))
            chosen = jnp.min(jnp.where(fits == 1, entry, last))
        most_rows = jnp.int32(levels[kind][-1])
        for number, level in enumerate(levels[kind][:-1]):
            most_rows = jnp.where(chosen == number, level, most_rows)

        lower, before, after = own_edge(kind, before_edge, after_edge)
        most = jnp.int32(0)
        least = jnp.int32(heads)
        for count in range(1, heads + 1):
            most += jnp.where(round_up(after) * count <= most_rows, 1, 0)
            least -= jnp.where(round_up(before) * count <= most_rows, 1, 0)
        low = jnp.clip(jnp.int32(heads // 2), least, most)
        crossed = before > 0
        base = kind * FIELDS
        plan[base + BEFORE] = before
        plan[base + AFTER] = after
        plan[base + LOWER] = lower.astype(jnp.int32)
        plan[base + JOBS] = jnp.where(crossed, jnp.where(lower, low, heads - low), 0)
        plan[base + JOB_HEAD] = jnp.where(lower, 0, low)
        plan[base + SENT] = jnp.where(crossed, jnp.where(lower, heads - low, low), 0)
        plan[base + SENT_HEAD] = jnp.where(lower, low, 0)
        plan[base + LEVEL] = chosen
        choices[kind][0] = chosen


class Edge:
    def __init__(self, plan, kind, rows):
        read = lambda field: plan[kind * FIELDS + field]
        self.lower = read(LOWER) == 1
        self.jobs, self.job_head = read(JOBS), read(JOB_HEAD)
        self.sent, self.sent_head = read(SENT), read(SENT_HEAD)
        self.level = read(LEVEL)
        before, after = read(BEFORE), read(AFTER)
        self.before, self.after = before, after
        self.own_begin = jnp.where(self.lower, rows - before, 0)
        self.own_end = jnp.where(self.lower, rows, after)
        self.own_rows = round_up(jnp.where(self.lower, before, after))
        self.other_rows = round_up(jnp.where(self.lower, after, before))
        self.own = jnp.where(self.lower, rows - self.own_rows, 0)
        self.other = jnp.where(self.lower, 0, rows - self.other_rows)
        self.first_block = blocks_of(self.own_begin, BLOCK)
        self.last_block = blocks_of(self.own_end + BLOCK - 1, BLOCK)


def tiles(start, size):
    return pl.ds(pl.multiple_of(start, TILE), pl.multiple_of(size, TILE))


def lanes(head):
    return pl.ds(pl.multiple_of(head * HEAD_DIM, HEAD_DIM), HEAD_DIM)


def attention(query, key, value, grad, mask_columns, store, chunk):
    count = query.shape[0]
    key_t = key.T
    value_t = value.T
    grad_t = grad.T
    across = (((1,), (1,)), ((), ()))
    chunks = [slice(first, first + chunk) for first in range(0, count, chunk)]
    scores = [
        lax.dot_general(key, query[cols], across, preferred_element_type=jnp.float32)
        for cols in chunks
    ]
    grad_probs = [
        lax.dot_general(value, grad[cols], across, preferred_element_type=jnp.float32)
        for cols in chunks
    ]
    probs_low = []
    grad_scores = []
    for number, cols in enumerate(chunks):
        masked = jnp.where(mask_columns(cols), scores[number], -1e30)
        top = jnp.max(masked, axis=0, keepdims=True)
        weights = jnp.exp2((masked - top) * (FACTOR * LOG2E))
        total = jnp.sum(weights, axis=0, keepdims=True)
        probs = weights * (1.0 / total)
        probs_low.append(probs.astype(jnp.bfloat16))
        result_t = jnp.dot(value_t, probs_low[-1], preferred_element_type=jnp.float32)
        result_t = result_t.astype(jnp.bfloat16)
        centre = jnp.sum(
            grad_t[:, cols].astype(jnp.float32) * result_t.astype(jnp.float32),
            axis=0,
            keepdims=True,
        )
        grad_scores.append((probs * (grad_probs[number] - centre)).astype(jnp.bfloat16))
        grad_query_t = jnp.dot(key_t, grad_scores[-1], preferred_element_type=jnp.float32) * FACTOR
        store(0, cols, result_t.T)
        store(1, cols, grad_query_t.astype(jnp.bfloat16).T)
    probs_low = jnp.concatenate(probs_low, axis=1)
    grad_scores = jnp.concatenate(grad_scores, axis=1)
    grad_value = jnp.dot(probs_low, grad, preferred_element_type=jnp.float32)
    store(3, slice(None), grad_value.astype(jnp.bfloat16))
    grad_key = jnp.dot(grad_scores, query, preferred_element_type=jnp.float32)
    store(2, slice(None), (grad_key * FACTOR).astype(jnp.bfloat16))


def find_images(lengths, image_rows):
    count = image_rows.shape[1]
    position = lax.axis_index("dp") * count + lax.broadcasted_iota(jnp.int32, (8, count), 1)

    def place(image, carry):
        start, begin = carry
        return start + lengths[image], jnp.where(position >= start, start, begin)

    first = (jnp.int32(0), jnp.zeros((8, count), jnp.int32))
    _, begin = lax.fori_loop(0, lengths.shape[0], place, first)
    image_rows[...] = begin.astype(jnp.float32)


def local_head(operands, image_rows, outs):
    image_col = image_rows[...].T[:, :1]

    def store(which, rows, part):
        outs[which][rows, :] = part

    attention(
        *(operand[...] for operand in operands),
        lambda cols: image_col == image_rows[:1, cols],
        store,
        LOCAL_CHUNK,
    )


def local_kernel(lengths, *rest):
    operands, outs, image_rows = rest[:4], rest[4:8], rest[8]

    @pl.when(pl.program_id(0) == 0)
    def _():
        find_images(lengths, image_rows)

    local_head(operands, image_rows, outs)


def local_attention(lengths, arrays, heads):
    rows, width = arrays[0].shape
    block = pl.BlockSpec((rows, HEAD_DIM), lambda head: (0, head))
    return pl.pallas_call(
        local_kernel,
        grid=(heads,),
        in_specs=[SCALARS] + [block] * 4,
        out_specs=[block] * 4,
        out_shape=[pltpu.HBM((rows, width), jnp.bfloat16)] * 4,
        scratch_shapes=[pltpu.VMEM((8, rows), jnp.float32)],
        compiler_params=pltpu.CompilerParams(vmem_limit_bytes=VMEM_LIMIT),
        cost_estimate=SCHEDULED_LAST,
        name="local_images",
    )(lengths, *in_hbm(arrays))


START = lambda copy: copy.start()
WAIT = lambda copy: copy.wait()
ANYWHERE = pl.BlockSpec(memory_space=pl.ANY)
SCALARS = pl.BlockSpec(memory_space=pltpu.SMEM)


def in_hbm(arrays):
    return [pltpu.with_memory_space_constraint(array, pltpu.HBM) for array in arrays]


def pieces(levels):
    return [(0, levels[0])] + [(levels[0], level - levels[0]) for level in levels[1:]]


def piece_shapes(levels):
    return [pltpu.HBM((size, 4 * HEAD_DIM), jnp.bfloat16) for _, size in pieces(levels)]


def copy_pieces(levels, level, used, staged, offset, arrays, sems, out, action, first=0):
    for number, (start, size) in enumerate(pieces(levels)):
        if number < first:
            continue
        taken = jnp.clip(used - start, 0, size)
        inside = staged.at[tiles(offset + start, taken)]
        outside = arrays[number].at[tiles(0, taken)]
        source, target = (inside, outside) if out else (outside, inside)

        @pl.when((taken > 0) & (True if number == 0 else level == number))
        def _():
            action(pltpu.make_async_copy(source, target, sems.at[number]))


def gather(edge, held, staged):
    steps = blocks_of(edge.own_rows + BLOCK - 1, BLOCK)

    def one_head(slot, carry):
        def one_block(step, carry):
            source = pl.ds(pl.multiple_of(edge.own + step * BLOCK, TILE), BLOCK)
            target = pl.ds(pl.multiple_of(slot * edge.own_rows + step * BLOCK, TILE), BLOCK)
            for which in range(4):
                staged[target, which * HEAD_DIM:(which + 1) * HEAD_DIM] = held[
                    which, source, lanes(edge.sent_head + slot)]
            return carry

        return lax.fori_loop(0, steps, one_block, carry)

    lax.fori_loop(0, edge.sent, one_head, 0)


def pack_even_kernel(levels, blocks, lengths, query, key, value, grad, *rest):
    count = len(levels[EVEN])
    plan, choices, outs = rest[0], rest[1:3], rest[3:3 + count]
    before_edge, after_edge, held, staged, load_sem, out_sem, far_sem = rest[3 + count:]
    rows, width = query.shape
    half = rows // 2
    block = lax.axis_index("dp")
    near = tiles(jnp.where(lax.rem(block, 2) == 1, rows - half, 0), half)
    operands = (query, key, value, grad)

    def load(part, sem):
        return [
            pltpu.make_async_copy(array.at[part], held.at[which, part], sem.at[which])
            for which, array in enumerate(operands)
        ]

    near_loads = load(near, load_sem)
    for copy in near_loads:
        copy.start()
    find_crossings(rows, blocks, lengths, before_edge, after_edge)
    lower, before, after = own_edge(EVEN, before_edge, after_edge)
    own_rows = round_up(jnp.where(lower, before, after))
    far_rows = jnp.maximum(own_rows - half, 0)
    far_loads = load(tiles(jnp.where(lower, rows - half - far_rows, half), far_rows), far_sem)

    @pl.when(far_rows > 0)
    def _():
        for copy in far_loads:
            copy.start()

    make_plan(width // HEAD_DIM, blocks, levels, plan, choices, before_edge, after_edge)
    for copy in near_loads:
        copy.wait()

    @pl.when(far_rows > 0)
    def _():
        for copy in far_loads:
            copy.wait()

    @pl.when(before > 0)
    def _():
        edge = Edge(plan, EVEN, rows)
        gather(edge, held, staged)
        send = functools.partial(
            copy_pieces, levels[EVEN], edge.level, edge.sent * edge.own_rows, staged, 0, outs,
            out_sem, True, first=1)
        send(START)
        outs[0][...] = staged[:outs[0].shape[0], :]
        send(WAIT)


def pack_odd_kernel(levels, plan, query, key, value, grad, *rest):
    count = len(levels)
    outs = rest[:count]
    held, staged, load_sem, out_sem = rest[count:]
    rows = query.shape[0]
    edge = Edge(plan, ODD, rows)
    part = tiles(edge.own, edge.own_rows)
    loads = [
        pltpu.make_async_copy(array.at[part], held.at[which, part], load_sem.at[which])
        for which, array in enumerate((query, key, value, grad))
    ]

    @pl.when(edge.sent > 0)
    def _():
        for copy in loads:
            copy.start()
        for copy in loads:
            copy.wait()
        gather(edge, held, staged)
        move = functools.partial(
            copy_pieces, levels, edge.level, edge.sent * edge.own_rows, staged, 0, outs,
            out_sem, True)
        move(START)
        move(WAIT)


def pack_scratch(rows, width, levels):
    return [
        pltpu.VMEM((4, rows + BLOCK, width), jnp.bfloat16),
        pltpu.VMEM((levels[-1] + BLOCK, 4 * HEAD_DIM), jnp.bfloat16),
        pltpu.SemaphoreType.DMA((4,)),
        pltpu.SemaphoreType.DMA((len(levels),)),
    ]


def pack_even(lengths, arrays, levels, blocks):
    rows, width = arrays[0].shape
    one = jax.ShapeDtypeStruct((1,), jnp.int32)
    plan, odd_level, even_level, *even = pl.pallas_call(
        functools.partial(pack_even_kernel, levels, blocks),
        in_specs=[SCALARS] + [ANYWHERE] * 4,
        out_specs=[SCALARS] * 3 + [pl.BlockSpec(memory_space=pltpu.VMEM)]
        + [ANYWHERE] * (len(levels[EVEN]) - 1),
        out_shape=[jax.ShapeDtypeStruct((2 * FIELDS,), jnp.int32), one, one]
        + [pltpu.VMEM((levels[EVEN][0], 4 * HEAD_DIM), jnp.bfloat16)]
        + piece_shapes(levels[EVEN])[1:],
        scratch_shapes=[
            pltpu.SMEM((blocks + 2,), jnp.int32),
            pltpu.SMEM((blocks + 2,), jnp.int32),
        ] + pack_scratch(rows, width, levels[EVEN]) + [pltpu.SemaphoreType.DMA((4,))],
        compiler_params=pltpu.CompilerParams(vmem_limit_bytes=PACK_VMEM_LIMIT),
        name="pack_even",
    )(lengths, *in_hbm(arrays))
    return plan, (odd_level, even_level), even


def pack_odd(plan, arrays, levels):
    rows, width = arrays[0].shape
    return pl.pallas_call(
        functools.partial(pack_odd_kernel, levels),
        in_specs=[SCALARS] + [ANYWHERE] * 4,
        out_specs=[ANYWHERE] * len(levels),
        out_shape=piece_shapes(levels),
        scratch_shapes=pack_scratch(rows, width, levels),
        compiler_params=pltpu.CompilerParams(vmem_limit_bytes=VMEM_LIMIT),
        name="pack_odd",
    )(plan, *in_hbm(arrays))


def crossing_kernel(levels, kind, plan, query, key, value, grad, *rest):
    count = len(levels)
    received, back, kept = rest[:count], rest[count:2 * count], rest[2 * count]
    own, staged_in, staged_out, result, own_sem, in_sem, out_sem, kept_sem = rest[2 * count + 1:]
    rows, width = query.shape
    edge = Edge(plan, kind, rows)
    jobs = edge.jobs
    own_part = tiles(edge.own, edge.own_rows)
    margin = rows

    def load_own(action):
        for which, array in enumerate((query, key, value, grad)):
            action(pltpu.make_async_copy(
                array.at[own_part], own.at[which, own_part], own_sem.at[which]))

    def keep(job):
        buffer = lax.rem(job, 2)
        return pltpu.make_async_copy(
            result.at[buffer, own_part], kept.at[job, own_part], kept_sem.at[buffer])

    position = lax.broadcasted_iota(jnp.int32, (rows, HEAD_DIM), 0)
    in_own = (position >= edge.own_begin) & (position < edge.own_end)
    key_position = lax.broadcasted_iota(jnp.int32, (rows, 1), 0)
    in_image = (key_position < edge.after) | (key_position >= rows - edge.before)
    in_window = (position < edge.after) | (position >= rows - edge.before)

    def one_job(step, carry):
        job = jnp.where(edge.lower, step, jobs - 1 - step)
        buffer = lax.rem(job, 2)
        start = margin + job * edge.other_rows - edge.other
        window = pl.ds(pl.multiple_of(start, TILE), rows)

        @pl.when(step >= 2)
        def _():
            keep(job).wait()

        zero = jnp.zeros((rows, HEAD_DIM), jnp.bfloat16)
        operands = []
        for which in range(4):
            columns = slice(which * HEAD_DIM, (which + 1) * HEAD_DIM)
            operands.append(jnp.where(
                in_own,
                own[which, :, lanes(edge.job_head + job)],
                jnp.where(in_window, staged_in[window, columns], zero),
            ))

        def store(which, part_rows, part):
            result[buffer, part_rows, which * HEAD_DIM:(which + 1) * HEAD_DIM] = part

        attention(*operands, lambda cols: in_image, store, CROSSING_CHUNK)
        staged_out[window, :] = result[buffer]
        keep(job).start()
        return carry

    @pl.when(jobs > 0)
    def _():
        stage = functools.partial(
            copy_pieces, levels, edge.level, jobs * edge.other_rows, staged_in, margin, received,
            in_sem, False)
        send = functools.partial(
            copy_pieces, levels, edge.level, jobs * edge.other_rows, staged_out, margin, back,
            out_sem, True)
        stage(START)
        load_own(START)
        load_own(WAIT)
        stage(WAIT)
        lax.fori_loop(0, jobs, one_job, 0)
        send(START)

        @pl.when(jobs >= 2)
        def _():
            keep(1).wait()

        keep(0).wait()
        send(WAIT)


def crossing_images(kind, plan, arrays, received, levels):
    rows, width = arrays[0].shape
    heads = width // HEAD_DIM
    four = 4 * HEAD_DIM
    count = len(levels)
    staged = pltpu.VMEM((rows + levels[-1] + rows, four), jnp.bfloat16)
    outs = pl.pallas_call(
        functools.partial(crossing_kernel, levels, kind),
        in_specs=[SCALARS] + [ANYWHERE] * (4 + count),
        out_specs=[ANYWHERE] * (count + 1),
        out_shape=piece_shapes(levels)
        + [pltpu.HBM((heads, rows, four), jnp.bfloat16)],
        scratch_shapes=[
            pltpu.VMEM((4, rows, width), jnp.bfloat16),
            staged,
            staged,
            pltpu.VMEM((2, rows, four), jnp.bfloat16),
            pltpu.SemaphoreType.DMA((4,)),
            pltpu.SemaphoreType.DMA((count,)),
            pltpu.SemaphoreType.DMA((count,)),
            pltpu.SemaphoreType.DMA((2,)),
        ],
        compiler_params=pltpu.CompilerParams(vmem_limit_bytes=VMEM_LIMIT),
        cost_estimate=pl.CostEstimate(
            flops=12 * rows * rows * width, bytes_accessed=16 * rows * width, transcendentals=0
        ),
        name="odd_edge_images" if kind == ODD else "even_edge_images",
    )(plan, *in_hbm(arrays), *received)
    return outs[:count], outs[count]


def overlay(whole, which, edge, first_head, heads, source):
    mixed = jnp.where(edge.lower, edge.first_block, edge.last_block - 1)
    full = jnp.where(edge.lower, edge.first_block + 1, edge.first_block)

    def one_head(slot, carry):
        place = lanes(first_head + slot)

        def one_block(step, carry):
            first = (full + step) * BLOCK
            part = pl.ds(pl.multiple_of(first, BLOCK), BLOCK)
            whole[which, part, place] = source(slot, first)
            return carry

        first = mixed * BLOCK
        part = pl.ds(pl.multiple_of(first, BLOCK), BLOCK)
        position = first + lax.broadcasted_iota(jnp.int32, (BLOCK, HEAD_DIM), 0)
        whole[which, part, place] = jnp.where(
            (position >= edge.own_begin) & (position < edge.own_end),
            source(slot, first),
            whole[which, part, place],
        )
        return lax.fori_loop(0, edge.last_block - edge.first_block - 1, one_block, carry)

    lax.fori_loop(0, heads, one_head, 0)


def returned_source(edge, staged, columns):
    def source(slot, first):
        start = BLOCK + slot * edge.own_rows + first - edge.own
        return staged[pl.ds(pl.multiple_of(start, TILE), BLOCK), columns]

    return source


def rest_kernel(done, plan, lengths, *rest):
    operands, before, kept = rest[:4], rest[4:8], rest[8:10]
    outs = rest[10:14]
    image_rows, held, held_sem = rest[14:]
    head = pl.program_id(0)
    rows = image_rows.shape[1]
    edges = [Edge(plan, kind, rows) for kind in (ODD, EVEN)]

    def kept_copy(kind, slot):
        part = tiles(edges[kind].own, edges[kind].own_rows)
        return pltpu.make_async_copy(
            kept[kind].at[slot, part], held.at[kind, slot, part], held_sem.at[kind, slot])

    @pl.when(head == 0)
    def _():
        for kind in (ODD, EVEN):
            def start(slot, carry):
                kept_copy(kind, slot).start()
                return carry

            lax.fori_loop(0, edges[kind].jobs, start, 0)

        find_images(lengths, image_rows)

    @pl.when(head < done)
    def _():
        for old, out in zip(before, outs):
            out[...] = old[...]

    @pl.when(head >= done)
    def _():
        local_head(operands, image_rows, outs)

    for kind in (ODD, EVEN):
        edge = edges[kind]
        slot = head - edge.job_head

        @pl.when((slot >= 0) & (slot < edge.jobs))
        def _():
            kept_copy(kind, slot).wait()

            def one_block(block, carry):
                first = block * BLOCK
                part = pl.ds(pl.multiple_of(first, BLOCK), BLOCK)
                position = first + lax.broadcasted_iota(jnp.int32, (BLOCK, HEAD_DIM), 0)
                wanted = (position >= edge.own_begin) & (position < edge.own_end)
                for which, out in enumerate(outs):
                    columns = slice(which * HEAD_DIM, (which + 1) * HEAD_DIM)
                    out[part, :] = jnp.where(wanted, held[kind, slot, part, columns], out[part, :])
                return carry

            lax.fori_loop(edge.first_block, edge.last_block, one_block, 0)


def rest_of_images(plan, lengths, arrays, done, local, kept_odd, kept_even):
    rows, width = arrays[0].shape
    heads = width // HEAD_DIM
    todo = pl.BlockSpec((rows, HEAD_DIM), lambda head: (0, jnp.maximum(head, done)))
    old = pl.BlockSpec((rows, HEAD_DIM), lambda head: (0, jnp.minimum(head, done - 1)))
    return pl.pallas_call(
        functools.partial(rest_kernel, done),
        grid=(heads,),
        in_specs=[SCALARS] * 2 + [todo] * 4 + [old] * 4 + [ANYWHERE] * 2,
        out_specs=[pl.BlockSpec((rows, HEAD_DIM), lambda head: (0, head))] * 4,
        out_shape=[pltpu.HBM((rows, width), jnp.bfloat16)] * 4,
        scratch_shapes=[
            pltpu.VMEM((8, rows), jnp.float32),
            pltpu.VMEM((2, heads, rows, 4 * HEAD_DIM), jnp.bfloat16),
            pltpu.SemaphoreType.DMA((2, heads)),
        ],
        compiler_params=pltpu.CompilerParams(vmem_limit_bytes=VMEM_LIMIT),
        cost_estimate=SCHEDULED_LAST,
        name="rest_of_images",
    )(plan, lengths, *in_hbm([*arrays, *local, kept_odd, kept_even]))


def return_kernel(levels, plan, *rest):
    counts = [len(levels[ODD]), len(levels[EVEN])]
    total = sum(counts)
    returned = rest[:counts[ODD]], rest[counts[ODD]:total]
    outs = rest[total + 4:total + 8]
    whole, odd_staged, even_staged, whole_sem, odd_sem, even_sem = rest[total + 8:]
    staged = odd_staged, even_staged
    rows = whole.shape[1]
    edges = [Edge(plan, kind, rows) for kind in (ODD, EVEN)]
    stages = [
        functools.partial(
            copy_pieces, levels[kind], edges[kind].level, edges[kind].sent * edges[kind].own_rows,
            staged[kind], BLOCK, returned[kind], sem, False)
        for kind, sem in ((ODD, odd_sem), (EVEN, even_sem))
    ]

    ends = []
    for edge, other in (edges, edges[::-1]):
        meets = jnp.logical_not(edge.lower) & (other.sent > 0)
        ends.append(jnp.where(
            meets, jnp.minimum(edge.last_block, other.first_block), edge.last_block))

    def move(kind, which, out, action):
        first, last = edges[kind].first_block, ends[kind]

        @pl.when((edges[kind].sent > 0) & (last > first))
        def _():
            part = pl.ds(
                pl.multiple_of(first * BLOCK, BLOCK), pl.multiple_of((last - first) * BLOCK, BLOCK))
            inside, outside = whole.at[which, part], outs[which].at[part]
            source, target = (inside, outside) if out else (outside, inside)
            action(pltpu.make_async_copy(source, target, whole_sem.at[kind, which]))

    for stage in stages:
        stage(START)
    for which in range(4):
        for kind in (ODD, EVEN):
            move(kind, which, False, START)
    for stage in stages:
        stage(WAIT)
    for which in range(4):
        columns = slice(which * HEAD_DIM, (which + 1) * HEAD_DIM)
        for kind in (ODD, EVEN):
            move(kind, which, False, WAIT)
        for kind in (ODD, EVEN):
            edge = edges[kind]
            overlay(whole, which, edge, edge.sent_head, edge.sent,
                    returned_source(edge, staged[kind], columns))
        for kind in (ODD, EVEN):
            move(kind, which, True, START)
    for which in range(4):
        for kind in (ODD, EVEN):
            move(kind, which, True, WAIT)


def merge_returned(plan, odd, even, outs, levels):
    rows, width = outs[0].shape
    counts = [len(levels[ODD]), len(levels[EVEN])]
    return pl.pallas_call(
        functools.partial(return_kernel, levels),
        in_specs=[SCALARS] + [ANYWHERE] * (sum(counts) + 4),
        out_specs=[ANYWHERE] * 4,
        out_shape=[pltpu.HBM((rows, width), jnp.bfloat16)] * 4,
        input_output_aliases={1 + sum(counts) + which: which for which in range(4)},
        scratch_shapes=[
            pltpu.VMEM((4, rows, width), jnp.bfloat16),
            pltpu.VMEM((levels[ODD][-1] + 2 * BLOCK, 4 * HEAD_DIM), jnp.bfloat16),
            pltpu.VMEM((levels[EVEN][-1] + 2 * BLOCK, 4 * HEAD_DIM), jnp.bfloat16),
            pltpu.SemaphoreType.DMA((2, 4)),
            pltpu.SemaphoreType.DMA((counts[ODD],)),
            pltpu.SemaphoreType.DMA((counts[EVEN],)),
        ],
        compiler_params=pltpu.CompilerParams(vmem_limit_bytes=VMEM_LIMIT),
        name="merge_returned",
    )(plan, *odd, *even, *in_hbm(outs))


def swapped(value, kind):
    first = 0 if kind == ODD else 1
    pairs = [(block, block + 1) for block in range(first, lax.axis_size("dp") - 1, 2)]
    return lax.ppermute(value, "dp", pairs + [(after, before) for before, after in pairs])


def swap_further(choices, odd, even):
    counts = [len(odd), len(even)]
    if not sum(counts):
        return [], []
    pairs = [(first, second) for first in range(counts[0] + 1) for second in range(counts[1] + 1)]

    def send(used, odd, even):
        return tuple(
            [
                swapped(array, kind) if number == used[kind] else array
                for number, array in enumerate(arrays, start=1)
            ]
            for kind, arrays in ((ODD, odd), (EVEN, even))
        )

    index = 0
    for choice, count in zip(choices, counts):
        if count:
            index = index * (count + 1) + choice[0]
    branches = [functools.partial(send, pair) for pair in pairs]
    return lax.switch(index, branches, list(odd), list(even))


def body(queries, keys, values, out_grad, lengths):
    rows, width = queries.shape
    arrays = (queries, keys, values, out_grad)
    levels = [size_levels(kind, rows, width // HEAD_DIM) for kind in (ODD, EVEN)]
    plan, choices, even = pack_even(lengths, arrays, levels, lax.axis_size("dp"))
    even_first = swapped(even[0], EVEN)
    odd = pack_odd(plan, arrays, levels[ODD])
    odd_first = swapped(odd[0], ODD)
    done = width // HEAD_DIM // 2
    local = local_attention(lengths, arrays, done)
    choices, local = lax.optimization_barrier((choices, local))
    _, more = swap_further(choices, [], even[1:])
    back_even, kept_even = crossing_images(EVEN, plan, arrays, [even_first, *more], levels[EVEN])
    choices, kept_even = lax.optimization_barrier((choices, kept_even))
    more, _ = swap_further(choices, odd[1:], [])
    received = [odd_first, *more]
    first, received = lax.optimization_barrier((back_even[0], received))
    even_first = swapped(first, EVEN)
    back_odd, kept_odd = crossing_images(ODD, plan, arrays, received, levels[ODD])
    odd_first = swapped(back_odd[0], ODD)
    kept_odd, local = lax.optimization_barrier((kept_odd, local))
    outs = rest_of_images(plan, lengths, arrays, done, local, kept_odd, kept_even)
    even_first, choices, outs = lax.optimization_barrier((even_first, choices, outs))
    more_odd, more_even = swap_further(choices, back_odd[1:], back_even[1:])
    return tuple(merge_returned(
        plan, [odd_first, *more_odd], [even_first, *more_even], outs, levels))


def solution(mesh):
    in_specs = (P("dp", "tensor"), P("dp", "tensor"), P("dp", "tensor"), P("dp", "tensor"), P())
    out_specs = (P("dp", "tensor"), P("dp", "tensor"), P("dp", "tensor"), P("dp", "tensor"))
    return jax.shard_map(body, mesh=mesh, in_specs=in_specs, out_specs=out_specs, check_vma=False)
```
